32 devices in a mesh: fsdp: 4 (over y, x), ctx: 8 (over z, core).
Axes of the slice: x: 2, y: 2, z: 4, core: 2. Of those that a mesh axis runs over, the one named last changes fastest.
Arguments:
- hidden_in: bfloat16 [4, 2048, 1024], P('fsdp', 'ctx'), may hold values from -6 to 6
- teacher: bfloat16 [4, 2048, 1024], P('fsdp', 'ctx'), may hold values from -8 to 8
- valid: int32 [4, 2048], P('fsdp', 'ctx'), may hold values from 0 to 1, as said below
- positions: int32 [4, 2048], P('fsdp', 'ctx'), may hold values from 0 to 3071, as said below
- norm_attn: bfloat16 [1024], P('fsdp'), may hold values from 0.5 to 1.5
- w_query: bfloat16 [1024, 2048], P('fsdp'), may hold values from -0.1875 to 0.1875
- key_projection: bfloat16 [1024, 1024], P('fsdp'), may hold values from -0.1875 to 0.1875
- value_projection: bfloat16 [1024, 1024], P('fsdp'), may hold values from -0.1875 to 0.1875
- gain_query: bfloat16 [128], P('fsdp'), may hold values from 0.5 to 1.5
- gain_key: bfloat16 [128], P('fsdp'), may hold values from 0.5 to 1.5
- w_out: bfloat16 [2048, 1024], P('fsdp'), may hold values from -3 to 3
- norm_mlp: bfloat16 [1024], P('fsdp'), may hold values from 0.5 to 1.5
- w_gate: bfloat16 [1024, 3072], P('fsdp'), may hold values from -0.1875 to 0.1875
- w_up: bfloat16 [1024, 3072], P('fsdp'), may hold values from -0.1875 to 0.1875
- w_down: bfloat16 [3072, 1024], P('fsdp'), may hold values from -0.109375 to 0.109375
Outputs:
- output: bfloat16 [4, 2048, 1024], P('fsdp', 'ctx')
- loss: float32 [], replicated
- input_grad: float32 [4, 2048, 1024], P('fsdp', 'ctx')
- grad_norm_attn: float32 [1024], P('fsdp')
- grad_w_query: float32 [1024, 2048], P('fsdp')
- grad_w_key: float32 [1024, 1024], P('fsdp')
- grad_w_value: float32 [1024, 1024], P('fsdp')
- grad_gain_query: float32 [128], P('fsdp')
- grad_gain_key: float32 [128], P('fsdp')
- grad_w_out: float32 [2048, 1024], P('fsdp')
- grad_norm_mlp: float32 [1024], P('fsdp')
- grad_w_gate: float32 [1024, 3072], P('fsdp')
- grad_w_up: float32 [1024, 3072], P('fsdp')
- grad_w_down: float32 [3072, 1024], P('fsdp')
The draws below stay inside these ranges and needn't reach their ends.
Inputs may be any that keep to these rules, and one draw needn't show every extreme that they name: `valid`: 1 marks a token that the loss counts. positions start at 0 in each sequence and rise by 1 or 2 from token to token, by 2 at exactly 1024 of the steps.
All inputs are finite; a program needn't handle non-finite values.
Results may differ from the reference program's by a relative error of at most 0.028.
Values may be sent and summed in bfloat16 or wider, within the bound.
A program may use at most 192 MiB of HBM per device.

```python
import math
import jax
import jax.numpy as jnp
from jax import lax

MODEL_WIDTH = 1024
QUERY_HEADS = 16
KEY_VALUE_HEADS = 8
HEAD_SIZE = 128
FF = 3072
SEQ = 2048
SEQS = 4
TOKENS = 8192


def draw_teacher(key, part):
    key = jax.random.fold_in(key, 11)
    position = jnp.arange(SEQ, dtype=jnp.float32) / SEQ
    sequence_share = jnp.arange(SEQS, dtype=jnp.float32) / max(SEQS - 1, 1)
    values = jnp.clip(jax.random.normal(key, (SEQS, SEQ, MODEL_WIDTH), jnp.float32), -2.8, 2.8)
    spread = (0.5 + 1.5 * position)[None, :] * (0.6 + 0.8 * sequence_share)[:, None]
    return (values * spread[:, :, None]).astype(jnp.bfloat16)


def draw_valid(key, part):
    key = jax.random.fold_in(key, 23)
    token_level = 250 * jnp.arange(SEQ, dtype=jnp.int32) // SEQ
    sequence_level = 600 * jnp.arange(SEQS, dtype=jnp.int32) // max(SEQS - 1, 1)
    levels = 100 + sequence_level[:, None] + token_level[None, :]
    ticket = jax.random.randint(key, (SEQS, SEQ), 0, 1000, dtype=jnp.int32)
    return (ticket < levels).astype(jnp.int32)


def draw_positions(key, part):
    key = jax.random.fold_in(key, 37)
    row_keys = jax.random.split(key, SEQS)

    def one_row(row_key):
        order = jax.random.permutation(row_key, SEQ - 1)
        steps_row = 1 + (order < SEQ // 2).astype(jnp.int32)
        return jnp.concatenate([jnp.zeros((1,), jnp.int32), jnp.cumsum(steps_row).astype(jnp.int32)])
    return jax.vmap(one_row)(row_keys).astype(jnp.int32)


def steps_of(key, shape, shards, least, top_value):
    def one(dim, blocks):
        draws = jax.random.uniform(jax.random.fold_in(jax.random.fold_in(key, 6), dim), (blocks,), jnp.float32, least / len(shards), top_value / len(shards))
        return jnp.repeat(jnp.exp(draws), shape[dim] // blocks).reshape((-1,) + (1,) * (len(shape) - dim - 1))

    level = one(*shards[0])
    for cut in shards[1:]:
        level = level * one(*cut)
    return level


def noise(rng, extent, scale, limit, shards=(), held_as=jnp.bfloat16):
    array = jax.random.normal(rng, extent, jnp.float32) * scale
    if len(shards) > 0:
        array = steps_of(rng, extent, shards, -0.22, 0.18) * array
    return jnp.clip(array, min=-limit, max=limit).astype(held_as)


def setup_inputs(seed: int = 0) -> dict:
    keys = jax.random.split(jax.random.key(seed), 16)
    return {
        "hidden_in": noise(keys[0], (SEQS, SEQ, MODEL_WIDTH), 1.0, 6.0, ((0, 4), (1, 8))),
        "teacher": draw_teacher(jax.random.fold_in(keys[15], 71), 0),
        "valid": draw_valid(jax.random.fold_in(keys[15], 71), 0),
        "positions": draw_positions(jax.random.fold_in(keys[15], 71), 0),
        "norm_attn": jnp.clip(1.0 + 0.1 * jax.random.normal(keys[4], (MODEL_WIDTH,), jnp.float32), 0.5, 1.5).astype(jnp.bfloat16),
        "w_query": noise(keys[5], (MODEL_WIDTH, QUERY_HEADS * HEAD_SIZE), MODEL_WIDTH ** -0.5, 0.1875, ((0, 4),)),
        "key_projection": noise(keys[6], (MODEL_WIDTH, KEY_VALUE_HEADS * HEAD_SIZE), MODEL_WIDTH ** -0.5, 0.1875, ((0, 4),)),
        "value_projection": noise(keys[7], (MODEL_WIDTH, KEY_VALUE_HEADS * HEAD_SIZE), MODEL_WIDTH ** -0.5, 0.1875, ((0, 4),)),
        "gain_query": jnp.clip(1.0 + 0.1 * jax.random.normal(keys[8], (HEAD_SIZE,), jnp.float32), 0.5, 1.5).astype(jnp.bfloat16),
        "gain_key": jnp.clip(1.0 + 0.1 * jax.random.normal(keys[9], (HEAD_SIZE,), jnp.float32), 0.5, 1.5).astype(jnp.bfloat16),
        "w_out": noise(keys[10], (QUERY_HEADS * HEAD_SIZE, MODEL_WIDTH), (max(1, 4 * QUERY_HEADS * HEAD_SIZE // SEQ)) ** -0.5, 3.0, ((0, 4),)),
        "norm_mlp": jnp.clip(1.0 + 0.1 * jax.random.normal(keys[11], (MODEL_WIDTH,), jnp.float32), 0.5, 1.5).astype(jnp.bfloat16),
        "w_gate": noise(keys[12], (MODEL_WIDTH, FF), MODEL_WIDTH ** -0.5, 0.1875, ((0, 4),)),
        "w_up": noise(keys[13], (MODEL_WIDTH, FF), MODEL_WIDTH ** -0.5, 0.1875, ((0, 4),)),
        "w_down": noise(keys[14], (FF, MODEL_WIDTH), FF ** -0.5, 0.109375, ((0, 4),)),
    }


EPSILON = 1e-06
BEST_PRECISION = lax.Precision.HIGHEST

@jax.custom_vjp
def reduced_precision(v):
    return lax.optimization_barrier(v.astype(jnp.bfloat16)).astype(jnp.float32)

@jax.custom_vjp
def low_back(v):
    return v

def low_keep(v):
    return (reduced_precision(v), None)

def low_pass(kept, grad):
    return (grad,)

def back_keep(v):
    return (v, None)

def back_low(kept, grad):
    return (reduced_precision(grad),)
reduced_precision.defvjp(low_keep, low_pass)
low_back.defvjp(back_keep, back_low)

def root_mean_norm(values, norm_gain):
    return values * lax.rsqrt(lax.optimization_barrier(jnp.mean(values * values, axis=-1, keepdims=True)) + EPSILON) * norm_gain

def rope_tables(position_ids):
    half_width = HEAD_SIZE // 2
    freq_table = jnp.exp(jnp.arange(half_width, dtype=jnp.float32) * (-2.0 * math.log(1000000.0) / HEAD_SIZE))
    angle_table = position_ids.astype(jnp.float32)[:, None] * freq_table[None, :]
    cosine_table = jnp.cos(angle_table)
    sine_table = jnp.sin(angle_table)
    return (jnp.concatenate([cosine_table, cosine_table], -1), jnp.concatenate([-sine_table, sine_table], -1))

def apply_rotary(values, cosine_table, sine_table):
    half_width = HEAD_SIZE // 2
    swapped = jnp.concatenate([values[..., half_width:], values[..., :half_width]], -1)
    return values * cosine_table[:, None, :] + swapped * sine_table[:, None, :]

def attend_block(block_of_queries, block_start, rows_of_keys, rows_of_values):
    block_extent = block_of_queries.shape[0]
    score_matrix = jnp.einsum('alci,wli->lcaw', block_of_queries, rows_of_keys, precision=BEST_PRECISION)
    score_matrix = low_back(score_matrix)
    logits = score_matrix * (1.0 / math.sqrt(HEAD_SIZE))
    query_index = block_start + jnp.arange(block_extent, dtype=jnp.int32)
    key_index = jnp.arange(rows_of_keys.shape[0], dtype=jnp.int32)
    allowed = key_index[None, :] <= query_index[:, None]
    logits = jnp.where(allowed, logits, -1e+30)
    top_logit = lax.optimization_barrier(jnp.max(logits, axis=-1, keepdims=True))
    expo = jnp.exp(logits - top_logit)
    attention_probabilities = expo / lax.optimization_barrier(jnp.sum(expo, axis=-1, keepdims=True))
    attention_probabilities = reduced_precision(attention_probabilities)
    return jnp.einsum('jyux,xji->ujyi', attention_probabilities, rows_of_values, precision=BEST_PRECISION)

def layer(sequence_in, seq_positions, params):
    gain_one, wq_full, wk_full, wv_full, gain_q, key_gain, wo_full, gain_two, wg_full, wu_full, wd_full = params
    sequence_rows = sequence_in.shape[0]
    grouped_heads = QUERY_HEADS // KEY_VALUE_HEADS
    hidden_one = reduced_precision(root_mean_norm(sequence_in, gain_one))
    proj_query = low_back(jnp.dot(hidden_one, wq_full, precision=BEST_PRECISION))
    projected_key = low_back(jnp.dot(hidden_one, wk_full, precision=BEST_PRECISION))
    projected_value = low_back(jnp.dot(hidden_one, wv_full, precision=BEST_PRECISION))
    cosine_table, sine_table = rope_tables(seq_positions)
    query_rows = reduced_precision(apply_rotary(root_mean_norm(proj_query.reshape(sequence_rows, QUERY_HEADS, HEAD_SIZE), gain_q), cosine_table, sine_table))
    rows_of_keys = reduced_precision(apply_rotary(root_mean_norm(projected_key.reshape(sequence_rows, KEY_VALUE_HEADS, HEAD_SIZE), key_gain), cosine_table, sine_table))
    rows_of_values = reduced_precision(projected_value).reshape(sequence_rows, KEY_VALUE_HEADS, HEAD_SIZE)
    block_extent = math.gcd(sequence_rows, 512)
    total_blocks = sequence_rows // block_extent
    query_block_list = query_rows.reshape(total_blocks, block_extent, KEY_VALUE_HEADS, grouped_heads, HEAD_SIZE)
    starts = jnp.arange(total_blocks, dtype=jnp.int32) * block_extent
    checked = jax.checkpoint(attend_block)
    attended = lax.map(lambda scan_item: checked(scan_item[0], scan_item[1], rows_of_keys, rows_of_values), (query_block_list, starts))
    attn_low = reduced_precision(low_back(attended.reshape(sequence_rows, QUERY_HEADS * HEAD_SIZE)))
    mid_resid = sequence_in + low_back(jnp.dot(attn_low, wo_full, precision=BEST_PRECISION))
    hidden_two = reduced_precision(root_mean_norm(mid_resid, gain_two))
    gate_proj = low_back(jnp.dot(hidden_two, wg_full, precision=BEST_PRECISION))
    up_proj = low_back(jnp.dot(hidden_two, wu_full, precision=BEST_PRECISION))
    gated = reduced_precision(gate_proj / (1.0 + jnp.exp(-gate_proj)) * up_proj)
    return mid_resid + low_back(jnp.dot(gated, wd_full, precision=BEST_PRECISION))

def reference(hidden_in, teacher, valid, positions, norm_attn, w_query, key_projection, value_projection, gain_query, gain_key, w_out, norm_mlp, w_gate, w_up, w_down):
    params = tuple((weight_arr.astype(jnp.float32) for weight_arr in (norm_attn, w_query, key_projection, value_projection, gain_query, gain_key, w_out, norm_mlp, w_gate, w_up, w_down)))
    layer_in = hidden_in.astype(jnp.float32)
    target = teacher.astype(jnp.float32)
    weight_rows = valid.astype(jnp.float32)

    def total_loss(layer_input, layer_params):
        final_rows = lax.map(lambda scan_item: layer(scan_item[0], scan_item[1], layer_params), (layer_input, positions))
        count_total = jnp.sum(weight_rows)
        mismatch = final_rows - target
        sq_total = jnp.sum(weight_rows[..., None] * mismatch * mismatch)
        return (sq_total / count_total, final_rows)
    loss_value, backward, final_rows = jax.vjp(total_loss, layer_in, params, has_aux=True)
    grad_input, grads = backward(jnp.asarray(TOKENS / 4.0, dtype=jnp.float32))
    return (final_rows.astype(jnp.bfloat16), loss_value, grad_input, grads[0], grads[1], grads[2], grads[3], grads[4], grads[5], grads[6], grads[7], grads[8], grads[9], grads[10])
```

```python
from functools import partial
import math

import jax
import jax.numpy as jnp
from jax import lax
from jax.experimental import pallas as pl
from jax.experimental.pallas import tpu as pltpu
from jax.sharding import PartitionSpec as P

QUERY_HEADS = 16
KEY_VALUE_HEADS = 8
HEAD_SIZE = 128


EPSILON = 1e-06


def root_mean_norm(values, norm_gain):
    return (
        values * lax.rsqrt(jnp.mean(values * values, axis=-1, keepdims=True) + EPSILON) * norm_gain
    )


def rope_tables(position_ids):
    half_width = HEAD_SIZE // 2
    freq_table = jnp.exp(
        jnp.arange(half_width, dtype=jnp.float32) * (-2.0 * math.log(1000000.0) / HEAD_SIZE)
    )
    angle_table = position_ids.astype(jnp.float32)[:, None] * freq_table[None, :]
    cosine_table = jnp.cos(angle_table)
    sine_table = jnp.sin(angle_table)
    return (
        jnp.concatenate([cosine_table, cosine_table], -1),
        jnp.concatenate([-sine_table, sine_table], -1),
    )


def apply_rotary(values, cosine_table, sine_table):
    half_width = HEAD_SIZE // 2
    swapped = jnp.concatenate([values[..., half_width:], values[..., :half_width]], -1)
    return values * cosine_table[:, None, :] + swapped * sine_table[:, None, :]


def shape_heads(cosine_table, sine_table, proj_query, projected_key, gain_q, key_gain):
    token_rows = proj_query.shape[0]
    query_rows = apply_rotary(
        root_mean_norm(proj_query.reshape(token_rows, QUERY_HEADS, HEAD_SIZE), gain_q),
        cosine_table,
        sine_table,
    )
    rows_of_keys = apply_rotary(
        root_mean_norm(projected_key.reshape(token_rows, KEY_VALUE_HEADS, HEAD_SIZE), key_gain),
        cosine_table,
        sine_table,
    )
    return (query_rows, rows_of_keys)


def swiglu(gate_proj, up_proj):
    return gate_proj / (1.0 + jnp.exp(-gate_proj)) * up_proj


def contract_rows(left_arr, right_arr):
    return lax.dot_general(
        left_arr, right_arr, (((0,), (0,)), ((), ())), preferred_element_type=jnp.float32
    )


def against(left_arr, right_arr):
    return lax.dot_general(
        left_arr, right_arr, (((1,), (1,)), ((), ())), preferred_element_type=jnp.float32
    )


def in_blocks(block_step, running, shard_portion):
    total_rows = shard_portion.shape[0]
    block_extent = 512
    block_count = total_rows // block_extent
    blocks = shard_portion.reshape((block_count, block_extent) + shard_portion.shape[1:])
    starts = jnp.arange(block_count, dtype=jnp.int32) * block_extent

    def scan_body(state, scan_item):
        return (block_step(state, scan_item[0], scan_item[1]), None)

    running, unused = lax.scan(scan_body, running, (blocks, starts))
    return running


def score_terms(
    query_rows,
    output_gradients,
    lse_heads,
    delta_heads,
    rows_of_keys,
    rows_of_values,
    query_index,
    key_index,
    score_scale,
):
    score_matrix = (
        jnp.einsum("alci,wli->lcaw", query_rows, rows_of_keys, preferred_element_type=jnp.float32)
        * score_scale
    )
    allowed = key_index[None, :] <= query_index[:, None]
    attention_probabilities = jnp.where(allowed, jnp.exp(score_matrix - lse_heads[..., None]), 0.0)
    grad_probs = jnp.einsum(
        "alci,wli->lcaw", output_gradients, rows_of_values, preferred_element_type=jnp.float32
    )
    score_gradient = (
        score_scale * attention_probabilities * (grad_probs - delta_heads[..., None])
    ).astype(jnp.bfloat16)
    return (attention_probabilities, score_gradient)


def per_device(
    hidden_in,
    teacher,
    valid,
    positions,
    norm_attn,
    w_query,
    key_projection,
    value_projection,
    gain_query,
    gain_key,
    w_out,
    norm_mlp,
    w_gate,
    w_up,
    w_down,
):
    gathered = (
        lax.all_gather(norm_attn, "fsdp", axis=0, tiled=True),
        lax.all_gather(w_query, "fsdp", axis=0, tiled=True),
        lax.all_gather(key_projection, "fsdp", axis=0, tiled=True),
        lax.all_gather(value_projection, "fsdp", axis=0, tiled=True),
        lax.all_gather(gain_query, "fsdp", axis=0, tiled=True),
        lax.all_gather(gain_key, "fsdp", axis=0, tiled=True),
        lax.all_gather(w_out, "fsdp", axis=0, tiled=True),
        lax.all_gather(norm_mlp, "fsdp", axis=0, tiled=True),
        lax.all_gather(w_gate, "fsdp", axis=0, tiled=True),
        lax.all_gather(w_up, "fsdp", axis=0, tiled=True),
        lax.all_gather(w_down, "fsdp", axis=0, tiled=True),
    )
    (
        full_norm_attn,
        full_query,
        full_key,
        full_value,
        full_gain_q,
        full_gain_k,
        full_out,
        full_norm_mlp,
        full_gate,
        full_up,
        full_down,
    ) = gathered
    grouped_heads = QUERY_HEADS // KEY_VALUE_HEADS
    score_scale = 1.0 / math.sqrt(HEAD_SIZE)
    residual = hidden_in[0].astype(jnp.float32)
    token_rows = residual.shape[0]
    query_index = lax.axis_index("ctx") * token_rows + jnp.arange(token_rows, dtype=jnp.int32)
    normed_one, norm_one_back = jax.vjp(
        root_mean_norm, residual, full_norm_attn.astype(jnp.float32)
    )
    hidden_one = normed_one.astype(jnp.bfloat16)
    proj_query = jnp.dot(hidden_one, full_query, preferred_element_type=jnp.float32)
    projected_key = jnp.dot(hidden_one, full_key, preferred_element_type=jnp.float32)
    projected_value = jnp.dot(hidden_one, full_value, preferred_element_type=jnp.float32)
    cosine_table, sine_table = rope_tables(positions[0])
    (query_per_head, heads_key), heads_back = jax.vjp(
        partial(shape_heads, cosine_table, sine_table),
        proj_query,
        projected_key,
        full_gain_q.astype(jnp.float32),
        full_gain_k.astype(jnp.float32),
    )
    query_reduced = query_per_head.astype(jnp.bfloat16).reshape(
        token_rows, KEY_VALUE_HEADS, grouped_heads, HEAD_SIZE
    )
    key_reduced = heads_key.astype(jnp.bfloat16)
    value_reduced = projected_value.astype(jnp.bfloat16).reshape(
        token_rows, KEY_VALUE_HEADS, HEAD_SIZE
    )
    key_value = jnp.stack(
        [
            key_reduced.reshape(token_rows, KEY_VALUE_HEADS * HEAD_SIZE),
            value_reduced.reshape(token_rows, KEY_VALUE_HEADS * HEAD_SIZE),
        ],
        axis=1,
    )

    def forward_block(running, shard_portion, first_row):
        run_max, run_total, run_acc = running
        rows_per_block = shard_portion.shape[0]
        rows_of_keys = shard_portion[:, 0].reshape(rows_per_block, KEY_VALUE_HEADS, HEAD_SIZE)
        rows_of_values = shard_portion[:, 1].reshape(rows_per_block, KEY_VALUE_HEADS, HEAD_SIZE)
        key_index = first_row + jnp.arange(rows_per_block, dtype=jnp.int32)
        allowed = key_index[None, :] <= query_index[:, None]
        score_matrix = (
            jnp.einsum(
                "alci,wli->lcaw", query_reduced, rows_of_keys, preferred_element_type=jnp.float32
            )
            * score_scale
        )
        score_matrix = jnp.where(allowed, score_matrix, -1e30)
        new_max = jnp.maximum(run_max, jnp.max(score_matrix, axis=-1))
        weights_part = jnp.where(allowed, jnp.exp(score_matrix - new_max[..., None]), 0.0)
        factor = jnp.exp(run_max - new_max)
        run_total = run_total * factor + jnp.sum(weights_part, axis=-1)
        run_acc = run_acc * factor[..., None] + jnp.einsum(
            "exfw,weq->exfq",
            weights_part.astype(jnp.bfloat16),
            rows_of_values,
            preferred_element_type=jnp.float32,
        )
        return (new_max, run_total, run_acc)

    start_state = (
        jnp.full((KEY_VALUE_HEADS, grouped_heads, token_rows), -1e30, jnp.float32),
        jnp.zeros((KEY_VALUE_HEADS, grouped_heads, token_rows), jnp.float32),
        jnp.zeros((KEY_VALUE_HEADS, grouped_heads, token_rows, HEAD_SIZE), jnp.float32),
    )
    run_max, run_total, run_acc = in_blocks(
        forward_block, start_state, lax.all_gather(key_value, "ctx", axis=0, tiled=True)
    )
    log_total = run_max + jnp.log(run_total)
    attn_rows = jnp.transpose(run_acc / run_total[..., None], (2, 0, 1, 3))
    attn_low = attn_rows.reshape(token_rows, QUERY_HEADS * HEAD_SIZE).astype(jnp.bfloat16)
    mid_resid = residual + jnp.dot(attn_low, full_out, preferred_element_type=jnp.float32)
    normed_two, norm_two_back = jax.vjp(
        root_mean_norm, mid_resid, full_norm_mlp.astype(jnp.float32)
    )
    hidden_two = normed_two.astype(jnp.bfloat16)
    gate_proj = jnp.dot(hidden_two, full_gate, preferred_element_type=jnp.float32)
    up_proj = jnp.dot(hidden_two, full_up, preferred_element_type=jnp.float32)
    gated, gated_back = jax.vjp(swiglu, gate_proj, up_proj)
    gated_low = gated.astype(jnp.bfloat16)
    final_rows = mid_resid + jnp.dot(gated_low, full_down, preferred_element_type=jnp.float32)
    target = teacher[0].astype(jnp.float32)
    weight_rows = valid[0].astype(jnp.float32)
    mismatch = final_rows - target
    sq_local = jnp.sum(weight_rows[:, None] * mismatch * mismatch)
    count_local = jnp.sum(weight_rows)
    sq_total, count_total = lax.psum((sq_local, count_local), ("fsdp", "ctx"))
    loss_value = sq_total / count_total
    loss_scale = token_rows * lax.axis_size("ctx") * lax.axis_size("fsdp") / 4.0
    grad_final = 2.0 * loss_scale / count_total * weight_rows[:, None] * mismatch
    grad_down_in = grad_final.astype(jnp.bfloat16)
    grad_w_down = contract_rows(gated_low, grad_down_in)
    grad_gated = against(grad_down_in, full_down)
    grad_gate_proj, grad_up_proj = gated_back(grad_gated)
    gate_low = grad_gate_proj.astype(jnp.bfloat16)
    up_low = grad_up_proj.astype(jnp.bfloat16)
    grad_w_gate = contract_rows(hidden_two, gate_low)
    grad_w_up = contract_rows(hidden_two, up_low)
    grad_hidden_two = against(gate_low, full_gate) + against(up_low, full_up)
    grad_mid_norm, grad_norm_mlp = norm_two_back(grad_hidden_two)
    grad_mid = grad_final + grad_mid_norm
    grad_branch = grad_mid.astype(jnp.bfloat16)
    grad_w_out = contract_rows(attn_low, grad_branch)
    attention_gradient = against(grad_branch, full_out).astype(jnp.bfloat16)
    attention_head_gradient = attention_gradient.reshape(
        token_rows, KEY_VALUE_HEADS, grouped_heads, HEAD_SIZE
    )
    row_delta = jnp.sum(attention_head_gradient.astype(jnp.float32) * attn_rows, axis=-1)
    delta_heads = jnp.transpose(row_delta, (1, 2, 0))
    row_stats = jnp.stack(
        [
            jnp.transpose(log_total, (2, 0, 1)).reshape(token_rows, QUERY_HEADS),
            row_delta.reshape(token_rows, QUERY_HEADS),
        ],
        axis=1,
    )

    def block_of_queries(grad_query, shard_portion, first_row):
        rows_per_block = shard_portion.shape[0]
        rows_of_keys = shard_portion[:, 0].reshape(rows_per_block, KEY_VALUE_HEADS, HEAD_SIZE)
        rows_of_values = shard_portion[:, 1].reshape(rows_per_block, KEY_VALUE_HEADS, HEAD_SIZE)
        key_index = first_row + jnp.arange(rows_per_block, dtype=jnp.int32)
        attention_probabilities, score_gradient = score_terms(
            query_reduced,
            attention_head_gradient,
            log_total,
            delta_heads,
            rows_of_keys,
            rows_of_values,
            query_index,
            key_index,
            score_scale,
        )
        return grad_query + jnp.einsum(
            "jyux,xji->ujyi", score_gradient, rows_of_keys, preferred_element_type=jnp.float32
        )

    grad_query = in_blocks(
        block_of_queries,
        jnp.zeros((token_rows, KEY_VALUE_HEADS, grouped_heads, HEAD_SIZE), jnp.float32),
        lax.all_gather(key_value, "ctx", axis=0, tiled=True),
    )
    all_stats = lax.all_gather(row_stats.astype(jnp.bfloat16), "ctx", axis=0, tiled=True).astype(
        row_stats.dtype
    )
    query_pair = jnp.stack(
        [query_reduced.reshape(token_rows, QUERY_HEADS * HEAD_SIZE), attention_gradient], axis=1
    )

    def key_block(running, shard_portion, first_row):
        grad_key, value_gradient = running
        rows_per_block = shard_portion.shape[0]
        query_rows = shard_portion[:, 0].reshape(
            rows_per_block, KEY_VALUE_HEADS, grouped_heads, HEAD_SIZE
        )
        output_gradients = shard_portion[:, 1].reshape(
            rows_per_block, KEY_VALUE_HEADS, grouped_heads, HEAD_SIZE
        )
        partial_statistics = lax.dynamic_slice_in_dim(all_stats, first_row, rows_per_block, 0)
        partial_logsumexp = jnp.transpose(
            partial_statistics[:, 0].reshape(rows_per_block, KEY_VALUE_HEADS, grouped_heads),
            (1, 2, 0),
        )
        partial_delta = jnp.transpose(
            partial_statistics[:, 1].reshape(rows_per_block, KEY_VALUE_HEADS, grouped_heads),
            (1, 2, 0),
        )
        part_index = first_row + jnp.arange(rows_per_block, dtype=jnp.int32)
        attention_probabilities, score_gradient = score_terms(
            query_rows,
            output_gradients,
            partial_logsumexp,
            partial_delta,
            key_reduced,
            value_reduced,
            part_index,
            query_index,
            score_scale,
        )
        grad_key = grad_key + jnp.einsum(
            "wzlj,lwzy->jwy", score_gradient, query_rows, preferred_element_type=jnp.float32
        )
        value_gradient = value_gradient + jnp.einsum(
            "wzlj,lwzy->jwy",
            attention_probabilities.astype(jnp.bfloat16),
            output_gradients,
            preferred_element_type=jnp.float32,
        )
        return (grad_key, value_gradient)

    key_state = (
        jnp.zeros((token_rows, KEY_VALUE_HEADS, HEAD_SIZE), jnp.float32),
        jnp.zeros((token_rows, KEY_VALUE_HEADS, HEAD_SIZE), jnp.float32),
    )
    grad_key, value_gradient = in_blocks(
        key_block, key_state, lax.all_gather(query_pair, "ctx", axis=0, tiled=True)
    )
    grad_proj_q, grad_proj_k, grad_gain_q, grad_gain_k = heads_back(
        (grad_query.reshape(token_rows, QUERY_HEADS, HEAD_SIZE), grad_key)
    )
    query_grad_low = grad_proj_q.astype(jnp.bfloat16)
    key_grad_low = grad_proj_k.astype(jnp.bfloat16)
    value_gradient_reduced = value_gradient.reshape(token_rows, KEY_VALUE_HEADS * HEAD_SIZE).astype(
        jnp.bfloat16
    )
    grad_w_query = contract_rows(hidden_one, query_grad_low)
    grad_w_key = contract_rows(hidden_one, key_grad_low)
    grad_w_value = contract_rows(hidden_one, value_gradient_reduced)
    grad_hidden_one = (
        against(query_grad_low, full_query)
        + against(key_grad_low, full_key)
        + against(value_gradient_reduced, full_value)
    )
    grad_resid_norm, grad_norm_attn = norm_one_back(grad_hidden_one)
    grad_input = grad_mid + grad_resid_norm
    grads = (
        grad_norm_attn,
        grad_w_query,
        grad_w_key,
        grad_w_value,
        grad_gain_q,
        grad_gain_k,
        grad_w_out,
        grad_norm_mlp,
        grad_w_gate,
        grad_w_up,
        grad_w_down,
    )
    shares = (
        lax.psum_scatter(grads[0], ("fsdp", "ctx"), scatter_dimension=0, tiled=True),
        lax.psum_scatter(grads[1], ("fsdp", "ctx"), scatter_dimension=0, tiled=True),
        lax.psum_scatter(grads[2], ("fsdp", "ctx"), scatter_dimension=0, tiled=True),
        lax.psum_scatter(grads[3], ("fsdp", "ctx"), scatter_dimension=0, tiled=True),
        lax.psum_scatter(grads[4], ("fsdp", "ctx"), scatter_dimension=0, tiled=True),
        lax.psum_scatter(grads[5], ("fsdp", "ctx"), scatter_dimension=0, tiled=True),
        lax.psum_scatter(grads[6], ("fsdp", "ctx"), scatter_dimension=0, tiled=True),
        lax.psum_scatter(grads[7], ("fsdp", "ctx"), scatter_dimension=0, tiled=True),
        lax.psum_scatter(grads[8], ("fsdp", "ctx"), scatter_dimension=0, tiled=True),
        lax.psum_scatter(grads[9], ("fsdp", "ctx"), scatter_dimension=0, tiled=True),
        lax.psum_scatter(grads[10], ("fsdp", "ctx"), scatter_dimension=0, tiled=True),
    )
    shares = (
        lax.all_gather(shares[0].astype(jnp.bfloat16), "ctx", axis=0, tiled=True).astype(
            jnp.float32
        ),
        lax.all_gather(shares[1].astype(jnp.bfloat16), "ctx", axis=0, tiled=True).astype(
            jnp.float32
        ),
        lax.all_gather(shares[2].astype(jnp.bfloat16), "ctx", axis=0, tiled=True).astype(
            jnp.float32
        ),
        lax.all_gather(shares[3].astype(jnp.bfloat16), "ctx", axis=0, tiled=True).astype(
            jnp.float32
        ),
        lax.all_gather(shares[4].astype(jnp.bfloat16), "ctx", axis=0, tiled=True).astype(
            jnp.float32
        ),
        lax.all_gather(shares[5].astype(jnp.bfloat16), "ctx", axis=0, tiled=True).astype(
            jnp.float32
        ),
        lax.all_gather(shares[6].astype(jnp.bfloat16), "ctx", axis=0, tiled=True).astype(
            jnp.float32
        ),
        lax.all_gather(shares[7].astype(jnp.bfloat16), "ctx", axis=0, tiled=True).astype(
            jnp.float32
        ),
        lax.all_gather(shares[8].astype(jnp.bfloat16), "ctx", axis=0, tiled=True).astype(
            jnp.float32
        ),
        lax.all_gather(shares[9].astype(jnp.bfloat16), "ctx", axis=0, tiled=True).astype(
            jnp.float32
        ),
        lax.all_gather(shares[10].astype(jnp.bfloat16), "ctx", axis=0, tiled=True).astype(
            jnp.float32
        ),
    )
    return (
        final_rows.astype(jnp.bfloat16)[None],
        loss_value,
        grad_input[None],
        shares[0],
        shares[1],
        shares[2],
        shares[3],
        shares[4],
        shares[5],
        shares[6],
        shares[7],
        shares[8],
        shares[9],
        shares[10],
    )


MESH = pl.DeviceIdType.MESH
BF16 = jnp.bfloat16
F32 = jnp.float32
GROUP = QUERY_HEADS // KEY_VALUE_HEADS
HEAD_COLUMNS = (GROUP + 2) * HEAD_SIZE
SCALE = 1.0 / math.sqrt(HEAD_SIZE)
VMEM_LIMIT = 56 * 1024 * 1024


class Place:
    def __init__(self):
        self.f = lax.axis_index("fsdp")
        self.c = lax.axis_index("ctx")
        self.z = self.c // 2
        self.k = self.c % 2
        self.fx = self.f + 1 - 2 * (self.f % 2)
        self.fy = (self.f + 2) % 4
        self.fd = 3 - self.f
        self.xp = (self.fx, self.c)
        self.yp = (self.fy, self.c)
        self.dp = (self.fd, self.c)
        self.sib = (self.f, self.c + 1 - 2 * self.k)

    def along_z(self, step):
        other = (self.z + step) % 4
        return other, (self.f, 2 * other + self.k)

    def along_ctx(self, step):
        other = (self.c + step) % 8
        return other, (self.f, other)


def greet(partners):
    barrier = pltpu.get_barrier_semaphore()
    for partner in partners:
        pl.semaphore_signal(barrier, inc=1, device_id=partner, device_id_type=MESH)
    pl.semaphore_wait(barrier, len(partners))


class Copies:
    def __init__(self, send, recv):
        self.send, self.recv, self.used = send, recv, 0

    def take(self, count):
        first = self.used
        self.used += count
        return first

    def at(self, index, src, dst, partner):
        return pltpu.make_async_remote_copy(
            src_ref=src,
            dst_ref=dst,
            send_sem=self.send.at[index],
            recv_sem=self.recv.at[index],
            device_id=partner,
            device_id_type=MESH,
        )

    def __call__(self, src, dst, partner):
        return self.at(self.take(1), src, dst, partner)


class Locals:
    def __init__(self, sems):
        self.sems, self.used, self.open = sems, 0, []

    def __call__(self, src, dst):
        copy = pltpu.make_async_copy(src, dst, self.sems.at[self.used])
        self.used += 1
        copy.start()
        self.open.append(copy)
        return copy

    def wait(self):
        for copy in self.open:
            copy.wait()
        self.open = []


def add_rows(dst, sources):
    rows = dst.shape[0]
    step = 32

    @pl.loop(0, rows // step)
    def _(i):
        part = pl.ds(pl.multiple_of(i * step, step), step)
        total = sources[0][part, :].astype(F32)
        for source in sources[1:]:
            total = total + source[part, :].astype(F32)
        dst[part, :] = total.astype(dst.dtype)


class Gather:
    def __init__(self, me, copies, buf):
        half = buf.shape[1] // 2
        a, b = pl.ds(0, half), pl.ds(half, half)
        own_a, own_b = buf.at[me.f, a], buf.at[me.f, b]
        self.a_x = copies(own_a, own_a, me.xp)
        self.b_y = copies(own_b, own_b, me.yp)
        self.b_x = copies(own_b, own_b, me.xp)
        self.a_y = copies(own_a, own_a, me.yp)
        self.on_y = copies(buf.at[me.fx, a], buf.at[me.fx, a], me.yp)
        self.on_x = copies(buf.at[me.fy, b], buf.at[me.fy, b], me.xp)

    def first(self):
        self.a_x.start()
        self.b_y.start()

    def second(self):
        self.b_x.start()
        self.a_y.start()

    def relay(self):
        self.a_x.wait_recv()
        self.on_y.start()
        self.b_y.wait_recv()
        self.on_x.start()

    def finish(self):
        for copy in (self.b_x, self.a_y, self.on_y, self.on_x):
            copy.wait_recv()
        for copy in (self.a_x, self.b_y, self.b_x, self.a_y, self.on_y, self.on_x):
            copy.wait_send()


def scatter_buffers(rows, columns):
    half = rows // 2
    return [pltpu.VMEM((12, half, columns), BF16)]


class Scatter:
    def __init__(self, me, copies, local, part, bufs):
        half = part.shape[1] // 2
        a, b = pl.ds(0, half), pl.ds(half, half)
        slot = [bufs.at[i] for i in range(12)]
        self.fwd_a, self.fwd_b, self.own_a, self.own_b = slot[0:4]
        self.rx_own, self.rx_fwd, self.ry_own, self.ry_fwd, self.r2_a, self.r2_b = slot[4:10]
        self.sum_a, self.sum_b = slot[10:12]
        self.d_x = copies(part.at[me.fd, a], self.rx_fwd, me.xp)
        self.d_y = copies(part.at[me.fd, b], self.ry_fwd, me.yp)
        self.o_x = copies(part.at[me.fx, a], self.rx_own, me.xp)
        self.o_y = copies(part.at[me.fy, b], self.ry_own, me.yp)
        self.to_y = copies(self.fwd_a, self.r2_a, me.yp)
        self.to_x = copies(self.fwd_b, self.r2_b, me.xp)
        self.local, self.me, self.part, self.a, self.b = local, me, part, a, b

    def first(self):
        self.d_x.start()
        self.d_y.start()

    def second(self):
        self.o_x.start()
        self.o_y.start()
        me, part = self.me, self.part
        self.mine = [
            self.local(part.at[me.fy, self.a], self.fwd_a),
            self.local(part.at[me.fx, self.b], self.fwd_b),
            self.local(part.at[me.f, self.a], self.own_a),
            self.local(part.at[me.f, self.b], self.own_b),
        ]

    def relay(self):
        for copy in self.mine:
            copy.wait()
        self.d_x.wait_recv()
        add_rows(self.fwd_a, [self.fwd_a, self.rx_fwd])
        self.to_y.start()
        self.d_y.wait_recv()
        add_rows(self.fwd_b, [self.fwd_b, self.ry_fwd])
        self.to_x.start()

    def finish(self, sum_a, sum_b):
        self.o_x.wait_recv()
        self.to_y.wait_recv()
        add_rows(sum_a, [self.own_a, self.rx_own, self.r2_a])
        self.o_y.wait_recv()
        self.to_x.wait_recv()
        add_rows(sum_b, [self.own_b, self.ry_own, self.r2_b])

    def drain(self):
        for copy in (self.d_x, self.d_y, self.o_x, self.o_y, self.to_y, self.to_x):
            copy.wait_send()


class LineSum:
    def __init__(self, me, copies, own, bufs):
        z, f, k = me.z, me.f, me.k
        self.inner = (z == 1) | (z == 2)
        self.outer = (z == 0) | (z == 3)
        self.mine = z - 1
        self.theirs = 2 - z
        self.own, self.from_outer, self.total, self.from_inner = own, bufs.at[0:2], bufs.at[2:4], bufs.at[4]
        self.copies = copies
        self.base = copies.take(8)
        self.inner_of = (f, 2 * (1 + z // 3) + k)
        self.outer_of = (f, 2 * (3 * (z - 1)) + k)
        self.partner = (f, 2 * (3 - z) + k)

    def inward(self, half):
        return self.copies.at(
            self.base + half, self.own.at[half], self.from_outer.at[half], self.inner_of
        )

    def across(self, half):
        return self.copies.at(
            self.base + 2 + half, self.own.at[half], self.from_inner, self.partner
        )

    def back_across(self, half):
        return self.copies.at(
            self.base + 4 + half, self.total.at[half], self.total.at[half], self.partner
        )

    def outward(self, half):
        return self.copies.at(
            self.base + 6 + half, self.total.at[half], self.total.at[half], self.outer_of
        )

    def start(self):
        @pl.when(self.outer)
        def _():
            self.inward(0).start()
            self.inward(1).start()

    def meet(self):
        @pl.when(self.inner)
        def _():
            t, m = self.theirs, self.mine
            self.inward(t).wait_recv()
            add_rows(self.own.at[t], [self.own.at[t], self.from_outer.at[t]])
            self.across(t).start()

    def close(self):
        @pl.when(self.inner)
        def _():
            m = self.mine
            self.inward(m).wait_recv()
            self.across(m).wait_recv()
            add_rows(
                self.total.at[m], [self.own.at[m], self.from_outer.at[m], self.from_inner]
            )
            self.back_across(m).start()
            self.outward(m).start()

    def spread(self):
        @pl.when(self.inner)
        def _():
            t = self.theirs
            self.back_across(t).wait_recv()
            self.outward(t).start()

    def arrive(self):
        @pl.when(self.outer)
        def _():
            self.outward(0).wait_recv()
            self.outward(1).wait_recv()

    def drain(self):
        @pl.when(self.outer)
        def _():
            self.inward(0).wait_send()
            self.inward(1).wait_send()

        @pl.when(self.inner)
        def _():
            self.across(self.theirs).wait_send()
            self.back_across(self.mine).wait_send()
            self.outward(0).wait_send()
            self.outward(1).wait_send()


class SmallSum:
    def __init__(self, me, copies, own, plane, line):
        self.me, self.own, self.plane, self.line = me, own, plane, line
        f = me.f
        self.step_one = [
            copies(own, plane.at[f], partner) for partner in (me.xp, me.yp, me.dp)
        ]
        self.step_two = [
            copies(line.at[me.c], line.at[me.c], me.along_ctx(step)[1]) for step in range(1, 8)
        ]

    def first(self):
        for copy in self.step_one:
            copy.start()
        self.plane[self.me.f] = self.own[...]

    def second(self):
        for copy in self.step_one:
            copy.wait_recv()
        plane = self.plane
        self.line[self.me.c] = (plane[0] + plane[1]) + (plane[2] + plane[3])
        for copy in self.step_two:
            copy.start()

    def finish(self, dst):
        for copy in self.step_two:
            copy.wait_recv()
        line = self.line
        total = line[0]
        for i in range(1, 8):
            total = total + line[i]
        dst[...] = total

    def drain(self):
        for copy in self.step_one + self.step_two:
            copy.wait_send()


HBM = pl.BlockSpec(memory_space=pl.ANY)
VM = pl.BlockSpec(memory_space=pltpu.VMEM)


def transfer(kernel, name, number, args, in_specs, outs, out_specs, scratch, copies, local):
    return pl.pallas_call(
        kernel,
        out_shape=outs,
        in_specs=in_specs,
        out_specs=out_specs,
        scratch_shapes=scratch
        + [
            pltpu.SemaphoreType.DMA((copies,)),
            pltpu.SemaphoreType.DMA((copies,)),
            pltpu.SemaphoreType.DMA((local,)),
        ],
        compiler_params=pltpu.CompilerParams(
            collective_id=number, has_side_effects=True, vmem_limit_bytes=VMEM_LIMIT
        ),
        name=name,
    )(*args)


def shape(dims, dtype):
    return jax.ShapeDtypeStruct(dims, dtype)


def kernel_begin(
    wq, wk, wv, x, t, misc, gains, count,
    w_all, x_pair, t_pair, misc_pair, gains_all, count_out,
    plane, line, send, recv, lsem,
):
    me = Place()
    ctx = [me.along_ctx(step)[1] for step in range(1, 8)]
    greet([me.xp, me.yp, me.dp] + ctx)
    copies, local = Copies(send, recv), Locals(lsem)
    q = GROUP * HEAD_SIZE
    for i in range(KEY_VALUE_HEADS // 2):
        head = 2 * i + me.k
        at = HEAD_COLUMNS * i
        q_at = pl.ds(pl.multiple_of(head * q, HEAD_SIZE), q)
        k_at = pl.ds(pl.multiple_of(head * HEAD_SIZE, HEAD_SIZE), HEAD_SIZE)
        local(wq.at[:, q_at], w_all.at[me.f, :, pl.ds(at, q)])
        local(wk.at[:, k_at], w_all.at[me.f, :, pl.ds(at + q, HEAD_SIZE)])
        local(wv.at[:, k_at], w_all.at[me.f, :, pl.ds(at + q + HEAD_SIZE, HEAD_SIZE)])
    small = SmallSum(me, copies, count, plane, line)
    small.first()
    others = [copies(gains, gains_all.at[me.f], partner) for partner in (me.xp, me.yp, me.dp)]
    for src, dst in ((x, x_pair), (t, t_pair), (misc, misc_pair)):
        others.append(copies(src, dst.at[me.k], me.sib))
    for copy in others:
        copy.start()
    local.wait()
    weights = Gather(me, copies, w_all)
    weights.first()
    weights.second()
    for src, dst in ((x, x_pair), (t, t_pair), (misc, misc_pair)):
        local(src, dst.at[me.k])
    local(gains, gains_all.at[me.f])
    small.second()
    weights.relay()
    local.wait()
    small.finish(count_out)
    for copy in others:
        copy.wait_recv()
    weights.finish()
    for copy in others:
        copy.wait_send()
    small.drain()


def begin(wq, wk, wv, x, t, misc, gains, count):
    rows = wq.shape[0]
    columns = (KEY_VALUE_HEADS // 2) * HEAD_COLUMNS
    return transfer(
        kernel_begin, "begin", 1,
        (wq, wk, wv, x, t, misc, gains, count),
        [HBM] * 7 + [VM],
        [
            shape((4, rows, columns), BF16),
            shape((2,) + x.shape, BF16),
            shape((2,) + t.shape, BF16),
            shape((2, 8, 128), F32),
            shape((4, 8, 128), F32),
            shape((8, 128), F32),
        ],
        [HBM] * 5 + [VM],
        [pltpu.VMEM((4, 8, 128), F32), pltpu.VMEM((8, 8, 128), F32)],
        24, 20,
    )


class Exchange:
    def __init__(self, me, copies, local, piece, place):
        self.me, self.local, self.piece, self.place = me, local, piece, place
        self.sends = []
        for step in (2, 1, 3):
            other, partner = me.along_z(step)
            self.sends.append(copies(piece(other), place(me.z), partner))

    def start(self):
        for copy in self.sends:
            copy.start()
        self.own = self.local(self.piece(self.me.z), self.place(self.me.z))

    def finish(self):
        self.own.wait()
        for copy in self.sends:
            copy.wait()


def kernel_to_heads(qkv, wg, wu, qkv_all, wg_all, wu_all, send, recv, lsem):
    me = Place()
    greet([me.xp, me.yp] + [me.along_z(step)[1] for step in (1, 2, 3)])
    copies, local, second = Copies(send, recv), Locals(lsem), Locals(lsem)
    move = Exchange(
        me, copies, local, lambda z: qkv.at[z], lambda z: qkv_all.at[z]
    )
    move.start()
    second.used = 1
    width = wg.shape[1] // 8
    for src, dst in ((wg, wg_all), (wu, wu_all)):
        for i in range(4):
            at = pl.ds(pl.multiple_of((2 * i + me.k) * width, 128), width)
            second(src.at[:, at], dst.at[me.f, :, pl.ds(i * width, width)])
    second.wait()
    gathers = [Gather(me, copies, wg_all), Gather(me, copies, wu_all)]
    for gather in gathers:
        gather.first()
    for gather in gathers:
        gather.second()
    for gather in gathers:
        gather.relay()
    move.finish()
    for gather in gathers:
        gather.finish()


def to_heads(qkv, wg, wu):
    rows, columns = wg.shape
    return transfer(
        kernel_to_heads, "to_heads", 2,
        (qkv, wg, wu), [HBM] * 3,
        [
            shape(qkv.shape, BF16),
            shape((4, rows, columns // 2), BF16),
            shape((4, rows, columns // 2), BF16),
        ],
        [HBM] * 3, [], 15, 9,
    )


def kernel_to_tokens(att, wd, wo, att_all, wd_all, wo_all, send, recv, lsem):
    me = Place()
    greet([me.xp, me.yp] + [me.along_z(step)[1] for step in (1, 2, 3)])
    copies, local, second = Copies(send, recv), Locals(lsem), Locals(lsem)
    tokens, width = att_all.shape[0], att.shape[1]
    second.used = 1
    for src, dst in ((wd, wd_all), (wo, wo_all)):
        rows = dst.shape[1]
        second(src.at[pl.ds(pl.multiple_of(me.k * rows, 16), rows)], dst.at[me.f])
    move = Exchange(
        me, copies, local,
        lambda z: att.at[pl.ds(pl.multiple_of(z * tokens, 16), tokens)],
        lambda z: att_all.at[:, pl.ds(pl.multiple_of(z * width, 128), width)],
    )
    move.start()
    second.wait()
    gathers = [Gather(me, copies, wo_all), Gather(me, copies, wd_all)]
    for gather in gathers:
        gather.first()
    for gather in gathers:
        gather.second()
    for gather in gathers:
        gather.relay()
    move.finish()
    for gather in gathers:
        gather.finish()


def to_tokens(att, wd, wo):
    return transfer(
        kernel_to_tokens, "to_tokens", 3,
        (att, wd, wo), [HBM] * 3,
        [
            shape((att.shape[0] // 4, att.shape[1] * 4), BF16),
            shape((4, wd.shape[0] // 2, wd.shape[1]), BF16),
            shape((4, wo.shape[0] // 2, wo.shape[1]), BF16),
        ],
        [HBM] * 3, [], 15, 3,
    )


def kernel_swap(src, dst, send, recv, lsem):
    me = Place()
    greet([me.sib])
    copy = Copies(send, recv)(src, dst, me.sib)
    copy.start()
    copy.wait()


def swap(value, number):
    return transfer(
        kernel_swap, "swap%d" % number, number, (value,), [HBM], shape(value.shape, value.dtype), HBM, [], 1, 1
    )


def run_scatters(me, copies, local, move, scatters, outs):
    move.start()
    for scatter in scatters:
        scatter.first()
    for scatter in scatters:
        scatter.second()
    for scatter in scatters:
        scatter.relay()
    writes = []
    for scatter, out in zip(scatters, outs):
        scatter.finish(scatter.sum_a, scatter.sum_b)
        half = out.shape[0] // 2
        writes.append(local(scatter.sum_a, out.at[pl.ds(0, half)]))
        writes.append(local(scatter.sum_b, out.at[pl.ds(half, half)]))
    move.finish()
    for scatter in scatters:
        scatter.drain()
    for write in writes:
        write.wait()


def kernel_grads_to_heads(grads, down, grads_all, down_sum, bufs, send, recv, lsem):
    me = Place()
    greet([me.xp, me.yp] + [me.along_z(step)[1] for step in (1, 2, 3)])
    copies, local = Copies(send, recv), Locals(lsem)
    width = grads_all.shape[2]
    move = Exchange(
        me, copies, local,
        lambda z: grads.at[:, pl.ds(pl.multiple_of(z * width, 128), width)],
        lambda z: grads_all.at[z],
    )
    run_scatters(me, copies, local, move, [Scatter(me, copies, local, down, bufs)], [down_sum])


def grads_to_heads(grads, down):
    tokens, columns = grads.shape
    return transfer(
        kernel_grads_to_heads, "grads_to_heads", 4,
        (grads, down), [HBM] * 2,
        [shape((4, tokens, columns // 4), BF16), shape(down.shape[1:], BF16)],
        [HBM] * 2, scatter_buffers(*down.shape[1:]), 9, 7,
    )


def kernel_grads_to_tokens(grads, gate, up, grads_all, gate_sum, up_sum, bufs_g, bufs_u, send, recv, lsem):
    me = Place()
    greet([me.xp, me.yp] + [me.along_z(step)[1] for step in (1, 2, 3)])
    copies, local = Copies(send, recv), Locals(lsem)
    tokens, width = grads_all.shape[0], grads.shape[1]
    move = Exchange(
        me, copies, local,
        lambda z: grads.at[pl.ds(pl.multiple_of(z * tokens, 16), tokens)],
        lambda z: grads_all.at[:, pl.ds(pl.multiple_of(z * width, 128), width)],
    )
    run_scatters(
        me, copies, local, move,
        [Scatter(me, copies, local, gate, bufs_g), Scatter(me, copies, local, up, bufs_u)],
        [gate_sum, up_sum],
    )


def grads_to_tokens(grads, gate, up):
    return transfer(
        kernel_grads_to_tokens, "grads_to_tokens", 5,
        (grads, gate, up), [HBM] * 3,
        [
            shape((grads.shape[0] // 4, grads.shape[1] * 4), BF16),
            shape(gate.shape[1:], BF16),
            shape(up.shape[1:], BF16),
        ],
        [HBM] * 3,
        scatter_buffers(*gate.shape[1:]) + scatter_buffers(*up.shape[1:]), 15, 13,
    )


def kernel_end(
    down, gate, up, out, qkv, small,
    down_tot, gate_tot, up_tot, out_tot, qkv_tot, small_tot,
    own_d, own_g, own_u, own_o, own_q, line_d, line_g, line_u, line_o, line_q, sc_o, sc_q, plane, line,
    send, recv, lsem,
):
    me = Place()
    greet([me.xp, me.yp, me.dp] + [me.along_ctx(step)[1] for step in range(1, 8)])
    copies, local = Copies(send, recv), Locals(lsem)
    total = SmallSum(me, copies, small, plane, line)
    total.first()
    loads = []
    for src, own in ((down, own_d), (gate, own_g), (up, own_u)):
        half = own.shape[1]
        loads.append(
            [local(src.at[pl.ds(i * half, half)], own.at[i]) for i in range(2)]
        )
    scatters = [Scatter(me, copies, local, out, sc_o), Scatter(me, copies, local, qkv, sc_q)]
    for scatter in scatters:
        scatter.first()
    for scatter in scatters:
        scatter.second()
    total.second()
    sums = [
        LineSum(me, copies, own, bufs)
        for own, bufs in (
            (own_d, line_d), (own_g, line_g), (own_u, line_u), (own_o, line_o), (own_q, line_q)
        )
    ]
    totals = (down_tot, gate_tot, up_tot, out_tot, qkv_tot)
    for load, entry in zip(loads, sums):
        for copy in load:
            copy.wait()
        entry.start()
    base = copies.take(len(sums) * 2)
    swaps, writes = [], []

    def finish(i):
        sums[i].spread()
        sums[i].arrive()
        half = sums[i].total.shape[1]
        for j in range(2):
            dst = totals[i].at[me.k, pl.ds(j * half, half)]
            copy = copies.at(base + 2 * i + j, sums[i].total.at[j], dst, me.sib)
            copy.start()
            swaps.append(copy)
            writes.append(local(sums[i].total.at[j], dst))

    sums[0].meet()
    scatters[0].relay()
    sums[0].close()
    sums[1].meet()
    scatters[1].relay()
    scatters[0].finish(own_o.at[0], own_o.at[1])
    sums[3].start()
    sums[1].close()
    sums[2].meet()
    finish(0)
    scatters[1].finish(own_q.at[0], own_q.at[1])
    sums[4].start()
    sums[2].close()
    sums[3].meet()
    finish(1)
    sums[3].close()
    sums[4].meet()
    finish(2)
    sums[4].close()
    finish(3)
    finish(4)
    total.finish(small_tot)
    total.drain()
    for scatter in scatters:
        scatter.drain()
    for entry in sums:
        entry.drain()
    for copy in swaps:
        copy.wait()
    for copy in writes:
        copy.wait()


def end(down, gate, up, out, qkv, small):
    sizes = [down.shape, gate.shape, up.shape, out.shape[1:], qkv.shape[1:]]
    own = [pltpu.VMEM((2, r // 2, c), BF16) for r, c in sizes]
    line = [pltpu.VMEM((5, r // 2, c), BF16) for r, c in sizes]
    return transfer(
        kernel_end, "end", 6,
        (down, gate, up, out, qkv, small), [HBM] * 5 + [VM],
        [shape((2,) + tuple(s), BF16) for s in sizes] + [shape(small.shape, F32)],
        [HBM] * 5 + [VM],
        own + line
        + scatter_buffers(*out.shape[1:])
        + scatter_buffers(*qkv.shape[1:])
        + [pltpu.VMEM((4,) + small.shape, F32), pltpu.VMEM((8,) + small.shape, F32)],
        10 + 12 + 5 * 8 + 10, 6 + 8 + 10,
    )


def dot_nt(a, b, **kw):
    return lax.dot_general(a, b, (((1,), (1,)), ((), ())), preferred_element_type=F32, **kw)


def dot_nn(a, b):
    return lax.dot_general(a, b, (((1,), (0,)), ((), ())), preferred_element_type=F32)


def dot_tn(a, b):
    return lax.dot_general(a, b, (((0,), (0,)), ((), ())), preferred_element_type=F32)


BLOCK = 512
HIGHEST = lax.Precision.HIGHEST


def attend_kernel(qkv, att, lse, values):
    blocks = qkv.shape[0] // BLOCK
    k_at = pl.ds(GROUP * HEAD_SIZE, HEAD_SIZE)
    values[:, 0:HEAD_SIZE] = qkv[:, (GROUP + 1) * HEAD_SIZE :]
    values[:, HEAD_SIZE:] = jnp.ones((qkv.shape[0], HEAD_SIZE), BF16)
    row = lax.broadcasted_iota(jnp.int32, (BLOCK, BLOCK), 0)
    column = lax.broadcasted_iota(jnp.int32, (BLOCK, BLOCK), 1)
    allowed = column <= row

    @pl.loop(0, blocks)
    def _(i):
        rows = pl.ds(pl.multiple_of(i * BLOCK, BLOCK), BLOCK)
        for g in range(GROUP):
            q = qkv[rows, pl.ds(g * HEAD_SIZE, HEAD_SIZE)]

            def part(j, acc, q=q):
                keys = pl.ds(pl.multiple_of(j * BLOCK, BLOCK), BLOCK)
                e = jnp.exp(dot_nt(q, qkv[keys, k_at]) * SCALE)
                return acc + dot_nn(e.astype(BF16), values[keys, :])

            acc = lax.fori_loop(0, i, part, jnp.zeros((BLOCK, 2 * HEAD_SIZE), F32))
            e = jnp.exp(dot_nt(q, qkv[rows, k_at]) * SCALE)
            acc = acc + dot_nn(jnp.where(allowed, e, 0.0).astype(BF16), values[rows, :])
            total = acc[:, HEAD_SIZE:]
            att[rows, pl.ds(g * HEAD_SIZE, HEAD_SIZE)] = (acc[:, :HEAD_SIZE] / total).astype(BF16)
            mean = jnp.full((8, HEAD_SIZE), 1.0 / HEAD_SIZE, F32)
            lse[g, :, rows] = dot_nt(mean, jnp.log(total), precision=HIGHEST)


def attend(qkv):
    tokens = qkv.shape[0]
    return pl.pallas_call(
        attend_kernel,
        out_shape=[shape((tokens, GROUP * HEAD_SIZE), BF16), shape((GROUP, 8, tokens), F32)],
        in_specs=[VM],
        out_specs=[VM, VM],
        scratch_shapes=[pltpu.VMEM((tokens, 2 * HEAD_SIZE), BF16)],
        compiler_params=pltpu.CompilerParams(vmem_limit_bytes=VMEM_LIMIT),
        name="attend",
    )(qkv)


def attend_back_kernel(qkv, att, g_out, lse, grads, g_k, g_v):
    blocks = qkv.shape[0] // BLOCK
    k_at = pl.ds(GROUP * HEAD_SIZE, HEAD_SIZE)
    v_at = pl.ds((GROUP + 1) * HEAD_SIZE, HEAD_SIZE)
    g_k[...] = jnp.zeros_like(g_k)
    g_v[...] = jnp.zeros_like(g_v)
    key = lax.broadcasted_iota(jnp.int32, (BLOCK, BLOCK), 0)
    query = lax.broadcasted_iota(jnp.int32, (BLOCK, BLOCK), 1)
    allowed = key <= query

    @pl.loop(0, blocks)
    def _(i):
        rows = pl.ds(pl.multiple_of(i * BLOCK, BLOCK), BLOCK)
        for g in range(GROUP):
            head = pl.ds(g * HEAD_SIZE, HEAD_SIZE)
            q = qkv[rows, head]
            go = g_out[rows, head]
            product = go.astype(F32) * att[rows, head].astype(F32)
            delta = dot_nt(jnp.ones((8, HEAD_SIZE), F32), product, precision=HIGHEST)[0:1, :]
            log_sum = lse[g, 0:1, rows]

            def part(keys, masked, q=q, go=go, delta=delta, log_sum=log_sum):
                k, v = qkv[keys, k_at], qkv[keys, v_at]
                p = jnp.exp(dot_nt(k, q) * SCALE - log_sum)
                if masked:
                    p = jnp.where(allowed, p, 0.0)
                gs = (p * (dot_nt(v, go) - delta) * SCALE).astype(BF16)
                g_v[keys, :] += dot_nn(p.astype(BF16), go)
                g_k[keys, :] += dot_nn(gs, q)
                return dot_tn(gs, k)

            def step(j, acc, part=part):
                return acc + part(pl.ds(pl.multiple_of(j * BLOCK, BLOCK), BLOCK), False)

            acc = lax.fori_loop(0, i, step, jnp.zeros((BLOCK, HEAD_SIZE), F32))
            grads[rows, head] = (acc + part(rows, True)).astype(BF16)

    grads[:, k_at] = g_k[...].astype(BF16)
    grads[:, v_at] = g_v[...].astype(BF16)


def attend_back(qkv, att, g_out, lse):
    tokens = qkv.shape[0]
    return pl.pallas_call(
        attend_back_kernel,
        out_shape=shape(qkv.shape, BF16),
        in_specs=[VM] * 4,
        out_specs=VM,
        scratch_shapes=[pltpu.VMEM((tokens, HEAD_SIZE), F32)] * 2,
        compiler_params=pltpu.CompilerParams(vmem_limit_bytes=VMEM_LIMIT),
        name="attend_back",
    )(qkv, att, g_out, lse)


def turn(values, cosine_table, sine_table):
    half_width = HEAD_SIZE // 2
    swapped = jnp.concatenate([values[..., half_width:], values[..., :half_width]], -1)
    return values * cosine_table + swapped * sine_table


def heads_of(cosine_table, sine_table, projected, gain_q, gain_k):
    gain = jnp.concatenate([jnp.broadcast_to(gain_q, (GROUP, HEAD_SIZE)), gain_k[None]], 0)
    first = root_mean_norm(projected[:, :, : GROUP + 1], gain)
    first = turn(first, cosine_table[:, None, None, :], sine_table[:, None, None, :])
    return jnp.concatenate([first, projected[:, :, GROUP + 1 :]], 2)


def chip_step(
    hidden_in, teacher, valid, positions, norm_attn, w_query, key_projection, value_projection,
    gain_query, gain_key, w_out, norm_mlp, w_gate, w_up, w_down,
):
    f, c = lax.axis_index("fsdp"), lax.axis_index("ctx")
    k = c % 2
    rows = hidden_in.shape[1]
    tokens = 2 * rows
    width = hidden_in.shape[2]
    heads = KEY_VALUE_HEADS // 2
    misc = jnp.concatenate(
        [positions.reshape(-1, 128), valid.reshape(-1, 128), jnp.zeros((4, 128), jnp.int32)], 0
    ).astype(F32)
    gains = jnp.concatenate(
        [norm_attn, norm_mlp, gain_query, gain_key, jnp.zeros((448,), BF16)]
    ).astype(F32).reshape(8, 128)
    count = jnp.full((8, 128), jnp.sum(valid).astype(F32))
    w_qkv, x_pair, t_pair, misc_pair, gains_all, count = begin(
        w_query, key_projection, value_projection, hidden_in[0], teacher[0], misc, gains, count
    )
    w_qkv = w_qkv.reshape(width, -1)
    count_total = count[0, 0]
    x = x_pair.reshape(tokens, width).astype(F32)
    target = t_pair.reshape(tokens, width).astype(F32)
    token_positions = misc_pair[:, 0:2].reshape(tokens)
    weight_rows = misc_pair[:, 2:4].reshape(tokens)
    gain_one = gains_all[:, 0:2].reshape(width)
    gain_two = gains_all[:, 2:4].reshape(width)
    gain_q = gains_all[:, 4, 0:32].reshape(HEAD_SIZE)
    gain_k = gains_all[:, 4, 32:64].reshape(HEAD_SIZE)

    normed_one, norm_one_back = jax.vjp(root_mean_norm, x, gain_one)
    hidden_one = normed_one.astype(BF16)
    projected = jnp.dot(hidden_one, w_qkv, preferred_element_type=F32)
    cosine_table, sine_table = rope_tables(token_positions)
    qkv, heads_back = jax.vjp(
        partial(heads_of, cosine_table, sine_table),
        projected.reshape(tokens, heads, GROUP + 2, HEAD_SIZE), gain_q, gain_k,
    )
    qkv = qkv.astype(BF16).reshape(tokens, heads, HEAD_COLUMNS).transpose(1, 0, 2)
    qkv_all, wg, wu = to_heads(qkv, w_gate, w_up)
    qkv_all = qkv_all.reshape(4 * tokens, HEAD_COLUMNS)
    wg, wu = wg.reshape(width, -1), wu.reshape(width, -1)
    att, lse = attend(qkv_all)
    att_all, wd, wo = to_tokens(att, w_down, w_out)
    wd, wo = wd.reshape(-1, width), wo.reshape(-1, width)

    def over_cores(part, number):
        part = part.astype(BF16)
        return part.astype(F32) + swap(part, number).astype(F32)

    x2 = x + over_cores(jnp.dot(att_all, wo, preferred_element_type=F32), 7)
    normed_two, norm_two_back = jax.vjp(root_mean_norm, x2, gain_two)
    hidden_two = normed_two.astype(BF16)
    gate = jnp.dot(hidden_two, wg, preferred_element_type=F32)
    up = jnp.dot(hidden_two, wu, preferred_element_type=F32)
    gated, gated_back = jax.vjp(swiglu, gate, up)
    mid = gated.astype(BF16)
    fin = x2 + over_cores(jnp.dot(mid, wd, preferred_element_type=F32), 8)
    mismatch = fin - target
    sq_local = 0.5 * jnp.sum(weight_rows[:, None] * mismatch * mismatch)
    loss_scale = tokens // 2 * lax.axis_size("ctx") * lax.axis_size("fsdp") / 4.0
    g_fin = 2.0 * loss_scale / count_total * weight_rows[:, None] * mismatch
    g_dn = g_fin.astype(BF16)
    g_gate, g_up = gated_back(against(g_dn, wd))
    g_gate, g_up = g_gate.astype(BF16), g_up.astype(BF16)
    g_h2 = over_cores(against(g_gate, wg) + against(g_up, wu), 9)
    g_norm, grad_norm_mlp = norm_two_back(g_h2)
    g_x2 = g_fin + g_norm
    g_a = g_x2.astype(BF16)
    g_o = against(g_a, wo).astype(BF16)
    p_down = contract_rows(mid, g_dn).astype(BF16).reshape(4, -1, width)
    g_o_all, s_down = grads_to_heads(g_o, p_down)
    p_gate = contract_rows(hidden_two, g_gate).astype(BF16).reshape(4, width // 4, -1)
    p_up = contract_rows(hidden_two, g_up).astype(BF16).reshape(4, width // 4, -1)
    p_out = contract_rows(att_all, g_a).astype(BF16).reshape(4, -1, width)
    g_qkv = attend_back(qkv_all, att, g_o_all.reshape(4 * tokens, -1), lse)
    g_qkv_all, s_gate, s_up = grads_to_tokens(g_qkv, p_gate, p_up)
    g_proj, grad_gain_q, grad_gain_k = heads_back(
        g_qkv_all.reshape(tokens, heads, GROUP + 2, HEAD_SIZE).astype(F32)
    )
    g_proj = g_proj.astype(BF16).reshape(tokens, -1)
    p_qkv = contract_rows(hidden_one, g_proj).astype(BF16).reshape(4, width // 4, -1)
    g_h1 = over_cores(against(g_proj, w_qkv), 10)
    g_norm, grad_norm_attn = norm_one_back(g_h1)
    grad_input = lax.dynamic_slice_in_dim(g_x2 + g_norm, k * rows, rows, 0)
    small = jnp.concatenate(
        [
            0.5 * grad_norm_attn, 0.5 * grad_norm_mlp, grad_gain_q, grad_gain_k,
            jnp.full((128,), sq_local), jnp.zeros((640,), F32),
        ]
    ).reshape(24, 128)
    down, gate, up, out, qkv, small = end(s_down, s_gate, s_up, p_out, p_qkv, small)

    def columns(both, size):
        both = both.reshape(2, both.shape[1], 4, -1)
        return both.transpose(1, 2, 0, 3).reshape(both.shape[1], -1).astype(F32)

    def mine(values):
        size = values.shape[0] // 4
        return lax.dynamic_slice_in_dim(values, f * size, size, 0)

    qkv = qkv.reshape(2, -1, heads, HEAD_COLUMNS)
    q_end = GROUP * HEAD_SIZE
    output = lax.dynamic_slice_in_dim(fin.astype(BF16), k * rows, rows, 0)
    return (
        output[None],
        small[18, 0] / count_total,
        grad_input[None],
        mine(small[0:8].reshape(-1)),
        columns(qkv[..., :q_end], 0),
        columns(qkv[..., q_end : q_end + HEAD_SIZE], 0),
        columns(qkv[..., q_end + HEAD_SIZE :], 0),
        mine(small[16]),
        mine(small[17]),
        out.reshape(-1, width).astype(F32),
        mine(small[8:16].reshape(-1)),
        columns(gate, 0),
        columns(up, 0),
        down.reshape(-1, width).astype(F32),
    )


def solution(mesh):
    chips = mesh.shape["fsdp"] == 4 and mesh.shape["ctx"] == KEY_VALUE_HEADS
    return jax.shard_map(
        chip_step if chips else per_device,
        mesh=mesh,
        in_specs=(
            P("fsdp", "ctx", None),
            P("fsdp", "ctx", None),
            P("fsdp", "ctx"),
            P("fsdp", "ctx"),
            P("fsdp"),
            P("fsdp", None),
            P("fsdp", None),
            P("fsdp", None),
            P("fsdp"),
            P("fsdp"),
            P("fsdp", None),
            P("fsdp"),
            P("fsdp", None),
            P("fsdp", None),
            P("fsdp", None),
        ),
        out_specs=(
            P("fsdp", "ctx", None),
            P(),
            P("fsdp", "ctx", None),
            P("fsdp"),
            P("fsdp", None),
            P("fsdp", None),
            P("fsdp", None),
            P("fsdp"),
            P("fsdp"),
            P("fsdp", None),
            P("fsdp"),
            P("fsdp", None),
            P("fsdp", None),
            P("fsdp", None),
        ),
        check_vma=False,
    )
```

```python
from functools import partial
import math

import jax
import jax.numpy as jnp
from jax import lax
from jax.experimental import pallas as pl
from jax.experimental.pallas import tpu as pltpu
from jax.sharding import PartitionSpec as P

QUERY_HEADS = 16
KEY_VALUE_HEADS = 8
HEAD_SIZE = 128


EPSILON = 1e-06


def root_mean_norm(values, norm_gain):
    return (
        values * lax.rsqrt(jnp.mean(values * values, axis=-1, keepdims=True) + EPSILON) * norm_gain
    )


def rope_tables(position_ids):
    half_width = HEAD_SIZE // 2
    freq_table = jnp.exp(
        jnp.arange(half_width, dtype=jnp.float32) * (-2.0 * math.log(1000000.0) / HEAD_SIZE)
    )
    angle_table = position_ids.astype(jnp.float32)[:, None] * freq_table[None, :]
    cosine_table = jnp.cos(angle_table)
    sine_table = jnp.sin(angle_table)
    return (
        jnp.concatenate([cosine_table, cosine_table], -1),
        jnp.concatenate([-sine_table, sine_table], -1),
    )


def apply_rotary(values, cosine_table, sine_table):
    half_width = HEAD_SIZE // 2
    swapped = jnp.concatenate([values[..., half_width:], values[..., :half_width]], -1)
    return values * cosine_table[:, None, :] + swapped * sine_table[:, None, :]


def shape_heads(cosine_table, sine_table, proj_query, projected_key, gain_q, key_gain):
    token_rows = proj_query.shape[0]
    query_rows = apply_rotary(
        root_mean_norm(proj_query.reshape(token_rows, QUERY_HEADS, HEAD_SIZE), gain_q),
        cosine_table,
        sine_table,
    )
    rows_of_keys = apply_rotary(
        root_mean_norm(projected_key.reshape(token_rows, KEY_VALUE_HEADS, HEAD_SIZE), key_gain),
        cosine_table,
        sine_table,
    )
    return (query_rows, rows_of_keys)


def swiglu(gate_proj, up_proj):
    return gate_proj / (1.0 + jnp.exp(-gate_proj)) * up_proj


def contract_rows(left_arr, right_arr):
    return lax.dot_general(
        left_arr, right_arr, (((0,), (0,)), ((), ())), preferred_element_type=jnp.float32
    )


def against(left_arr, right_arr):
    return lax.dot_general(
        left_arr, right_arr, (((1,), (1,)), ((), ())), preferred_element_type=jnp.float32
    )


def in_blocks(block_step, running, shard_portion):
    total_rows = shard_portion.shape[0]
    block_extent = 512
    block_count = total_rows // block_extent
    blocks = shard_portion.reshape((block_count, block_extent) + shard_portion.shape[1:])
    starts = jnp.arange(block_count, dtype=jnp.int32) * block_extent

    def scan_body(state, scan_item):
        return (block_step(state, scan_item[0], scan_item[1]), None)

    running, unused = lax.scan(scan_body, running, (blocks, starts))
    return running


def score_terms(
    query_rows,
    output_gradients,
    lse_heads,
    delta_heads,
    rows_of_keys,
    rows_of_values,
    query_index,
    key_index,
    score_scale,
):
    score_matrix = (
        jnp.einsum("alci,wli->lcaw", query_rows, rows_of_keys, preferred_element_type=jnp.float32)
        * score_scale
    )
    allowed = key_index[None, :] <= query_index[:, None]
    attention_probabilities = jnp.where(allowed, jnp.exp(score_matrix - lse_heads[..., None]), 0.0)
    grad_probs = jnp.einsum(
        "alci,wli->lcaw", output_gradients, rows_of_values, preferred_element_type=jnp.float32
    )
    score_gradient = (
        score_scale * attention_probabilities * (grad_probs - delta_heads[..., None])
    ).astype(jnp.bfloat16)
    return (attention_probabilities, score_gradient)


def per_device(
    hidden_in,
    teacher,
    valid,
    positions,
    norm_attn,
    w_query,
    key_projection,
    value_projection,
    gain_query,
    gain_key,
    w_out,
    norm_mlp,
    w_gate,
    w_up,
    w_down,
):
    gathered = (
        lax.all_gather(norm_attn, "fsdp", axis=0, tiled=True),
        lax.all_gather(w_query, "fsdp", axis=0, tiled=True),
        lax.all_gather(key_projection, "fsdp", axis=0, tiled=True),
        lax.all_gather(value_projection, "fsdp", axis=0, tiled=True),
        lax.all_gather(gain_query, "fsdp", axis=0, tiled=True),
        lax.all_gather(gain_key, "fsdp", axis=0, tiled=True),
        lax.all_gather(w_out, "fsdp", axis=0, tiled=True),
        lax.all_gather(norm_mlp, "fsdp", axis=0, tiled=True),
        lax.all_gather(w_gate, "fsdp", axis=0, tiled=True),
        lax.all_gather(w_up, "fsdp", axis=0, tiled=True),
        lax.all_gather(w_down, "fsdp", axis=0, tiled=True),
    )
    (
        full_norm_attn,
        full_query,
        full_key,
        full_value,
        full_gain_q,
        full_gain_k,
        full_out,
        full_norm_mlp,
        full_gate,
        full_up,
        full_down,
    ) = gathered
    grouped_heads = QUERY_HEADS // KEY_VALUE_HEADS
    score_scale = 1.0 / math.sqrt(HEAD_SIZE)
    residual = hidden_in[0].astype(jnp.float32)
    token_rows = residual.shape[0]
    query_index = lax.axis_index("ctx") * token_rows + jnp.arange(token_rows, dtype=jnp.int32)
    normed_one, norm_one_back = jax.vjp(
        root_mean_norm, residual, full_norm_attn.astype(jnp.float32)
    )
    hidden_one = normed_one.astype(jnp.bfloat16)
    proj_query = jnp.dot(hidden_one, full_query, preferred_element_type=jnp.float32)
    projected_key = jnp.dot(hidden_one, full_key, preferred_element_type=jnp.float32)
    projected_value = jnp.dot(hidden_one, full_value, preferred_element_type=jnp.float32)
    cosine_table, sine_table = rope_tables(positions[0])
    (query_per_head, heads_key), heads_back = jax.vjp(
        partial(shape_heads, cosine_table, sine_table),
        proj_query,
        projected_key,
        full_gain_q.astype(jnp.float32),
        full_gain_k.astype(jnp.float32),
    )
    query_reduced = query_per_head.astype(jnp.bfloat16).reshape(
        token_rows, KEY_VALUE_HEADS, grouped_heads, HEAD_SIZE
    )
    key_reduced = heads_key.astype(jnp.bfloat16)
    value_reduced = projected_value.astype(jnp.bfloat16).reshape(
        token_rows, KEY_VALUE_HEADS, HEAD_SIZE
    )
    key_value = jnp.stack(
        [
            key_reduced.reshape(token_rows, KEY_VALUE_HEADS * HEAD_SIZE),
            value_reduced.reshape(token_rows, KEY_VALUE_HEADS * HEAD_SIZE),
        ],
        axis=1,
    )

    def forward_block(running, shard_portion, first_row):
        run_max, run_total, run_acc = running
        rows_per_block = shard_portion.shape[0]
        rows_of_keys = shard_portion[:, 0].reshape(rows_per_block, KEY_VALUE_HEADS, HEAD_SIZE)
        rows_of_values = shard_portion[:, 1].reshape(rows_per_block, KEY_VALUE_HEADS, HEAD_SIZE)
        key_index = first_row + jnp.arange(rows_per_block, dtype=jnp.int32)
        allowed = key_index[None, :] <= query_index[:, None]
        score_matrix = (
            jnp.einsum(
                "alci,wli->lcaw", query_reduced, rows_of_keys, preferred_element_type=jnp.float32
            )
            * score_scale
        )
        score_matrix = jnp.where(allowed, score_matrix, -1e30)
        new_max = jnp.maximum(run_max, jnp.max(score_matrix, axis=-1))
        weights_part = jnp.where(allowed, jnp.exp(score_matrix - new_max[..., None]), 0.0)
        factor = jnp.exp(run_max - new_max)
        run_total = run_total * factor + jnp.sum(weights_part, axis=-1)
        run_acc = run_acc * factor[..., None] + jnp.einsum(
            "exfw,weq->exfq",
            weights_part.astype(jnp.bfloat16),
            rows_of_values,
            preferred_element_type=jnp.float32,
        )
        return (new_max, run_total, run_acc)

    start_state = (
        jnp.full((KEY_VALUE_HEADS, grouped_heads, token_rows), -1e30, jnp.float32),
        jnp.zeros((KEY_VALUE_HEADS, grouped_heads, token_rows), jnp.float32),
        jnp.zeros((KEY_VALUE_HEADS, grouped_heads, token_rows, HEAD_SIZE), jnp.float32),
    )
    run_max, run_total, run_acc = in_blocks(
        forward_block, start_state, lax.all_gather(key_value, "ctx", axis=0, tiled=True)
    )
    log_total = run_max + jnp.log(run_total)
    attn_rows = jnp.transpose(run_acc / run_total[..., None], (2, 0, 1, 3))
    attn_low = attn_rows.reshape(token_rows, QUERY_HEADS * HEAD_SIZE).astype(jnp.bfloat16)
    mid_resid = residual + jnp.dot(attn_low, full_out, preferred_element_type=jnp.float32)
    normed_two, norm_two_back = jax.vjp(
        root_mean_norm, mid_resid, full_norm_mlp.astype(jnp.float32)
    )
    hidden_two = normed_two.astype(jnp.bfloat16)
    gate_proj = jnp.dot(hidden_two, full_gate, preferred_element_type=jnp.float32)
    up_proj = jnp.dot(hidden_two, full_up, preferred_element_type=jnp.float32)
    gated, gated_back = jax.vjp(swiglu, gate_proj, up_proj)
    gated_low = gated.astype(jnp.bfloat16)
    final_rows = mid_resid + jnp.dot(gated_low, full_down, preferred_element_type=jnp.float32)
    target = teacher[0].astype(jnp.float32)
    weight_rows = valid[0].astype(jnp.float32)
    mismatch = final_rows - target
    sq_local = jnp.sum(weight_rows[:, None] * mismatch * mismatch)
    count_local = jnp.sum(weight_rows)
    sq_total, count_total = lax.psum((sq_local, count_local), ("fsdp", "ctx"))
    loss_value = sq_total / count_total
    loss_scale = token_rows * lax.axis_size("ctx") * lax.axis_size("fsdp") / 4.0
    grad_final = 2.0 * loss_scale / count_total * weight_rows[:, None] * mismatch
    grad_down_in = grad_final.astype(jnp.bfloat16)
    grad_w_down = contract_rows(gated_low, grad_down_in)
    grad_gated = against(grad_down_in, full_down)
    grad_gate_proj, grad_up_proj = gated_back(grad_gated)
    gate_low = grad_gate_proj.astype(jnp.bfloat16)
    up_low = grad_up_proj.astype(jnp.bfloat16)
    grad_w_gate = contract_rows(hidden_two, gate_low)
    grad_w_up = contract_rows(hidden_two, up_low)
    grad_hidden_two = against(gate_low, full_gate) + against(up_low, full_up)
    grad_mid_norm, grad_norm_mlp = norm_two_back(grad_hidden_two)
    grad_mid = grad_final + grad_mid_norm
    grad_branch = grad_mid.astype(jnp.bfloat16)
    grad_w_out = contract_rows(attn_low, grad_branch)
    attention_gradient = against(grad_branch, full_out).astype(jnp.bfloat16)
    attention_head_gradient = attention_gradient.reshape(
        token_rows, KEY_VALUE_HEADS, grouped_heads, HEAD_SIZE
    )
    row_delta = jnp.sum(attention_head_gradient.astype(jnp.float32) * attn_rows, axis=-1)
    delta_heads = jnp.transpose(row_delta, (1, 2, 0))
    row_stats = jnp.stack(
        [
            jnp.transpose(log_total, (2, 0, 1)).reshape(token_rows, QUERY_HEADS),
            row_delta.reshape(token_rows, QUERY_HEADS),
        ],
        axis=1,
    )

    def block_of_queries(grad_query, shard_portion, first_row):
        rows_per_block = shard_portion.shape[0]
        rows_of_keys = shard_portion[:, 0].reshape(rows_per_block, KEY_VALUE_HEADS, HEAD_SIZE)
        rows_of_values = shard_portion[:, 1].reshape(rows_per_block, KEY_VALUE_HEADS, HEAD_SIZE)
        key_index = first_row + jnp.arange(rows_per_block, dtype=jnp.int32)
        attention_probabilities, score_gradient = score_terms(
            query_reduced,
            attention_head_gradient,
            log_total,
            delta_heads,
            rows_of_keys,
            rows_of_values,
            query_index,
            key_index,
            score_scale,
        )
        return grad_query + jnp.einsum(
            "jyux,xji->ujyi", score_gradient, rows_of_keys, preferred_element_type=jnp.float32
        )

    grad_query = in_blocks(
        block_of_queries,
        jnp.zeros((token_rows, KEY_VALUE_HEADS, grouped_heads, HEAD_SIZE), jnp.float32),
        lax.all_gather(key_value, "ctx", axis=0, tiled=True),
    )
    all_stats = lax.all_gather(row_stats.astype(jnp.bfloat16), "ctx", axis=0, tiled=True).astype(
        row_stats.dtype
    )
    query_pair = jnp.stack(
        [query_reduced.reshape(token_rows, QUERY_HEADS * HEAD_SIZE), attention_gradient], axis=1
    )

    def key_block(running, shard_portion, first_row):
        grad_key, value_gradient = running
        rows_per_block = shard_portion.shape[0]
        query_rows = shard_portion[:, 0].reshape(
            rows_per_block, KEY_VALUE_HEADS, grouped_heads, HEAD_SIZE
        )
        output_gradients = shard_portion[:, 1].reshape(
            rows_per_block, KEY_VALUE_HEADS, grouped_heads, HEAD_SIZE
        )
        partial_statistics = lax.dynamic_slice_in_dim(all_stats, first_row, rows_per_block, 0)
        partial_logsumexp = jnp.transpose(
            partial_statistics[:, 0].reshape(rows_per_block, KEY_VALUE_HEADS, grouped_heads),
            (1, 2, 0),
        )
        partial_delta = jnp.transpose(
            partial_statistics[:, 1].reshape(rows_per_block, KEY_VALUE_HEADS, grouped_heads),
            (1, 2, 0),
        )
        part_index = first_row + jnp.arange(rows_per_block, dtype=jnp.int32)
        attention_probabilities, score_gradient = score_terms(
            query_rows,
            output_gradients,
            partial_logsumexp,
            partial_delta,
            key_reduced,
            value_reduced,
            part_index,
            query_index,
            score_scale,
        )
        grad_key = grad_key + jnp.einsum(
            "wzlj,lwzy->jwy", score_gradient, query_rows, preferred_element_type=jnp.float32
        )
        value_gradient = value_gradient + jnp.einsum(
            "wzlj,lwzy->jwy",
            attention_probabilities.astype(jnp.bfloat16),
            output_gradients,
            preferred_element_type=jnp.float32,
        )
        return (grad_key, value_gradient)

    key_state = (
        jnp.zeros((token_rows, KEY_VALUE_HEADS, HEAD_SIZE), jnp.float32),
        jnp.zeros((token_rows, KEY_VALUE_HEADS, HEAD_SIZE), jnp.float32),
    )
    grad_key, value_gradient = in_blocks(
        key_block, key_state, lax.all_gather(query_pair, "ctx", axis=0, tiled=True)
    )
    grad_proj_q, grad_proj_k, grad_gain_q, grad_gain_k = heads_back(
        (grad_query.reshape(token_rows, QUERY_HEADS, HEAD_SIZE), grad_key)
    )
    query_grad_low = grad_proj_q.astype(jnp.bfloat16)
    key_grad_low = grad_proj_k.astype(jnp.bfloat16)
    value_gradient_reduced = value_gradient.reshape(token_rows, KEY_VALUE_HEADS * HEAD_SIZE).astype(
        jnp.bfloat16
    )
    grad_w_query = contract_rows(hidden_one, query_grad_low)
    grad_w_key = contract_rows(hidden_one, key_grad_low)
    grad_w_value = contract_rows(hidden_one, value_gradient_reduced)
    grad_hidden_one = (
        against(query_grad_low, full_query)
        + against(key_grad_low, full_key)
        + against(value_gradient_reduced, full_value)
    )
    grad_resid_norm, grad_norm_attn = norm_one_back(grad_hidden_one)
    grad_input = grad_mid + grad_resid_norm
    grads = (
        grad_norm_attn,
        grad_w_query,
        grad_w_key,
        grad_w_value,
        grad_gain_q,
        grad_gain_k,
        grad_w_out,
        grad_norm_mlp,
        grad_w_gate,
        grad_w_up,
        grad_w_down,
    )
    shares = (
        lax.psum_scatter(grads[0], ("fsdp", "ctx"), scatter_dimension=0, tiled=True),
        lax.psum_scatter(grads[1], ("fsdp", "ctx"), scatter_dimension=0, tiled=True),
        lax.psum_scatter(grads[2], ("fsdp", "ctx"), scatter_dimension=0, tiled=True),
        lax.psum_scatter(grads[3], ("fsdp", "ctx"), scatter_dimension=0, tiled=True),
        lax.psum_scatter(grads[4], ("fsdp", "ctx"), scatter_dimension=0, tiled=True),
        lax.psum_scatter(grads[5], ("fsdp", "ctx"), scatter_dimension=0, tiled=True),
        lax.psum_scatter(grads[6], ("fsdp", "ctx"), scatter_dimension=0, tiled=True),
        lax.psum_scatter(grads[7], ("fsdp", "ctx"), scatter_dimension=0, tiled=True),
        lax.psum_scatter(grads[8], ("fsdp", "ctx"), scatter_dimension=0, tiled=True),
        lax.psum_scatter(grads[9], ("fsdp", "ctx"), scatter_dimension=0, tiled=True),
        lax.psum_scatter(grads[10], ("fsdp", "ctx"), scatter_dimension=0, tiled=True),
    )
    shares = (
        lax.all_gather(shares[0].astype(jnp.bfloat16), "ctx", axis=0, tiled=True).astype(
            jnp.float32
        ),
        lax.all_gather(shares[1].astype(jnp.bfloat16), "ctx", axis=0, tiled=True).astype(
            jnp.float32
        ),
        lax.all_gather(shares[2].astype(jnp.bfloat16), "ctx", axis=0, tiled=True).astype(
            jnp.float32
        ),
        lax.all_gather(shares[3].astype(jnp.bfloat16), "ctx", axis=0, tiled=True).astype(
            jnp.float32
        ),
        lax.all_gather(shares[4].astype(jnp.bfloat16), "ctx", axis=0, tiled=True).astype(
            jnp.float32
        ),
        lax.all_gather(shares[5].astype(jnp.bfloat16), "ctx", axis=0, tiled=True).astype(
            jnp.float32
        ),
        lax.all_gather(shares[6].astype(jnp.bfloat16), "ctx", axis=0, tiled=True).astype(
            jnp.float32
        ),
        lax.all_gather(shares[7].astype(jnp.bfloat16), "ctx", axis=0, tiled=True).astype(
            jnp.float32
        ),
        lax.all_gather(shares[8].astype(jnp.bfloat16), "ctx", axis=0, tiled=True).astype(
            jnp.float32
        ),
        lax.all_gather(shares[9].astype(jnp.bfloat16), "ctx", axis=0, tiled=True).astype(
            jnp.float32
        ),
        lax.all_gather(shares[10].astype(jnp.bfloat16), "ctx", axis=0, tiled=True).astype(
            jnp.float32
        ),
    )
    return (
        final_rows.astype(jnp.bfloat16)[None],
        loss_value,
        grad_input[None],
        shares[0],
        shares[1],
        shares[2],
        shares[3],
        shares[4],
        shares[5],
        shares[6],
        shares[7],
        shares[8],
        shares[9],
        shares[10],
    )


MESH = pl.DeviceIdType.MESH
BF16 = jnp.bfloat16
F32 = jnp.float32
GROUP = QUERY_HEADS // KEY_VALUE_HEADS
HEAD_COLUMNS = (GROUP + 2) * HEAD_SIZE
SCALE = 1.0 / math.sqrt(HEAD_SIZE)
VMEM_LIMIT = 56 * 1024 * 1024


class Place:
    def __init__(self):
        self.f = lax.axis_index("fsdp")
        self.c = lax.axis_index("ctx")
        self.z = self.c // 2
        self.k = self.c % 2
        self.fx = self.f + 1 - 2 * (self.f % 2)
        self.fy = (self.f + 2) % 4
        self.fd = 3 - self.f
        self.xp = (self.fx, self.c)
        self.yp = (self.fy, self.c)
        self.dp = (self.fd, self.c)
        self.sib = (self.f, self.c + 1 - 2 * self.k)

    def along_z(self, step):
        other = (self.z + step) % 4
        return other, (self.f, 2 * other + self.k)

    def along_ctx(self, step):
        other = (self.c + step) % 8
        return other, (self.f, other)


def greet(partners):
    barrier = pltpu.get_barrier_semaphore()
    for partner in partners:
        pl.semaphore_signal(barrier, inc=1, device_id=partner, device_id_type=MESH)
    pl.semaphore_wait(barrier, len(partners))


class Copies:
    def __init__(self, send, recv):
        self.send, self.recv, self.used = send, recv, 0

    def take(self, count):
        first = self.used
        self.used += count
        return first

    def at(self, index, src, dst, partner):
        return pltpu.make_async_remote_copy(
            src_ref=src,
            dst_ref=dst,
            send_sem=self.send.at[index],
            recv_sem=self.recv.at[index],
            device_id=partner,
            device_id_type=MESH,
        )

    def __call__(self, src, dst, partner):
        return self.at(self.take(1), src, dst, partner)


class Locals:
    def __init__(self, sems):
        self.sems, self.used, self.open = sems, 0, []

    def __call__(self, src, dst):
        copy = pltpu.make_async_copy(src, dst, self.sems.at[self.used])
        self.used += 1
        copy.start()
        self.open.append(copy)
        return copy

    def wait(self):
        for copy in self.open:
            copy.wait()
        self.open = []

    def alone(self, src, dst):
        copy = self(src, dst)
        self.open.pop()
        return copy


def add_rows(dst, sources):
    rows = dst.shape[0]
    step = 32

    @pl.loop(0, rows // step)
    def _(i):
        part = pl.ds(pl.multiple_of(i * step, step), step)
        total = sources[0][part, :].astype(F32)
        for source in sources[1:]:
            total = total + source[part, :].astype(F32)
        dst[part, :] = total.astype(dst.dtype)


class Gather:
    def __init__(self, me, copies, local, own, buf):
        half = buf.shape[1] // 2
        a, b = pl.ds(0, half), pl.ds(half, half)
        own_a, own_b = buf.at[me.f, a], buf.at[me.f, b]
        self.local, self.own, self.slot = local, own, buf.at[me.f]
        self.a_x = copies(own.at[a], own_a, me.xp)
        self.b_y = copies(own.at[b], own_b, me.yp)
        self.b_x = copies(own.at[b], own_b, me.xp)
        self.a_y = copies(own.at[a], own_a, me.yp)
        self.on_y = copies(buf.at[me.fx, a], buf.at[me.fx, a], me.yp)
        self.on_x = copies(buf.at[me.fy, b], buf.at[me.fy, b], me.xp)

    def first(self):
        self.a_x.start()
        self.b_y.start()

    def second(self):
        self.b_x.start()
        self.a_y.start()
        self.kept = self.local.alone(self.own, self.slot)

    def relay(self):
        self.a_x.wait_recv()
        self.on_y.start()
        self.b_y.wait_recv()
        self.on_x.start()

    def finish(self):
        for copy in (self.b_x, self.a_y, self.on_y, self.on_x):
            copy.wait_recv()
        for copy in (self.a_x, self.b_y, self.b_x, self.a_y, self.on_y, self.on_x):
            copy.wait_send()
        self.kept.wait()


def scatter_buffers(rows, columns):
    half = rows // 2
    return [pltpu.VMEM((12, half, columns), BF16)]


class Scatter:
    def __init__(self, me, copies, local, part, bufs):
        half = part.shape[1] // 2
        a, b = pl.ds(0, half), pl.ds(half, half)
        slot = [bufs.at[i] for i in range(12)]
        self.fwd_a, self.fwd_b, self.own_a, self.own_b = slot[0:4]
        self.rx_own, self.rx_fwd, self.ry_own, self.ry_fwd, self.r2_a, self.r2_b = slot[4:10]
        self.sum_a, self.sum_b = slot[10:12]
        self.d_x = copies(part.at[me.fd, a], self.rx_fwd, me.xp)
        self.d_y = copies(part.at[me.fd, b], self.ry_fwd, me.yp)
        self.o_x = copies(part.at[me.fx, a], self.rx_own, me.xp)
        self.o_y = copies(part.at[me.fy, b], self.ry_own, me.yp)
        self.to_y = copies(self.fwd_a, self.r2_a, me.yp)
        self.to_x = copies(self.fwd_b, self.r2_b, me.xp)
        self.local, self.me, self.part, self.a, self.b = local, me, part, a, b

    def first(self):
        self.d_x.start()
        self.d_y.start()

    def second(self):
        self.o_x.start()
        self.o_y.start()
        me, part = self.me, self.part
        self.mine = [
            self.local(part.at[me.fy, self.a], self.fwd_a),
            self.local(part.at[me.fx, self.b], self.fwd_b),
            self.local(part.at[me.f, self.a], self.own_a),
            self.local(part.at[me.f, self.b], self.own_b),
        ]

    def relay(self):
        for copy in self.mine:
            copy.wait()
        self.d_x.wait_recv()
        add_rows(self.fwd_a, [self.fwd_a, self.rx_fwd])
        self.to_y.start()
        self.d_y.wait_recv()
        add_rows(self.fwd_b, [self.fwd_b, self.ry_fwd])
        self.to_x.start()

    def finish(self, sum_a, sum_b):
        self.o_x.wait_recv()
        self.to_y.wait_recv()
        add_rows(sum_a, [self.own_a, self.rx_own, self.r2_a])
        self.o_y.wait_recv()
        self.to_x.wait_recv()
        add_rows(sum_b, [self.own_b, self.ry_own, self.r2_b])

    def drain(self):
        for copy in (self.d_x, self.d_y, self.o_x, self.o_y, self.to_y, self.to_x):
            copy.wait_send()


class LineSum:
    def __init__(self, me, copies, own, bufs):
        z, f, k = me.z, me.f, me.k
        self.inner = (z == 1) | (z == 2)
        self.outer = (z == 0) | (z == 3)
        self.mine = z - 1
        self.theirs = 2 - z
        self.own, self.from_outer, self.total, self.from_inner = own, bufs.at[0:2], bufs.at[2:4], bufs.at[4]
        self.copies = copies
        self.base = copies.take(8)
        self.inner_of = (f, 2 * (1 + z // 3) + k)
        self.outer_of = (f, 2 * (3 * (z - 1)) + k)
        self.partner = (f, 2 * (3 - z) + k)

    def inward(self, half):
        return self.copies.at(
            self.base + half, self.own.at[half], self.from_outer.at[half], self.inner_of
        )

    def across(self, half):
        return self.copies.at(
            self.base + 2 + half, self.own.at[half], self.from_inner, self.partner
        )

    def back_across(self, half):
        return self.copies.at(
            self.base + 4 + half, self.total.at[half], self.total.at[half], self.partner
        )

    def outward(self, half):
        return self.copies.at(
            self.base + 6 + half, self.total.at[half], self.total.at[half], self.outer_of
        )

    def start(self):
        @pl.when(self.outer)
        def _():
            self.inward(0).start()
            self.inward(1).start()

    def meet(self):
        @pl.when(self.inner)
        def _():
            t, m = self.theirs, self.mine
            self.inward(t).wait_recv()
            add_rows(self.own.at[t], [self.own.at[t], self.from_outer.at[t]])
            self.across(t).start()

    def close(self):
        @pl.when(self.inner)
        def _():
            m = self.mine
            self.inward(m).wait_recv()
            self.across(m).wait_recv()
            add_rows(
                self.total.at[m], [self.own.at[m], self.from_outer.at[m], self.from_inner]
            )
            self.back_across(m).start()
            self.outward(m).start()

    def spread(self):
        @pl.when(self.inner)
        def _():
            t = self.theirs
            self.back_across(t).wait_recv()
            self.outward(t).start()

    def arrive(self):
        @pl.when(self.outer)
        def _():
            self.outward(0).wait_recv()
            self.outward(1).wait_recv()

    def drain(self):
        @pl.when(self.outer)
        def _():
            self.inward(0).wait_send()
            self.inward(1).wait_send()

        @pl.when(self.inner)
        def _():
            self.across(self.theirs).wait_send()
            self.back_across(self.mine).wait_send()
            self.outward(0).wait_send()
            self.outward(1).wait_send()


class SmallSum:
    def __init__(self, me, copies, own, plane, line):
        self.me, self.own, self.plane, self.line = me, own, plane, line
        f = me.f
        self.step_one = [
            copies(own, plane.at[f], partner) for partner in (me.xp, me.yp, me.dp)
        ]
        self.step_two = [
            copies(line.at[me.c], line.at[me.c], me.along_ctx(step)[1]) for step in range(1, 8)
        ]

    def first(self):
        for copy in self.step_one:
            copy.start()
        self.plane[self.me.f] = self.own[...]

    def second(self):
        for copy in self.step_one:
            copy.wait_recv()
        plane = self.plane
        self.line[self.me.c] = (plane[0] + plane[1]) + (plane[2] + plane[3])
        for copy in self.step_two:
            copy.start()

    def finish(self, dst):
        for copy in self.step_two:
            copy.wait_recv()
        line = self.line
        total = line[0]
        for i in range(1, 8):
            total = total + line[i]
        dst[...] = total

    def drain(self):
        for copy in self.step_one + self.step_two:
            copy.wait_send()


HBM = pl.BlockSpec(memory_space=pl.ANY)
VM = pl.BlockSpec(memory_space=pltpu.VMEM)


def transfer(kernel, name, number, args, in_specs, outs, out_specs, scratch, copies, local):
    return pl.pallas_call(
        kernel,
        out_shape=outs,
        in_specs=in_specs,
        out_specs=out_specs,
        scratch_shapes=scratch
        + [
            pltpu.SemaphoreType.DMA((copies,)),
            pltpu.SemaphoreType.DMA((copies,)),
            pltpu.SemaphoreType.DMA((local,)),
        ],
        compiler_params=pltpu.CompilerParams(
            collective_id=number, has_side_effects=True, vmem_limit_bytes=VMEM_LIMIT
        ),
        name=name,
    )(*args)


def shape(dims, dtype):
    return jax.ShapeDtypeStruct(dims, dtype)


def kernel_begin(
    wq, wk, wv, x, t, misc, gains, count,
    w_all, x_pair, t_pair, misc_pair, gains_all, count_out,
    own, plane, line, send, recv, lsem,
):
    me = Place()
    ctx = [me.along_ctx(step)[1] for step in range(1, 8)]
    greet([me.xp, me.yp, me.dp] + ctx)
    copies, local = Copies(send, recv), Locals(lsem)
    q = GROUP * HEAD_SIZE
    for i in range(KEY_VALUE_HEADS // 2):
        head = 2 * i + me.k
        at = HEAD_COLUMNS * i
        q_at = pl.ds(pl.multiple_of(head * q, HEAD_SIZE), q)
        k_at = pl.ds(pl.multiple_of(head * HEAD_SIZE, HEAD_SIZE), HEAD_SIZE)
        local(wq.at[:, q_at], own.at[:, pl.ds(at, q)])
        local(wk.at[:, k_at], own.at[:, pl.ds(at + q, HEAD_SIZE)])
        local(wv.at[:, k_at], own.at[:, pl.ds(at + q + HEAD_SIZE, HEAD_SIZE)])
    small = SmallSum(me, copies, count, plane, line)
    small.first()
    others = [copies(gains, gains_all.at[me.f], partner) for partner in (me.xp, me.yp, me.dp)]
    for src, dst in ((x, x_pair), (t, t_pair), (misc, misc_pair)):
        others.append(copies(src, dst.at[me.k], me.sib))
    for copy in others:
        copy.start()
    local.wait()
    weights = Gather(me, copies, local, own, w_all)
    weights.first()
    weights.second()
    for src, dst in ((x, x_pair), (t, t_pair), (misc, misc_pair)):
        local(src, dst.at[me.k])
    local(gains, gains_all.at[me.f])
    small.second()
    weights.relay()
    local.wait()
    small.finish(count_out)
    for copy in others:
        copy.wait_recv()
    weights.finish()
    for copy in others:
        copy.wait_send()
    small.drain()


def begin(wq, wk, wv, x, t, misc, gains, count):
    rows = wq.shape[0]
    columns = (KEY_VALUE_HEADS // 2) * HEAD_COLUMNS
    return transfer(
        kernel_begin, "begin", 1,
        (wq, wk, wv, x, t, misc, gains, count),
        [HBM] * 3 + [VM] * 5,
        [
            shape((4, rows, columns), BF16),
            shape((2,) + x.shape, BF16),
            shape((2,) + t.shape, BF16),
            shape((2, 8, 128), F32),
            shape((4, 8, 128), F32),
            shape((8, 128), F32),
        ],
        [HBM] * 5 + [VM],
        [pltpu.VMEM((rows, columns), BF16), pltpu.VMEM((4, 8, 128), F32), pltpu.VMEM((8, 8, 128), F32)],
        24, 20,
    )


class Exchange:
    def __init__(self, me, copies, local, stage, piece, place):
        self.me, self.local, self.piece, self.place, self.stage = me, local, piece, place, stage
        self.sends = []
        for step in (2, 1, 3):
            other, partner = me.along_z(step)
            self.sends.append(copies(piece(other), place(me.z), partner))

    def start(self):
        for copy in self.sends:
            copy.start()
        self.own = self.local.alone(self.piece(self.me.z), self.stage)

    def pass_own(self):
        self.own.wait()
        self.own = self.local.alone(self.stage, self.place(self.me.z))

    def finish(self):
        self.own.wait()
        for copy in self.sends:
            copy.wait()


def kernel_to_heads(qkv, wg, wu, qkv_all, wg_all, wu_all, stage, own_g, own_u, send, recv, lsem):
    me = Place()
    greet([me.xp, me.yp] + [me.along_z(step)[1] for step in (1, 2, 3)])
    copies, local = Copies(send, recv), Locals(lsem)
    move = Exchange(
        me, copies, local, stage, lambda z: qkv.at[z], lambda z: qkv_all.at[z]
    )
    move.start()
    width = wg.shape[1] // 8
    for src, own in ((wg, own_g), (wu, own_u)):
        for i in range(4):
            at = pl.ds(pl.multiple_of((2 * i + me.k) * width, 128), width)
            local(src.at[:, at], own.at[:, pl.ds(i * width, width)])
    local.wait()
    gathers = [
        Gather(me, copies, local, own_g, wg_all), Gather(me, copies, local, own_u, wu_all)
    ]
    for gather in gathers:
        gather.first()
    for gather in gathers:
        gather.second()
    for gather in gathers:
        gather.relay()
    move.pass_own()
    move.finish()
    for gather in gathers:
        gather.finish()


def to_heads(qkv, wg, wu):
    rows, columns = wg.shape
    return transfer(
        kernel_to_heads, "to_heads", 2,
        (qkv, wg, wu), [HBM] * 3,
        [
            shape(qkv.shape, BF16),
            shape((4, rows, columns // 2), BF16),
            shape((4, rows, columns // 2), BF16),
        ],
        [HBM] * 3,
        [pltpu.VMEM(qkv.shape[1:], BF16)] + [pltpu.VMEM((rows, columns // 2), BF16)] * 2,
        15, 12,
    )


def kernel_to_tokens(att, wd, wo, att_all, wd_all, wo_all, stage, own_d, own_o, send, recv, lsem):
    me = Place()
    greet([me.xp, me.yp] + [me.along_z(step)[1] for step in (1, 2, 3)])
    copies, local = Copies(send, recv), Locals(lsem)
    tokens, width = att_all.shape[0], att.shape[1]
    for src, own in ((wd, own_d), (wo, own_o)):
        rows = own.shape[0]
        local(src.at[pl.ds(pl.multiple_of(me.k * rows, 16), rows)], own)
    move = Exchange(
        me, copies, local, stage,
        lambda z: att.at[pl.ds(pl.multiple_of(z * tokens, 16), tokens)],
        lambda z: att_all.at[:, pl.ds(pl.multiple_of(z * width, 128), width)],
    )
    move.start()
    local.wait()
    gathers = [
        Gather(me, copies, local, own_o, wo_all), Gather(me, copies, local, own_d, wd_all)
    ]
    for gather in gathers:
        gather.first()
    for gather in gathers:
        gather.second()
    for gather in gathers:
        gather.relay()
    move.pass_own()
    move.finish()
    for gather in gathers:
        gather.finish()


def to_tokens(att, wd, wo):
    return transfer(
        kernel_to_tokens, "to_tokens", 3,
        (att, wd, wo), [HBM] * 3,
        [
            shape((att.shape[0] // 4, att.shape[1] * 4), BF16),
            shape((4, wd.shape[0] // 2, wd.shape[1]), BF16),
            shape((4, wo.shape[0] // 2, wo.shape[1]), BF16),
        ],
        [HBM] * 3,
        [
            pltpu.VMEM((att.shape[0] // 4, att.shape[1]), BF16),
            pltpu.VMEM((wd.shape[0] // 2, wd.shape[1]), BF16),
            pltpu.VMEM((wo.shape[0] // 2, wo.shape[1]), BF16),
        ],
        15, 6,
    )


def kernel_swap(src, dst, send, recv, lsem):
    me = Place()
    greet([me.sib])
    copy = Copies(send, recv)(src, dst, me.sib)
    copy.start()
    copy.wait()


def swap(value, number):
    return transfer(
        kernel_swap, "swap%d" % number, number, (value,), [HBM], shape(value.shape, value.dtype), HBM, [], 1, 1
    )


def run_scatters(me, copies, local, move, scatters, outs):
    move.start()
    for scatter in scatters:
        scatter.first()
    for scatter in scatters:
        scatter.second()
    for scatter in scatters:
        scatter.relay()
    move.pass_own()
    writes = []
    for scatter, out in zip(scatters, outs):
        scatter.finish(scatter.sum_a, scatter.sum_b)
        half = out.shape[0] // 2
        writes.append(local(scatter.sum_a, out.at[pl.ds(0, half)]))
        writes.append(local(scatter.sum_b, out.at[pl.ds(half, half)]))
    move.finish()
    for scatter in scatters:
        scatter.drain()
    for write in writes:
        write.wait()


def kernel_grads_to_heads(grads, down, grads_all, down_sum, stage, bufs, send, recv, lsem):
    me = Place()
    greet([me.xp, me.yp] + [me.along_z(step)[1] for step in (1, 2, 3)])
    copies, local = Copies(send, recv), Locals(lsem)
    width = grads_all.shape[2]
    move = Exchange(
        me, copies, local, stage,
        lambda z: grads.at[:, pl.ds(pl.multiple_of(z * width, 128), width)],
        lambda z: grads_all.at[z],
    )
    run_scatters(me, copies, local, move, [Scatter(me, copies, local, down, bufs)], [down_sum])


def grads_to_heads(grads, down):
    tokens, columns = grads.shape
    return transfer(
        kernel_grads_to_heads, "grads_to_heads", 4,
        (grads, down), [HBM] * 2,
        [shape((4, tokens, columns // 4), BF16), shape(down.shape[1:], BF16)],
        [HBM] * 2,
        [pltpu.VMEM((tokens, columns // 4), BF16)] + scatter_buffers(*down.shape[1:]), 9, 8,
    )


def kernel_grads_to_tokens(grads, gate, up, grads_all, gate_sum, up_sum, stage, bufs_g, bufs_u, send, recv, lsem):
    me = Place()
    greet([me.xp, me.yp] + [me.along_z(step)[1] for step in (1, 2, 3)])
    copies, local = Copies(send, recv), Locals(lsem)
    tokens, width = grads_all.shape[0], grads.shape[1]
    move = Exchange(
        me, copies, local, stage,
        lambda z: grads.at[pl.ds(pl.multiple_of(z * tokens, 16), tokens)],
        lambda z: grads_all.at[:, pl.ds(pl.multiple_of(z * width, 128), width)],
    )
    run_scatters(
        me, copies, local, move,
        [Scatter(me, copies, local, gate, bufs_g), Scatter(me, copies, local, up, bufs_u)],
        [gate_sum, up_sum],
    )


def grads_to_tokens(grads, gate, up):
    return transfer(
        kernel_grads_to_tokens, "grads_to_tokens", 5,
        (grads, gate, up), [HBM] * 3,
        [
            shape((grads.shape[0] // 4, grads.shape[1] * 4), BF16),
            shape(gate.shape[1:], BF16),
            shape(up.shape[1:], BF16),
        ],
        [HBM] * 3,
        [pltpu.VMEM((grads.shape[0] // 4, grads.shape[1]), BF16)]
        + scatter_buffers(*gate.shape[1:])
        + scatter_buffers(*up.shape[1:]),
        15, 14,
    )


def kernel_end(
    down, gate, up, out, qkv, small,
    down_tot, gate_tot, up_tot, out_tot, qkv_tot, small_tot,
    own_d, own_g, own_u, own_o, own_q, line_d, line_g, line_u, line_o, line_q, sc_o, sc_q, plane, line,
    send, recv, lsem,
):
    me = Place()
    greet([me.xp, me.yp, me.dp] + [me.along_ctx(step)[1] for step in range(1, 8)])
    copies, local = Copies(send, recv), Locals(lsem)
    total = SmallSum(me, copies, small, plane, line)
    total.first()
    loads = []
    for src, own in ((down, own_d), (gate, own_g), (up, own_u)):
        half = own.shape[1]
        loads.append(
            [local(src.at[pl.ds(i * half, half)], own.at[i]) for i in range(2)]
        )
    scatters = [Scatter(me, copies, local, out, sc_o), Scatter(me, copies, local, qkv, sc_q)]
    for scatter in scatters:
        scatter.first()
    for scatter in scatters:
        scatter.second()
    total.second()
    sums = [
        LineSum(me, copies, own, bufs)
        for own, bufs in (
            (own_d, line_d), (own_g, line_g), (own_u, line_u), (own_o, line_o), (own_q, line_q)
        )
    ]
    totals = (down_tot, gate_tot, up_tot, out_tot, qkv_tot)
    for load, entry in zip(loads, sums):
        for copy in load:
            copy.wait()
        entry.start()
    base = copies.take(len(sums) * 2)
    swaps, writes = [], []

    def finish(i):
        sums[i].spread()
        sums[i].arrive()
        half = sums[i].total.shape[1]
        for j in range(2):
            dst = totals[i].at[me.k, pl.ds(j * half, half)]
            copy = copies.at(base + 2 * i + j, sums[i].total.at[j], dst, me.sib)
            copy.start()
            swaps.append(copy)
            writes.append(local(sums[i].total.at[j], dst))

    sums[0].meet()
    scatters[0].relay()
    sums[0].close()
    sums[1].meet()
    scatters[1].relay()
    scatters[0].finish(own_o.at[0], own_o.at[1])
    sums[3].start()
    sums[1].close()
    sums[2].meet()
    finish(0)
    scatters[1].finish(own_q.at[0], own_q.at[1])
    sums[4].start()
    sums[2].close()
    sums[3].meet()
    finish(1)
    sums[3].close()
    sums[4].meet()
    finish(2)
    sums[4].close()
    finish(3)
    finish(4)
    total.finish(small_tot)
    total.drain()
    for scatter in scatters:
        scatter.drain()
    for entry in sums:
        entry.drain()
    for copy in swaps:
        copy.wait()
    for copy in writes:
        copy.wait()


def end(down, gate, up, out, qkv, small):
    sizes = [down.shape, gate.shape, up.shape, out.shape[1:], qkv.shape[1:]]
    own = [pltpu.VMEM((2, r // 2, c), BF16) for r, c in sizes]
    line = [pltpu.VMEM((5, r // 2, c), BF16) for r, c in sizes]
    return transfer(
        kernel_end, "end", 6,
        (down, gate, up, out, qkv, small), [HBM] * 5 + [VM],
        [shape((2,) + tuple(s), BF16) for s in sizes] + [shape(small.shape, F32)],
        [HBM] * 5 + [VM],
        own + line
        + scatter_buffers(*out.shape[1:])
        + scatter_buffers(*qkv.shape[1:])
        + [pltpu.VMEM((4,) + small.shape, F32), pltpu.VMEM((8,) + small.shape, F32)],
        10 + 12 + 5 * 8 + 10, 6 + 8 + 10,
    )


def assemble_kernel(gate, up, qkv, down, out, g_gate, g_up, g_q, g_k, g_v, g_down, g_out):
    for src, dst in ((gate, g_gate), (up, g_up)):
        width = src.shape[2] // 4
        for i in range(4):
            for j in range(2):
                dst[:, pl.ds((2 * i + j) * width, width)] = src[j, :, pl.ds(i * width, width)].astype(F32)
    q_size, size = GROUP * HEAD_SIZE, HEAD_SIZE
    for i in range(4):
        for j in range(2):
            head, at = 2 * i + j, HEAD_COLUMNS * i
            g_q[:, pl.ds(head * q_size, q_size)] = qkv[j, :, pl.ds(at, q_size)].astype(F32)
            g_k[:, pl.ds(head * size, size)] = qkv[j, :, pl.ds(at + q_size, size)].astype(F32)
            g_v[:, pl.ds(head * size, size)] = qkv[j, :, pl.ds(at + q_size + size, size)].astype(F32)
    g_down[...] = down[...].astype(F32)
    g_out[...] = out[...].astype(F32)


def assemble(gate, up, qkv, down, out):
    steps = 8

    def cut(dims):
        return pl.BlockSpec((2, dims[1] // steps, dims[2]), lambda i: (0, i, 0))

    def flat(rows, columns):
        return pl.BlockSpec((rows // steps, columns), lambda i: (i, 0)), shape((rows, columns), F32)

    rows, width = gate.shape[1], 2 * gate.shape[2]
    heads = KEY_VALUE_HEADS * HEAD_SIZE
    outs = [
        flat(rows, width), flat(rows, width), flat(rows, GROUP * heads), flat(rows, heads), flat(rows, heads),
        (cut(down.shape), shape(down.shape, F32)), (cut(out.shape), shape(out.shape, F32)),
    ]
    return pl.pallas_call(
        assemble_kernel,
        grid=(steps,),
        out_shape=[s for _, s in outs],
        in_specs=[cut(a.shape) for a in (gate, up, qkv, down, out)],
        out_specs=[b for b, _ in outs],
        compiler_params=pltpu.CompilerParams(vmem_limit_bytes=VMEM_LIMIT),
        name="assemble",
    )(gate, up, qkv, down, out)


def dot_nt(a, b, **kw):
    return lax.dot_general(a, b, (((1,), (1,)), ((), ())), preferred_element_type=F32, **kw)


def dot_nn(a, b):
    return lax.dot_general(a, b, (((1,), (0,)), ((), ())), preferred_element_type=F32)


def dot_tn(a, b):
    return lax.dot_general(a, b, (((0,), (0,)), ((), ())), preferred_element_type=F32)


BLOCK = 512
HIGHEST = lax.Precision.HIGHEST


def attend_kernel(qkv, att, lse, values):
    blocks = qkv.shape[0] // BLOCK
    k_at = pl.ds(GROUP * HEAD_SIZE, HEAD_SIZE)
    values[:, 0:HEAD_SIZE] = qkv[:, (GROUP + 1) * HEAD_SIZE :]
    values[:, HEAD_SIZE:] = jnp.ones((qkv.shape[0], HEAD_SIZE), BF16)
    row = lax.broadcasted_iota(jnp.int32, (BLOCK, BLOCK), 0)
    column = lax.broadcasted_iota(jnp.int32, (BLOCK, BLOCK), 1)
    allowed = column <= row

    @pl.loop(0, blocks)
    def _(i):
        rows = pl.ds(pl.multiple_of(i * BLOCK, BLOCK), BLOCK)
        for g in range(GROUP):
            q = qkv[rows, pl.ds(g * HEAD_SIZE, HEAD_SIZE)]

            def part(j, acc, q=q):
                keys = pl.ds(pl.multiple_of(j * BLOCK, BLOCK), BLOCK)
                e = jnp.exp(dot_nt(q, qkv[keys, k_at]) * SCALE)
                return acc + dot_nn(e.astype(BF16), values[keys, :])

            acc = lax.fori_loop(0, i, part, jnp.zeros((BLOCK, 2 * HEAD_SIZE), F32))
            e = jnp.exp(dot_nt(q, qkv[rows, k_at]) * SCALE)
            acc = acc + dot_nn(jnp.where(allowed, e, 0.0).astype(BF16), values[rows, :])
            total = acc[:, HEAD_SIZE:]
            att[rows, pl.ds(g * HEAD_SIZE, HEAD_SIZE)] = (acc[:, :HEAD_SIZE] / total).astype(BF16)
            mean = jnp.full((8, HEAD_SIZE), 1.0 / HEAD_SIZE, F32)
            lse[g, :, rows] = dot_nt(mean, jnp.log(total), precision=HIGHEST)


def attend(qkv):
    tokens = qkv.shape[0]
    return pl.pallas_call(
        attend_kernel,
        out_shape=[shape((tokens, GROUP * HEAD_SIZE), BF16), shape((GROUP, 8, tokens), F32)],
        in_specs=[VM],
        out_specs=[VM, VM],
        scratch_shapes=[pltpu.VMEM((tokens, 2 * HEAD_SIZE), BF16)],
        compiler_params=pltpu.CompilerParams(vmem_limit_bytes=VMEM_LIMIT),
        name="attend",
    )(qkv)


def attend_back_kernel(qkv, att, g_out, lse, grads, g_k, g_v):
    blocks = qkv.shape[0] // BLOCK
    k_at = pl.ds(GROUP * HEAD_SIZE, HEAD_SIZE)
    v_at = pl.ds((GROUP + 1) * HEAD_SIZE, HEAD_SIZE)
    g_k[...] = jnp.zeros_like(g_k)
    g_v[...] = jnp.zeros_like(g_v)
    key = lax.broadcasted_iota(jnp.int32, (BLOCK, BLOCK), 0)
    query = lax.broadcasted_iota(jnp.int32, (BLOCK, BLOCK), 1)
    allowed = key <= query

    @pl.loop(0, blocks)
    def _(i):
        rows = pl.ds(pl.multiple_of(i * BLOCK, BLOCK), BLOCK)
        for g in range(GROUP):
            head = pl.ds(g * HEAD_SIZE, HEAD_SIZE)
            q = qkv[rows, head]
            go = g_out[rows, head]
            product = go.astype(F32) * att[rows, head].astype(F32)
            delta = dot_nt(jnp.ones((8, HEAD_SIZE), F32), product, precision=HIGHEST)[0:1, :]
            log_sum = lse[g, 0:1, rows]

            def part(keys, masked, q=q, go=go, delta=delta, log_sum=log_sum):
                k, v = qkv[keys, k_at], qkv[keys, v_at]
                p = jnp.exp(dot_nt(k, q) * SCALE - log_sum)
                if masked:
                    p = jnp.where(allowed, p, 0.0)
                gs = (p * (dot_nt(v, go) - delta) * SCALE).astype(BF16)
                g_v[keys, :] += dot_nn(p.astype(BF16), go)
                g_k[keys, :] += dot_nn(gs, q)
                return dot_tn(gs, k)

            def step(j, acc, part=part):
                return acc + part(pl.ds(pl.multiple_of(j * BLOCK, BLOCK), BLOCK), False)

            acc = lax.fori_loop(0, i, step, jnp.zeros((BLOCK, HEAD_SIZE), F32))
            grads[rows, head] = (acc + part(rows, True)).astype(BF16)

    grads[:, k_at] = g_k[...].astype(BF16)
    grads[:, v_at] = g_v[...].astype(BF16)


def attend_back(qkv, att, g_out, lse):
    tokens = qkv.shape[0]
    return pl.pallas_call(
        attend_back_kernel,
        out_shape=shape(qkv.shape, BF16),
        in_specs=[VM] * 4,
        out_specs=VM,
        scratch_shapes=[pltpu.VMEM((tokens, HEAD_SIZE), F32)] * 2,
        compiler_params=pltpu.CompilerParams(vmem_limit_bytes=VMEM_LIMIT),
        name="attend_back",
    )(qkv, att, g_out, lse)


def turn(values, cosine_table, sine_table):
    half_width = HEAD_SIZE // 2
    swapped = jnp.concatenate([values[..., half_width:], values[..., :half_width]], -1)
    return values * cosine_table + swapped * sine_table


def heads_of(cosine_table, sine_table, projected, gain_q, gain_k):
    gain = jnp.concatenate([jnp.broadcast_to(gain_q, (GROUP, HEAD_SIZE)), gain_k[None]], 0)
    first = root_mean_norm(projected[:, :, : GROUP + 1], gain)
    first = turn(first, cosine_table[:, None, None, :], sine_table[:, None, None, :])
    return jnp.concatenate([first, projected[:, :, GROUP + 1 :]], 2)


def chip_step(
    hidden_in, teacher, valid, positions, norm_attn, w_query, key_projection, value_projection,
    gain_query, gain_key, w_out, norm_mlp, w_gate, w_up, w_down,
):
    f, c = lax.axis_index("fsdp"), lax.axis_index("ctx")
    k = c % 2
    rows = hidden_in.shape[1]
    tokens = 2 * rows
    width = hidden_in.shape[2]
    heads = KEY_VALUE_HEADS // 2
    misc = jnp.concatenate(
        [positions.reshape(-1, 128), valid.reshape(-1, 128), jnp.zeros((4, 128), jnp.int32)], 0
    ).astype(F32)
    gains = jnp.concatenate(
        [norm_attn, norm_mlp, gain_query, gain_key, jnp.zeros((448,), BF16)]
    ).astype(F32).reshape(8, 128)
    count = jnp.full((8, 128), jnp.sum(valid).astype(F32))
    w_qkv, x_pair, t_pair, misc_pair, gains_all, count = begin(
        w_query, key_projection, value_projection, hidden_in[0], teacher[0], misc, gains, count
    )
    w_qkv = w_qkv.reshape(width, -1)
    count_total = count[0, 0]
    x = x_pair.reshape(tokens, width).astype(F32)
    target = t_pair.reshape(tokens, width).astype(F32)
    token_positions = misc_pair[:, 0:2].reshape(tokens)
    weight_rows = misc_pair[:, 2:4].reshape(tokens)
    gain_one = gains_all[:, 0:2].reshape(width)
    gain_two = gains_all[:, 2:4].reshape(width)
    gain_q = gains_all[:, 4, 0:32].reshape(HEAD_SIZE)
    gain_k = gains_all[:, 4, 32:64].reshape(HEAD_SIZE)

    normed_one, norm_one_back = jax.vjp(root_mean_norm, x, gain_one)
    hidden_one = normed_one.astype(BF16)
    projected = jnp.dot(hidden_one, w_qkv, preferred_element_type=F32)
    cosine_table, sine_table = rope_tables(token_positions)
    qkv, heads_back = jax.vjp(
        partial(heads_of, cosine_table, sine_table),
        projected.reshape(tokens, heads, GROUP + 2, HEAD_SIZE), gain_q, gain_k,
    )
    qkv = qkv.astype(BF16).reshape(tokens, heads, HEAD_COLUMNS).transpose(1, 0, 2)
    qkv_all, wg, wu = to_heads(qkv, w_gate, w_up)
    qkv_all = qkv_all.reshape(4 * tokens, HEAD_COLUMNS)
    wg, wu = wg.reshape(width, -1), wu.reshape(width, -1)
    att, lse = attend(qkv_all)
    att_all, wd, wo = to_tokens(att, w_down, w_out)
    wd, wo = wd.reshape(-1, width), wo.reshape(-1, width)

    def over_cores(part, number):
        part = part.astype(BF16)
        return part.astype(F32) + swap(part, number).astype(F32)

    x2 = x + over_cores(jnp.dot(att_all, wo, preferred_element_type=F32), 7)
    normed_two, norm_two_back = jax.vjp(root_mean_norm, x2, gain_two)
    hidden_two = normed_two.astype(BF16)
    gate = jnp.dot(hidden_two, wg, preferred_element_type=F32)
    up = jnp.dot(hidden_two, wu, preferred_element_type=F32)
    gated, gated_back = jax.vjp(swiglu, gate, up)
    mid = gated.astype(BF16)
    fin = x2 + over_cores(jnp.dot(mid, wd, preferred_element_type=F32), 8)
    mismatch = fin - target
    sq_local = 0.5 * jnp.sum(weight_rows[:, None] * mismatch * mismatch)
    loss_scale = tokens // 2 * lax.axis_size("ctx") * lax.axis_size("fsdp") / 4.0
    g_fin = 2.0 * loss_scale / count_total * weight_rows[:, None] * mismatch
    g_dn = g_fin.astype(BF16)
    g_gate, g_up = gated_back(against(g_dn, wd))
    g_gate, g_up = g_gate.astype(BF16), g_up.astype(BF16)
    g_h2 = over_cores(against(g_gate, wg) + against(g_up, wu), 9)
    g_norm, grad_norm_mlp = norm_two_back(g_h2)
    g_x2 = g_fin + g_norm
    g_a = g_x2.astype(BF16)
    g_o = against(g_a, wo).astype(BF16)
    p_down = contract_rows(mid, g_dn).astype(BF16).reshape(4, -1, width)
    g_o_all, s_down = grads_to_heads(g_o, p_down)
    p_gate = contract_rows(hidden_two, g_gate).astype(BF16).reshape(4, width // 4, -1)
    p_up = contract_rows(hidden_two, g_up).astype(BF16).reshape(4, width // 4, -1)
    p_out = contract_rows(att_all, g_a).astype(BF16).reshape(4, -1, width)
    g_qkv = attend_back(qkv_all, att, g_o_all.reshape(4 * tokens, -1), lse)
    g_qkv_all, s_gate, s_up = grads_to_tokens(g_qkv, p_gate, p_up)
    g_proj, grad_gain_q, grad_gain_k = heads_back(
        g_qkv_all.reshape(tokens, heads, GROUP + 2, HEAD_SIZE).astype(F32)
    )
    g_proj = g_proj.astype(BF16).reshape(tokens, -1)
    p_qkv = contract_rows(hidden_one, g_proj).astype(BF16).reshape(4, width // 4, -1)
    g_h1 = over_cores(against(g_proj, w_qkv), 10)
    g_norm, grad_norm_attn = norm_one_back(g_h1)
    grad_input = lax.dynamic_slice_in_dim(g_x2 + g_norm, k * rows, rows, 0)
    small = jnp.concatenate(
        [
            0.5 * grad_norm_attn, 0.5 * grad_norm_mlp, grad_gain_q, grad_gain_k,
            jnp.full((128,), sq_local), jnp.zeros((640,), F32),
        ]
    ).reshape(24, 128)
    down, gate, up, out, qkv, small = end(s_down, s_gate, s_up, p_out, p_qkv, small)

    def mine(values):
        size = values.shape[0] // 4
        return lax.dynamic_slice_in_dim(values, f * size, size, 0)

    g_gate, g_up, g_q, g_k, g_v, g_down, g_out = assemble(gate, up, qkv, down, out)
    output = lax.dynamic_slice_in_dim(fin.astype(BF16), k * rows, rows, 0)
    return (
        output[None],
        small[18, 0] / count_total,
        grad_input[None],
        mine(small[0:8].reshape(-1)),
        g_q,
        g_k,
        g_v,
        mine(small[16]),
        mine(small[17]),
        g_out.reshape(-1, width),
        mine(small[8:16].reshape(-1)),
        g_gate,
        g_up,
        g_down.reshape(-1, width),
    )


def solution(mesh):
    chips = mesh.shape["fsdp"] == 4 and mesh.shape["ctx"] == KEY_VALUE_HEADS
    return jax.shard_map(
        chip_step if chips else per_device,
        mesh=mesh,
        in_specs=(
            P("fsdp", "ctx", None),
            P("fsdp", "ctx", None),
            P("fsdp", "ctx"),
            P("fsdp", "ctx"),
            P("fsdp"),
            P("fsdp", None),
            P("fsdp", None),
            P("fsdp", None),
            P("fsdp"),
            P("fsdp"),
            P("fsdp", None),
            P("fsdp"),
            P("fsdp", None),
            P("fsdp", None),
            P("fsdp", None),
        ),
        out_specs=(
            P("fsdp", "ctx", None),
            P(),
            P("fsdp", "ctx", None),
            P("fsdp"),
            P("fsdp", None),
            P("fsdp", None),
            P("fsdp", None),
            P("fsdp"),
            P("fsdp"),
            P("fsdp", None),
            P("fsdp"),
            P("fsdp", None),
            P("fsdp", None),
            P("fsdp", None),
        ),
        check_vma=False,
    )
```

```python
from functools import partial
import math

import jax
import jax.numpy as jnp
from jax import lax
from jax.experimental import pallas as pl
from jax.experimental.pallas import tpu as pltpu
from jax.sharding import PartitionSpec as P

QUERY_HEADS = 16
KEY_VALUE_HEADS = 8
HEAD_SIZE = 128


EPSILON = 1e-06


def root_mean_norm(values, norm_gain):
    return (
        values * lax.rsqrt(jnp.mean(values * values, axis=-1, keepdims=True) + EPSILON) * norm_gain
    )


def rope_tables(position_ids):
    half_width = HEAD_SIZE // 2
    freq_table = jnp.exp(
        jnp.arange(half_width, dtype=jnp.float32) * (-2.0 * math.log(1000000.0) / HEAD_SIZE)
    )
    angle_table = position_ids.astype(jnp.float32)[:, None] * freq_table[None, :]
    cosine_table = jnp.cos(angle_table)
    sine_table = jnp.sin(angle_table)
    return (
        jnp.concatenate([cosine_table, cosine_table], -1),
        jnp.concatenate([-sine_table, sine_table], -1),
    )


def apply_rotary(values, cosine_table, sine_table):
    half_width = HEAD_SIZE // 2
    swapped = jnp.concatenate([values[..., half_width:], values[..., :half_width]], -1)
    return values * cosine_table[:, None, :] + swapped * sine_table[:, None, :]


def shape_heads(cosine_table, sine_table, proj_query, projected_key, gain_q, key_gain):
    token_rows = proj_query.shape[0]
    query_rows = apply_rotary(
        root_mean_norm(proj_query.reshape(token_rows, QUERY_HEADS, HEAD_SIZE), gain_q),
        cosine_table,
        sine_table,
    )
    rows_of_keys = apply_rotary(
        root_mean_norm(projected_key.reshape(token_rows, KEY_VALUE_HEADS, HEAD_SIZE), key_gain),
        cosine_table,
        sine_table,
    )
    return (query_rows, rows_of_keys)


def swiglu(gate_proj, up_proj):
    return gate_proj / (1.0 + jnp.exp(-gate_proj)) * up_proj


def contract_rows(left_arr, right_arr):
    return lax.dot_general(
        left_arr, right_arr, (((0,), (0,)), ((), ())), preferred_element_type=jnp.float32
    )


def against(left_arr, right_arr):
    return lax.dot_general(
        left_arr, right_arr, (((1,), (1,)), ((), ())), preferred_element_type=jnp.float32
    )


def in_blocks(block_step, running, shard_portion):
    total_rows = shard_portion.shape[0]
    block_extent = 512
    block_count = total_rows // block_extent
    blocks = shard_portion.reshape((block_count, block_extent) + shard_portion.shape[1:])
    starts = jnp.arange(block_count, dtype=jnp.int32) * block_extent

    def scan_body(state, scan_item):
        return (block_step(state, scan_item[0], scan_item[1]), None)

    running, unused = lax.scan(scan_body, running, (blocks, starts))
    return running


def score_terms(
    query_rows,
    output_gradients,
    lse_heads,
    delta_heads,
    rows_of_keys,
    rows_of_values,
    query_index,
    key_index,
    score_scale,
):
    score_matrix = (
        jnp.einsum("alci,wli->lcaw", query_rows, rows_of_keys, preferred_element_type=jnp.float32)
        * score_scale
    )
    allowed = key_index[None, :] <= query_index[:, None]
    attention_probabilities = jnp.where(allowed, jnp.exp(score_matrix - lse_heads[..., None]), 0.0)
    grad_probs = jnp.einsum(
        "alci,wli->lcaw", output_gradients, rows_of_values, preferred_element_type=jnp.float32
    )
    score_gradient = (
        score_scale * attention_probabilities * (grad_probs - delta_heads[..., None])
    ).astype(jnp.bfloat16)
    return (attention_probabilities, score_gradient)


def per_device(
    hidden_in,
    teacher,
    valid,
    positions,
    norm_attn,
    w_query,
    key_projection,
    value_projection,
    gain_query,
    gain_key,
    w_out,
    norm_mlp,
    w_gate,
    w_up,
    w_down,
):
    gathered = (
        lax.all_gather(norm_attn, "fsdp", axis=0, tiled=True),
        lax.all_gather(w_query, "fsdp", axis=0, tiled=True),
        lax.all_gather(key_projection, "fsdp", axis=0, tiled=True),
        lax.all_gather(value_projection, "fsdp", axis=0, tiled=True),
        lax.all_gather(gain_query, "fsdp", axis=0, tiled=True),
        lax.all_gather(gain_key, "fsdp", axis=0, tiled=True),
        lax.all_gather(w_out, "fsdp", axis=0, tiled=True),
        lax.all_gather(norm_mlp, "fsdp", axis=0, tiled=True),
        lax.all_gather(w_gate, "fsdp", axis=0, tiled=True),
        lax.all_gather(w_up, "fsdp", axis=0, tiled=True),
        lax.all_gather(w_down, "fsdp", axis=0, tiled=True),
    )
    (
        full_norm_attn,
        full_query,
        full_key,
        full_value,
        full_gain_q,
        full_gain_k,
        full_out,
        full_norm_mlp,
        full_gate,
        full_up,
        full_down,
    ) = gathered
    grouped_heads = QUERY_HEADS // KEY_VALUE_HEADS
    score_scale = 1.0 / math.sqrt(HEAD_SIZE)
    residual = hidden_in[0].astype(jnp.float32)
    token_rows = residual.shape[0]
    query_index = lax.axis_index("ctx") * token_rows + jnp.arange(token_rows, dtype=jnp.int32)
    normed_one, norm_one_back = jax.vjp(
        root_mean_norm, residual, full_norm_attn.astype(jnp.float32)
    )
    hidden_one = normed_one.astype(jnp.bfloat16)
    proj_query = jnp.dot(hidden_one, full_query, preferred_element_type=jnp.float32)
    projected_key = jnp.dot(hidden_one, full_key, preferred_element_type=jnp.float32)
    projected_value = jnp.dot(hidden_one, full_value, preferred_element_type=jnp.float32)
    cosine_table, sine_table = rope_tables(positions[0])
    (query_per_head, heads_key), heads_back = jax.vjp(
        partial(shape_heads, cosine_table, sine_table),
        proj_query,
        projected_key,
        full_gain_q.astype(jnp.float32),
        full_gain_k.astype(jnp.float32),
    )
    query_reduced = query_per_head.astype(jnp.bfloat16).reshape(
        token_rows, KEY_VALUE_HEADS, grouped_heads, HEAD_SIZE
    )
    key_reduced = heads_key.astype(jnp.bfloat16)
    value_reduced = projected_value.astype(jnp.bfloat16).reshape(
        token_rows, KEY_VALUE_HEADS, HEAD_SIZE
    )
    key_value = jnp.stack(
        [
            key_reduced.reshape(token_rows, KEY_VALUE_HEADS * HEAD_SIZE),
            value_reduced.reshape(token_rows, KEY_VALUE_HEADS * HEAD_SIZE),
        ],
        axis=1,
    )

    def forward_block(running, shard_portion, first_row):
        run_max, run_total, run_acc = running
        rows_per_block = shard_portion.shape[0]
        rows_of_keys = shard_portion[:, 0].reshape(rows_per_block, KEY_VALUE_HEADS, HEAD_SIZE)
        rows_of_values = shard_portion[:, 1].reshape(rows_per_block, KEY_VALUE_HEADS, HEAD_SIZE)
        key_index = first_row + jnp.arange(rows_per_block, dtype=jnp.int32)
        allowed = key_index[None, :] <= query_index[:, None]
        score_matrix = (
            jnp.einsum(
                "alci,wli->lcaw", query_reduced, rows_of_keys, preferred_element_type=jnp.float32
            )
            * score_scale
        )
        score_matrix = jnp.where(allowed, score_matrix, -1e30)
        new_max = jnp.maximum(run_max, jnp.max(score_matrix, axis=-1))
        weights_part = jnp.where(allowed, jnp.exp(score_matrix - new_max[..., None]), 0.0)
        factor = jnp.exp(run_max - new_max)
        run_total = run_total * factor + jnp.sum(weights_part, axis=-1)
        run_acc = run_acc * factor[..., None] + jnp.einsum(
            "exfw,weq->exfq",
            weights_part.astype(jnp.bfloat16),
            rows_of_values,
            preferred_element_type=jnp.float32,
        )
        return (new_max, run_total, run_acc)

    start_state = (
        jnp.full((KEY_VALUE_HEADS, grouped_heads, token_rows), -1e30, jnp.float32),
        jnp.zeros((KEY_VALUE_HEADS, grouped_heads, token_rows), jnp.float32),
        jnp.zeros((KEY_VALUE_HEADS, grouped_heads, token_rows, HEAD_SIZE), jnp.float32),
    )
    run_max, run_total, run_acc = in_blocks(
        forward_block, start_state, lax.all_gather(key_value, "ctx", axis=0, tiled=True)
    )
    log_total = run_max + jnp.log(run_total)
    attn_rows = jnp.transpose(run_acc / run_total[..., None], (2, 0, 1, 3))
    attn_low = attn_rows.reshape(token_rows, QUERY_HEADS * HEAD_SIZE).astype(jnp.bfloat16)
    mid_resid = residual + jnp.dot(attn_low, full_out, preferred_element_type=jnp.float32)
    normed_two, norm_two_back = jax.vjp(
        root_mean_norm, mid_resid, full_norm_mlp.astype(jnp.float32)
    )
    hidden_two = normed_two.astype(jnp.bfloat16)
    gate_proj = jnp.dot(hidden_two, full_gate, preferred_element_type=jnp.float32)
    up_proj = jnp.dot(hidden_two, full_up, preferred_element_type=jnp.float32)
    gated, gated_back = jax.vjp(swiglu, gate_proj, up_proj)
    gated_low = gated.astype(jnp.bfloat16)
    final_rows = mid_resid + jnp.dot(gated_low, full_down, preferred_element_type=jnp.float32)
    target = teacher[0].astype(jnp.float32)
    weight_rows = valid[0].astype(jnp.float32)
    mismatch = final_rows - target
    sq_local = jnp.sum(weight_rows[:, None] * mismatch * mismatch)
    count_local = jnp.sum(weight_rows)
    sq_total, count_total = lax.psum((sq_local, count_local), ("fsdp", "ctx"))
    loss_value = sq_total / count_total
    loss_scale = token_rows * lax.axis_size("ctx") * lax.axis_size("fsdp") / 4.0
    grad_final = 2.0 * loss_scale / count_total * weight_rows[:, None] * mismatch
    grad_down_in = grad_final.astype(jnp.bfloat16)
    grad_w_down = contract_rows(gated_low, grad_down_in)
    grad_gated = against(grad_down_in, full_down)
    grad_gate_proj, grad_up_proj = gated_back(grad_gated)
    gate_low = grad_gate_proj.astype(jnp.bfloat16)
    up_low = grad_up_proj.astype(jnp.bfloat16)
    grad_w_gate = contract_rows(hidden_two, gate_low)
    grad_w_up = contract_rows(hidden_two, up_low)
    grad_hidden_two = against(gate_low, full_gate) + against(up_low, full_up)
    grad_mid_norm, grad_norm_mlp = norm_two_back(grad_hidden_two)
    grad_mid = grad_final + grad_mid_norm
    grad_branch = grad_mid.astype(jnp.bfloat16)
    grad_w_out = contract_rows(attn_low, grad_branch)
    attention_gradient = against(grad_branch, full_out).astype(jnp.bfloat16)
    attention_head_gradient = attention_gradient.reshape(
        token_rows, KEY_VALUE_HEADS, grouped_heads, HEAD_SIZE
    )
    row_delta = jnp.sum(attention_head_gradient.astype(jnp.float32) * attn_rows, axis=-1)
    delta_heads = jnp.transpose(row_delta, (1, 2, 0))
    row_stats = jnp.stack(
        [
            jnp.transpose(log_total, (2, 0, 1)).reshape(token_rows, QUERY_HEADS),
            row_delta.reshape(token_rows, QUERY_HEADS),
        ],
        axis=1,
    )

    def block_of_queries(grad_query, shard_portion, first_row):
        rows_per_block = shard_portion.shape[0]
        rows_of_keys = shard_portion[:, 0].reshape(rows_per_block, KEY_VALUE_HEADS, HEAD_SIZE)
        rows_of_values = shard_portion[:, 1].reshape(rows_per_block, KEY_VALUE_HEADS, HEAD_SIZE)
        key_index = first_row + jnp.arange(rows_per_block, dtype=jnp.int32)
        attention_probabilities, score_gradient = score_terms(
            query_reduced,
            attention_head_gradient,
            log_total,
            delta_heads,
            rows_of_keys,
            rows_of_values,
            query_index,
            key_index,
            score_scale,
        )
        return grad_query + jnp.einsum(
            "jyux,xji->ujyi", score_gradient, rows_of_keys, preferred_element_type=jnp.float32
        )

    grad_query = in_blocks(
        block_of_queries,
        jnp.zeros((token_rows, KEY_VALUE_HEADS, grouped_heads, HEAD_SIZE), jnp.float32),
        lax.all_gather(key_value, "ctx", axis=0, tiled=True),
    )
    all_stats = lax.all_gather(row_stats.astype(jnp.bfloat16), "ctx", axis=0, tiled=True).astype(
        row_stats.dtype
    )
    query_pair = jnp.stack(
        [query_reduced.reshape(token_rows, QUERY_HEADS * HEAD_SIZE), attention_gradient], axis=1
    )

    def key_block(running, shard_portion, first_row):
        grad_key, value_gradient = running
        rows_per_block = shard_portion.shape[0]
        query_rows = shard_portion[:, 0].reshape(
            rows_per_block, KEY_VALUE_HEADS, grouped_heads, HEAD_SIZE
        )
        output_gradients = shard_portion[:, 1].reshape(
            rows_per_block, KEY_VALUE_HEADS, grouped_heads, HEAD_SIZE
        )
        partial_statistics = lax.dynamic_slice_in_dim(all_stats, first_row, rows_per_block, 0)
        partial_logsumexp = jnp.transpose(
            partial_statistics[:, 0].reshape(rows_per_block, KEY_VALUE_HEADS, grouped_heads),
            (1, 2, 0),
        )
        partial_delta = jnp.transpose(
            partial_statistics[:, 1].reshape(rows_per_block, KEY_VALUE_HEADS, grouped_heads),
            (1, 2, 0),
        )
        part_index = first_row + jnp.arange(rows_per_block, dtype=jnp.int32)
        attention_probabilities, score_gradient = score_terms(
            query_rows,
            output_gradients,
            partial_logsumexp,
            partial_delta,
            key_reduced,
            value_reduced,
            part_index,
            query_index,
            score_scale,
        )
        grad_key = grad_key + jnp.einsum(
            "wzlj,lwzy->jwy", score_gradient, query_rows, preferred_element_type=jnp.float32
        )
        value_gradient = value_gradient + jnp.einsum(
            "wzlj,lwzy->jwy",
            attention_probabilities.astype(jnp.bfloat16),
            output_gradients,
            preferred_element_type=jnp.float32,
        )
        return (grad_key, value_gradient)

    key_state = (
        jnp.zeros((token_rows, KEY_VALUE_HEADS, HEAD_SIZE), jnp.float32),
        jnp.zeros((token_rows, KEY_VALUE_HEADS, HEAD_SIZE), jnp.float32),
    )
    grad_key, value_gradient = in_blocks(
        key_block, key_state, lax.all_gather(query_pair, "ctx", axis=0, tiled=True)
    )
    grad_proj_q, grad_proj_k, grad_gain_q, grad_gain_k = heads_back(
        (grad_query.reshape(token_rows, QUERY_HEADS, HEAD_SIZE), grad_key)
    )
    query_grad_low = grad_proj_q.astype(jnp.bfloat16)
    key_grad_low = grad_proj_k.astype(jnp.bfloat16)
    value_gradient_reduced = value_gradient.reshape(token_rows, KEY_VALUE_HEADS * HEAD_SIZE).astype(
        jnp.bfloat16
    )
    grad_w_query = contract_rows(hidden_one, query_grad_low)
    grad_w_key = contract_rows(hidden_one, key_grad_low)
    grad_w_value = contract_rows(hidden_one, value_gradient_reduced)
    grad_hidden_one = (
        against(query_grad_low, full_query)
        + against(key_grad_low, full_key)
        + against(value_gradient_reduced, full_value)
    )
    grad_resid_norm, grad_norm_attn = norm_one_back(grad_hidden_one)
    grad_input = grad_mid + grad_resid_norm
    grads = (
        grad_norm_attn,
        grad_w_query,
        grad_w_key,
        grad_w_value,
        grad_gain_q,
        grad_gain_k,
        grad_w_out,
        grad_norm_mlp,
        grad_w_gate,
        grad_w_up,
        grad_w_down,
    )
    shares = (
        lax.psum_scatter(grads[0], ("fsdp", "ctx"), scatter_dimension=0, tiled=True),
        lax.psum_scatter(grads[1], ("fsdp", "ctx"), scatter_dimension=0, tiled=True),
        lax.psum_scatter(grads[2], ("fsdp", "ctx"), scatter_dimension=0, tiled=True),
        lax.psum_scatter(grads[3], ("fsdp", "ctx"), scatter_dimension=0, tiled=True),
        lax.psum_scatter(grads[4], ("fsdp", "ctx"), scatter_dimension=0, tiled=True),
        lax.psum_scatter(grads[5], ("fsdp", "ctx"), scatter_dimension=0, tiled=True),
        lax.psum_scatter(grads[6], ("fsdp", "ctx"), scatter_dimension=0, tiled=True),
        lax.psum_scatter(grads[7], ("fsdp", "ctx"), scatter_dimension=0, tiled=True),
        lax.psum_scatter(grads[8], ("fsdp", "ctx"), scatter_dimension=0, tiled=True),
        lax.psum_scatter(grads[9], ("fsdp", "ctx"), scatter_dimension=0, tiled=True),
        lax.psum_scatter(grads[10], ("fsdp", "ctx"), scatter_dimension=0, tiled=True),
    )
    shares = (
        lax.all_gather(shares[0].astype(jnp.bfloat16), "ctx", axis=0, tiled=True).astype(
            jnp.float32
        ),
        lax.all_gather(shares[1].astype(jnp.bfloat16), "ctx", axis=0, tiled=True).astype(
            jnp.float32
        ),
        lax.all_gather(shares[2].astype(jnp.bfloat16), "ctx", axis=0, tiled=True).astype(
            jnp.float32
        ),
        lax.all_gather(shares[3].astype(jnp.bfloat16), "ctx", axis=0, tiled=True).astype(
            jnp.float32
        ),
        lax.all_gather(shares[4].astype(jnp.bfloat16), "ctx", axis=0, tiled=True).astype(
            jnp.float32
        ),
        lax.all_gather(shares[5].astype(jnp.bfloat16), "ctx", axis=0, tiled=True).astype(
            jnp.float32
        ),
        lax.all_gather(shares[6].astype(jnp.bfloat16), "ctx", axis=0, tiled=True).astype(
            jnp.float32
        ),
        lax.all_gather(shares[7].astype(jnp.bfloat16), "ctx", axis=0, tiled=True).astype(
            jnp.float32
        ),
        lax.all_gather(shares[8].astype(jnp.bfloat16), "ctx", axis=0, tiled=True).astype(
            jnp.float32
        ),
        lax.all_gather(shares[9].astype(jnp.bfloat16), "ctx", axis=0, tiled=True).astype(
            jnp.float32
        ),
        lax.all_gather(shares[10].astype(jnp.bfloat16), "ctx", axis=0, tiled=True).astype(
            jnp.float32
        ),
    )
    return (
        final_rows.astype(jnp.bfloat16)[None],
        loss_value,
        grad_input[None],
        shares[0],
        shares[1],
        shares[2],
        shares[3],
        shares[4],
        shares[5],
        shares[6],
        shares[7],
        shares[8],
        shares[9],
        shares[10],
    )


MESH = pl.DeviceIdType.MESH
BF16 = jnp.bfloat16
F32 = jnp.float32
GROUP = QUERY_HEADS // KEY_VALUE_HEADS
HEAD_COLUMNS = (GROUP + 2) * HEAD_SIZE
SCALE = 1.0 / math.sqrt(HEAD_SIZE)
VMEM_LIMIT = 60 * 1024 * 1024


class Place:
    def __init__(self):
        self.f = lax.axis_index("fsdp")
        self.c = lax.axis_index("ctx")
        self.z = self.c // 2
        self.k = self.c % 2
        self.fx = self.f + 1 - 2 * (self.f % 2)
        self.fy = (self.f + 2) % 4
        self.fd = 3 - self.f
        self.xp = (self.fx, self.c)
        self.yp = (self.fy, self.c)
        self.dp = (self.fd, self.c)
        self.sib = (self.f, self.c + 1 - 2 * self.k)

    def along_z(self, step):
        other = (self.z + step) % 4
        return other, (self.f, 2 * other + self.k)

    def along_ctx(self, step):
        other = (self.c + step) % 8
        return other, (self.f, other)


def greet(partners):
    barrier = pltpu.get_barrier_semaphore()
    for partner in partners:
        pl.semaphore_signal(barrier, inc=1, device_id=partner, device_id_type=MESH)
    pl.semaphore_wait(barrier, len(partners))


class Copies:
    def __init__(self, send, recv):
        self.send, self.recv, self.used = send, recv, 0

    def take(self, count):
        first = self.used
        self.used += count
        return first

    def at(self, index, src, dst, partner):
        return pltpu.make_async_remote_copy(
            src_ref=src,
            dst_ref=dst,
            send_sem=self.send.at[index],
            recv_sem=self.recv.at[index],
            device_id=partner,
            device_id_type=MESH,
        )

    def __call__(self, src, dst, partner):
        return self.at(self.take(1), src, dst, partner)


class Locals:
    def __init__(self, sems):
        self.sems, self.used, self.open = sems, 0, []

    def __call__(self, src, dst):
        copy = pltpu.make_async_copy(src, dst, self.sems.at[self.used])
        self.used += 1
        copy.start()
        self.open.append(copy)
        return copy

    def wait(self):
        for copy in self.open:
            copy.wait()
        self.open = []

    def alone(self, src, dst):
        copy = self(src, dst)
        self.open.pop()
        return copy


def add_rows(dst, sources):
    rows = dst.shape[0]
    step = 32

    @pl.loop(0, rows // step)
    def _(i):
        part = pl.ds(pl.multiple_of(i * step, step), step)
        total = sources[0][part, :].astype(F32)
        for source in sources[1:]:
            total = total + source[part, :].astype(F32)
        dst[part, :] = total.astype(dst.dtype)


class Gather:
    def __init__(self, me, copies, local, own, buf):
        half = buf.shape[1] // 2
        a, b = pl.ds(0, half), pl.ds(half, half)
        own_a, own_b = buf.at[me.f, a], buf.at[me.f, b]
        self.local, self.own, self.slot = local, own, buf.at[me.f]
        self.a_x = copies(own.at[a], own_a, me.xp)
        self.b_y = copies(own.at[b], own_b, me.yp)
        self.b_x = copies(own.at[b], own_b, me.xp)
        self.a_y = copies(own.at[a], own_a, me.yp)
        self.on_y = copies(buf.at[me.fx, a], buf.at[me.fx, a], me.yp)
        self.on_x = copies(buf.at[me.fy, b], buf.at[me.fy, b], me.xp)

    def first(self):
        self.a_x.start()
        self.b_y.start()

    def second(self):
        self.b_x.start()
        self.a_y.start()
        self.kept = self.local.alone(self.own, self.slot)

    def relay(self):
        self.a_x.wait_recv()
        self.on_y.start()
        self.b_y.wait_recv()
        self.on_x.start()

    def finish(self):
        for copy in (self.b_x, self.a_y, self.on_y, self.on_x):
            copy.wait_recv()
        for copy in (self.a_x, self.b_y, self.b_x, self.a_y, self.on_y, self.on_x):
            copy.wait_send()
        self.kept.wait()


class Scatter:
    def __init__(self, me, copies, local, part, bufs):
        half = part.shape[1] // 2
        a, b = pl.ds(0, half), pl.ds(half, half)
        slot = [bufs.at[i] for i in range(10)]
        self.fwd_a, self.fwd_b, self.own_a, self.own_b = slot[0:4]
        self.rx_own, self.rx_fwd, self.ry_own, self.ry_fwd, self.r2_a, self.r2_b = slot[4:10]
        self.d_x = copies(part.at[me.fd, a], self.rx_fwd, me.xp)
        self.d_y = copies(part.at[me.fd, b], self.ry_fwd, me.yp)
        self.o_x = copies(part.at[me.fx, a], self.rx_own, me.xp)
        self.o_y = copies(part.at[me.fy, b], self.ry_own, me.yp)
        self.to_y = copies(self.fwd_a, self.r2_a, me.yp)
        self.to_x = copies(self.fwd_b, self.r2_b, me.xp)
        self.local, self.me, self.part, self.a, self.b = local, me, part, a, b

    def first(self):
        self.d_x.start()
        self.d_y.start()

    def second(self):
        self.o_x.start()
        self.o_y.start()
        me, part = self.me, self.part
        self.mine = [
            self.local.alone(part.at[me.fy, self.a], self.fwd_a),
            self.local.alone(part.at[me.fx, self.b], self.fwd_b),
            self.local.alone(part.at[me.f, self.a], self.own_a),
            self.local.alone(part.at[me.f, self.b], self.own_b),
        ]

    def relay(self):
        for copy in self.mine:
            copy.wait()
        self.d_x.wait_recv()
        add_rows(self.fwd_a, [self.fwd_a, self.rx_fwd])
        self.to_y.start()
        self.d_y.wait_recv()
        add_rows(self.fwd_b, [self.fwd_b, self.ry_fwd])
        self.to_x.start()

    def finish(self, sum_a, sum_b):
        self.o_x.wait_recv()
        self.to_y.wait_recv()
        add_rows(sum_a, [self.own_a, self.rx_own, self.r2_a])
        self.o_y.wait_recv()
        self.to_x.wait_recv()
        add_rows(sum_b, [self.own_b, self.ry_own, self.r2_b])

    def drain(self):
        for copy in (self.d_x, self.d_y, self.o_x, self.o_y, self.to_y, self.to_x):
            copy.wait_send()


class LineSum:
    def __init__(self, me, copies, own, bufs):
        z, f, k = me.z, me.f, me.k
        self.inner = (z == 1) | (z == 2)
        self.outer = (z == 0) | (z == 3)
        self.mine = z - 1
        self.theirs = 2 - z
        self.own, self.from_outer, self.total, self.from_inner = own, bufs.at[0:2], bufs.at[2:4], bufs.at[4]
        self.copies = copies
        self.base = copies.take(8)
        self.inner_of = (f, 2 * (1 + z // 3) + k)
        self.outer_of = (f, 2 * (3 * (z - 1)) + k)
        self.partner = (f, 2 * (3 - z) + k)

    def inward(self, half):
        return self.copies.at(
            self.base + half, self.own.at[half], self.from_outer.at[half], self.inner_of
        )

    def across(self, half):
        return self.copies.at(
            self.base + 2 + half, self.own.at[half], self.from_inner, self.partner
        )

    def back_across(self, half):
        return self.copies.at(
            self.base + 4 + half, self.total.at[half], self.total.at[half], self.partner
        )

    def outward(self, half):
        return self.copies.at(
            self.base + 6 + half, self.total.at[half], self.total.at[half], self.outer_of
        )

    def start(self):
        @pl.when(self.outer)
        def _():
            self.inward(0).start()
            self.inward(1).start()

    def meet(self):
        @pl.when(self.inner)
        def _():
            t, m = self.theirs, self.mine
            self.inward(t).wait_recv()
            add_rows(self.own.at[t], [self.own.at[t], self.from_outer.at[t]])
            self.across(t).start()

    def close(self):
        @pl.when(self.inner)
        def _():
            m = self.mine
            self.inward(m).wait_recv()
            self.across(m).wait_recv()
            add_rows(
                self.total.at[m], [self.own.at[m], self.from_outer.at[m], self.from_inner]
            )
            self.back_across(m).start()
            self.outward(m).start()

    def spread(self):
        @pl.when(self.inner)
        def _():
            t = self.theirs
            self.back_across(t).wait_recv()
            self.outward(t).start()

    def arrive(self):
        @pl.when(self.outer)
        def _():
            self.outward(0).wait_recv()
            self.outward(1).wait_recv()

    def drain(self):
        @pl.when(self.outer)
        def _():
            self.inward(0).wait_send()
            self.inward(1).wait_send()

        @pl.when(self.inner)
        def _():
            self.across(self.theirs).wait_send()
            self.back_across(self.mine).wait_send()
            self.outward(0).wait_send()
            self.outward(1).wait_send()


HBM = pl.BlockSpec(memory_space=pl.ANY)
VM = pl.BlockSpec(memory_space=pltpu.VMEM)


def transfer(kernel, name, number, args, in_specs, outs, out_specs, scratch, copies, local):
    return pl.pallas_call(
        kernel,
        out_shape=outs,
        in_specs=in_specs,
        out_specs=out_specs,
        scratch_shapes=scratch
        + [
            pltpu.SemaphoreType.DMA((copies,)),
            pltpu.SemaphoreType.DMA((copies,)),
            pltpu.SemaphoreType.DMA((local,)),
        ],
        compiler_params=pltpu.CompilerParams(
            collective_id=number, has_side_effects=True, vmem_limit_bytes=VMEM_LIMIT
        ),
        name=name,
    )(*args)


def shape(dims, dtype):
    return jax.ShapeDtypeStruct(dims, dtype)


def kernel_swap(src, dst, send, recv, lsem):
    me = Place()
    greet([me.sib])
    copy = Copies(send, recv)(src, dst, me.sib)
    copy.start()
    copy.wait()


def swap(value, number):
    return transfer(
        kernel_swap, "swap%d" % number, number, (value,), [HBM], shape(value.shape, value.dtype), HBM, [], 1, 1
    )


def assemble_kernel(gate, up, heads, down, out, g_gate, g_up, g_q, g_k, g_v, g_down, g_out):
    for src, dst in ((gate, g_gate), (up, g_up)):
        width = src.shape[2] // 4
        for i in range(4):
            for j in range(2):
                dst[:, pl.ds((2 * i + j) * width, width)] = src[j, :, pl.ds(i * width, width)].astype(F32)
    q_size, size = GROUP * HEAD_SIZE, HEAD_SIZE
    for head in range(KEY_VALUE_HEADS):
        g_q[:, pl.ds(head * q_size, q_size)] = heads[head, :, pl.ds(0, q_size)].astype(F32)
        g_k[:, pl.ds(head * size, size)] = heads[head, :, pl.ds(q_size, size)].astype(F32)
        g_v[:, pl.ds(head * size, size)] = heads[head, :, pl.ds(q_size + size, size)].astype(F32)
    g_down[...] = down[...].astype(F32)
    g_out[...] = out[...].astype(F32)


def assemble(gate, up, heads, down, out):
    steps = 8

    def cut(dims):
        return pl.BlockSpec((dims[0], dims[1] // steps, dims[2]), lambda i: (0, i, 0))

    def flat(rows, columns):
        return pl.BlockSpec((rows // steps, columns), lambda i: (i, 0)), shape((rows, columns), F32)

    rows, width = gate.shape[1], 2 * gate.shape[2]
    all_heads = KEY_VALUE_HEADS * HEAD_SIZE
    outs = [
        flat(rows, width), flat(rows, width), flat(rows, GROUP * all_heads), flat(rows, all_heads), flat(rows, all_heads),
        (cut(down.shape), shape(down.shape, F32)), (cut(out.shape), shape(out.shape, F32)),
    ]
    return pl.pallas_call(
        assemble_kernel,
        grid=(steps,),
        out_shape=[s for _, s in outs],
        in_specs=[cut(a.shape) for a in (gate, up, heads, down, out)],
        out_specs=[b for b, _ in outs],
        compiler_params=pltpu.CompilerParams(vmem_limit_bytes=VMEM_LIMIT),
        name="assemble",
    )(gate, up, heads, down, out)


def dot_nt(a, b, **kw):
    return lax.dot_general(a, b, (((1,), (1,)), ((), ())), preferred_element_type=F32, **kw)


def dot_nn(a, b):
    return lax.dot_general(a, b, (((1,), (0,)), ((), ())), preferred_element_type=F32)


def dot_tn(a, b):
    return lax.dot_general(a, b, (((0,), (0,)), ((), ())), preferred_element_type=F32)


HIGHEST = lax.Precision.HIGHEST


class SmallSum:
    def __init__(self, me, copies, own, plane, pair, line):
        self.me, self.own, self.plane, self.pair, self.line = me, own, plane, pair, line
        self.one = [copies(own, plane.at[me.f], partner) for partner in (me.xp, me.yp, me.dp)]
        self.two = [copies(pair.at[me.k], pair.at[me.k], me.sib)]
        self.three = [
            copies(line.at[me.z], line.at[me.z], me.along_z(step)[1]) for step in (1, 2, 3)
        ]

    def first(self):
        for copy in self.one:
            copy.start()
        self.plane[self.me.f] = self.own[...]

    def second(self):
        for copy in self.one:
            copy.wait_recv()
        plane = self.plane
        self.pair[self.me.k] = (plane[0] + plane[1]) + (plane[2] + plane[3])
        self.two[0].start()

    def third(self):
        self.two[0].wait_recv()
        self.line[self.me.z] = self.pair[0] + self.pair[1]
        for copy in self.three:
            copy.start()

    def finish(self, dst):
        for copy in self.three:
            copy.wait_recv()
        line = self.line
        dst[...] = (line[0] + line[1]) + (line[2] + line[3])

    def drain(self):
        for copy in self.one + self.two + self.three:
            copy.wait_send()


class Spread:
    def __init__(self, me, copies, held):
        self.me, self.held, self.copies = me, held, copies
        self.up, self.down = copies.take(3), copies.take(3)
        self.cross_own, self.cross_up, self.cross_down = copies.take(1), copies.take(3), copies.take(3)

    def hop(self, base, hop, block, partner):
        ref = self.held.at[block]
        return self.copies.at(base + hop - 1, ref, ref, partner)

    def rise(self, hop):
        me = self.me
        return self.hop(self.up, hop, me.c - 2 * (hop - 1), (me.f, me.c + 2))

    def fall(self, hop):
        me = self.me
        return self.hop(self.down, hop, me.c + 2 * (hop - 1), (me.f, me.c - 2))

    def across(self, base, hop, block):
        return self.hop(base, hop, block, self.me.sib)

    def start(self):
        z = self.me.z

        @pl.when(z < 3)
        def _():
            self.rise(1).start()

        @pl.when(z > 0)
        def _():
            self.fall(1).start()

        self.across(self.cross_own, 1, self.me.c).start()

    def step(self, hop):
        z, c = self.me.z, self.me.c

        @pl.when(z >= hop)
        def _():
            self.rise(hop).wait_recv()
            if hop < 3:

                @pl.when(z < 3)
                def _():
                    self.rise(hop + 1).start()

            self.across(self.cross_up, hop, c - 2 * hop).start()

        @pl.when(z + hop <= 3)
        def _():
            self.fall(hop).wait_recv()
            if hop < 3:

                @pl.when(z > 0)
                def _():
                    self.fall(hop + 1).start()

            self.across(self.cross_down, hop, c + 2 * hop).start()

    def crossed(self, hop):
        z, c = self.me.z, self.me.c
        if hop == 0:
            self.across(self.cross_own, 1, c).wait_recv()
            return

        @pl.when(z >= hop)
        def _():
            self.across(self.cross_up, hop, c - 2 * hop).wait_recv()

        @pl.when(z + hop <= 3)
        def _():
            self.across(self.cross_down, hop, c + 2 * hop).wait_recv()

    def drain(self):
        z, c = self.me.z, self.me.c
        self.across(self.cross_own, 1, c).wait_send()
        for hop in (1, 2, 3):

            @pl.when((z >= hop - 1) & (z < 3))
            def _(hop=hop):
                self.rise(hop).wait_send()

            @pl.when((z + hop - 1 <= 3) & (z > 0))
            def _(hop=hop):
                self.fall(hop).wait_send()

            @pl.when(z >= hop)
            def _(hop=hop):
                self.across(self.cross_up, hop, c - 2 * hop).wait_send()

            @pl.when(z + hop <= 3)
            def _(hop=hop):
                self.across(self.cross_down, hop, c + 2 * hop).wait_send()


def half_turn(values):
    return pltpu.roll(values, HEAD_SIZE // 2, 1)


def rotary_tables(position_rows, freq, cosines, sines, at):
    columns = jnp.transpose(position_rows)
    lane = lax.broadcasted_iota(jnp.int32, (HEAD_SIZE, HEAD_SIZE), 1)
    first = lane < HEAD_SIZE // 2
    for r in range(2):
        angle = columns[:, r : r + 1] * freq
        turns = jnp.floor(angle * (2.0 / math.pi) + 0.5)
        rest = ((angle - turns * 1.5703125) - turns * 4.837512969970703125e-04) - turns * 7.549789954891882e-08
        square = rest * rest
        sine = rest + rest * square * (
            -1.6666654611e-01 + square * (8.3321608736e-03 - square * 1.9515295891e-04)
        )
        cosine = 1.0 + square * (
            -0.5 + square * (4.166664568298827e-02 + square * (-1.388731625493765e-03 + square * 2.443315711809948e-05))
        )
        quarter = (turns.astype(jnp.int32) + jnp.where(first, 0, 3)) & 3
        odd = (quarter & 1) == 1
        value = jnp.where(odd, sine, cosine)
        value = jnp.where((quarter == 1) | (quarter == 2), -value, value)
        other = half_turn(value)
        rows = pl.ds(pl.multiple_of(at + r * 128, 128), 128)
        cosines[rows, :] = jnp.where(first, value, other)
        sines[rows, :] = jnp.where(first, -other, value)


def head_norm(u):
    return lax.rsqrt(jnp.mean(u * u, axis=-1, keepdims=True) + EPSILON)


def kernel_forward(
    wq, wk, wv, wo, wg, wu, wd, x, t, misc, gains, count, freq,
    x_pair, t_pair, misc_all, gains_all, count_out,
    w_head, wo_all, wg_all, wu_all, wd_all,
    h_all, proj, qkv, att, lse, cosines, sines, att_all,
    x_all, values, own_h, own_o, own_g, own_u, own_d, gain_row, plane, pair, line,
    send, recv, lsem,
):
    me = Place()
    z, k, f, c = me.z, me.k, me.f, me.c
    rows = x.shape[0]
    greet([me.xp, me.yp, me.dp, me.sib] + [me.along_z(step)[1] for step in (1, 2, 3)])
    copies, local = Copies(send, recv), Locals(lsem)
    q_size = GROUP * HEAD_SIZE
    head_loads = [
        local.alone(wq.at[:, pl.ds(pl.multiple_of(c * q_size, 128), q_size)], own_h.at[:, pl.ds(0, q_size)]),
        local.alone(wk.at[:, pl.ds(pl.multiple_of(c * HEAD_SIZE, 128), HEAD_SIZE)], own_h.at[:, pl.ds(q_size, HEAD_SIZE)]),
        local.alone(
            wv.at[:, pl.ds(pl.multiple_of(c * HEAD_SIZE, 128), HEAD_SIZE)],
            own_h.at[:, pl.ds(q_size + HEAD_SIZE, HEAD_SIZE)],
        ),
    ]
    width = wg.shape[1] // 8
    for src, own in ((wo, own_o), (wd, own_d)):
        local(src.at[pl.ds(pl.multiple_of(k * own.shape[0], 16), own.shape[0])], own)
    for src, own in ((wg, own_g), (wu, own_u)):
        for i in range(4):
            at = pl.ds(pl.multiple_of((2 * i + k) * width, 128), width)
            local(src.at[:, at], own.at[:, pl.ds(i * width, width)])
    small = SmallSum(me, copies, count, plane, pair, line)
    small.first()
    gain_sends = [copies(gains, gains_all.at[f], partner) for partner in (me.xp, me.yp, me.dp)]
    misc_sends = [
        copies(misc, misc_all.at[k, z], me.along_z(step)[1]) for step in (1, 2, 3)
    ]
    for copy in misc_sends + gain_sends:
        copy.start()
    x_all[c] = x[...]
    spread = Spread(me, copies, x_all)
    spread.start()
    pair_sends = [copies(t, t_pair.at[k], me.sib)]
    pair_sends[0].start()
    for copy in head_loads:
        copy.wait()
    head = Gather(me, copies, local, own_h, w_head)
    head.first()
    head.second()
    local.wait()
    out = Gather(me, copies, local, own_o, wo_all)
    gate = Gather(me, copies, local, own_g, wg_all)
    up = Gather(me, copies, local, own_u, wu_all)
    down = Gather(me, copies, local, own_d, wd_all)
    out.first()
    out.second()
    gate.first()
    gate.second()
    keep = [local.alone(t, t_pair.at[k])]
    for copy in misc_sends:
        copy.wait_recv()
    misc_all[k, z] = misc[...]
    gains_all[f] = gains[...]
    misc_pass = copies(misc_all.at[k], misc_all.at[k], me.sib)
    misc_pass.start()
    small.second()
    for copy in gain_sends:
        copy.wait_recv()
    for i in range(4):
        for r in range(2):
            gain_row[0:1, pl.ds((2 * i + r) * 128, 128)] = gains_all[i, r : r + 1, :]
    gain_q = (gains_all[0, 4:5, :] + gains_all[1, 4:5, :]) + (gains_all[2, 4:5, :] + gains_all[3, 4:5, :])
    gain_k = (gains_all[0, 5:6, :] + gains_all[1, 5:6, :]) + (gains_all[2, 5:6, :] + gains_all[3, 5:6, :])
    misc_pass.wait_recv()
    small.third()
    head.relay()

    @pl.loop(0, 8)
    def _(i):
        rotary_tables(
            misc_all[i % 2, i // 2], freq[0:1, :], cosines, sines, pl.multiple_of(i * 256, 256)
        )

    head.finish()
    spread.step(1)
    out.relay()

    def project(block):
        @pl.loop(0, 2)
        def _(u):
            piece = 2 * block + u
            at = pl.ds(pl.multiple_of(piece * rows, rows), rows)
            xin = x_all[piece].astype(F32)
            r = lax.rsqrt(jnp.mean(xin * xin, axis=-1, keepdims=True) + EPSILON)
            h = (xin * r * gain_row[0:1, :]).astype(BF16)
            h_all[at, :] = h
            p = dot_nn(h, w_head[...].reshape(w_head.shape[0] * w_head.shape[1], w_head.shape[2]))
            cosine, sine = cosines[at, :], sines[at, :]
            for g in range(GROUP + 1):
                lanes = slice(g * HEAD_SIZE, (g + 1) * HEAD_SIZE)
                one = p[:, lanes]
                proj[at, lanes] = one
                one = one * head_norm(one) * (gain_q if g < GROUP else gain_k)
                qkv[at, lanes] = (one * cosine + half_turn(one) * sine).astype(BF16)
            qkv[at, (GROUP + 1) * HEAD_SIZE :] = p[:, (GROUP + 1) * HEAD_SIZE :].astype(BF16)

    way = 1 - 2 * (z // 2)
    spread.crossed(0)
    project(z)
    spread.step(2)
    up.first()
    up.second()
    gate.relay()
    spread.crossed(1)
    spread.step(3)
    down.first()
    down.second()
    spread.crossed(2)
    spread.crossed(3)

    @pl.loop(1, 4)
    def _(step):
        project((z + way * step + 4) % 4)

    values[:, 0:HEAD_SIZE] = qkv[:, (GROUP + 1) * HEAD_SIZE :]
    values[:, HEAD_SIZE:] = jnp.ones((qkv.shape[0], HEAD_SIZE), BF16)
    base = copies.take(4)
    block = 2 * rows
    for step in (1, 2, 3, 0):
        to, partner = me.along_z(step)
        attend_rows(qkv, values, att, lse, to, block)
        piece = att.at[pl.ds(pl.multiple_of(to * block, block), block)]
        place = att_all.at[:, pl.ds(pl.multiple_of(z * q_size, 128), q_size)]
        if step:
            copy = pltpu.make_async_remote_copy(
                src_ref=piece, dst_ref=place, send_sem=send.at[base + step], recv_sem=recv.at[base + step],
                device_id=partner, device_id_type=MESH,
            )
            copy.start()
            keep.append(copy)
        else:
            keep.append(local.alone(piece, place))
        if step == 1:
            up.relay()
        if step == 3:
            down.relay()
    small.finish(count_out)
    for i in range(2):
        keep.append(local.alone(x_all.at[2 * z + i], x_pair.at[i]))
    for gather in (out, gate, up, down):
        gather.finish()
    for copy in pair_sends + [misc_pass]:
        copy.wait_send()
    pair_sends[0].wait_recv()
    for copy in misc_sends + gain_sends:
        copy.wait_send()
    for copy in keep:
        copy.wait()
    spread.drain()
    small.drain()


def forward(wq, wk, wv, wo, wg, wu, wd, x, t, misc, gains, count, freq):
    rows, width = x.shape
    tokens = 8 * rows
    row = wq.shape[0]
    half_ff = wg.shape[1] // 2
    out_rows, down_rows = wo.shape[0] // 2, wd.shape[0] // 2
    return transfer(
        kernel_forward, "forward", 1,
        (wq, wk, wv, wo, wg, wu, wd, x, t, misc, gains, count, freq),
        [HBM] * 7 + [VM] * 6,
        [
            shape((2, rows, width), BF16),
            shape((2, rows, width), BF16),
            shape((2, 4, 8, 128), F32),
            shape((4, 8, 128), F32),
            shape((8, 128), F32),
            shape((4, row, HEAD_COLUMNS), BF16),
            shape((4, out_rows, width), BF16),
            shape((4, row, half_ff), BF16),
            shape((4, row, half_ff), BF16),
            shape((4, down_rows, width), BF16),
            shape((tokens, width), BF16),
            shape((tokens, (GROUP + 1) * HEAD_SIZE), F32),
            shape((tokens, HEAD_COLUMNS), BF16),
            shape((tokens, GROUP * HEAD_SIZE), BF16),
            shape((GROUP, 8, tokens), F32),
            shape((tokens, HEAD_SIZE), F32),
            shape((tokens, HEAD_SIZE), F32),
            shape((2 * rows, 4 * GROUP * HEAD_SIZE), BF16),
        ],
        [HBM] * 2 + [VM] * 4 + [HBM] * 4 + [VM] * 7 + [HBM],
        [
            pltpu.VMEM((8, rows, width), BF16),
            pltpu.VMEM((tokens, 2 * HEAD_SIZE), BF16),
            pltpu.VMEM((row, HEAD_COLUMNS), BF16),
            pltpu.VMEM((out_rows, width), BF16),
            pltpu.VMEM((row, half_ff), BF16),
            pltpu.VMEM((row, half_ff), BF16),
            pltpu.VMEM((down_rows, width), BF16),
            pltpu.VMEM((8, width), F32),
            pltpu.VMEM((4, 8, 128), F32),
            pltpu.VMEM((2, 8, 128), F32),
            pltpu.VMEM((4, 8, 128), F32),
        ],
        7 + 3 + 3 + 13 + 1 + 30 + 1 + 4, 3 + 2 + 8 + 5 + 1 + 1 + 2,
    )


def attend_rows(qkv, values, att, lse, i, block):
    rows = pl.ds(pl.multiple_of(i * block, block), block)
    k_at = pl.ds(GROUP * HEAD_SIZE, HEAD_SIZE)
    row = lax.broadcasted_iota(jnp.int32, (block, block), 0)
    column = lax.broadcasted_iota(jnp.int32, (block, block), 1)
    for g in range(GROUP):
        q = qkv[rows, pl.ds(g * HEAD_SIZE, HEAD_SIZE)]

        def part(j, acc, q=q):
            keys = pl.ds(pl.multiple_of(j * block, block), block)
            e = jnp.exp(dot_nt(q, qkv[keys, k_at]) * SCALE)
            return acc + dot_nn(e.astype(BF16), values[keys, :])

        acc = lax.fori_loop(0, i, part, jnp.zeros((block, 2 * HEAD_SIZE), F32))
        e = jnp.exp(dot_nt(q, qkv[rows, k_at]) * SCALE)
        acc = acc + dot_nn(jnp.where(column <= row, e, 0.0).astype(BF16), values[rows, :])
        total = acc[:, HEAD_SIZE:]
        att[rows, pl.ds(g * HEAD_SIZE, HEAD_SIZE)] = (acc[:, :HEAD_SIZE] / total).astype(BF16)
        mean = jnp.full((8, HEAD_SIZE), 1.0 / HEAD_SIZE, F32)
        lse[g, :, rows] = dot_nt(mean, jnp.log(total), precision=HIGHEST)


def head_back(g, u, cosine, sine, gain):
    g = g * cosine + half_turn(g * sine)
    r = head_norm(u)
    n = u * r
    g_gain = jnp.sum(g * n, axis=0, keepdims=True)
    g = g * gain
    return r * (g - n * jnp.mean(g * n, axis=-1, keepdims=True)), g_gain


def kernel_backward(
    g_o, p_down, p_gate, p_up, p_out,
    qkv_in, att_in, lse_in, proj_in, cos_in, sin_in, h_in, w_in,
    x, g_x2, gains_all, small,
    down_tot, gate_tot, up_tot, out_tot, head_tot, grad_in, small_tot,
    g_out, qkv, att, lse, proj, cosines, sines, h_all, w_head, g_proj, g_k, g_v, p_head,
    gh_send, gh_sib, gh_own, gh_in, gain_row, work, plane, pair, line,
    sc_d, sc_g, sc_u, sc_o, sc_h, own_d, own_g, own_u, own_o, own_h, line_d, line_g, line_u, line_o,
    send, recv, lsem,
):
    me = Place()
    z, k, f, c = me.z, me.k, me.f, me.c
    rows = x.shape[0]
    block = 2 * rows
    greet([me.xp, me.yp, me.dp, me.sib] + [me.along_z(step)[1] for step in (1, 2, 3)])
    copies, local = Copies(send, recv), Locals(lsem)
    size, q_size = HEAD_SIZE, GROUP * HEAD_SIZE

    def to_device(src, dst, base, there, partner):
        return pltpu.make_async_remote_copy(
            src_ref=src, dst_ref=dst, send_sem=send.at[base + there], recv_sem=recv.at[base + z],
            device_id=partner, device_id_type=MESH,
        )

    def from_device(dst, base, there):
        return pltpu.make_async_remote_copy(
            src_ref=dst, dst_ref=dst, send_sem=send.at[base + there], recv_sem=recv.at[base + there],
            device_id=me.sib, device_id_type=MESH,
        )

    base = copies.take(4)
    go_sends = []
    for step in (2, 1, 3):
        to, partner = me.along_z(step)
        piece = g_o.at[:, pl.ds(pl.multiple_of(to * q_size, 128), q_size)]
        place = g_out.at[pl.ds(pl.multiple_of(z * block, block), block)]
        go_sends.append(to_device(piece, place, base, to, partner))
        go_sends[-1].start()
    own_go = local.alone(
        g_o.at[:, pl.ds(pl.multiple_of(z * q_size, 128), q_size)],
        g_out.at[pl.ds(pl.multiple_of(z * block, block), block)],
    )
    for src, dst in ((qkv_in, qkv), (att_in, att), (lse_in, lse), (proj_in, proj), (cos_in, cosines), (sin_in, sines)):
        local(src, dst)
    late = [local.alone(w_in, w_head), local.alone(h_in, h_all)]
    s_down = Scatter(me, copies, local, p_down, sc_d)
    s_gate = Scatter(me, copies, local, p_gate, sc_g)
    s_up = Scatter(me, copies, local, p_up, sc_u)
    s_out = Scatter(me, copies, local, p_out, sc_o)
    s_head = Scatter(me, copies, local, p_head, sc_h)
    for scatter in (s_down, s_gate):
        scatter.first()
        scatter.second()
    lines = [
        LineSum(me, copies, own, bufs)
        for own, bufs in ((own_d, line_d), (own_g, line_g), (own_u, line_u), (own_o, line_o))
    ]
    l_down, l_gate, l_up, l_out = lines
    totals = (down_tot, gate_tot, up_tot, out_tot)
    swap_base = copies.take(8)
    swaps, writes = [], []

    def finish(i):
        lines[i].spread()
        lines[i].arrive()
        half = lines[i].total.shape[1]
        for j in range(2):
            dst = totals[i].at[k, pl.ds(j * half, half)]
            copy = copies.at(swap_base + 2 * i + j, lines[i].total.at[j], dst, me.sib)
            copy.start()
            swaps.append(copy)
            writes.append(local.alone(lines[i].total.at[j], dst))

    def scattered(scatter, entry, own):
        scatter.finish(own.at[0], own.at[1])
        entry.start()

    work[...] = small[...]
    for i in range(4):
        for r in range(2):
            gain_row[0:1, pl.ds((2 * i + r) * 128, 128)] = gains_all[i, r : r + 1, :]
    gain_q = (gains_all[0, 4:5, :] + gains_all[1, 4:5, :]) + (gains_all[2, 4:5, :] + gains_all[3, 4:5, :])
    gain_k = (gains_all[0, 5:6, :] + gains_all[1, 5:6, :]) + (gains_all[2, 5:6, :] + gains_all[3, 5:6, :])
    k_at = pl.ds(q_size, size)
    v_at = pl.ds(q_size + size, size)
    g_k[...] = jnp.zeros_like(g_k)
    g_v[...] = jnp.zeros_like(g_v)
    key = lax.broadcasted_iota(jnp.int32, (block, block), 0)
    query = lax.broadcasted_iota(jnp.int32, (block, block), 1)
    local.wait()
    own_go.wait()
    for step in (1, 2, 3):
        other, _ = me.along_z(step)
        from_device(g_out.at[pl.ds(pl.multiple_of(other * block, block), block)], base, other).wait_recv()

    def queries(i):
        at = pl.ds(i * block, block)
        for g in range(GROUP):
            head = pl.ds(g * size, size)
            q = qkv[at, head]
            go = g_out[at, head]
            product = go.astype(F32) * att[at, head].astype(F32)
            delta = dot_nt(jnp.ones((8, size), F32), product, precision=HIGHEST)[0:1, :]
            log_sum = lse[g, 0:1, at]

            def part(keys, masked, q=q, go=go, delta=delta, log_sum=log_sum):
                kk, vv = qkv[keys, k_at], qkv[keys, v_at]
                p = jnp.exp(dot_nt(kk, q) * SCALE - log_sum)
                if masked:
                    p = jnp.where(key <= query, p, 0.0)
                gs = (p * (dot_nt(vv, go) - delta) * SCALE).astype(BF16)
                g_v[keys, :] += dot_nn(p.astype(BF16), go)
                g_k[keys, :] += dot_nn(gs, q)
                return dot_tn(gs, kk)

            def step(j, acc, part=part):
                return acc + part(pl.ds(pl.multiple_of(j * block, block), block), False)

            acc = lax.fori_loop(0, i, step, jnp.zeros((block, size), F32))
            acc = acc + part(at, True)
            g_u, g_gain = head_back(acc, proj[at, head], cosines[at, :], sines[at, :], gain_q)
            g_proj[at, head] = g_u.astype(BF16)
            work[16:17, :] += g_gain

    queries(0)
    queries(1)
    s_down.relay()
    s_up.first()
    s_up.second()
    queries(2)
    scattered(s_down, l_down, own_d)
    queries(3)

    @pl.loop(0, 4)
    def _(i):
        at = pl.ds(pl.multiple_of(i * block, block), block)
        g_u, g_gain = head_back(g_k[at, :], proj[at, k_at], cosines[at, :], sines[at, :], gain_k)
        g_proj[at, k_at] = g_u.astype(BF16)
        g_proj[at, v_at] = g_v[at, :].astype(BF16)
        work[17:18, :] += g_gain

    s_gate.relay()
    s_out.first()
    s_out.second()
    l_down.meet()
    for copy in late:
        copy.wait()
    sib_base, gh_base = copies.take(4), copies.take(4)
    gh_copies = []

    def input_part(to, mine, dst):
        at = pl.ds(pl.multiple_of((2 * to + mine) * rows, rows), rows)
        weights = w_head[...].reshape(w_head.shape[0] * w_head.shape[1], w_head.shape[2])
        dst[...] = dot_nt(g_proj[at, :], weights).astype(BF16)

    def crossing(to):
        return copies.at(sib_base + to, gh_send.at[to], gh_sib.at[to], me.sib)

    def join(to, partner):
        crossing(to).wait_recv()
        add_rows(gh_own.at[to], [gh_own.at[to], gh_sib.at[to]])
        if partner is not None:
            copy = to_device(gh_own.at[to], gh_in.at[z], gh_base, to, partner)
            copy.start()
            gh_copies.append(copy)

    previous = None
    for step in (2, 1, 3, 0):
        to, partner = me.along_z(step)
        input_part(to, 1 - k, gh_send.at[to])
        crossing(to).start()
        input_part(to, k, gh_own.at[to])
        if previous is not None:
            join(*previous)
        previous = (to, partner if step else None)
    join(*previous)
    l_down.close()
    scattered(s_gate, l_gate, own_g)
    @pl.loop(0, 4)
    def _(i):
        columns = pl.ds(pl.multiple_of(i * rows, rows), rows)
        p_head[i] = dot_tn(h_all[:, columns], g_proj[...]).astype(BF16)

    s_head.first()
    s_head.second()
    s_up.relay()
    finish(0)
    l_gate.meet()
    s_head.relay()
    s_out.relay()
    s_head.finish(own_h.at[0], own_h.at[1])
    head_base, pass_base = copies.take(4), copies.take(4)
    head_sends = []
    for step in (2, 1, 3):
        to, partner = me.along_z(step)
        copy = to_device(own_h, head_tot.at[c], head_base, to, partner)
        copy.start()
        head_sends.append(copy)

    def passing(other):
        block_at = head_tot.at[2 * other + k]
        return copies.at(pass_base + other, block_at, block_at, me.sib)

    head_pass = copies.at(pass_base + z, own_h, head_tot.at[c], me.sib)
    head_pass.start()
    writes.append(local.alone(own_h, head_tot.at[c]))
    l_gate.close()
    scattered(s_up, l_up, own_u)
    for step in (1, 2, 3):
        other, _ = me.along_z(step)
        from_device(gh_in.at[other], gh_base, other).wait_recv()

    a, b, d = [me.along_z(step)[0] for step in (1, 2, 3)]
    work[0:8, :] = jnp.zeros((8, 128), F32)

    @pl.loop(0, rows // 64)
    def _(i):
        at = pl.ds(pl.multiple_of(i * 64, 64), 64)
        g = gh_own[z, at, :].astype(F32) + gh_in[a, at, :].astype(F32)
        g = g + gh_in[b, at, :].astype(F32) + gh_in[d, at, :].astype(F32)
        xin = x[at, :].astype(F32)
        r = lax.rsqrt(jnp.mean(xin * xin, axis=-1, keepdims=True) + EPSILON)
        n = xin * r
        g_gain = jnp.sum(g * n, axis=0, keepdims=True)
        for j in range(8):
            work[j : j + 1, :] += g_gain[:, j * 128 : (j + 1) * 128]
        g = g * gain_row[0:1, :]
        grad_in[at, :] = g_x2[at, :] + r * (g - n * jnp.mean(g * n, axis=-1, keepdims=True))

    total = SmallSum(me, copies, work, plane, pair, line)
    total.first()
    finish(1)
    l_up.meet()
    scattered(s_out, l_out, own_o)
    total.second()
    l_up.close()
    total.third()
    l_out.meet()
    finish(2)
    l_out.close()
    passes = []
    for step in (1, 2, 3):
        other, _ = me.along_z(step)
        from_device(head_tot.at[2 * other + k], head_base, other).wait_recv()
        copy = passing(other)
        copy.start()
        passes.append(copy)
    total.finish(small_tot)
    finish(3)
    for copy in go_sends + gh_copies + head_sends:
        copy.wait_send()
    for i in range(4):
        crossing(i).wait_send()
    total.drain()
    for scatter in (s_down, s_gate, s_up, s_out, s_head):
        scatter.drain()
    for entry in lines:
        entry.drain()
    for copy in swaps + passes + [head_pass]:
        copy.wait()
    for copy in writes:
        copy.wait()


def backward(g_o, parts, saved, x, g_x2, gains_all, small):
    rows, width = x.shape
    tokens = 8 * rows
    sizes = [p.shape[1:] for p in parts]
    head = (width // 4, HEAD_COLUMNS)

    def held(a):
        return pltpu.VMEM(a.shape, a.dtype)

    pieces = pltpu.VMEM((4, rows, width), BF16)
    scatters = [pltpu.VMEM((10, r // 2, n), BF16) for r, n in sizes + [head]]
    own = [pltpu.VMEM((2, r // 2, n), BF16) for r, n in sizes + [head]]
    line = [pltpu.VMEM((5, r // 2, n), BF16) for r, n in sizes]
    return transfer(
        kernel_backward, "backward", 2,
        (g_o,) + tuple(parts) + tuple(saved) + (x, g_x2, gains_all, small),
        [HBM] * 13 + [VM] * 4,
        [shape((2,) + s, BF16) for s in sizes]
        + [
            shape((8, 2, head[0] // 2, head[1]), BF16),
            shape((rows, width), F32),
            shape(small.shape, F32),
        ],
        [HBM] * 5 + [VM] * 2,
        [pltpu.VMEM((tokens, GROUP * HEAD_SIZE), BF16)]
        + [held(a) for a in saved]
        + [
            pltpu.VMEM((tokens, HEAD_COLUMNS), BF16),
            pltpu.VMEM((tokens, HEAD_SIZE), F32),
            pltpu.VMEM((tokens, HEAD_SIZE), F32),
            pltpu.VMEM((4,) + head, BF16),
            pieces, pieces, pieces, pieces,
            pltpu.VMEM((8, width), F32),
            pltpu.VMEM(small.shape, F32),
            pltpu.VMEM((4,) + small.shape, F32),
            pltpu.VMEM((2,) + small.shape, F32),
            pltpu.VMEM((4,) + small.shape, F32),
        ]
        + scatters + own + line,
        4 + 30 + 32 + 8 + 8 + 8 + 7, 1 + 8 + 20 + 8 + 1,
    )


def chip_step(
    hidden_in, teacher, valid, positions, norm_attn, w_query, key_projection, value_projection,
    gain_query, gain_key, w_out, norm_mlp, w_gate, w_up, w_down,
):
    f, c = lax.axis_index("fsdp"), lax.axis_index("ctx")
    k, z = c % 2, c // 2
    rows = hidden_in.shape[1]
    tokens = 2 * rows
    width = hidden_in.shape[2]
    misc = jnp.concatenate(
        [positions.reshape(-1, 128), valid.reshape(-1, 128), jnp.zeros((4, 128), jnp.int32)], 0
    ).astype(F32)
    here = jnp.arange(HEAD_SIZE, dtype=jnp.int32) // gain_query.shape[0] == f
    gains = jnp.concatenate(
        [
            norm_attn.reshape(-1, 128), norm_mlp.reshape(-1, 128),
            jnp.where(here, jnp.tile(gain_query, 4), 0)[None], jnp.where(here, jnp.tile(gain_key, 4), 0)[None],
            jnp.zeros((2, 128), BF16),
        ]
    ).astype(F32)
    count = jnp.full((8, 128), jnp.sum(valid).astype(F32))
    half_width = HEAD_SIZE // 2
    freq = jnp.exp(jnp.arange(half_width, dtype=F32) * (-2.0 * math.log(1000000.0) / HEAD_SIZE))
    freq = jnp.broadcast_to(jnp.concatenate([freq, freq]), (8, HEAD_SIZE))
    (
        x_pair, t_pair, misc_all, gains_all, count, w_head, wo, wg, wu, wd,
        h_all, proj, qkv, att, lse, cosines, sines, att_all,
    ) = forward(
        w_query, key_projection, value_projection, w_out, w_gate, w_up, w_down,
        hidden_in[0], teacher[0], misc, gains, count, freq,
    )
    count_total = count[0, 0]
    x = x_pair.reshape(tokens, width).astype(F32)
    target = t_pair.reshape(tokens, width).astype(F32)
    weight_rows = lax.dynamic_index_in_dim(misc_all, z, 1, False)[:, 2:4].reshape(tokens)
    gain_two = gains_all[:, 2:4].reshape(width)
    wg, wu = wg.reshape(width, -1), wu.reshape(width, -1)
    wd, wo = wd.reshape(-1, width), wo.reshape(-1, width)

    def over_cores(part, number):
        part = part.astype(BF16)
        return part.astype(F32) + swap(part, number).astype(F32)

    x2 = x + over_cores(jnp.dot(att_all, wo, preferred_element_type=F32), 7)
    normed_two, norm_two_back = jax.vjp(root_mean_norm, x2, gain_two)
    hidden_two = normed_two.astype(BF16)
    gate = jnp.dot(hidden_two, wg, preferred_element_type=F32)
    up = jnp.dot(hidden_two, wu, preferred_element_type=F32)
    gated, gated_back = jax.vjp(swiglu, gate, up)
    mid = gated.astype(BF16)
    fin = x2 + over_cores(jnp.dot(mid, wd, preferred_element_type=F32), 8)
    mismatch = fin - target
    sq_local = 0.5 * jnp.sum(weight_rows[:, None] * mismatch * mismatch)
    loss_scale = rows * lax.axis_size("ctx") * lax.axis_size("fsdp") / 4.0
    g_fin = 2.0 * loss_scale / count_total * weight_rows[:, None] * mismatch
    g_dn = g_fin.astype(BF16)
    g_gate, g_up = gated_back(against(g_dn, wd))
    g_gate, g_up = g_gate.astype(BF16), g_up.astype(BF16)
    g_h2 = over_cores(against(g_gate, wg) + against(g_up, wu), 9)
    g_norm, grad_norm_mlp = norm_two_back(g_h2)
    g_x2 = g_fin + g_norm
    g_a = g_x2.astype(BF16)
    g_o = against(g_a, wo).astype(BF16)
    p_down = contract_rows(mid, g_dn).astype(BF16).reshape(4, -1, width)
    p_gate = contract_rows(hidden_two, g_gate).astype(BF16).reshape(4, width // 4, -1)
    p_up = contract_rows(hidden_two, g_up).astype(BF16).reshape(4, width // 4, -1)
    p_out = contract_rows(att_all, g_a).astype(BF16).reshape(4, -1, width)
    small = jnp.concatenate(
        [
            jnp.zeros((8, 128), F32), 0.5 * grad_norm_mlp.reshape(-1, 128), jnp.zeros((2, 128), F32),
            jnp.full((1, 128), sq_local), jnp.zeros((5, 128), F32),
        ]
    )
    down, gate, up, out, heads, grad_input, small = backward(
        g_o, (p_down, p_gate, p_up, p_out),
        (qkv, att, lse, proj, cosines, sines, h_all, w_head),
        hidden_in[0], lax.dynamic_slice_in_dim(g_x2, k * rows, rows, 0), gains_all, small,
    )

    def mine(values):
        size = values.shape[0] // 4
        return lax.dynamic_slice_in_dim(values, f * size, size, 0)

    g_gate, g_up, g_q, g_k, g_v, g_down, g_out = assemble(
        gate, up, heads.reshape(8, -1, HEAD_COLUMNS), down, out
    )
    output = lax.dynamic_slice_in_dim(fin.astype(BF16), k * rows, rows, 0)
    return (
        output[None],
        small[18, 0] / count_total,
        grad_input[None],
        mine(small[0:8].reshape(-1)),
        g_q,
        g_k,
        g_v,
        mine(small[16]),
        mine(small[17]),
        g_out.reshape(-1, width),
        mine(small[8:16].reshape(-1)),
        g_gate,
        g_up,
        g_down.reshape(-1, width),
    )


def solution(mesh):
    chips = mesh.shape["fsdp"] == 4 and mesh.shape["ctx"] == KEY_VALUE_HEADS
    return jax.shard_map(
        chip_step if chips else per_device,
        mesh=mesh,
        in_specs=(
            P("fsdp", "ctx", None),
            P("fsdp", "ctx", None),
            P("fsdp", "ctx"),
            P("fsdp", "ctx"),
            P("fsdp"),
            P("fsdp", None),
            P("fsdp", None),
            P("fsdp", None),
            P("fsdp"),
            P("fsdp"),
            P("fsdp", None),
            P("fsdp"),
            P("fsdp", None),
            P("fsdp", None),
            P("fsdp", None),
        ),
        out_specs=(
            P("fsdp", "ctx", None),
            P(),
            P("fsdp", "ctx", None),
            P("fsdp"),
            P("fsdp", None),
            P("fsdp", None),
            P("fsdp", None),
            P("fsdp"),
            P("fsdp"),
            P("fsdp", None),
            P("fsdp"),
            P("fsdp", None),
            P("fsdp", None),
            P("fsdp", None),
        ),
        check_vma=False,
    )
```

```python
from functools import partial
import math

import jax
import jax.numpy as jnp
from jax import lax
from jax.experimental import pallas as pl
from jax.experimental.pallas import tpu as pltpu
from jax.sharding import PartitionSpec as P

QUERY_HEADS = 16
KEY_VALUE_HEADS = 8
HEAD_SIZE = 128


EPSILON = 1e-06


def root_mean_norm(values, norm_gain):
    return (
        values * lax.rsqrt(jnp.mean(values * values, axis=-1, keepdims=True) + EPSILON) * norm_gain
    )


def rope_tables(position_ids):
    half_width = HEAD_SIZE // 2
    freq_table = jnp.exp(
        jnp.arange(half_width, dtype=jnp.float32) * (-2.0 * math.log(1000000.0) / HEAD_SIZE)
    )
    angle_table = position_ids.astype(jnp.float32)[:, None] * freq_table[None, :]
    cosine_table = jnp.cos(angle_table)
    sine_table = jnp.sin(angle_table)
    return (
        jnp.concatenate([cosine_table, cosine_table], -1),
        jnp.concatenate([-sine_table, sine_table], -1),
    )


def apply_rotary(values, cosine_table, sine_table):
    half_width = HEAD_SIZE // 2
    swapped = jnp.concatenate([values[..., half_width:], values[..., :half_width]], -1)
    return values * cosine_table[:, None, :] + swapped * sine_table[:, None, :]


def shape_heads(cosine_table, sine_table, proj_query, projected_key, gain_q, key_gain):
    token_rows = proj_query.shape[0]
    query_rows = apply_rotary(
        root_mean_norm(proj_query.reshape(token_rows, QUERY_HEADS, HEAD_SIZE), gain_q),
        cosine_table,
        sine_table,
    )
    rows_of_keys = apply_rotary(
        root_mean_norm(projected_key.reshape(token_rows, KEY_VALUE_HEADS, HEAD_SIZE), key_gain),
        cosine_table,
        sine_table,
    )
    return (query_rows, rows_of_keys)


def swiglu(gate_proj, up_proj):
    return gate_proj / (1.0 + jnp.exp(-gate_proj)) * up_proj


def contract_rows(left_arr, right_arr):
    return lax.dot_general(
        left_arr, right_arr, (((0,), (0,)), ((), ())), preferred_element_type=jnp.float32
    )


def against(left_arr, right_arr):
    return lax.dot_general(
        left_arr, right_arr, (((1,), (1,)), ((), ())), preferred_element_type=jnp.float32
    )


def in_blocks(block_step, running, shard_portion):
    total_rows = shard_portion.shape[0]
    block_extent = 512
    block_count = total_rows // block_extent
    blocks = shard_portion.reshape((block_count, block_extent) + shard_portion.shape[1:])
    starts = jnp.arange(block_count, dtype=jnp.int32) * block_extent

    def scan_body(state, scan_item):
        return (block_step(state, scan_item[0], scan_item[1]), None)

    running, unused = lax.scan(scan_body, running, (blocks, starts))
    return running


def score_terms(
    query_rows,
    output_gradients,
    lse_heads,
    delta_heads,
    rows_of_keys,
    rows_of_values,
    query_index,
    key_index,
    score_scale,
):
    score_matrix = (
        jnp.einsum("alci,wli->lcaw", query_rows, rows_of_keys, preferred_element_type=jnp.float32)
        * score_scale
    )
    allowed = key_index[None, :] <= query_index[:, None]
    attention_probabilities = jnp.where(allowed, jnp.exp(score_matrix - lse_heads[..., None]), 0.0)
    grad_probs = jnp.einsum(
        "alci,wli->lcaw", output_gradients, rows_of_values, preferred_element_type=jnp.float32
    )
    score_gradient = (
        score_scale * attention_probabilities * (grad_probs - delta_heads[..., None])
    ).astype(jnp.bfloat16)
    return (attention_probabilities, score_gradient)


def per_device(
    hidden_in,
    teacher,
    valid,
    positions,
    norm_attn,
    w_query,
    key_projection,
    value_projection,
    gain_query,
    gain_key,
    w_out,
    norm_mlp,
    w_gate,
    w_up,
    w_down,
):
    gathered = (
        lax.all_gather(norm_attn, "fsdp", axis=0, tiled=True),
        lax.all_gather(w_query, "fsdp", axis=0, tiled=True),
        lax.all_gather(key_projection, "fsdp", axis=0, tiled=True),
        lax.all_gather(value_projection, "fsdp", axis=0, tiled=True),
        lax.all_gather(gain_query, "fsdp", axis=0, tiled=True),
        lax.all_gather(gain_key, "fsdp", axis=0, tiled=True),
        lax.all_gather(w_out, "fsdp", axis=0, tiled=True),
        lax.all_gather(norm_mlp, "fsdp", axis=0, tiled=True),
        lax.all_gather(w_gate, "fsdp", axis=0, tiled=True),
        lax.all_gather(w_up, "fsdp", axis=0, tiled=True),
        lax.all_gather(w_down, "fsdp", axis=0, tiled=True),
    )
    (
        full_norm_attn,
        full_query,
        full_key,
        full_value,
        full_gain_q,
        full_gain_k,
        full_out,
        full_norm_mlp,
        full_gate,
        full_up,
        full_down,
    ) = gathered
    grouped_heads = QUERY_HEADS // KEY_VALUE_HEADS
    score_scale = 1.0 / math.sqrt(HEAD_SIZE)
    residual = hidden_in[0].astype(jnp.float32)
    token_rows = residual.shape[0]
    query_index = lax.axis_index("ctx") * token_rows + jnp.arange(token_rows, dtype=jnp.int32)
    normed_one, norm_one_back = jax.vjp(
        root_mean_norm, residual, full_norm_attn.astype(jnp.float32)
    )
    hidden_one = normed_one.astype(jnp.bfloat16)
    proj_query = jnp.dot(hidden_one, full_query, preferred_element_type=jnp.float32)
    projected_key = jnp.dot(hidden_one, full_key, preferred_element_type=jnp.float32)
    projected_value = jnp.dot(hidden_one, full_value, preferred_element_type=jnp.float32)
    cosine_table, sine_table = rope_tables(positions[0])
    (query_per_head, heads_key), heads_back = jax.vjp(
        partial(shape_heads, cosine_table, sine_table),
        proj_query,
        projected_key,
        full_gain_q.astype(jnp.float32),
        full_gain_k.astype(jnp.float32),
    )
    query_reduced = query_per_head.astype(jnp.bfloat16).reshape(
        token_rows, KEY_VALUE_HEADS, grouped_heads, HEAD_SIZE
    )
    key_reduced = heads_key.astype(jnp.bfloat16)
    value_reduced = projected_value.astype(jnp.bfloat16).reshape(
        token_rows, KEY_VALUE_HEADS, HEAD_SIZE
    )
    key_value = jnp.stack(
        [
            key_reduced.reshape(token_rows, KEY_VALUE_HEADS * HEAD_SIZE),
            value_reduced.reshape(token_rows, KEY_VALUE_HEADS * HEAD_SIZE),
        ],
        axis=1,
    )

    def forward_block(running, shard_portion, first_row):
        run_max, run_total, run_acc = running
        rows_per_block = shard_portion.shape[0]
        rows_of_keys = shard_portion[:, 0].reshape(rows_per_block, KEY_VALUE_HEADS, HEAD_SIZE)
        rows_of_values = shard_portion[:, 1].reshape(rows_per_block, KEY_VALUE_HEADS, HEAD_SIZE)
        key_index = first_row + jnp.arange(rows_per_block, dtype=jnp.int32)
        allowed = key_index[None, :] <= query_index[:, None]
        score_matrix = (
            jnp.einsum(
                "alci,wli->lcaw", query_reduced, rows_of_keys, preferred_element_type=jnp.float32
            )
            * score_scale
        )
        score_matrix = jnp.where(allowed, score_matrix, -1e30)
        new_max = jnp.maximum(run_max, jnp.max(score_matrix, axis=-1))
        weights_part = jnp.where(allowed, jnp.exp(score_matrix - new_max[..., None]), 0.0)
        factor = jnp.exp(run_max - new_max)
        run_total = run_total * factor + jnp.sum(weights_part, axis=-1)
        run_acc = run_acc * factor[..., None] + jnp.einsum(
            "exfw,weq->exfq",
            weights_part.astype(jnp.bfloat16),
            rows_of_values,
            preferred_element_type=jnp.float32,
        )
        return (new_max, run_total, run_acc)

    start_state = (
        jnp.full((KEY_VALUE_HEADS, grouped_heads, token_rows), -1e30, jnp.float32),
        jnp.zeros((KEY_VALUE_HEADS, grouped_heads, token_rows), jnp.float32),
        jnp.zeros((KEY_VALUE_HEADS, grouped_heads, token_rows, HEAD_SIZE), jnp.float32),
    )
    run_max, run_total, run_acc = in_blocks(
        forward_block, start_state, lax.all_gather(key_value, "ctx", axis=0, tiled=True)
    )
    log_total = run_max + jnp.log(run_total)
    attn_rows = jnp.transpose(run_acc / run_total[..., None], (2, 0, 1, 3))
    attn_low = attn_rows.reshape(token_rows, QUERY_HEADS * HEAD_SIZE).astype(jnp.bfloat16)
    mid_resid = residual + jnp.dot(attn_low, full_out, preferred_element_type=jnp.float32)
    normed_two, norm_two_back = jax.vjp(
        root_mean_norm, mid_resid, full_norm_mlp.astype(jnp.float32)
    )
    hidden_two = normed_two.astype(jnp.bfloat16)
    gate_proj = jnp.dot(hidden_two, full_gate, preferred_element_type=jnp.float32)
    up_proj = jnp.dot(hidden_two, full_up, preferred_element_type=jnp.float32)
    gated, gated_back = jax.vjp(swiglu, gate_proj, up_proj)
    gated_low = gated.astype(jnp.bfloat16)
    final_rows = mid_resid + jnp.dot(gated_low, full_down, preferred_element_type=jnp.float32)
    target = teacher[0].astype(jnp.float32)
    weight_rows = valid[0].astype(jnp.float32)
    mismatch = final_rows - target
    sq_local = jnp.sum(weight_rows[:, None] * mismatch * mismatch)
    count_local = jnp.sum(weight_rows)
    sq_total, count_total = lax.psum((sq_local, count_local), ("fsdp", "ctx"))
    loss_value = sq_total / count_total
    loss_scale = token_rows * lax.axis_size("ctx") * lax.axis_size("fsdp") / 4.0
    grad_final = 2.0 * loss_scale / count_total * weight_rows[:, None] * mismatch
    grad_down_in = grad_final.astype(jnp.bfloat16)
    grad_w_down = contract_rows(gated_low, grad_down_in)
    grad_gated = against(grad_down_in, full_down)
    grad_gate_proj, grad_up_proj = gated_back(grad_gated)
    gate_low = grad_gate_proj.astype(jnp.bfloat16)
    up_low = grad_up_proj.astype(jnp.bfloat16)
    grad_w_gate = contract_rows(hidden_two, gate_low)
    grad_w_up = contract_rows(hidden_two, up_low)
    grad_hidden_two = against(gate_low, full_gate) + against(up_low, full_up)
    grad_mid_norm, grad_norm_mlp = norm_two_back(grad_hidden_two)
    grad_mid = grad_final + grad_mid_norm
    grad_branch = grad_mid.astype(jnp.bfloat16)
    grad_w_out = contract_rows(attn_low, grad_branch)
    attention_gradient = against(grad_branch, full_out).astype(jnp.bfloat16)
    attention_head_gradient = attention_gradient.reshape(
        token_rows, KEY_VALUE_HEADS, grouped_heads, HEAD_SIZE
    )
    row_delta = jnp.sum(attention_head_gradient.astype(jnp.float32) * attn_rows, axis=-1)
    delta_heads = jnp.transpose(row_delta, (1, 2, 0))
    row_stats = jnp.stack(
        [
            jnp.transpose(log_total, (2, 0, 1)).reshape(token_rows, QUERY_HEADS),
            row_delta.reshape(token_rows, QUERY_HEADS),
        ],
        axis=1,
    )

    def block_of_queries(grad_query, shard_portion, first_row):
        rows_per_block = shard_portion.shape[0]
        rows_of_keys = shard_portion[:, 0].reshape(rows_per_block, KEY_VALUE_HEADS, HEAD_SIZE)
        rows_of_values = shard_portion[:, 1].reshape(rows_per_block, KEY_VALUE_HEADS, HEAD_SIZE)
        key_index = first_row + jnp.arange(rows_per_block, dtype=jnp.int32)
        attention_probabilities, score_gradient = score_terms(
            query_reduced,
            attention_head_gradient,
            log_total,
            delta_heads,
            rows_of_keys,
            rows_of_values,
            query_index,
            key_index,
            score_scale,
        )
        return grad_query + jnp.einsum(
            "jyux,xji->ujyi", score_gradient, rows_of_keys, preferred_element_type=jnp.float32
        )

    grad_query = in_blocks(
        block_of_queries,
        jnp.zeros((token_rows, KEY_VALUE_HEADS, grouped_heads, HEAD_SIZE), jnp.float32),
        lax.all_gather(key_value, "ctx", axis=0, tiled=True),
    )
    all_stats = lax.all_gather(row_stats.astype(jnp.bfloat16), "ctx", axis=0, tiled=True).astype(
        row_stats.dtype
    )
    query_pair = jnp.stack(
        [query_reduced.reshape(token_rows, QUERY_HEADS * HEAD_SIZE), attention_gradient], axis=1
    )

    def key_block(running, shard_portion, first_row):
        grad_key, value_gradient = running
        rows_per_block = shard_portion.shape[0]
        query_rows = shard_portion[:, 0].reshape(
            rows_per_block, KEY_VALUE_HEADS, grouped_heads, HEAD_SIZE
        )
        output_gradients = shard_portion[:, 1].reshape(
            rows_per_block, KEY_VALUE_HEADS, grouped_heads, HEAD_SIZE
        )
        partial_statistics = lax.dynamic_slice_in_dim(all_stats, first_row, rows_per_block, 0)
        partial_logsumexp = jnp.transpose(
            partial_statistics[:, 0].reshape(rows_per_block, KEY_VALUE_HEADS, grouped_heads),
            (1, 2, 0),
        )
        partial_delta = jnp.transpose(
            partial_statistics[:, 1].reshape(rows_per_block, KEY_VALUE_HEADS, grouped_heads),
            (1, 2, 0),
        )
        part_index = first_row + jnp.arange(rows_per_block, dtype=jnp.int32)
        attention_probabilities, score_gradient = score_terms(
            query_rows,
            output_gradients,
            partial_logsumexp,
            partial_delta,
            key_reduced,
            value_reduced,
            part_index,
            query_index,
            score_scale,
        )
        grad_key = grad_key + jnp.einsum(
            "wzlj,lwzy->jwy", score_gradient, query_rows, preferred_element_type=jnp.float32
        )
        value_gradient = value_gradient + jnp.einsum(
            "wzlj,lwzy->jwy",
            attention_probabilities.astype(jnp.bfloat16),
            output_gradients,
            preferred_element_type=jnp.float32,
        )
        return (grad_key, value_gradient)

    key_state = (
        jnp.zeros((token_rows, KEY_VALUE_HEADS, HEAD_SIZE), jnp.float32),
        jnp.zeros((token_rows, KEY_VALUE_HEADS, HEAD_SIZE), jnp.float32),
    )
    grad_key, value_gradient = in_blocks(
        key_block, key_state, lax.all_gather(query_pair, "ctx", axis=0, tiled=True)
    )
    grad_proj_q, grad_proj_k, grad_gain_q, grad_gain_k = heads_back(
        (grad_query.reshape(token_rows, QUERY_HEADS, HEAD_SIZE), grad_key)
    )
    query_grad_low = grad_proj_q.astype(jnp.bfloat16)
    key_grad_low = grad_proj_k.astype(jnp.bfloat16)
    value_gradient_reduced = value_gradient.reshape(token_rows, KEY_VALUE_HEADS * HEAD_SIZE).astype(
        jnp.bfloat16
    )
    grad_w_query = contract_rows(hidden_one, query_grad_low)
    grad_w_key = contract_rows(hidden_one, key_grad_low)
    grad_w_value = contract_rows(hidden_one, value_gradient_reduced)
    grad_hidden_one = (
        against(query_grad_low, full_query)
        + against(key_grad_low, full_key)
        + against(value_gradient_reduced, full_value)
    )
    grad_resid_norm, grad_norm_attn = norm_one_back(grad_hidden_one)
    grad_input = grad_mid + grad_resid_norm
    grads = (
        grad_norm_attn,
        grad_w_query,
        grad_w_key,
        grad_w_value,
        grad_gain_q,
        grad_gain_k,
        grad_w_out,
        grad_norm_mlp,
        grad_w_gate,
        grad_w_up,
        grad_w_down,
    )
    shares = (
        lax.psum_scatter(grads[0], ("fsdp", "ctx"), scatter_dimension=0, tiled=True),
        lax.psum_scatter(grads[1], ("fsdp", "ctx"), scatter_dimension=0, tiled=True),
        lax.psum_scatter(grads[2], ("fsdp", "ctx"), scatter_dimension=0, tiled=True),
        lax.psum_scatter(grads[3], ("fsdp", "ctx"), scatter_dimension=0, tiled=True),
        lax.psum_scatter(grads[4], ("fsdp", "ctx"), scatter_dimension=0, tiled=True),
        lax.psum_scatter(grads[5], ("fsdp", "ctx"), scatter_dimension=0, tiled=True),
        lax.psum_scatter(grads[6], ("fsdp", "ctx"), scatter_dimension=0, tiled=True),
        lax.psum_scatter(grads[7], ("fsdp", "ctx"), scatter_dimension=0, tiled=True),
        lax.psum_scatter(grads[8], ("fsdp", "ctx"), scatter_dimension=0, tiled=True),
        lax.psum_scatter(grads[9], ("fsdp", "ctx"), scatter_dimension=0, tiled=True),
        lax.psum_scatter(grads[10], ("fsdp", "ctx"), scatter_dimension=0, tiled=True),
    )
    shares = (
        lax.all_gather(shares[0].astype(jnp.bfloat16), "ctx", axis=0, tiled=True).astype(
            jnp.float32
        ),
        lax.all_gather(shares[1].astype(jnp.bfloat16), "ctx", axis=0, tiled=True).astype(
            jnp.float32
        ),
        lax.all_gather(shares[2].astype(jnp.bfloat16), "ctx", axis=0, tiled=True).astype(
            jnp.float32
        ),
        lax.all_gather(shares[3].astype(jnp.bfloat16), "ctx", axis=0, tiled=True).astype(
            jnp.float32
        ),
        lax.all_gather(shares[4].astype(jnp.bfloat16), "ctx", axis=0, tiled=True).astype(
            jnp.float32
        ),
        lax.all_gather(shares[5].astype(jnp.bfloat16), "ctx", axis=0, tiled=True).astype(
            jnp.float32
        ),
        lax.all_gather(shares[6].astype(jnp.bfloat16), "ctx", axis=0, tiled=True).astype(
            jnp.float32
        ),
        lax.all_gather(shares[7].astype(jnp.bfloat16), "ctx", axis=0, tiled=True).astype(
            jnp.float32
        ),
        lax.all_gather(shares[8].astype(jnp.bfloat16), "ctx", axis=0, tiled=True).astype(
            jnp.float32
        ),
        lax.all_gather(shares[9].astype(jnp.bfloat16), "ctx", axis=0, tiled=True).astype(
            jnp.float32
        ),
        lax.all_gather(shares[10].astype(jnp.bfloat16), "ctx", axis=0, tiled=True).astype(
            jnp.float32
        ),
    )
    return (
        final_rows.astype(jnp.bfloat16)[None],
        loss_value,
        grad_input[None],
        shares[0],
        shares[1],
        shares[2],
        shares[3],
        shares[4],
        shares[5],
        shares[6],
        shares[7],
        shares[8],
        shares[9],
        shares[10],
    )


MESH = pl.DeviceIdType.MESH
BF16 = jnp.bfloat16
F32 = jnp.float32
GROUP = QUERY_HEADS // KEY_VALUE_HEADS
HEAD_COLUMNS = (GROUP + 2) * HEAD_SIZE
SCALE = 1.0 / math.sqrt(HEAD_SIZE)
VMEM_LIMIT = 60 * 1024 * 1024


class Place:
    def __init__(self):
        self.f = lax.axis_index("fsdp")
        self.c = lax.axis_index("ctx")
        self.z = self.c // 2
        self.k = self.c % 2
        self.fx = self.f + 1 - 2 * (self.f % 2)
        self.fy = (self.f + 2) % 4
        self.fd = 3 - self.f
        self.xp = (self.fx, self.c)
        self.yp = (self.fy, self.c)
        self.dp = (self.fd, self.c)
        self.sib = (self.f, self.c + 1 - 2 * self.k)

    def along_z(self, step):
        other = (self.z + step) % 4
        return other, (self.f, 2 * other + self.k)

    def along_ctx(self, step):
        other = (self.c + step) % 8
        return other, (self.f, other)


def greet(partners):
    barrier = pltpu.get_barrier_semaphore()
    for partner in partners:
        pl.semaphore_signal(barrier, inc=1, device_id=partner, device_id_type=MESH)
    pl.semaphore_wait(barrier, len(partners))


class Copies:
    def __init__(self, send, recv):
        self.send, self.recv, self.used = send, recv, 0

    def take(self, count):
        first = self.used
        self.used += count
        return first

    def at(self, index, src, dst, partner):
        return pltpu.make_async_remote_copy(
            src_ref=src,
            dst_ref=dst,
            send_sem=self.send.at[index],
            recv_sem=self.recv.at[index],
            device_id=partner,
            device_id_type=MESH,
        )

    def __call__(self, src, dst, partner):
        return self.at(self.take(1), src, dst, partner)


class Locals:
    def __init__(self, sems):
        self.sems, self.used, self.open = sems, 0, []

    def __call__(self, src, dst):
        copy = pltpu.make_async_copy(src, dst, self.sems.at[self.used])
        self.used += 1
        copy.start()
        self.open.append(copy)
        return copy

    def wait(self):
        for copy in self.open:
            copy.wait()
        self.open = []

    def take(self, count):
        first = self.used
        self.used += count
        return first

    def alone(self, src, dst):
        copy = self(src, dst)
        self.open.pop()
        return copy


def add_rows(dst, sources):
    rows = dst.shape[0]
    step = 32

    @pl.loop(0, rows // step)
    def _(i):
        part = pl.ds(pl.multiple_of(i * step, step), step)
        total = sources[0][part, :].astype(F32)
        for source in sources[1:]:
            total = total + source[part, :].astype(F32)
        dst[part, :] = total.astype(dst.dtype)


class Gather:
    def __init__(self, me, copies, local, own, buf):
        half = buf.shape[1] // 2
        a, b = pl.ds(0, half), pl.ds(half, half)
        own_a, own_b = buf.at[me.f, a], buf.at[me.f, b]
        self.local, self.own, self.slot = local, own, buf.at[me.f]
        self.a_x = copies(own.at[a], own_a, me.xp)
        self.b_y = copies(own.at[b], own_b, me.yp)
        self.b_x = copies(own.at[b], own_b, me.xp)
        self.a_y = copies(own.at[a], own_a, me.yp)
        self.on_y = copies(buf.at[me.fx, a], buf.at[me.fx, a], me.yp)
        self.on_x = copies(buf.at[me.fy, b], buf.at[me.fy, b], me.xp)

    def first(self):
        self.a_x.start()
        self.b_y.start()

    def second(self):
        self.b_x.start()
        self.a_y.start()
        self.kept = self.local.alone(self.own, self.slot)

    def relay(self):
        self.a_x.wait_recv()
        self.on_y.start()
        self.b_y.wait_recv()
        self.on_x.start()

    def finish(self):
        for copy in (self.b_x, self.a_y, self.on_y, self.on_x):
            copy.wait_recv()
        for copy in (self.a_x, self.b_y, self.b_x, self.a_y, self.on_y, self.on_x):
            copy.wait_send()
        self.kept.wait()


class Scatter:
    def __init__(self, me, copies, local, part, bufs):
        half = part.shape[1] // 2
        a, b = pl.ds(0, half), pl.ds(half, half)
        slot = [bufs.at[i] for i in range(10)]
        self.fwd_a, self.fwd_b, self.own_a, self.own_b = slot[0:4]
        self.rx_own, self.rx_fwd, self.ry_own, self.ry_fwd, self.r2_a, self.r2_b = slot[4:10]
        self.d_x = copies(part.at[me.fd, a], self.rx_fwd, me.xp)
        self.d_y = copies(part.at[me.fd, b], self.ry_fwd, me.yp)
        self.o_x = copies(part.at[me.fx, a], self.rx_own, me.xp)
        self.o_y = copies(part.at[me.fy, b], self.ry_own, me.yp)
        self.to_y = copies(self.fwd_a, self.r2_a, me.yp)
        self.to_x = copies(self.fwd_b, self.r2_b, me.xp)
        self.local, self.me, self.part, self.a, self.b = local, me, part, a, b

    def first(self):
        self.d_x.start()
        self.d_y.start()

    def second(self):
        self.o_x.start()
        self.o_y.start()
        me, part = self.me, self.part
        self.mine = [
            self.local.alone(part.at[me.fy, self.a], self.fwd_a),
            self.local.alone(part.at[me.fx, self.b], self.fwd_b),
            self.local.alone(part.at[me.f, self.a], self.own_a),
            self.local.alone(part.at[me.f, self.b], self.own_b),
        ]

    def relay(self):
        for copy in self.mine:
            copy.wait()
        self.d_x.wait_recv()
        add_rows(self.fwd_a, [self.fwd_a, self.rx_fwd])
        self.to_y.start()
        self.d_y.wait_recv()
        add_rows(self.fwd_b, [self.fwd_b, self.ry_fwd])
        self.to_x.start()

    def finish(self, sum_a, sum_b):
        self.o_x.wait_recv()
        self.to_y.wait_recv()
        add_rows(sum_a, [self.own_a, self.rx_own, self.r2_a])
        self.o_y.wait_recv()
        self.to_x.wait_recv()
        add_rows(sum_b, [self.own_b, self.ry_own, self.r2_b])

    def drain(self):
        for copy in (self.d_x, self.d_y, self.o_x, self.o_y, self.to_y, self.to_x):
            copy.wait_send()


class LineSum:
    def __init__(self, me, copies, own, bufs):
        z, f, k = me.z, me.f, me.k
        self.z = z
        self.inner = (z == 1) | (z == 2)
        self.outer = (z == 0) | (z == 3)
        self.mine = z - 1
        self.theirs = 2 - z
        self.own, self.from_outer, self.total, self.from_inner = own, bufs.at[0:2], bufs.at[2:4], bufs.at[4]
        self.copies = copies
        self.base = copies.take(8)
        self.inner_of = (f, 2 * (1 + z // 3) + k)
        self.outer_of = (f, 2 * (3 * (z - 1)) + k)
        self.partner = (f, 2 * (3 - z) + k)

    def inward(self, half):
        return self.copies.at(
            self.base + half, self.own.at[half], self.from_outer.at[half], self.inner_of
        )

    def across(self, half):
        return self.copies.at(
            self.base + 2 + half, self.own.at[half], self.from_inner, self.partner
        )

    def back_across(self, half):
        return self.copies.at(
            self.base + 4 + half, self.total.at[half], self.total.at[half], self.partner
        )

    def outward(self, half):
        return self.copies.at(
            self.base + 6 + half, self.total.at[half], self.total.at[half], self.outer_of
        )

    def start(self):
        @pl.when(self.outer)
        def _():
            first = 1 - self.z // 3
            self.inward(first).start()
            self.inward(1 - first).start()

    def meet(self):
        @pl.when(self.inner)
        def _():
            t, m = self.theirs, self.mine
            self.inward(t).wait_recv()
            add_rows(self.own.at[t], [self.own.at[t], self.from_outer.at[t]])
            self.across(t).start()

    def close(self):
        @pl.when(self.inner)
        def _():
            m = self.mine
            self.inward(m).wait_recv()
            self.across(m).wait_recv()
            add_rows(
                self.total.at[m], [self.own.at[m], self.from_outer.at[m], self.from_inner]
            )
            self.back_across(m).start()
            self.outward(m).start()

    def spread(self):
        @pl.when(self.inner)
        def _():
            t = self.theirs
            self.back_across(t).wait_recv()
            self.outward(t).start()

    def arrive(self):
        @pl.when(self.outer)
        def _():
            self.outward(0).wait_recv()
            self.outward(1).wait_recv()

    def drain(self):
        @pl.when(self.outer)
        def _():
            self.inward(0).wait_send()
            self.inward(1).wait_send()

        @pl.when(self.inner)
        def _():
            self.across(self.theirs).wait_send()
            self.back_across(self.mine).wait_send()
            self.outward(0).wait_send()
            self.outward(1).wait_send()


HBM = pl.BlockSpec(memory_space=pl.ANY)
VM = pl.BlockSpec(memory_space=pltpu.VMEM)


def transfer(kernel, name, number, args, in_specs, outs, out_specs, scratch, copies, local):
    return pl.pallas_call(
        kernel,
        out_shape=outs,
        in_specs=in_specs,
        out_specs=out_specs,
        scratch_shapes=scratch
        + [
            pltpu.SemaphoreType.DMA((copies,)),
            pltpu.SemaphoreType.DMA((copies,)),
            pltpu.SemaphoreType.DMA((local,)),
        ],
        compiler_params=pltpu.CompilerParams(
            collective_id=number, has_side_effects=True, vmem_limit_bytes=VMEM_LIMIT
        ),
        name=name,
    )(*args)


def shape(dims, dtype):
    return jax.ShapeDtypeStruct(dims, dtype)


def assemble_kernel(gate, up, heads, down, out, g_gate, g_up, g_q, g_k, g_v, g_down, g_out):
    for src, dst in ((gate, g_gate), (up, g_up)):
        width = src.shape[2] // 4
        for i in range(4):
            for j in range(2):
                dst[:, pl.ds((2 * i + j) * width, width)] = src[j, :, pl.ds(i * width, width)].astype(F32)
    q_size, size = GROUP * HEAD_SIZE, HEAD_SIZE
    for head in range(KEY_VALUE_HEADS):
        g_q[:, pl.ds(head * q_size, q_size)] = heads[head, :, pl.ds(0, q_size)].astype(F32)
        g_k[:, pl.ds(head * size, size)] = heads[head, :, pl.ds(q_size, size)].astype(F32)
        g_v[:, pl.ds(head * size, size)] = heads[head, :, pl.ds(q_size + size, size)].astype(F32)
    g_down[...] = down[...].astype(F32)
    g_out[...] = out[...].astype(F32)


def assemble(gate, up, heads, down, out):
    steps = 8

    def cut(dims):
        return pl.BlockSpec((dims[0], dims[1] // steps, dims[2]), lambda i: (0, i, 0))

    def flat(rows, columns):
        return pl.BlockSpec((rows // steps, columns), lambda i: (i, 0)), shape((rows, columns), F32)

    rows, width = gate.shape[1], 2 * gate.shape[2]
    all_heads = KEY_VALUE_HEADS * HEAD_SIZE
    outs = [
        flat(rows, width), flat(rows, width), flat(rows, GROUP * all_heads), flat(rows, all_heads), flat(rows, all_heads),
        (cut(down.shape), shape(down.shape, F32)), (cut(out.shape), shape(out.shape, F32)),
    ]
    return pl.pallas_call(
        assemble_kernel,
        grid=(steps,),
        out_shape=[s for _, s in outs],
        in_specs=[cut(a.shape) for a in (gate, up, heads, down, out)],
        out_specs=[b for b, _ in outs],
        compiler_params=pltpu.CompilerParams(vmem_limit_bytes=VMEM_LIMIT),
        name="assemble",
    )(gate, up, heads, down, out)


def dot_nt(a, b, **kw):
    return lax.dot_general(a, b, (((1,), (1,)), ((), ())), preferred_element_type=F32, **kw)


def dot_nn(a, b):
    return lax.dot_general(a, b, (((1,), (0,)), ((), ())), preferred_element_type=F32)


def dot_tn(a, b):
    return lax.dot_general(a, b, (((0,), (0,)), ((), ())), preferred_element_type=F32)


HIGHEST = lax.Precision.HIGHEST


class SmallSum:
    def __init__(self, me, copies, own, plane, pair, line):
        self.me, self.own, self.plane, self.pair, self.line = me, own, plane, pair, line
        self.one = [copies(own, plane.at[me.f], partner) for partner in (me.xp, me.yp, me.dp)]
        self.two = [copies(pair.at[me.k], pair.at[me.k], me.sib)]
        self.three = [
            copies(line.at[me.z], line.at[me.z], me.along_z(step)[1]) for step in (1, 2, 3)
        ]

    def first(self):
        for copy in self.one:
            copy.start()
        self.plane[self.me.f] = self.own[...]

    def second(self):
        for copy in self.one:
            copy.wait_recv()
        plane = self.plane
        self.pair[self.me.k] = (plane[0] + plane[1]) + (plane[2] + plane[3])
        self.two[0].start()

    def third(self):
        self.two[0].wait_recv()
        self.line[self.me.z] = self.pair[0] + self.pair[1]
        for copy in self.three:
            copy.start()

    def finish(self, dst):
        for copy in self.three:
            copy.wait_recv()
        line = self.line
        dst[...] = (line[0] + line[1]) + (line[2] + line[3])

    def drain(self):
        for copy in self.one + self.two + self.three:
            copy.wait_send()


class Spread:
    def __init__(self, me, copies, held):
        self.me, self.held, self.copies = me, held, copies
        self.up, self.down = copies.take(3), copies.take(3)
        self.cross_own, self.cross_up, self.cross_down = copies.take(1), copies.take(3), copies.take(3)

    def hop(self, base, hop, block, partner):
        ref = self.held.at[block]
        return self.copies.at(base + hop - 1, ref, ref, partner)

    def rise(self, hop):
        me = self.me
        return self.hop(self.up, hop, me.c - 2 * (hop - 1), (me.f, me.c + 2))

    def fall(self, hop):
        me = self.me
        return self.hop(self.down, hop, me.c + 2 * (hop - 1), (me.f, me.c - 2))

    def across(self, base, hop, block):
        return self.hop(base, hop, block, self.me.sib)

    def start(self):
        z = self.me.z

        @pl.when(z < 3)
        def _():
            self.rise(1).start()

        @pl.when(z > 0)
        def _():
            self.fall(1).start()

        self.across(self.cross_own, 1, self.me.c).start()

    def step(self, hop):
        z, c = self.me.z, self.me.c

        @pl.when(z >= hop)
        def _():
            self.rise(hop).wait_recv()
            if hop < 3:

                @pl.when(z < 3)
                def _():
                    self.rise(hop + 1).start()

            self.across(self.cross_up, hop, c - 2 * hop).start()

        @pl.when(z + hop <= 3)
        def _():
            self.fall(hop).wait_recv()
            if hop < 3:

                @pl.when(z > 0)
                def _():
                    self.fall(hop + 1).start()

            self.across(self.cross_down, hop, c + 2 * hop).start()

    def crossed(self, hop):
        z, c = self.me.z, self.me.c
        if hop == 0:
            self.across(self.cross_own, 1, c).wait_recv()
            return

        @pl.when(z >= hop)
        def _():
            self.across(self.cross_up, hop, c - 2 * hop).wait_recv()

        @pl.when(z + hop <= 3)
        def _():
            self.across(self.cross_down, hop, c + 2 * hop).wait_recv()

    def drain(self):
        z, c = self.me.z, self.me.c
        self.across(self.cross_own, 1, c).wait_send()
        for hop in (1, 2, 3):

            @pl.when((z >= hop - 1) & (z < 3))
            def _(hop=hop):
                self.rise(hop).wait_send()

            @pl.when((z + hop - 1 <= 3) & (z > 0))
            def _(hop=hop):
                self.fall(hop).wait_send()

            @pl.when(z >= hop)
            def _(hop=hop):
                self.across(self.cross_up, hop, c - 2 * hop).wait_send()

            @pl.when(z + hop <= 3)
            def _(hop=hop):
                self.across(self.cross_down, hop, c + 2 * hop).wait_send()


def half_turn(values):
    return pltpu.roll(values, HEAD_SIZE // 2, 1)


def rotary_tables(position_rows, freq, cosines, sines, at):
    columns = jnp.transpose(position_rows)
    lane = lax.broadcasted_iota(jnp.int32, (HEAD_SIZE, HEAD_SIZE), 1)
    first = lane < HEAD_SIZE // 2
    for r in range(2):
        angle = columns[:, r : r + 1] * freq
        turns = jnp.floor(angle * (2.0 / math.pi) + 0.5)
        rest = ((angle - turns * 1.5703125) - turns * 4.837512969970703125e-04) - turns * 7.549789954891882e-08
        square = rest * rest
        sine = rest + rest * square * (
            -1.6666654611e-01 + square * (8.3321608736e-03 - square * 1.9515295891e-04)
        )
        cosine = 1.0 + square * (
            -0.5 + square * (4.166664568298827e-02 + square * (-1.388731625493765e-03 + square * 2.443315711809948e-05))
        )
        quarter = (turns.astype(jnp.int32) + jnp.where(first, 0, 3)) & 3
        odd = (quarter & 1) == 1
        value = jnp.where(odd, sine, cosine)
        value = jnp.where((quarter == 1) | (quarter == 2), -value, value)
        other = half_turn(value)
        rows = pl.ds(pl.multiple_of(at + r * 128, 128), 128)
        cosines[rows, :] = jnp.where(first, value, other)
        sines[rows, :] = jnp.where(first, -other, value)


def head_norm(u):
    return lax.rsqrt(jnp.mean(u * u, axis=-1, keepdims=True) + EPSILON)


def kernel_forward(
    wq, wk, wv, wo, wg, wu, wd, x, t, misc, gains, count, freq,
    x_pair, t_pair, misc_all, gains_all, count_out,
    w_head, wo_all, wg_all, wu_all, wd_all,
    h_all, proj, qkv, att, lse, cosines, sines, att_all,
    x_all, values, own_h, own_o, own_g, own_u, own_d, gain_row, plane, pair, line,
    send, recv, lsem,
):
    me = Place()
    z, k, f, c = me.z, me.k, me.f, me.c
    rows = x.shape[0]
    greet([me.xp, me.yp, me.dp, me.sib] + [me.along_z(step)[1] for step in (1, 2, 3)])
    copies, local = Copies(send, recv), Locals(lsem)
    q_size = GROUP * HEAD_SIZE
    head_loads = [
        local.alone(wq.at[:, pl.ds(pl.multiple_of(c * q_size, 128), q_size)], own_h.at[:, pl.ds(0, q_size)]),
        local.alone(wk.at[:, pl.ds(pl.multiple_of(c * HEAD_SIZE, 128), HEAD_SIZE)], own_h.at[:, pl.ds(q_size, HEAD_SIZE)]),
        local.alone(
            wv.at[:, pl.ds(pl.multiple_of(c * HEAD_SIZE, 128), HEAD_SIZE)],
            own_h.at[:, pl.ds(q_size + HEAD_SIZE, HEAD_SIZE)],
        ),
    ]
    width = wg.shape[1] // 8
    for src, own in ((wo, own_o), (wd, own_d)):
        local(src.at[pl.ds(pl.multiple_of(k * own.shape[0], 16), own.shape[0])], own)
    for src, own in ((wg, own_g), (wu, own_u)):
        for i in range(4):
            at = pl.ds(pl.multiple_of((2 * i + k) * width, 128), width)
            local(src.at[:, at], own.at[:, pl.ds(i * width, width)])
    small = SmallSum(me, copies, count, plane, pair, line)
    small.first()
    gain_sends = [copies(gains, gains_all.at[f], partner) for partner in (me.xp, me.yp, me.dp)]
    misc_sends = [
        copies(misc, misc_all.at[k, z], me.along_z(step)[1]) for step in (1, 2, 3)
    ]
    for copy in misc_sends + gain_sends:
        copy.start()
    x_all[c] = x[...]
    spread = Spread(me, copies, x_all)
    spread.start()
    pair_sends = [copies(t, t_pair.at[k], me.sib)]
    pair_sends[0].start()
    for copy in head_loads:
        copy.wait()
    head = Gather(me, copies, local, own_h, w_head)
    head.first()
    head.second()
    local.wait()
    out = Gather(me, copies, local, own_o, wo_all)
    gate = Gather(me, copies, local, own_g, wg_all)
    up = Gather(me, copies, local, own_u, wu_all)
    down = Gather(me, copies, local, own_d, wd_all)
    out.first()
    out.second()
    gate.first()
    gate.second()
    keep = [local.alone(t, t_pair.at[k])]
    for copy in misc_sends:
        copy.wait_recv()
    misc_all[k, z] = misc[...]
    gains_all[f] = gains[...]
    misc_pass = copies(misc_all.at[k], misc_all.at[k], me.sib)
    misc_pass.start()
    small.second()
    for copy in gain_sends:
        copy.wait_recv()
    for i in range(4):
        for r in range(2):
            gain_row[0:1, pl.ds((2 * i + r) * 128, 128)] = gains_all[i, r : r + 1, :]
    gain_q = (gains_all[0, 4:5, :] + gains_all[1, 4:5, :]) + (gains_all[2, 4:5, :] + gains_all[3, 4:5, :])
    gain_k = (gains_all[0, 5:6, :] + gains_all[1, 5:6, :]) + (gains_all[2, 5:6, :] + gains_all[3, 5:6, :])
    misc_pass.wait_recv()
    small.third()
    head.relay()

    @pl.loop(0, 8)
    def _(i):
        rotary_tables(
            misc_all[i % 2, i // 2], freq[0:1, :], cosines, sines, pl.multiple_of(i * 256, 256)
        )

    head.finish()
    spread.step(1)
    out.relay()

    def project(block):
        @pl.loop(0, 2)
        def _(u):
            piece = 2 * block + u
            at = pl.ds(pl.multiple_of(piece * rows, rows), rows)
            xin = x_all[piece].astype(F32)
            r = lax.rsqrt(jnp.mean(xin * xin, axis=-1, keepdims=True) + EPSILON)
            h = (xin * r * gain_row[0:1, :]).astype(BF16)
            h_all[at, :] = h
            p = dot_nn(h, w_head[...].reshape(w_head.shape[0] * w_head.shape[1], w_head.shape[2]))
            cosine, sine = cosines[at, :], sines[at, :]
            for g in range(GROUP + 1):
                lanes = slice(g * HEAD_SIZE, (g + 1) * HEAD_SIZE)
                one = p[:, lanes]
                proj[at, lanes] = one
                one = one * head_norm(one) * (gain_q if g < GROUP else gain_k)
                qkv[at, lanes] = (one * cosine + half_turn(one) * sine).astype(BF16)
            qkv[at, (GROUP + 1) * HEAD_SIZE :] = p[:, (GROUP + 1) * HEAD_SIZE :].astype(BF16)

    way = 1 - 2 * (z // 2)
    spread.crossed(0)
    project(z)
    spread.step(2)
    up.first()
    up.second()
    gate.relay()
    spread.crossed(1)
    spread.step(3)
    down.first()
    down.second()
    spread.crossed(2)
    spread.crossed(3)

    @pl.loop(1, 4)
    def _(step):
        project((z + way * step + 4) % 4)

    values[:, 0:HEAD_SIZE] = qkv[:, (GROUP + 1) * HEAD_SIZE :]
    values[:, HEAD_SIZE:] = jnp.ones((qkv.shape[0], HEAD_SIZE), BF16)
    base = copies.take(4)
    block = 2 * rows
    for step in (1, 2, 3, 0):
        to, partner = me.along_z(step)
        attend_rows(qkv, values, att, lse, to, block)
        piece = att.at[pl.ds(pl.multiple_of(to * block, block), block)]
        place = att_all.at[:, pl.ds(pl.multiple_of(z * q_size, 128), q_size)]
        if step:
            copy = pltpu.make_async_remote_copy(
                src_ref=piece, dst_ref=place, send_sem=send.at[base + step], recv_sem=recv.at[base + step],
                device_id=partner, device_id_type=MESH,
            )
            copy.start()
            keep.append(copy)
        else:
            keep.append(local.alone(piece, place))
        if step == 1:
            up.relay()
        if step == 3:
            down.relay()
    small.finish(count_out)
    for i in range(2):
        keep.append(local.alone(x_all.at[2 * z + i], x_pair.at[i]))
    for gather in (out, gate, up, down):
        gather.finish()
    for copy in pair_sends + [misc_pass]:
        copy.wait_send()
    pair_sends[0].wait_recv()
    for copy in misc_sends + gain_sends:
        copy.wait_send()
    for copy in keep:
        copy.wait()
    spread.drain()
    small.drain()


def forward(wq, wk, wv, wo, wg, wu, wd, x, t, misc, gains, count, freq):
    rows, width = x.shape
    tokens = 8 * rows
    row = wq.shape[0]
    half_ff = wg.shape[1] // 2
    out_rows, down_rows = wo.shape[0] // 2, wd.shape[0] // 2
    return transfer(
        kernel_forward, "forward", 1,
        (wq, wk, wv, wo, wg, wu, wd, x, t, misc, gains, count, freq),
        [HBM] * 7 + [VM] * 6,
        [
            shape((2, rows, width), BF16),
            shape((2, rows, width), BF16),
            shape((2, 4, 8, 128), F32),
            shape((4, 8, 128), F32),
            shape((8, 128), F32),
            shape((4, row, HEAD_COLUMNS), BF16),
            shape((4, out_rows, width), BF16),
            shape((4, row, half_ff), BF16),
            shape((4, row, half_ff), BF16),
            shape((4, down_rows, width), BF16),
            shape((tokens, width), BF16),
            shape((tokens, (GROUP + 1) * HEAD_SIZE), F32),
            shape((tokens, HEAD_COLUMNS), BF16),
            shape((tokens, GROUP * HEAD_SIZE), BF16),
            shape((GROUP, 8, tokens), F32),
            shape((tokens, HEAD_SIZE), F32),
            shape((tokens, HEAD_SIZE), F32),
            shape((2 * rows, 4 * GROUP * HEAD_SIZE), BF16),
        ],
        [HBM] * 2 + [VM] * 4 + [HBM] * 4 + [VM] * 7 + [HBM],
        [
            pltpu.VMEM((8, rows, width), BF16),
            pltpu.VMEM((tokens, 2 * HEAD_SIZE), BF16),
            pltpu.VMEM((row, HEAD_COLUMNS), BF16),
            pltpu.VMEM((out_rows, width), BF16),
            pltpu.VMEM((row, half_ff), BF16),
            pltpu.VMEM((row, half_ff), BF16),
            pltpu.VMEM((down_rows, width), BF16),
            pltpu.VMEM((8, width), F32),
            pltpu.VMEM((4, 8, 128), F32),
            pltpu.VMEM((2, 8, 128), F32),
            pltpu.VMEM((4, 8, 128), F32),
        ],
        7 + 3 + 3 + 13 + 1 + 30 + 1 + 4, 3 + 2 + 8 + 5 + 1 + 1 + 2,
    )


def attend_rows(qkv, values, att, lse, i, block):
    rows = pl.ds(pl.multiple_of(i * block, block), block)
    k_at = pl.ds(GROUP * HEAD_SIZE, HEAD_SIZE)
    row = lax.broadcasted_iota(jnp.int32, (block, block), 0)
    column = lax.broadcasted_iota(jnp.int32, (block, block), 1)
    for g in range(GROUP):
        q = qkv[rows, pl.ds(g * HEAD_SIZE, HEAD_SIZE)]

        def part(j, acc, q=q):
            keys = pl.ds(pl.multiple_of(j * block, block), block)
            e = jnp.exp(dot_nt(q, qkv[keys, k_at]) * SCALE)
            return acc + dot_nn(e.astype(BF16), values[keys, :])

        acc = lax.fori_loop(0, i, part, jnp.zeros((block, 2 * HEAD_SIZE), F32))
        e = jnp.exp(dot_nt(q, qkv[rows, k_at]) * SCALE)
        acc = acc + dot_nn(jnp.where(column <= row, e, 0.0).astype(BF16), values[rows, :])
        total = acc[:, HEAD_SIZE:]
        att[rows, pl.ds(g * HEAD_SIZE, HEAD_SIZE)] = (acc[:, :HEAD_SIZE] / total).astype(BF16)
        mean = jnp.full((8, HEAD_SIZE), 1.0 / HEAD_SIZE, F32)
        lse[g, :, rows] = dot_nt(mean, jnp.log(total), precision=HIGHEST)


def kernel_middle(
    att_in, wo_in, wg_in, wu_in, wd_in, x_in, t_in, misc_all, gains_all, count,
    output, g_o, p_gate, p_up, p_out, down_sum, g_x2_own, small,
    att, wo, wg, wu, wd, x, t, x2, h2, gate, up, mid, g_gate, g_up, fin, g_fin, g_dn, g_a,
    send_1, recv_1, send_2, recv_2, send_3, recv_3, p_down, p_g, p_u, p_o, g_ob, sc_d, sum_d,
    gain_row, valid, loss_row, gain_sum,
    send, recv, lsem, loss_scale,
):
    me = Place()
    z, k = me.z, me.k
    tokens, width = att.shape
    rows = tokens // 2
    greet([me.xp, me.yp, me.sib])
    copies, local = Copies(send, recv), Locals(lsem)
    loads = [
        local.alone(src, dst)
        for src, dst in (
            (att_in, att), (wo_in, wo), (x_in, x), (wg_in, wg), (wu_in, wu), (wd_in, wd), (t_in, t)
        )
    ]
    for i in range(4):
        for r in range(2):
            gain_row[0:1, pl.ds((2 * i + r) * 128, 128)] = gains_all[i, r + 2 : r + 3, :]
    for u in range(2):
        columns = jnp.transpose(misc_all[u, z])
        for r in range(2):
            valid[pl.ds(u * rows + r * 128, 128), :] = jnp.broadcast_to(columns[:, r + 2 : r + 3], (128, 128))
    small[...] = jnp.zeros_like(small)
    loss_row[...] = jnp.zeros_like(loss_row)
    gain_sum[...] = jnp.zeros_like(gain_sum)
    step = 64
    bases = [copies.take(4) for _ in range(3)]

    def crossing(which, i, src, dst):
        at = pl.ds(pl.multiple_of(i * 256, 256), 256)
        return copies.at(bases[which] + i, src.at[:, at], dst.at[:, at], me.sib)

    def flat(ref, at):
        value = ref[:, :, at]
        return value.reshape(value.shape[0] * value.shape[1], value.shape[2])

    def strip(i, size):
        return pl.ds(pl.multiple_of(i * size, size), size)

    for copy in loads[0:2]:
        copy.wait()

    @pl.loop(0, 4)
    def _(i):
        at = strip(i, 256)
        send_1[:, at] = dot_nn(att[...], flat(wo, at)).astype(BF16)
        crossing(0, i, send_1, recv_1).start()

    for copy in loads[2:5]:
        copy.wait()
    for i in range(4):
        crossing(0, i, send_1, recv_1).wait_recv()

    @pl.loop(0, tokens // step)
    def _(i):
        at = strip(i, step)
        value = x[at, :].astype(F32) + (send_1[at, :].astype(F32) + recv_1[at, :].astype(F32))
        x2[at, :] = value
        r = lax.rsqrt(jnp.mean(value * value, axis=-1, keepdims=True) + EPSILON)
        h2[at, :] = (value * r * gain_row[0:1, :]).astype(BF16)

    @pl.loop(0, gate.shape[1] // 256)
    def _(i):
        at = strip(i, 256)
        a = dot_nn(h2[...], flat(wg, at))
        b = dot_nn(h2[...], flat(wu, at))
        gate[:, at] = a
        up[:, at] = b
        mid[:, at] = (a / (1.0 + jnp.exp(-a)) * b).astype(BF16)

    for copy in loads[5:7]:
        copy.wait()

    @pl.loop(0, 4)
    def _(i):
        at = strip(i, 256)
        send_2[:, at] = dot_nn(mid[...], flat(wd, at)).astype(BF16)
        crossing(1, i, send_2, recv_2).start()

    for i in range(4):
        crossing(1, i, send_2, recv_2).wait_recv()
    factor = 2.0 * loss_scale / count[0:1, 0:1]

    @pl.loop(0, tokens // step)
    def _(i):
        at = strip(i, step)
        value = x2[at, :] + (send_2[at, :].astype(F32) + recv_2[at, :].astype(F32))
        fin[at, :] = value.astype(BF16)
        miss = value - t[at, :].astype(F32)
        weighted = valid[at, 0:1] * miss
        loss_row[0:1, :] += jnp.sum(weighted * miss, axis=0, keepdims=True)
        g = factor * weighted
        g_fin[at, :] = g
        g_dn[at, :] = g.astype(BF16)

    writes = [local.alone(fin.at[pl.ds(pl.multiple_of(k * rows, rows), rows)], output)]
    down_rows = p_down.shape[1]

    @pl.loop(0, 4)
    def _(i):
        p_down[i] = dot_tn(mid[:, strip(i, down_rows)], g_dn[...]).astype(BF16)

    s_down = Scatter(me, copies, local, p_down, sc_d)
    s_down.first()
    s_down.second()

    @pl.loop(0, 4)
    def _(i):
        at = strip(i, down_rows)
        g = dot_nt(g_dn[...], wd[i])
        a, b = gate[:, at], up[:, at]
        s = 1.0 / (1.0 + jnp.exp(-a))
        g_gate[:, at] = (g * b * s * (1.0 + a * (1.0 - s))).astype(BF16)
        g_up[:, at] = (g * a * s).astype(BF16)

    @pl.loop(0, 4)
    def _(i):
        at = strip(i, 256)
        send_3[:, at] = (dot_nt(g_gate[...], wg[i]) + dot_nt(g_up[...], wu[i])).astype(BF16)
        crossing(2, i, send_3, recv_3).start()

    @pl.loop(0, 4)
    def _(i):
        p_g[i] = dot_tn(h2[:, strip(i, 256)], g_gate[...]).astype(BF16)

    writes.append(local.alone(p_g, p_gate))
    for i in range(4):
        crossing(2, i, send_3, recv_3).wait_recv()

    @pl.loop(0, tokens // step)
    def _(i):
        at = strip(i, step)
        g = send_3[at, :].astype(F32) + recv_3[at, :].astype(F32)
        value = x2[at, :]
        r = lax.rsqrt(jnp.mean(value * value, axis=-1, keepdims=True) + EPSILON)
        n = value * r
        gain_sum[0:1, :] += jnp.sum(g * n, axis=0, keepdims=True)
        g = g * gain_row[0:1, :]
        g = g_fin[at, :] + r * (g - n * jnp.mean(g * n, axis=-1, keepdims=True))
        g_fin[at, :] = g
        g_a[at, :] = g.astype(BF16)

    writes.append(local.alone(g_fin.at[pl.ds(pl.multiple_of(k * rows, rows), rows)], g_x2_own))
    s_down.relay()

    @pl.loop(0, 4)
    def _(i):
        g_ob[:, strip(i, 256)] = dot_nt(g_a[...], wo[i]).astype(BF16)

    writes.append(local.alone(g_ob, g_o))

    @pl.loop(0, 4)
    def _(i):
        p_u[i] = dot_tn(h2[:, strip(i, 256)], g_up[...]).astype(BF16)

    writes.append(local.alone(p_u, p_up))

    @pl.loop(0, 4)
    def _(i):
        p_o[i] = dot_tn(att[:, strip(i, 256)], g_a[...]).astype(BF16)

    writes.append(local.alone(p_o, p_out))
    for j in range(8):
        small[j + 8 : j + 9, :] = 0.5 * gain_sum[0:1, pl.ds(j * 128, 128)]
        small[18:19, :] += 0.5 * loss_row[0:1, pl.ds(j * 128, 128)]
    s_down.finish(sum_d.at[0], sum_d.at[1])
    writes.append(local.alone(sum_d, down_sum))
    for copy in writes:
        copy.wait()
    for which, src, dst in ((0, send_1, recv_1), (1, send_2, recv_2), (2, send_3, recv_3)):
        for i in range(4):
            crossing(which, i, src, dst).wait_send()
    s_down.drain()


def middle(att, wo, wg, wu, wd, x, t, misc_all, gains_all, count, loss_scale):
    tokens, width = att.shape
    rows = tokens // 2
    hidden = wg.shape[2]

    def bf(*dims):
        return pltpu.VMEM(dims, BF16)

    def held(a):
        return pltpu.VMEM(a.shape, a.dtype)

    def wide(*dims):
        return pltpu.VMEM(dims, F32)

    p_down, p_gate, p_out = (4, hidden // 4, width), (4, width // 4, hidden), (4, width // 4, width)
    return transfer(
        partial(kernel_middle, loss_scale=loss_scale), "middle", 3,
        (att, wo, wg, wu, wd, x.reshape(tokens, width), t.reshape(tokens, width), misc_all, gains_all, count),
        [HBM] * 7 + [VM] * 3,
        [
            shape((rows, width), BF16), shape((tokens, width), BF16),
            shape(p_gate, BF16), shape(p_gate, BF16), shape(p_out, BF16),
            shape((2, hidden // 8, width), BF16), shape((rows, width), F32), shape((24, 128), F32),
        ],
        [HBM] * 7 + [VM],
        [held(a) for a in (att, wo, wg, wu, wd)]
        + [bf(tokens, width)] * 2
        + [wide(tokens, width), bf(tokens, width), wide(tokens, hidden), wide(tokens, hidden)]
        + [bf(tokens, hidden)] * 3
        + [bf(tokens, width), wide(tokens, width), bf(tokens, width), bf(tokens, width)]
        + [bf(tokens, width)] * 6
        + [bf(*p_down), bf(*p_gate), bf(*p_gate), bf(*p_out), bf(tokens, width)]
        + [bf(10, hidden // 8, width), bf(2, hidden // 8, width)]
        + [wide(8, width), wide(tokens, 128), wide(8, width), wide(8, width)],
        12 + 6, 7 + 7 + 4,
    )


def head_back(g, u, cosine, sine, gain):
    g = g * cosine + half_turn(g * sine)
    r = head_norm(u)
    n = u * r
    g_gain = jnp.sum(g * n, axis=0, keepdims=True)
    g = g * gain
    return r * (g - n * jnp.mean(g * n, axis=-1, keepdims=True)), g_gain


def kernel_backward(
    g_o, down_sum, p_gate, p_up, p_out,
    qkv_in, att_in, lse_in, proj_in, cos_in, sin_in, h_in, w_in,
    x, g_x2, gains_all, small,
    down_tot, gate_tot, up_tot, out_tot, head_tot, grad_in, small_tot,
    g_out, qkv, att, lse, proj, cosines, sines, h_all, w_head, g_proj, g_k, g_v, p_head,
    gh_send, gh_sib, gh_own, gh_in, gain_row, work, plane, pair, line,
    sc_g, sc_u, sc_o, sc_h, own_d, own_g, own_u, own_o, line_d, line_g, line_u, line_o,
    send, recv, lsem,
):
    me = Place()
    z, k, f, c = me.z, me.k, me.f, me.c
    rows = x.shape[0]
    block = 2 * rows
    greet([me.xp, me.yp, me.dp, me.sib] + [me.along_z(step)[1] for step in (1, 2, 3)])
    copies, local = Copies(send, recv), Locals(lsem)
    size, q_size = HEAD_SIZE, GROUP * HEAD_SIZE

    def to_device(src, dst, base, there, partner):
        return pltpu.make_async_remote_copy(
            src_ref=src, dst_ref=dst, send_sem=send.at[base + there], recv_sem=recv.at[base + z],
            device_id=partner, device_id_type=MESH,
        )

    def from_device(dst, base, there):
        return pltpu.make_async_remote_copy(
            src_ref=dst, dst_ref=dst, send_sem=send.at[base + there], recv_sem=recv.at[base + there],
            device_id=me.sib, device_id_type=MESH,
        )

    base = copies.take(4)
    go_sends = []
    for step in (2, 1, 3):
        to, partner = me.along_z(step)
        piece = g_o.at[:, pl.ds(pl.multiple_of(to * q_size, 128), q_size)]
        place = g_out.at[pl.ds(pl.multiple_of(z * block, block), block)]
        go_sends.append(to_device(piece, place, base, to, partner))
        go_sends[-1].start()
    own_go = local.alone(
        g_o.at[:, pl.ds(pl.multiple_of(z * q_size, 128), q_size)],
        g_out.at[pl.ds(pl.multiple_of(z * block, block), block)],
    )
    for src, dst in ((qkv_in, qkv), (att_in, att), (lse_in, lse), (proj_in, proj), (cos_in, cosines), (sin_in, sines)):
        local(src, dst)
    late = [local.alone(w_in, w_head)]
    h_base = local.take(4)

    def h_load(i):
        columns = pl.ds(pl.multiple_of(i * rows, rows), rows)
        return pltpu.make_async_copy(h_in.at[:, columns], h_all.at[i % 2], lsem.at[h_base + i])

    h_load(0).start()
    h_load(1).start()
    s_gate = Scatter(me, copies, local, p_gate, sc_g)
    s_up = Scatter(me, copies, local, p_up, sc_u)
    s_out = Scatter(me, copies, local, p_out, sc_o)
    s_head = Scatter(me, copies, local, p_head, sc_h)
    s_gate.first()
    s_gate.second()
    own_down = local.alone(down_sum, own_d)
    lines = [
        LineSum(me, copies, own, bufs)
        for own, bufs in ((own_d, line_d), (own_g, line_g), (own_u, line_u), (own_o, line_o))
    ]
    l_down, l_gate, l_up, l_out = lines
    totals = (down_tot, gate_tot, up_tot, out_tot)
    swap_base = copies.take(8)
    swaps, writes = [], []

    def finish(i):
        lines[i].arrive()
        half = lines[i].total.shape[1]
        for j in range(2):
            dst = totals[i].at[k, pl.ds(j * half, half)]
            copy = copies.at(swap_base + 2 * i + j, lines[i].total.at[j], dst, me.sib)
            copy.start()
            swaps.append(copy)
            writes.append(local.alone(lines[i].total.at[j], dst))

    def scattered(scatter, entry, own):
        scatter.finish(own.at[0], own.at[1])
        entry.start()

    work[...] = small[...]
    for i in range(4):
        for r in range(2):
            gain_row[0:1, pl.ds((2 * i + r) * 128, 128)] = gains_all[i, r : r + 1, :]
    gain_q = (gains_all[0, 4:5, :] + gains_all[1, 4:5, :]) + (gains_all[2, 4:5, :] + gains_all[3, 4:5, :])
    gain_k = (gains_all[0, 5:6, :] + gains_all[1, 5:6, :]) + (gains_all[2, 5:6, :] + gains_all[3, 5:6, :])
    k_at = pl.ds(q_size, size)
    v_at = pl.ds(q_size + size, size)
    g_k[...] = jnp.zeros_like(g_k)
    g_v[...] = jnp.zeros_like(g_v)
    key = lax.broadcasted_iota(jnp.int32, (block, block), 0)
    query = lax.broadcasted_iota(jnp.int32, (block, block), 1)
    def queries(i):
        at = pl.ds(pl.multiple_of(i * block, block), block)
        for g in range(GROUP):
            head = pl.ds(g * size, size)
            q = qkv[at, head]
            go = g_out[at, head]
            product = go.astype(F32) * att[at, head].astype(F32)
            delta = dot_nt(jnp.ones((8, size), F32), product, precision=HIGHEST)[0:1, :]
            log_sum = lse[g, 0:1, at]

            def part(keys, masked, q=q, go=go, delta=delta, log_sum=log_sum):
                kk, vv = qkv[keys, k_at], qkv[keys, v_at]
                p = jnp.exp(dot_nt(kk, q) * SCALE - log_sum)
                if masked:
                    p = jnp.where(key <= query, p, 0.0)
                gs = (p * (dot_nt(vv, go) - delta) * SCALE).astype(BF16)
                g_v[keys, :] += dot_nn(p.astype(BF16), go)
                g_k[keys, :] += dot_nn(gs, q)
                return dot_tn(gs, kk)

            def step(j, acc, part=part):
                return acc + part(pl.ds(pl.multiple_of(j * block, block), block), False)

            acc = lax.fori_loop(0, i, step, jnp.zeros((block, size), F32))
            acc = acc + part(at, True)
            g_u, g_gain = head_back(acc, proj[at, head], cosines[at, :], sines[at, :], gain_q)
            g_proj[at, head] = g_u.astype(BF16)
            work[16:17, :] += g_gain

    local.wait()
    own_go.wait()
    queries(z)
    own_down.wait()
    l_down.start()
    for step in (1, 2, 3):
        other, _ = me.along_z(step)
        from_device(g_out.at[pl.ds(pl.multiple_of(other * block, block), block)], base, other).wait_recv()
    queries((z + 1) % 4)
    s_gate.relay()
    s_up.first()
    s_up.second()
    queries((z + 3) % 4)
    l_down.meet()
    scattered(s_gate, l_gate, own_g)
    queries((z + 2) % 4)
    l_down.close()
    s_up.relay()
    s_out.first()
    s_out.second()

    @pl.loop(0, 4)
    def _(i):
        at = pl.ds(pl.multiple_of(i * block, block), block)
        g_u, g_gain = head_back(g_k[at, :], proj[at, k_at], cosines[at, :], sines[at, :], gain_k)
        g_proj[at, k_at] = g_u.astype(BF16)
        g_proj[at, v_at] = g_v[at, :].astype(BF16)
        work[17:18, :] += g_gain


    for copy in late:
        copy.wait()
    l_gate.meet()
    sib_base, right_base, left_base = copies.take(4), copies.take(4), copies.take(4)
    last = (z == 0) | (z == 3)
    inner = (z == 1) | (z == 2)

    def input_part(to, mine, dst):
        at = pl.ds(pl.multiple_of((2 * to + mine) * rows, rows), rows)
        weights = w_head[...].reshape(w_head.shape[0] * w_head.shape[1], w_head.shape[2])
        dst[...] = dot_nt(g_proj[at, :], weights).astype(BF16)

    def crossing(to):
        return copies.at(sib_base + to, gh_send.at[to], gh_sib.at[to], me.sib)

    def rightward(to):
        return copies.at(right_base + to, gh_own.at[to], gh_in.at[to], (f, c + 2))

    def leftward(to):
        there = 1 - (z - to) // 2
        place = gh_in.at[to + (4 - to) * there]
        return copies.at(left_base + to, gh_own.at[to], place, (f, c - 2))

    def onward(to):
        @pl.when(to > z)
        def _():
            rightward(to).start()

        @pl.when(to < z)
        def _():
            leftward(to).start()

    def join(to):
        crossing(to).wait_recv()
        add_rows(gh_own.at[to], [gh_own.at[to], gh_sib.at[to]])

    def end_send(order):
        @pl.when(last)
        def _():
            onward(far_first(order))

    def inner_send(order):
        @pl.when(inner)
        def _():
            to = far_first(order)

            @pl.when(to > z)
            def _():
                rightward(to).wait_recv()

            @pl.when(to < z)
            def _():
                copies.at(left_base + to, gh_own.at[to], gh_in.at[to], (f, c - 2)).wait_recv()

            add_rows(gh_own.at[to], [gh_own.at[to], gh_in.at[to]])
            onward(to)

    def far_first(order):
        return order + (3 - 2 * order) * (z // 2)

    def parts_to(to, previous):
        input_part(to, 1 - k, gh_send.at[to])
        crossing(to).start()
        input_part(to, k, gh_own.at[to])
        if previous is not None:
            join(previous)
        return to


    previous = parts_to(far_first(3), None)
    previous = parts_to(far_first(2), previous)
    end_send(3)
    l_down.spread()
    l_gate.close()
    previous = parts_to(far_first(1), previous)
    previous = parts_to(far_first(0), previous)
    join(previous)
    scattered(s_up, l_up, own_u)
    end_send(2)

    @pl.loop(0, 4)
    def _(i):
        h_load(i).wait()
        p_head[i] = dot_tn(h_all[i % 2], g_proj[...]).astype(BF16)

        @pl.when(i < 2)
        def _():
            h_load(i + 2).start()


    s_head.first()
    s_head.second()
    finish(0)
    inner_send(3)
    s_out.relay()
    l_up.meet()
    l_gate.spread()
    s_head.relay()
    l_up.close()
    scattered(s_out, l_out, own_o)
    end_send(1)
    inner_send(2)
    finish(1)
    s_head.finish(head_tot.at[c, 0], head_tot.at[c, 1])
    spread = Spread(me, copies, head_tot)
    spread.start()
    l_up.spread()
    l_out.meet()
    inner_send(0)
    spread.step(1)
    finish(2)
    l_out.close()
    spread.step(2)
    spread.step(3)
    l_out.spread()
    work[0:8, :] = jnp.zeros((8, 128), F32)

    @pl.when(z > 0)
    def _():
        rightward(z).wait_recv()

    @pl.when(z < 3)
    def _():
        copies.at(left_base + z, gh_own.at[z], gh_in.at[4], (f, c - 2)).wait_recv()

    @pl.when(z == 0)
    def _():
        gh_in[0] = jnp.zeros(gh_in.shape[1:], BF16)

    @pl.when(z == 3)
    def _():
        gh_in[4] = jnp.zeros(gh_in.shape[1:], BF16)

    @pl.loop(0, rows // 64)
    def _(i):
        at = pl.ds(pl.multiple_of(i * 64, 64), 64)
        g = gh_own[z, at, :].astype(F32) + gh_in[z, at, :].astype(F32) + gh_in[4, at, :].astype(F32)
        xin = x[at, :].astype(F32)
        r = lax.rsqrt(jnp.mean(xin * xin, axis=-1, keepdims=True) + EPSILON)
        n = xin * r
        g_gain = jnp.sum(g * n, axis=0, keepdims=True)
        for j in range(8):
            work[j : j + 1, :] += g_gain[:, j * 128 : (j + 1) * 128]
        g = g * gain_row[0:1, :]
        grad_in[at, :] = g_x2[at, :] + r * (g - n * jnp.mean(g * n, axis=-1, keepdims=True))


    total = SmallSum(me, copies, work, plane, pair, line)
    total.first()
    total.second()
    total.third()
    finish(3)
    total.finish(small_tot)
    for hop in range(4):
        spread.crossed(hop)
    for copy in go_sends:
        copy.wait_send()
    for i in range(4):
        crossing(i).wait_send()

        @pl.when(i > z)
        def _(i=i):
            rightward(i).wait_send()

        @pl.when(i < z)
        def _(i=i):
            leftward(i).wait_send()

    spread.drain()
    total.drain()
    for scatter in (s_gate, s_up, s_out, s_head):
        scatter.drain()
    for entry in lines:
        entry.drain()
    for copy in swaps:
        copy.wait()
    for copy in writes:
        copy.wait()


def backward(g_o, parts, saved, x, g_x2, gains_all, small):
    rows, width = x.shape
    tokens = 8 * rows
    sizes = [(2 * parts[0].shape[1], width)] + [p.shape[1:] for p in parts[1:]]
    head = (width // 4, HEAD_COLUMNS)

    def held(a):
        return pltpu.VMEM(a.shape, a.dtype)

    pieces = pltpu.VMEM((4, rows, width), BF16)
    scatters = [pltpu.VMEM((10, r // 2, n), BF16) for r, n in sizes[1:] + [head]]
    own = [pltpu.VMEM((2, r // 2, n), BF16) for r, n in sizes]
    line = [pltpu.VMEM((5, r // 2, n), BF16) for r, n in sizes]
    return transfer(
        kernel_backward, "backward", 2,
        (g_o,) + tuple(parts) + tuple(saved) + (x, g_x2, gains_all, small),
        [HBM] * 13 + [VM] * 4,
        [shape((2,) + s, BF16) for s in sizes]
        + [
            shape((8, 2, head[0] // 2, head[1]), BF16),
            shape((rows, width), F32),
            shape(small.shape, F32),
        ],
        [HBM] * 4 + [VM] * 3,
        [pltpu.VMEM((tokens, GROUP * HEAD_SIZE), BF16)]
        + [held(a) for a in saved[:6]]
        + [pltpu.VMEM((2, tokens, rows), BF16), held(saved[7])]
        + [
            pltpu.VMEM((tokens, HEAD_COLUMNS), BF16),
            pltpu.VMEM((tokens, HEAD_SIZE), F32),
            pltpu.VMEM((tokens, HEAD_SIZE), F32),
            pltpu.VMEM((4,) + head, BF16),
            pieces, pieces, pieces, pltpu.VMEM((5, rows, width), BF16),
            pltpu.VMEM((8, width), F32),
            pltpu.VMEM(small.shape, F32),
            pltpu.VMEM((4,) + small.shape, F32),
            pltpu.VMEM((2,) + small.shape, F32),
            pltpu.VMEM((4,) + small.shape, F32),
        ]
        + scatters + own + line,
        4 + 24 + 32 + 8 + 12 + 7 + 13, 1 + 7 + 4 + 1 + 16 + 8,
    )


def chip_step(
    hidden_in, teacher, valid, positions, norm_attn, w_query, key_projection, value_projection,
    gain_query, gain_key, w_out, norm_mlp, w_gate, w_up, w_down,
):
    f = lax.axis_index("fsdp")
    rows = hidden_in.shape[1]
    width = hidden_in.shape[2]
    misc = jnp.concatenate(
        [positions.reshape(-1, 128), valid.reshape(-1, 128), jnp.zeros((4, 128), jnp.int32)], 0
    ).astype(F32)
    here = jnp.arange(HEAD_SIZE, dtype=jnp.int32) // gain_query.shape[0] == f
    gains = jnp.concatenate(
        [
            norm_attn.reshape(-1, 128), norm_mlp.reshape(-1, 128),
            jnp.where(here, jnp.tile(gain_query, 4), 0)[None], jnp.where(here, jnp.tile(gain_key, 4), 0)[None],
            jnp.zeros((2, 128), BF16),
        ]
    ).astype(F32)
    count = jnp.full((8, 128), jnp.sum(valid).astype(F32))
    half_width = HEAD_SIZE // 2
    freq = jnp.exp(jnp.arange(half_width, dtype=F32) * (-2.0 * math.log(1000000.0) / HEAD_SIZE))
    freq = jnp.broadcast_to(jnp.concatenate([freq, freq]), (8, HEAD_SIZE))
    (
        x_pair, t_pair, misc_all, gains_all, count, w_head, wo, wg, wu, wd,
        h_all, proj, qkv, att, lse, cosines, sines, att_all,
    ) = forward(
        w_query, key_projection, value_projection, w_out, w_gate, w_up, w_down,
        hidden_in[0], teacher[0], misc, gains, count, freq,
    )
    loss_scale = rows * lax.axis_size("ctx") * lax.axis_size("fsdp") / 4.0
    output, g_o, p_gate, p_up, p_out, s_down, g_x2, small = middle(
        att_all, wo, wg, wu, wd, x_pair, t_pair, misc_all, gains_all, count, loss_scale
    )
    down, gate, up, out, heads, grad_input, small = backward(
        g_o, (s_down, p_gate, p_up, p_out),
        (qkv, att, lse, proj, cosines, sines, h_all, w_head),
        hidden_in[0], g_x2, gains_all, small,
    )

    def mine(values):
        size = values.shape[0] // 4
        return lax.dynamic_slice_in_dim(values, f * size, size, 0)

    g_gate, g_up, g_q, g_k, g_v, g_down, g_out = assemble(
        gate, up, heads.reshape(8, -1, HEAD_COLUMNS), down, out
    )
    return (
        output[None],
        jnp.sum(small[18]) / count[0, 0],
        grad_input[None],
        mine(small[0:8].reshape(-1)),
        g_q,
        g_k,
        g_v,
        mine(small[16]),
        mine(small[17]),
        g_out.reshape(-1, width),
        mine(small[8:16].reshape(-1)),
        g_gate,
        g_up,
        g_down.reshape(-1, width),
    )


def solution(mesh):
    chips = mesh.shape["fsdp"] == 4 and mesh.shape["ctx"] == KEY_VALUE_HEADS
    return jax.shard_map(
        chip_step if chips else per_device,
        mesh=mesh,
        in_specs=(
            P("fsdp", "ctx", None),
            P("fsdp", "ctx", None),
            P("fsdp", "ctx"),
            P("fsdp", "ctx"),
            P("fsdp"),
            P("fsdp", None),
            P("fsdp", None),
            P("fsdp", None),
            P("fsdp"),
            P("fsdp"),
            P("fsdp", None),
            P("fsdp"),
            P("fsdp", None),
            P("fsdp", None),
            P("fsdp", None),
        ),
        out_specs=(
            P("fsdp", "ctx", None),
            P(),
            P("fsdp", "ctx", None),
            P("fsdp"),
            P("fsdp", None),
            P("fsdp", None),
            P("fsdp", None),
            P("fsdp"),
            P("fsdp"),
            P("fsdp", None),
            P("fsdp"),
            P("fsdp", None),
            P("fsdp", None),
            P("fsdp", None),
        ),
        check_vma=False,
    )
```

```python
from functools import partial
import math

import jax
import jax.numpy as jnp
import numpy as np
from jax import lax
from jax.experimental import pallas as pl
from jax.experimental.pallas import tpu as pltpu
from jax.sharding import PartitionSpec as P

QUERY_HEADS = 16
KEY_VALUE_HEADS = 8
HEAD_SIZE = 128


EPSILON = 1e-06


def root_mean_norm(values, norm_gain):
    return (
        values * lax.rsqrt(jnp.mean(values * values, axis=-1, keepdims=True) + EPSILON) * norm_gain
    )


def rope_tables(position_ids):
    half_width = HEAD_SIZE // 2
    freq_table = jnp.exp(
        jnp.arange(half_width, dtype=jnp.float32) * (-2.0 * math.log(1000000.0) / HEAD_SIZE)
    )
    angle_table = position_ids.astype(jnp.float32)[:, None] * freq_table[None, :]
    cosine_table = jnp.cos(angle_table)
    sine_table = jnp.sin(angle_table)
    return (
        jnp.concatenate([cosine_table, cosine_table], -1),
        jnp.concatenate([-sine_table, sine_table], -1),
    )


def apply_rotary(values, cosine_table, sine_table):
    half_width = HEAD_SIZE // 2
    swapped = jnp.concatenate([values[..., half_width:], values[..., :half_width]], -1)
    return values * cosine_table[:, None, :] + swapped * sine_table[:, None, :]


def shape_heads(cosine_table, sine_table, proj_query, projected_key, gain_q, key_gain):
    token_rows = proj_query.shape[0]
    query_rows = apply_rotary(
        root_mean_norm(proj_query.reshape(token_rows, QUERY_HEADS, HEAD_SIZE), gain_q),
        cosine_table,
        sine_table,
    )
    rows_of_keys = apply_rotary(
        root_mean_norm(projected_key.reshape(token_rows, KEY_VALUE_HEADS, HEAD_SIZE), key_gain),
        cosine_table,
        sine_table,
    )
    return (query_rows, rows_of_keys)


def swiglu(gate_proj, up_proj):
    return gate_proj / (1.0 + jnp.exp(-gate_proj)) * up_proj


def contract_rows(left_arr, right_arr):
    return lax.dot_general(
        left_arr, right_arr, (((0,), (0,)), ((), ())), preferred_element_type=jnp.float32
    )


def against(left_arr, right_arr):
    return lax.dot_general(
        left_arr, right_arr, (((1,), (1,)), ((), ())), preferred_element_type=jnp.float32
    )


def in_blocks(block_step, running, shard_portion):
    total_rows = shard_portion.shape[0]
    block_extent = 512
    block_count = total_rows // block_extent
    blocks = shard_portion.reshape((block_count, block_extent) + shard_portion.shape[1:])
    starts = jnp.arange(block_count, dtype=jnp.int32) * block_extent

    def scan_body(state, scan_item):
        return (block_step(state, scan_item[0], scan_item[1]), None)

    running, unused = lax.scan(scan_body, running, (blocks, starts))
    return running


def score_terms(
    query_rows,
    output_gradients,
    lse_heads,
    delta_heads,
    rows_of_keys,
    rows_of_values,
    query_index,
    key_index,
    score_scale,
):
    score_matrix = (
        jnp.einsum("alci,wli->lcaw", query_rows, rows_of_keys, preferred_element_type=jnp.float32)
        * score_scale
    )
    allowed = key_index[None, :] <= query_index[:, None]
    attention_probabilities = jnp.where(allowed, jnp.exp(score_matrix - lse_heads[..., None]), 0.0)
    grad_probs = jnp.einsum(
        "alci,wli->lcaw", output_gradients, rows_of_values, preferred_element_type=jnp.float32
    )
    score_gradient = (
        score_scale * attention_probabilities * (grad_probs - delta_heads[..., None])
    ).astype(jnp.bfloat16)
    return (attention_probabilities, score_gradient)


def per_device(
    hidden_in,
    teacher,
    valid,
    positions,
    norm_attn,
    w_query,
    key_projection,
    value_projection,
    gain_query,
    gain_key,
    w_out,
    norm_mlp,
    w_gate,
    w_up,
    w_down,
):
    gathered = (
        lax.all_gather(norm_attn, "fsdp", axis=0, tiled=True),
        lax.all_gather(w_query, "fsdp", axis=0, tiled=True),
        lax.all_gather(key_projection, "fsdp", axis=0, tiled=True),
        lax.all_gather(value_projection, "fsdp", axis=0, tiled=True),
        lax.all_gather(gain_query, "fsdp", axis=0, tiled=True),
        lax.all_gather(gain_key, "fsdp", axis=0, tiled=True),
        lax.all_gather(w_out, "fsdp", axis=0, tiled=True),
        lax.all_gather(norm_mlp, "fsdp", axis=0, tiled=True),
        lax.all_gather(w_gate, "fsdp", axis=0, tiled=True),
        lax.all_gather(w_up, "fsdp", axis=0, tiled=True),
        lax.all_gather(w_down, "fsdp", axis=0, tiled=True),
    )
    (
        full_norm_attn,
        full_query,
        full_key,
        full_value,
        full_gain_q,
        full_gain_k,
        full_out,
        full_norm_mlp,
        full_gate,
        full_up,
        full_down,
    ) = gathered
    grouped_heads = QUERY_HEADS // KEY_VALUE_HEADS
    score_scale = 1.0 / math.sqrt(HEAD_SIZE)
    residual = hidden_in[0].astype(jnp.float32)
    token_rows = residual.shape[0]
    query_index = lax.axis_index("ctx") * token_rows + jnp.arange(token_rows, dtype=jnp.int32)
    normed_one, norm_one_back = jax.vjp(
        root_mean_norm, residual, full_norm_attn.astype(jnp.float32)
    )
    hidden_one = normed_one.astype(jnp.bfloat16)
    proj_query = jnp.dot(hidden_one, full_query, preferred_element_type=jnp.float32)
    projected_key = jnp.dot(hidden_one, full_key, preferred_element_type=jnp.float32)
    projected_value = jnp.dot(hidden_one, full_value, preferred_element_type=jnp.float32)
    cosine_table, sine_table = rope_tables(positions[0])
    (query_per_head, heads_key), heads_back = jax.vjp(
        partial(shape_heads, cosine_table, sine_table),
        proj_query,
        projected_key,
        full_gain_q.astype(jnp.float32),
        full_gain_k.astype(jnp.float32),
    )
    query_reduced = query_per_head.astype(jnp.bfloat16).reshape(
        token_rows, KEY_VALUE_HEADS, grouped_heads, HEAD_SIZE
    )
    key_reduced = heads_key.astype(jnp.bfloat16)
    value_reduced = projected_value.astype(jnp.bfloat16).reshape(
        token_rows, KEY_VALUE_HEADS, HEAD_SIZE
    )
    key_value = jnp.stack(
        [
            key_reduced.reshape(token_rows, KEY_VALUE_HEADS * HEAD_SIZE),
            value_reduced.reshape(token_rows, KEY_VALUE_HEADS * HEAD_SIZE),
        ],
        axis=1,
    )

    def forward_block(running, shard_portion, first_row):
        run_max, run_total, run_acc = running
        rows_per_block = shard_portion.shape[0]
        rows_of_keys = shard_portion[:, 0].reshape(rows_per_block, KEY_VALUE_HEADS, HEAD_SIZE)
        rows_of_values = shard_portion[:, 1].reshape(rows_per_block, KEY_VALUE_HEADS, HEAD_SIZE)
        key_index = first_row + jnp.arange(rows_per_block, dtype=jnp.int32)
        allowed = key_index[None, :] <= query_index[:, None]
        score_matrix = (
            jnp.einsum(
                "alci,wli->lcaw", query_reduced, rows_of_keys, preferred_element_type=jnp.float32
            )
            * score_scale
        )
        score_matrix = jnp.where(allowed, score_matrix, -1e30)
        new_max = jnp.maximum(run_max, jnp.max(score_matrix, axis=-1))
        weights_part = jnp.where(allowed, jnp.exp(score_matrix - new_max[..., None]), 0.0)
        factor = jnp.exp(run_max - new_max)
        run_total = run_total * factor + jnp.sum(weights_part, axis=-1)
        run_acc = run_acc * factor[..., None] + jnp.einsum(
            "exfw,weq->exfq",
            weights_part.astype(jnp.bfloat16),
            rows_of_values,
            preferred_element_type=jnp.float32,
        )
        return (new_max, run_total, run_acc)

    start_state = (
        jnp.full((KEY_VALUE_HEADS, grouped_heads, token_rows), -1e30, jnp.float32),
        jnp.zeros((KEY_VALUE_HEADS, grouped_heads, token_rows), jnp.float32),
        jnp.zeros((KEY_VALUE_HEADS, grouped_heads, token_rows, HEAD_SIZE), jnp.float32),
    )
    run_max, run_total, run_acc = in_blocks(
        forward_block, start_state, lax.all_gather(key_value, "ctx", axis=0, tiled=True)
    )
    log_total = run_max + jnp.log(run_total)
    attn_rows = jnp.transpose(run_acc / run_total[..., None], (2, 0, 1, 3))
    attn_low = attn_rows.reshape(token_rows, QUERY_HEADS * HEAD_SIZE).astype(jnp.bfloat16)
    mid_resid = residual + jnp.dot(attn_low, full_out, preferred_element_type=jnp.float32)
    normed_two, norm_two_back = jax.vjp(
        root_mean_norm, mid_resid, full_norm_mlp.astype(jnp.float32)
    )
    hidden_two = normed_two.astype(jnp.bfloat16)
    gate_proj = jnp.dot(hidden_two, full_gate, preferred_element_type=jnp.float32)
    up_proj = jnp.dot(hidden_two, full_up, preferred_element_type=jnp.float32)
    gated, gated_back = jax.vjp(swiglu, gate_proj, up_proj)
    gated_low = gated.astype(jnp.bfloat16)
    final_rows = mid_resid + jnp.dot(gated_low, full_down, preferred_element_type=jnp.float32)
    target = teacher[0].astype(jnp.float32)
    weight_rows = valid[0].astype(jnp.float32)
    mismatch = final_rows - target
    sq_local = jnp.sum(weight_rows[:, None] * mismatch * mismatch)
    count_local = jnp.sum(weight_rows)
    sq_total, count_total = lax.psum((sq_local, count_local), ("fsdp", "ctx"))
    loss_value = sq_total / count_total
    loss_scale = token_rows * lax.axis_size("ctx") * lax.axis_size("fsdp") / 4.0
    grad_final = 2.0 * loss_scale / count_total * weight_rows[:, None] * mismatch
    grad_down_in = grad_final.astype(jnp.bfloat16)
    grad_w_down = contract_rows(gated_low, grad_down_in)
    grad_gated = against(grad_down_in, full_down)
    grad_gate_proj, grad_up_proj = gated_back(grad_gated)
    gate_low = grad_gate_proj.astype(jnp.bfloat16)
    up_low = grad_up_proj.astype(jnp.bfloat16)
    grad_w_gate = contract_rows(hidden_two, gate_low)
    grad_w_up = contract_rows(hidden_two, up_low)
    grad_hidden_two = against(gate_low, full_gate) + against(up_low, full_up)
    grad_mid_norm, grad_norm_mlp = norm_two_back(grad_hidden_two)
    grad_mid = grad_final + grad_mid_norm
    grad_branch = grad_mid.astype(jnp.bfloat16)
    grad_w_out = contract_rows(attn_low, grad_branch)
    attention_gradient = against(grad_branch, full_out).astype(jnp.bfloat16)
    attention_head_gradient = attention_gradient.reshape(
        token_rows, KEY_VALUE_HEADS, grouped_heads, HEAD_SIZE
    )
    row_delta = jnp.sum(attention_head_gradient.astype(jnp.float32) * attn_rows, axis=-1)
    delta_heads = jnp.transpose(row_delta, (1, 2, 0))
    row_stats = jnp.stack(
        [
            jnp.transpose(log_total, (2, 0, 1)).reshape(token_rows, QUERY_HEADS),
            row_delta.reshape(token_rows, QUERY_HEADS),
        ],
        axis=1,
    )

    def block_of_queries(grad_query, shard_portion, first_row):
        rows_per_block = shard_portion.shape[0]
        rows_of_keys = shard_portion[:, 0].reshape(rows_per_block, KEY_VALUE_HEADS, HEAD_SIZE)
        rows_of_values = shard_portion[:, 1].reshape(rows_per_block, KEY_VALUE_HEADS, HEAD_SIZE)
        key_index = first_row + jnp.arange(rows_per_block, dtype=jnp.int32)
        attention_probabilities, score_gradient = score_terms(
            query_reduced,
            attention_head_gradient,
            log_total,
            delta_heads,
            rows_of_keys,
            rows_of_values,
            query_index,
            key_index,
            score_scale,
        )
        return grad_query + jnp.einsum(
            "jyux,xji->ujyi", score_gradient, rows_of_keys, preferred_element_type=jnp.float32
        )

    grad_query = in_blocks(
        block_of_queries,
        jnp.zeros((token_rows, KEY_VALUE_HEADS, grouped_heads, HEAD_SIZE), jnp.float32),
        lax.all_gather(key_value, "ctx", axis=0, tiled=True),
    )
    all_stats = lax.all_gather(row_stats.astype(jnp.bfloat16), "ctx", axis=0, tiled=True).astype(
        row_stats.dtype
    )
    query_pair = jnp.stack(
        [query_reduced.reshape(token_rows, QUERY_HEADS * HEAD_SIZE), attention_gradient], axis=1
    )

    def key_block(running, shard_portion, first_row):
        grad_key, value_gradient = running
        rows_per_block = shard_portion.shape[0]
        query_rows = shard_portion[:, 0].reshape(
            rows_per_block, KEY_VALUE_HEADS, grouped_heads, HEAD_SIZE
        )
        output_gradients = shard_portion[:, 1].reshape(
            rows_per_block, KEY_VALUE_HEADS, grouped_heads, HEAD_SIZE
        )
        partial_statistics = lax.dynamic_slice_in_dim(all_stats, first_row, rows_per_block, 0)
        partial_logsumexp = jnp.transpose(
            partial_statistics[:, 0].reshape(rows_per_block, KEY_VALUE_HEADS, grouped_heads),
            (1, 2, 0),
        )
        partial_delta = jnp.transpose(
            partial_statistics[:, 1].reshape(rows_per_block, KEY_VALUE_HEADS, grouped_heads),
            (1, 2, 0),
        )
        part_index = first_row + jnp.arange(rows_per_block, dtype=jnp.int32)
        attention_probabilities, score_gradient = score_terms(
            query_rows,
            output_gradients,
            partial_logsumexp,
            partial_delta,
            key_reduced,
            value_reduced,
            part_index,
            query_index,
            score_scale,
        )
        grad_key = grad_key + jnp.einsum(
            "wzlj,lwzy->jwy", score_gradient, query_rows, preferred_element_type=jnp.float32
        )
        value_gradient = value_gradient + jnp.einsum(
            "wzlj,lwzy->jwy",
            attention_probabilities.astype(jnp.bfloat16),
            output_gradients,
            preferred_element_type=jnp.float32,
        )
        return (grad_key, value_gradient)

    key_state = (
        jnp.zeros((token_rows, KEY_VALUE_HEADS, HEAD_SIZE), jnp.float32),
        jnp.zeros((token_rows, KEY_VALUE_HEADS, HEAD_SIZE), jnp.float32),
    )
    grad_key, value_gradient = in_blocks(
        key_block, key_state, lax.all_gather(query_pair, "ctx", axis=0, tiled=True)
    )
    grad_proj_q, grad_proj_k, grad_gain_q, grad_gain_k = heads_back(
        (grad_query.reshape(token_rows, QUERY_HEADS, HEAD_SIZE), grad_key)
    )
    query_grad_low = grad_proj_q.astype(jnp.bfloat16)
    key_grad_low = grad_proj_k.astype(jnp.bfloat16)
    value_gradient_reduced = value_gradient.reshape(token_rows, KEY_VALUE_HEADS * HEAD_SIZE).astype(
        jnp.bfloat16
    )
    grad_w_query = contract_rows(hidden_one, query_grad_low)
    grad_w_key = contract_rows(hidden_one, key_grad_low)
    grad_w_value = contract_rows(hidden_one, value_gradient_reduced)
    grad_hidden_one = (
        against(query_grad_low, full_query)
        + against(key_grad_low, full_key)
        + against(value_gradient_reduced, full_value)
    )
    grad_resid_norm, grad_norm_attn = norm_one_back(grad_hidden_one)
    grad_input = grad_mid + grad_resid_norm
    grads = (
        grad_norm_attn,
        grad_w_query,
        grad_w_key,
        grad_w_value,
        grad_gain_q,
        grad_gain_k,
        grad_w_out,
        grad_norm_mlp,
        grad_w_gate,
        grad_w_up,
        grad_w_down,
    )
    shares = (
        lax.psum_scatter(grads[0], ("fsdp", "ctx"), scatter_dimension=0, tiled=True),
        lax.psum_scatter(grads[1], ("fsdp", "ctx"), scatter_dimension=0, tiled=True),
        lax.psum_scatter(grads[2], ("fsdp", "ctx"), scatter_dimension=0, tiled=True),
        lax.psum_scatter(grads[3], ("fsdp", "ctx"), scatter_dimension=0, tiled=True),
        lax.psum_scatter(grads[4], ("fsdp", "ctx"), scatter_dimension=0, tiled=True),
        lax.psum_scatter(grads[5], ("fsdp", "ctx"), scatter_dimension=0, tiled=True),
        lax.psum_scatter(grads[6], ("fsdp", "ctx"), scatter_dimension=0, tiled=True),
        lax.psum_scatter(grads[7], ("fsdp", "ctx"), scatter_dimension=0, tiled=True),
        lax.psum_scatter(grads[8], ("fsdp", "ctx"), scatter_dimension=0, tiled=True),
        lax.psum_scatter(grads[9], ("fsdp", "ctx"), scatter_dimension=0, tiled=True),
        lax.psum_scatter(grads[10], ("fsdp", "ctx"), scatter_dimension=0, tiled=True),
    )
    shares = (
        lax.all_gather(shares[0].astype(jnp.bfloat16), "ctx", axis=0, tiled=True).astype(
            jnp.float32
        ),
        lax.all_gather(shares[1].astype(jnp.bfloat16), "ctx", axis=0, tiled=True).astype(
            jnp.float32
        ),
        lax.all_gather(shares[2].astype(jnp.bfloat16), "ctx", axis=0, tiled=True).astype(
            jnp.float32
        ),
        lax.all_gather(shares[3].astype(jnp.bfloat16), "ctx", axis=0, tiled=True).astype(
            jnp.float32
        ),
        lax.all_gather(shares[4].astype(jnp.bfloat16), "ctx", axis=0, tiled=True).astype(
            jnp.float32
        ),
        lax.all_gather(shares[5].astype(jnp.bfloat16), "ctx", axis=0, tiled=True).astype(
            jnp.float32
        ),
        lax.all_gather(shares[6].astype(jnp.bfloat16), "ctx", axis=0, tiled=True).astype(
            jnp.float32
        ),
        lax.all_gather(shares[7].astype(jnp.bfloat16), "ctx", axis=0, tiled=True).astype(
            jnp.float32
        ),
        lax.all_gather(shares[8].astype(jnp.bfloat16), "ctx", axis=0, tiled=True).astype(
            jnp.float32
        ),
        lax.all_gather(shares[9].astype(jnp.bfloat16), "ctx", axis=0, tiled=True).astype(
            jnp.float32
        ),
        lax.all_gather(shares[10].astype(jnp.bfloat16), "ctx", axis=0, tiled=True).astype(
            jnp.float32
        ),
    )
    return (
        final_rows.astype(jnp.bfloat16)[None],
        loss_value,
        grad_input[None],
        shares[0],
        shares[1],
        shares[2],
        shares[3],
        shares[4],
        shares[5],
        shares[6],
        shares[7],
        shares[8],
        shares[9],
        shares[10],
    )


MESH = pl.DeviceIdType.MESH
BF16 = jnp.bfloat16
F32 = jnp.float32
GROUP = QUERY_HEADS // KEY_VALUE_HEADS
HEAD_COLUMNS = (GROUP + 2) * HEAD_SIZE
SCALE = 1.0 / math.sqrt(HEAD_SIZE)
LOG2_E = 1.0 / math.log(2.0)
VMEM_LIMIT = 60 * 1024 * 1024


class Place:
    def __init__(self):
        self.f = lax.axis_index("fsdp")
        self.c = lax.axis_index("ctx")
        self.z = self.c // 2
        self.k = self.c % 2
        self.fx = self.f + 1 - 2 * (self.f % 2)
        self.fy = (self.f + 2) % 4
        self.fd = 3 - self.f
        self.xp = (self.fx, self.c)
        self.yp = (self.fy, self.c)
        self.dp = (self.fd, self.c)
        self.sib = (self.f, self.c + 1 - 2 * self.k)

    def along_z(self, step):
        other = (self.z + step) % 4
        return other, (self.f, 2 * other + self.k)

    def along_ctx(self, step):
        other = (self.c + step) % 8
        return other, (self.f, other)


def greet(partners):
    barrier = pltpu.get_barrier_semaphore()
    for partner in partners:
        pl.semaphore_signal(barrier, inc=1, device_id=partner, device_id_type=MESH)
    pl.semaphore_wait(barrier, len(partners))


class Copies:
    def __init__(self, send, recv):
        self.send, self.recv, self.used = send, recv, 0

    def take(self, count):
        first = self.used
        self.used += count
        return first

    def at(self, index, src, dst, partner):
        return pltpu.make_async_remote_copy(
            src_ref=src,
            dst_ref=dst,
            send_sem=self.send.at[index],
            recv_sem=self.recv.at[index],
            device_id=partner,
            device_id_type=MESH,
        )

    def __call__(self, src, dst, partner):
        return self.at(self.take(1), src, dst, partner)


class Locals:
    def __init__(self, sems):
        self.sems, self.used, self.open = sems, 0, []

    def __call__(self, src, dst):
        copy = pltpu.make_async_copy(src, dst, self.sems.at[self.used])
        self.used += 1
        copy.start()
        self.open.append(copy)
        return copy

    def wait(self):
        for copy in self.open:
            copy.wait()
        self.open = []

    def take(self, count):
        first = self.used
        self.used += count
        return first

    def alone(self, src, dst):
        copy = self(src, dst)
        self.open.pop()
        return copy


def add_rows(dst, sources):
    rows = dst.shape[0]
    step = 32

    @pl.loop(0, rows // step)
    def _(i):
        part = pl.ds(pl.multiple_of(i * step, step), step)
        total = sources[0][part, :].astype(F32)
        for source in sources[1:]:
            total = total + source[part, :].astype(F32)
        dst[part, :] = total.astype(dst.dtype)


class Gather:
    def __init__(self, me, copies, local, own, buf):
        half = buf.shape[1] // 2
        a, b = pl.ds(0, half), pl.ds(half, half)
        own_a, own_b = buf.at[me.f, a], buf.at[me.f, b]
        self.local, self.own, self.slot = local, own, buf.at[me.f]
        self.a_x = copies(own.at[a], own_a, me.xp)
        self.b_y = copies(own.at[b], own_b, me.yp)
        self.b_x = copies(own.at[b], own_b, me.xp)
        self.a_y = copies(own.at[a], own_a, me.yp)
        self.on_y = copies(buf.at[me.fx, a], buf.at[me.fx, a], me.yp)
        self.on_x = copies(buf.at[me.fy, b], buf.at[me.fy, b], me.xp)

    def first(self):
        self.a_x.start()
        self.b_y.start()

    def second(self):
        self.b_x.start()
        self.a_y.start()
        self.kept = self.local.alone(self.own, self.slot)

    def relay(self):
        self.a_x.wait_recv()
        self.on_y.start()
        self.b_y.wait_recv()
        self.on_x.start()

    def finish(self):
        for copy in (self.b_x, self.a_y, self.on_y, self.on_x):
            copy.wait_recv()
        for copy in (self.a_x, self.b_y, self.b_x, self.a_y, self.on_y, self.on_x):
            copy.wait_send()
        self.kept.wait()


class Scatter:
    def __init__(self, me, copies, local, part, bufs):
        half = part.shape[1] // 2
        a, b = pl.ds(0, half), pl.ds(half, half)
        slot = [bufs.at[i] for i in range(10)]
        self.fwd_a, self.fwd_b, self.own_a, self.own_b = slot[0:4]
        self.rx_own, self.rx_fwd, self.ry_own, self.ry_fwd, self.r2_a, self.r2_b = slot[4:10]
        self.d_x = copies(part.at[me.fd, a], self.rx_fwd, me.xp)
        self.d_y = copies(part.at[me.fd, b], self.ry_fwd, me.yp)
        self.o_x = copies(part.at[me.fx, a], self.rx_own, me.xp)
        self.o_y = copies(part.at[me.fy, b], self.ry_own, me.yp)
        self.to_y = copies(self.fwd_a, self.r2_a, me.yp)
        self.to_x = copies(self.fwd_b, self.r2_b, me.xp)
        self.local, self.me, self.part, self.a, self.b = local, me, part, a, b

    def first(self):
        self.d_x.start()
        self.d_y.start()

    def second(self):
        self.o_x.start()
        self.o_y.start()
        me, part = self.me, self.part
        self.mine = [
            self.local.alone(part.at[me.fy, self.a], self.fwd_a),
            self.local.alone(part.at[me.fx, self.b], self.fwd_b),
            self.local.alone(part.at[me.f, self.a], self.own_a),
            self.local.alone(part.at[me.f, self.b], self.own_b),
        ]

    def relay(self):
        for copy in self.mine:
            copy.wait()
        self.d_x.wait_recv()
        add_rows(self.fwd_a, [self.fwd_a, self.rx_fwd])
        self.to_y.start()
        self.d_y.wait_recv()
        add_rows(self.fwd_b, [self.fwd_b, self.ry_fwd])
        self.to_x.start()

    def load_fwd(self):
        me, part = self.me, self.part
        self.mine = [
            self.local.alone(part.at[me.fy, self.a], self.fwd_a),
            self.local.alone(part.at[me.fx, self.b], self.fwd_b),
        ]

    def sum_fwd(self):
        for copy in self.mine:
            copy.wait()
        self.d_x.wait_recv()
        add_rows(self.fwd_a, [self.fwd_a, self.rx_fwd])
        self.d_y.wait_recv()
        add_rows(self.fwd_b, [self.fwd_b, self.ry_fwd])

    def resume(self, passed):
        me, part = self.me, self.part
        for copy in [self.local.alone(passed.at[0], self.fwd_a), self.local.alone(passed.at[1], self.fwd_b)]:
            copy.wait()
        self.to_y.start()
        self.to_x.start()
        self.o_x.start()
        self.o_y.start()
        self.mine = [
            self.local.alone(part.at[me.f, self.a], self.own_a),
            self.local.alone(part.at[me.f, self.b], self.own_b),
        ]

    def finish_resumed(self, sum_a, sum_b):
        for copy in self.mine:
            copy.wait()
        self.finish(sum_a, sum_b)

    def drain_resumed(self):
        for copy in (self.o_x, self.o_y, self.to_y, self.to_x):
            copy.wait_send()

    def finish(self, sum_a, sum_b):
        self.o_x.wait_recv()
        self.to_y.wait_recv()
        add_rows(sum_a, [self.own_a, self.rx_own, self.r2_a])
        self.o_y.wait_recv()
        self.to_x.wait_recv()
        add_rows(sum_b, [self.own_b, self.ry_own, self.r2_b])

    def drain(self):
        for copy in (self.d_x, self.d_y, self.o_x, self.o_y, self.to_y, self.to_x):
            copy.wait_send()


class LineSum:
    def __init__(self, me, copies, own, bufs):
        z, f, k = me.z, me.f, me.k
        self.z = z
        self.inner = (z == 1) | (z == 2)
        self.outer = (z == 0) | (z == 3)
        self.mine = z - 1
        self.theirs = 2 - z
        self.own, self.from_outer, self.total, self.from_inner = own, bufs.at[0:2], bufs.at[2:4], bufs.at[4]
        self.copies = copies
        self.base = copies.take(8)
        self.inner_of = (f, 2 * (1 + z // 3) + k)
        self.outer_of = (f, 2 * (3 * (z - 1)) + k)
        self.partner = (f, 2 * (3 - z) + k)

    def inward(self, half):
        return self.copies.at(
            self.base + half, self.own.at[half], self.from_outer.at[half], self.inner_of
        )

    def across(self, half):
        return self.copies.at(
            self.base + 2 + half, self.own.at[half], self.from_inner, self.partner
        )

    def back_across(self, half):
        return self.copies.at(
            self.base + 4 + half, self.total.at[half], self.total.at[half], self.partner
        )

    def outward(self, half):
        return self.copies.at(
            self.base + 6 + half, self.total.at[half], self.total.at[half], self.outer_of
        )

    def start(self):
        @pl.when(self.outer)
        def _():
            first = 1 - self.z // 3
            self.inward(first).start()
            self.inward(1 - first).start()

    def meet(self):
        @pl.when(self.inner)
        def _():
            t, m = self.theirs, self.mine
            self.inward(t).wait_recv()
            add_rows(self.own.at[t], [self.own.at[t], self.from_outer.at[t]])
            self.across(t).start()

    def close(self):
        @pl.when(self.inner)
        def _():
            m = self.mine
            self.inward(m).wait_recv()
            self.across(m).wait_recv()
            add_rows(
                self.total.at[m], [self.own.at[m], self.from_outer.at[m], self.from_inner]
            )
            self.back_across(m).start()
            self.outward(m).start()

    def spread(self):
        @pl.when(self.inner)
        def _():
            t = self.theirs
            self.back_across(t).wait_recv()
            self.outward(t).start()

    def arrive(self):
        @pl.when(self.outer)
        def _():
            self.outward(0).wait_recv()
            self.outward(1).wait_recv()

    def drain(self):
        @pl.when(self.outer)
        def _():
            self.inward(0).wait_send()
            self.inward(1).wait_send()

        @pl.when(self.inner)
        def _():
            self.across(self.theirs).wait_send()
            self.back_across(self.mine).wait_send()
            self.outward(0).wait_send()
            self.outward(1).wait_send()


HBM = pl.BlockSpec(memory_space=pl.ANY)
VM = pl.BlockSpec(memory_space=pltpu.VMEM)


def transfer(kernel, name, number, args, in_specs, outs, out_specs, scratch, copies, local):
    return pl.pallas_call(
        kernel,
        out_shape=outs,
        in_specs=in_specs,
        out_specs=out_specs,
        scratch_shapes=scratch
        + [
            pltpu.SemaphoreType.DMA((copies,)),
            pltpu.SemaphoreType.DMA((copies,)),
            pltpu.SemaphoreType.DMA((local,)),
        ],
        compiler_params=pltpu.CompilerParams(
            collective_id=number, has_side_effects=True, vmem_limit_bytes=VMEM_LIMIT
        ),
        name=name,
    )(*args)


def shape(dims, dtype):
    return jax.ShapeDtypeStruct(dims, dtype)


def assemble_kernel(
    gate, up, heads, down, out, small, count, tokens_out, tokens_grad,
    g_gate, g_up, g_q, g_k, g_v, g_down, g_out, g_norms, g_gains, loss, output, grad_in,
):
    for src, dst in ((gate, g_gate), (up, g_up)):
        width = src.shape[2] // 4
        for i in range(4):
            for j in range(2):
                dst[:, pl.ds((2 * i + j) * width, width)] = src[j, :, pl.ds(i * width, width)].astype(F32)
    q_size, size = GROUP * HEAD_SIZE, HEAD_SIZE
    for head in range(KEY_VALUE_HEADS):
        g_q[:, pl.ds(head * q_size, q_size)] = heads[head, :, pl.ds(0, q_size)].astype(F32)
        g_k[:, pl.ds(head * size, size)] = heads[head, :, pl.ds(q_size, size)].astype(F32)
        g_v[:, pl.ds(head * size, size)] = heads[head, :, pl.ds(q_size + size, size)].astype(F32)
    f = lax.axis_index("fsdp")
    output[...] = tokens_out[...]
    grad_in[...] = tokens_grad[...]
    for i in range(2):
        g_norms[i] = small[pl.ds(8 * i + 2 * f, 2), :]
    part = g_gains.shape[1]
    lane = lax.broadcasted_iota(jnp.int32, (HEAD_SIZE, part), 0)
    column = lax.broadcasted_iota(jnp.int32, (HEAD_SIZE, part), 1)
    pick = jnp.where(lane == column + part * f, 1.0, 0.0)
    g_gains[...] = lax.dot_general(
        small[16:24, :], pick, (((1,), (0,)), ((), ())), preferred_element_type=F32, precision=lax.Precision.HIGHEST
    )
    loss[...] = jnp.sum(small[18:19, :], axis=1, keepdims=True) / count[0:1, 0:1]
    g_down[...] = down[...].astype(F32)
    g_out[...] = out[...].astype(F32)


def assemble(gate, up, heads, down, out, small, count, tokens_out, tokens_grad):
    steps = 8

    def cut(dims):
        return pl.BlockSpec((dims[0], dims[1] // steps, dims[2]), lambda i: (0, i, 0))

    def whole(dims):
        return pl.BlockSpec(dims, lambda i: (0,) * len(dims))

    def rows_of(a):
        return pl.BlockSpec((a.shape[0] // steps, a.shape[1]), lambda i: (i, 0))

    def flat(rows, columns):
        return pl.BlockSpec((rows // steps, columns), lambda i: (i, 0)), shape((rows, columns), F32)

    rows, width = gate.shape[1], 2 * gate.shape[2]
    all_heads = KEY_VALUE_HEADS * HEAD_SIZE
    outs = [
        flat(rows, width), flat(rows, width), flat(rows, GROUP * all_heads), flat(rows, all_heads), flat(rows, all_heads),
        (cut(down.shape), shape(down.shape, F32)), (cut(out.shape), shape(out.shape, F32)),
        (whole((2, 2, 128)), shape((2, 2, 128), F32)), (whole((8, 32)), shape((8, 32), F32)),
        (whole((1, 1)), shape((1, 1), F32)),
    ] + [(rows_of(a), shape(a.shape, a.dtype)) for a in (tokens_out, tokens_grad)]
    return pl.pallas_call(
        assemble_kernel,
        grid=(steps,),
        out_shape=[s for _, s in outs],
        in_specs=[cut(a.shape) for a in (gate, up, heads, down, out)]
        + [whole(small.shape), whole(count.shape), rows_of(tokens_out), rows_of(tokens_grad)],
        out_specs=[b for b, _ in outs],
        compiler_params=pltpu.CompilerParams(vmem_limit_bytes=VMEM_LIMIT),
        name="assemble",
    )(gate, up, heads, down, out, small, count, tokens_out, tokens_grad)


def dot_nt(a, b, **kw):
    return lax.dot_general(a, b, (((1,), (1,)), ((), ())), preferred_element_type=F32, **kw)


def dot_nn(a, b):
    return lax.dot_general(a, b, (((1,), (0,)), ((), ())), preferred_element_type=F32)


def dot_tn(a, b):
    return lax.dot_general(a, b, (((0,), (0,)), ((), ())), preferred_element_type=F32)


HIGHEST = lax.Precision.HIGHEST


class SmallSum:
    def __init__(self, me, copies, own, plane, pair, line):
        self.me, self.own, self.plane, self.pair, self.line = me, own, plane, pair, line
        self.one = [copies(own, plane.at[me.f], partner) for partner in (me.xp, me.yp, me.dp)]
        self.two = [copies(pair.at[me.k], pair.at[me.k], me.sib)]
        self.three = [
            copies(line.at[me.z], line.at[me.z], me.along_z(step)[1]) for step in (1, 2, 3)
        ]

    def first(self):
        for copy in self.one:
            copy.start()
        self.plane[self.me.f] = self.own[...]

    def second(self):
        for copy in self.one:
            copy.wait_recv()
        plane = self.plane
        self.pair[self.me.k] = (plane[0] + plane[1]) + (plane[2] + plane[3])
        self.two[0].start()

    def third(self):
        self.two[0].wait_recv()
        self.line[self.me.z] = self.pair[0] + self.pair[1]
        for copy in self.three:
            copy.start()

    def finish(self, dst):
        for copy in self.three:
            copy.wait_recv()
        line = self.line
        dst[...] = (line[0] + line[1]) + (line[2] + line[3])

    def drain(self):
        for copy in self.one + self.two + self.three:
            copy.wait_send()


class Spread:
    def __init__(self, me, copies, held, cross=True):
        self.me, self.held, self.copies, self.cross = me, held, copies, cross
        self.here, self.stride = (me.c, 2) if cross else (me.z, 1)
        self.up, self.down = copies.take(3), copies.take(3)
        if cross:
            self.cross_own, self.cross_up, self.cross_down = copies.take(1), copies.take(3), copies.take(3)

    def hop(self, base, hop, block, partner):
        ref = self.held.at[block]
        return self.copies.at(base + hop - 1, ref, ref, partner)

    def rise(self, hop):
        me = self.me
        return self.hop(self.up, hop, self.here - self.stride * (hop - 1), (me.f, me.c + 2))

    def fall(self, hop):
        me = self.me
        return self.hop(self.down, hop, self.here + self.stride * (hop - 1), (me.f, me.c - 2))

    def across(self, base, hop, block):
        return self.hop(base, hop, block, self.me.sib)

    def start(self):
        z = self.me.z

        @pl.when(z < 3)
        def _():
            self.rise(1).start()

        @pl.when(z > 0)
        def _():
            self.fall(1).start()

        if self.cross:
            self.across(self.cross_own, 1, self.me.c).start()

    def step(self, hop):
        z, c = self.me.z, self.me.c

        @pl.when(z >= hop)
        def _():
            self.rise(hop).wait_recv()
            if hop < 3:

                @pl.when(z < 3)
                def _():
                    self.rise(hop + 1).start()

            if self.cross:
                self.across(self.cross_up, hop, c - 2 * hop).start()

        @pl.when(z + hop <= 3)
        def _():
            self.fall(hop).wait_recv()
            if hop < 3:

                @pl.when(z > 0)
                def _():
                    self.fall(hop + 1).start()

            if self.cross:
                self.across(self.cross_down, hop, c + 2 * hop).start()

    def crossed(self, hop):
        z, c = self.me.z, self.me.c
        if hop == 0:
            self.across(self.cross_own, 1, c).wait_recv()
            return

        @pl.when(z >= hop)
        def _():
            self.across(self.cross_up, hop, c - 2 * hop).wait_recv()

        @pl.when(z + hop <= 3)
        def _():
            self.across(self.cross_down, hop, c + 2 * hop).wait_recv()

    def drain(self):
        z, c = self.me.z, self.me.c
        if self.cross:
            self.across(self.cross_own, 1, c).wait_send()
        for hop in (1, 2, 3):

            @pl.when((z >= hop - 1) & (z < 3))
            def _(hop=hop):
                self.rise(hop).wait_send()

            @pl.when((z + hop - 1 <= 3) & (z > 0))
            def _(hop=hop):
                self.fall(hop).wait_send()

            if not self.cross:
                continue

            @pl.when(z >= hop)
            def _(hop=hop):
                self.across(self.cross_up, hop, c - 2 * hop).wait_send()

            @pl.when(z + hop <= 3)
            def _(hop=hop):
                self.across(self.cross_down, hop, c + 2 * hop).wait_send()


def half_turn(values):
    return pltpu.roll(values, HEAD_SIZE // 2, 1)


def rotary_tables(position_rows, freq, cosines, sines, at):
    columns = jnp.transpose(position_rows)
    lane = lax.broadcasted_iota(jnp.int32, (HEAD_SIZE, HEAD_SIZE), 1)
    first = lane < HEAD_SIZE // 2
    for r in range(2):
        angle = columns[:, r : r + 1] * freq
        turns = jnp.floor(angle * (2.0 / math.pi) + 0.5)
        rest = ((angle - turns * 1.5703125) - turns * 4.837512969970703125e-04) - turns * 7.549789954891882e-08
        square = rest * rest
        sine = rest + rest * square * (
            -1.6666654611e-01 + square * (8.3321608736e-03 - square * 1.9515295891e-04)
        )
        cosine = 1.0 + square * (
            -0.5 + square * (4.166664568298827e-02 + square * (-1.388731625493765e-03 + square * 2.443315711809948e-05))
        )
        quarter = (turns.astype(jnp.int32) + jnp.where(first, 0, 3)) & 3
        odd = (quarter & 1) == 1
        value = jnp.where(odd, sine, cosine)
        value = jnp.where((quarter == 1) | (quarter == 2), -value, value)
        other = half_turn(value)
        rows = pl.ds(pl.multiple_of(at + r * 128, 128), 128)
        cosines[rows, :] = jnp.where(first, value, other)
        sines[rows, :] = jnp.where(first, -other, value)


def head_norm(u):
    return lax.rsqrt(jnp.mean(u * u, axis=-1, keepdims=True) + EPSILON)


def small_arguments(f, positions, valid, norms, gain_heads, misc, gains, count):
    misc[...] = jnp.zeros_like(misc)
    for r in range(2):
        misc[r : r + 1, :] = positions[0:1, pl.ds(r * 128, 128)].astype(F32)
        misc[r + 2 : r + 3, :] = valid[0:1, pl.ds(r * 128, 128)].astype(F32)
    gains[...] = jnp.zeros_like(gains)
    gains[0:4, :] = norms[...]
    size = gain_heads.shape[1]
    lane = lax.broadcasted_iota(jnp.int32, (1, HEAD_SIZE), 1)
    for r in range(2):
        wide = jnp.concatenate([gain_heads[r : r + 1, :]] * (HEAD_SIZE // size), axis=1)
        gains[r + 4 : r + 5, :] = jnp.where(lane // size == f, wide, 0.0)
    count[...] = jnp.broadcast_to(jnp.sum(valid[...].astype(F32), axis=1, keepdims=True), count.shape)


def kernel_forward(
    wq, wk, wv, wo, wg, wu, wd, x, t, positions, valid, norms, gain_heads, freq,
    x_pair, t_pair, misc_all, gains_all, count_out,
    w_head, wo_all, wg_all, wu_all, wd_all,
    h_all, proj, qkv, att, lse, cosines, sines, att_all,
    x_all, values, own_h, own_o, own_g, own_u, own_d, gain_row, misc, gains, count, plane, pair, line,
    send, recv, lsem,
):
    me = Place()
    z, k, f, c = me.z, me.k, me.f, me.c
    rows = x.shape[0]
    small_arguments(f, positions, valid, norms, gain_heads, misc, gains, count)
    greet([me.xp, me.yp, me.dp, me.sib] + [me.along_z(step)[1] for step in (1, 2, 3)])
    copies, local = Copies(send, recv), Locals(lsem)
    q_size = GROUP * HEAD_SIZE
    head_loads = [
        local.alone(wq.at[:, pl.ds(pl.multiple_of(c * q_size, 128), q_size)], own_h.at[:, pl.ds(0, q_size)]),
        local.alone(wk.at[:, pl.ds(pl.multiple_of(c * HEAD_SIZE, 128), HEAD_SIZE)], own_h.at[:, pl.ds(q_size, HEAD_SIZE)]),
        local.alone(
            wv.at[:, pl.ds(pl.multiple_of(c * HEAD_SIZE, 128), HEAD_SIZE)],
            own_h.at[:, pl.ds(q_size + HEAD_SIZE, HEAD_SIZE)],
        ),
    ]
    width = wg.shape[1] // 8
    for src, own in ((wo, own_o), (wd, own_d)):
        local(src.at[pl.ds(pl.multiple_of(k * own.shape[0], 16), own.shape[0])], own)
    for src, own in ((wg, own_g), (wu, own_u)):
        for i in range(4):
            at = pl.ds(pl.multiple_of((2 * i + k) * width, 128), width)
            local(src.at[:, at], own.at[:, pl.ds(i * width, width)])
    small = SmallSum(me, copies, count, plane, pair, line)
    small.first()
    gain_sends = [copies(gains, gains_all.at[f], partner) for partner in (me.xp, me.yp, me.dp)]
    misc_sends = [
        copies(misc, misc_all.at[k, z], me.along_z(step)[1]) for step in (1, 2, 3)
    ]
    for copy in misc_sends + gain_sends:
        copy.start()
    x_all[c] = x[...]
    spread = Spread(me, copies, x_all)
    spread.start()
    pair_sends = [copies(t, t_pair.at[k], me.sib)]
    pair_sends[0].start()
    for copy in head_loads:
        copy.wait()
    head = Gather(me, copies, local, own_h, w_head)
    head.first()
    head.second()
    out = Gather(me, copies, local, own_o, wo_all)
    gate = Gather(me, copies, local, own_g, wg_all)
    up = Gather(me, copies, local, own_u, wu_all)
    down = Gather(me, copies, local, own_d, wd_all)
    keep = [local.alone(t, t_pair.at[k])]
    for copy in misc_sends:
        copy.wait_recv()
    misc_all[k, z] = misc[...]
    gains_all[f] = gains[...]
    misc_pass = copies(misc_all.at[k], misc_all.at[k], me.sib)
    misc_pass.start()
    small.second()
    for copy in gain_sends:
        copy.wait_recv()
    for i in range(4):
        for r in range(2):
            gain_row[0:1, pl.ds((2 * i + r) * 128, 128)] = gains_all[i, r : r + 1, :]
    gain_q = (gains_all[0, 4:5, :] + gains_all[1, 4:5, :]) + (gains_all[2, 4:5, :] + gains_all[3, 4:5, :])
    gain_k = (gains_all[0, 5:6, :] + gains_all[1, 5:6, :]) + (gains_all[2, 5:6, :] + gains_all[3, 5:6, :])
    head.relay()
    local.wait()
    for gather in (out, gate, up, down):
        gather.first()
    for gather in (out, gate, up, down):
        gather.second()
    misc_pass.wait_recv()
    small.third()

    @pl.loop(0, 8)
    def _(i):
        rotary_tables(
            misc_all[i % 2, i // 2], freq[0:1, :], cosines, sines, pl.multiple_of(i * 256, 256)
        )

    head.finish()
    spread.step(1)
    out.relay()

    def project(block):
        @pl.loop(0, 2)
        def _(u):
            piece = 2 * block + u
            at = pl.ds(pl.multiple_of(piece * rows, rows), rows)
            xin = x_all[piece].astype(F32)
            r = lax.rsqrt(jnp.mean(xin * xin, axis=-1, keepdims=True) + EPSILON)
            h = (xin * r * gain_row[0:1, :]).astype(BF16)
            h_all[at, :] = h
            p = dot_nn(h, w_head[...].reshape(w_head.shape[0] * w_head.shape[1], w_head.shape[2]))
            cosine, sine = cosines[at, :], sines[at, :]
            for g in range(GROUP + 1):
                lanes = slice(g * HEAD_SIZE, (g + 1) * HEAD_SIZE)
                one = p[:, lanes]
                proj[at, lanes] = one
                one = one * head_norm(one) * (gain_q if g < GROUP else gain_k)
                qkv[at, lanes] = (one * cosine + half_turn(one) * sine).astype(BF16)
            qkv[at, (GROUP + 1) * HEAD_SIZE :] = p[:, (GROUP + 1) * HEAD_SIZE :].astype(BF16)

    way = 1 - 2 * (z // 2)
    spread.crossed(0)
    project(z)
    spread.step(2)
    spread.crossed(1)
    spread.step(3)
    gate.relay()
    spread.crossed(2)
    spread.crossed(3)

    @pl.loop(1, 4)
    def _(step):
        project((z + way * step + 4) % 4)

    values[:, 0:HEAD_SIZE] = qkv[:, (GROUP + 1) * HEAD_SIZE :]
    values[:, HEAD_SIZE:] = jnp.ones((qkv.shape[0], HEAD_SIZE), BF16)
    base = copies.take(4)
    block = 2 * rows
    for step in (1, 2, 3, 0):
        to, partner = me.along_z(step)
        attend_rows(qkv, values, att, lse, to, block)
        piece = att.at[pl.ds(pl.multiple_of(to * block, block), block)]
        place = att_all.at[:, pl.ds(pl.multiple_of(z * q_size, 128), q_size)]
        if step:
            copy = pltpu.make_async_remote_copy(
                src_ref=piece, dst_ref=place, send_sem=send.at[base + step], recv_sem=recv.at[base + step],
                device_id=partner, device_id_type=MESH,
            )
            copy.start()
            keep.append(copy)
        else:
            keep.append(local.alone(piece, place))
        if step == 1:
            up.relay()
        if step == 2:
            down.relay()
    small.finish(count_out)
    for i in range(2):
        keep.append(local.alone(x_all.at[2 * z + i], x_pair.at[i]))
    for gather in (out, gate, up, down):
        gather.finish()
    for copy in pair_sends + [misc_pass]:
        copy.wait_send()
    pair_sends[0].wait_recv()
    for copy in misc_sends + gain_sends:
        copy.wait_send()
    for copy in keep:
        copy.wait()
    spread.drain()
    small.drain()


def forward(wq, wk, wv, wo, wg, wu, wd, x, t, positions, valid, norms, gain_heads, freq):
    rows, width = x.shape
    tokens = 8 * rows
    row = wq.shape[0]
    half_ff = wg.shape[1] // 2
    out_rows, down_rows = wo.shape[0] // 2, wd.shape[0] // 2
    return transfer(
        kernel_forward, "forward", 1,
        (wq, wk, wv, wo, wg, wu, wd, x, t, positions, valid, norms, gain_heads, freq),
        [HBM] * 7 + [VM] * 7,
        [
            shape((2, rows, width), BF16),
            shape((2, rows, width), BF16),
            shape((2, 4, 8, 128), F32),
            shape((4, 8, 128), F32),
            shape((8, 128), F32),
            shape((4, row, HEAD_COLUMNS), BF16),
            shape((4, out_rows, width), BF16),
            shape((4, row, half_ff), BF16),
            shape((4, row, half_ff), BF16),
            shape((4, down_rows, width), BF16),
            shape((tokens, width), BF16),
            shape((tokens, (GROUP + 1) * HEAD_SIZE), F32),
            shape((tokens, HEAD_COLUMNS), BF16),
            shape((tokens, GROUP * HEAD_SIZE), BF16),
            shape((GROUP, 8, tokens), F32),
            shape((tokens, HEAD_SIZE), F32),
            shape((tokens, HEAD_SIZE), F32),
            shape((2 * rows, 4 * GROUP * HEAD_SIZE), BF16),
        ],
        [HBM] * 2 + [VM] * 4 + [HBM] * 4 + [VM] * 7 + [HBM],
        [
            pltpu.VMEM((8, rows, width), BF16),
            pltpu.VMEM((tokens, 2 * HEAD_SIZE), BF16),
            pltpu.VMEM((row, HEAD_COLUMNS), BF16),
            pltpu.VMEM((out_rows, width), BF16),
            pltpu.VMEM((row, half_ff), BF16),
            pltpu.VMEM((row, half_ff), BF16),
            pltpu.VMEM((down_rows, width), BF16),
            pltpu.VMEM((8, width), F32),
            pltpu.VMEM((8, 128), F32),
            pltpu.VMEM((8, 128), F32),
            pltpu.VMEM((8, 128), F32),
            pltpu.VMEM((4, 8, 128), F32),
            pltpu.VMEM((2, 8, 128), F32),
            pltpu.VMEM((4, 8, 128), F32),
        ],
        7 + 3 + 3 + 13 + 1 + 30 + 1 + 4, 3 + 2 + 8 + 5 + 1 + 1 + 2,
    )


def attend_rows(qkv, values, att, lse, i, block):
    rows = pl.ds(pl.multiple_of(i * block, block), block)
    k_at = pl.ds(GROUP * HEAD_SIZE, HEAD_SIZE)
    row = lax.broadcasted_iota(jnp.int32, (block, block), 0)
    column = lax.broadcasted_iota(jnp.int32, (block, block), 1)
    for g in range(GROUP):
        q = qkv[rows, pl.ds(g * HEAD_SIZE, HEAD_SIZE)]

        def part(j, acc, q=q):
            keys = pl.ds(pl.multiple_of(j * block, block), block)
            e = jnp.exp2(dot_nt(q, qkv[keys, k_at]) * (SCALE * LOG2_E))
            return acc + dot_nn(e.astype(BF16), values[keys, :])

        acc = lax.fori_loop(0, i, part, jnp.zeros((block, 2 * HEAD_SIZE), F32))
        e = jnp.exp2(dot_nt(q, qkv[rows, k_at]) * (SCALE * LOG2_E))
        acc = acc + dot_nn(jnp.where(column <= row, e, 0.0).astype(BF16), values[rows, :])
        total = acc[:, HEAD_SIZE:]
        att[rows, pl.ds(g * HEAD_SIZE, HEAD_SIZE)] = (acc[:, :HEAD_SIZE] / total).astype(BF16)
        mean = jnp.full((8, HEAD_SIZE), 1.0 / HEAD_SIZE, F32)
        lse[g, :, rows] = dot_nt(mean, jnp.log(total), precision=HIGHEST)


def kernel_middle(
    att_in, wo_in, wg_in, wu_in, wd_in, x_in, t_in, misc_all, gains_all, count,
    output, g_out, p_gate, p_up, p_out, down_sum, gate_pass, g_x2_own, small,
    att, wo, wg, wu, wd, x, t, x2, h2, gate, up, mid, g_gate, g_up, fin, g_fin, g_dn, g_a,
    send_1, recv_1, send_2, recv_2, send_3, recv_3, p_down, p_g, p_u, p_o, g_ob, sc_d, sum_d, sc_g,
    gain_row, valid, loss_row, gain_sum,
    send, recv, lsem, loss_scale,
):
    me = Place()
    z, k = me.z, me.k
    tokens, width = att.shape
    rows = tokens // 2
    greet([me.xp, me.yp, me.sib] + [me.along_z(step)[1] for step in (1, 2, 3)])
    copies, local = Copies(send, recv), Locals(lsem)
    loads = [
        local.alone(src, dst)
        for src, dst in (
            (att_in, att), (wo_in, wo), (x_in, x), (wg_in, wg), (wu_in, wu), (wd_in, wd), (t_in, t)
        )
    ]
    for i in range(4):
        for r in range(2):
            gain_row[0:1, pl.ds((2 * i + r) * 128, 128)] = gains_all[i, r + 2 : r + 3, :]
    for u in range(2):
        columns = jnp.transpose(misc_all[u, z])
        for r in range(2):
            valid[pl.ds(u * rows + r * 128, 128), :] = jnp.broadcast_to(columns[:, r + 2 : r + 3], (128, 128))
    small[...] = jnp.zeros_like(small)
    loss_row[...] = jnp.zeros_like(loss_row)
    gain_sum[...] = jnp.zeros_like(gain_sum)
    step = 64
    bases = [copies.take(4) for _ in range(3)]

    def crossing(which, i, src, dst):
        at = pl.ds(pl.multiple_of(i * 256, 256), 256)
        return copies.at(bases[which] + i, src.at[:, at], dst.at[:, at], me.sib)

    def flat(ref, at):
        value = ref[:, :, at]
        return value.reshape(value.shape[0] * value.shape[1], value.shape[2])

    def strip(i, size):
        return pl.ds(pl.multiple_of(i * size, size), size)

    for copy in loads[0:2]:
        copy.wait()

    @pl.loop(0, 4)
    def _(i):
        at = strip(i, 256)
        send_1[:, at] = dot_nn(att[...], flat(wo, at)).astype(BF16)
        crossing(0, i, send_1, recv_1).start()

    for copy in loads[2:5]:
        copy.wait()
    for i in range(4):
        crossing(0, i, send_1, recv_1).wait_recv()

    @pl.loop(0, tokens // step)
    def _(i):
        at = strip(i, step)
        value = x[at, :].astype(F32) + (send_1[at, :].astype(F32) + recv_1[at, :].astype(F32))
        x2[at, :] = value
        r = lax.rsqrt(jnp.mean(value * value, axis=-1, keepdims=True) + EPSILON)
        h2[at, :] = (value * r * gain_row[0:1, :]).astype(BF16)

    @pl.loop(0, gate.shape[1] // 256)
    def _(i):
        at = strip(i, 256)
        a = dot_nn(h2[...], flat(wg, at))
        b = dot_nn(h2[...], flat(wu, at))
        gate[:, at] = a
        up[:, at] = b
        mid[:, at] = (a / (1.0 + jnp.exp(-a)) * b).astype(BF16)

    for copy in loads[5:7]:
        copy.wait()

    @pl.loop(0, 4)
    def _(i):
        at = strip(i, 256)
        send_2[:, at] = dot_nn(mid[...], flat(wd, at)).astype(BF16)
        crossing(1, i, send_2, recv_2).start()

    for i in range(4):
        crossing(1, i, send_2, recv_2).wait_recv()
    factor = 2.0 * loss_scale / count[0:1, 0:1]

    @pl.loop(0, tokens // step)
    def _(i):
        at = strip(i, step)
        value = x2[at, :] + (send_2[at, :].astype(F32) + recv_2[at, :].astype(F32))
        fin[at, :] = value.astype(BF16)
        miss = value - t[at, :].astype(F32)
        weighted = valid[at, 0:1] * miss
        loss_row[0:1, :] += jnp.sum(weighted * miss, axis=0, keepdims=True)
        g = factor * weighted
        g_fin[at, :] = g
        g_dn[at, :] = g.astype(BF16)

    writes = [local.alone(fin.at[pl.ds(pl.multiple_of(k * rows, rows), rows)], output)]
    down_rows = p_down.shape[1]

    @pl.loop(0, 4)
    def _(i):
        p_down[i] = dot_tn(mid[:, strip(i, down_rows)], g_dn[...]).astype(BF16)

    s_down = Scatter(me, copies, local, p_down, sc_d)
    s_down.first()
    s_down.second()

    @pl.loop(0, 4)
    def _(i):
        at = strip(i, down_rows)
        g = dot_nt(g_dn[...], wd[i])
        a, b = gate[:, at], up[:, at]
        s = 1.0 / (1.0 + jnp.exp(-a))
        g_gate[:, at] = (g * b * s * (1.0 + a * (1.0 - s))).astype(BF16)
        g_up[:, at] = (g * a * s).astype(BF16)

    @pl.loop(0, 4)
    def _(i):
        at = strip(i, 256)
        send_3[:, at] = (dot_nt(g_gate[...], wg[i]) + dot_nt(g_up[...], wu[i])).astype(BF16)
        crossing(2, i, send_3, recv_3).start()

    for i in range(4):
        crossing(2, i, send_3, recv_3).wait_recv()

    @pl.loop(0, tokens // step)
    def _(i):
        at = strip(i, step)
        g = send_3[at, :].astype(F32) + recv_3[at, :].astype(F32)
        value = x2[at, :]
        r = lax.rsqrt(jnp.mean(value * value, axis=-1, keepdims=True) + EPSILON)
        n = value * r
        gain_sum[0:1, :] += jnp.sum(g * n, axis=0, keepdims=True)
        g = g * gain_row[0:1, :]
        g = g_fin[at, :] + r * (g - n * jnp.mean(g * n, axis=-1, keepdims=True))
        g_fin[at, :] = g
        g_a[at, :] = g.astype(BF16)

    writes.append(local.alone(g_fin.at[pl.ds(pl.multiple_of(k * rows, rows), rows)], g_x2_own))
    go_base = copies.take(4)
    go_sends = []
    for turn in (2, 1, 3, 0):
        to, partner = me.along_z(turn)
        at = strip(to, 256)
        g_ob[:, at] = dot_nt(g_a[...], wo[to]).astype(BF16)
        place = g_out.at[pl.ds(pl.multiple_of(z * tokens, tokens), tokens)]
        if turn:
            go_sends.append(
                pltpu.make_async_remote_copy(
                    src_ref=g_ob.at[:, at], dst_ref=place, send_sem=send.at[go_base + to],
                    recv_sem=recv.at[go_base + z], device_id=partner, device_id_type=MESH,
                )
            )
            go_sends[-1].start()
        else:
            writes.append(local.alone(g_ob.at[:, at], place))
    s_down.relay()

    @pl.loop(0, 4)
    def _(i):
        p_g[i] = dot_tn(h2[:, strip(i, 256)], g_gate[...]).astype(BF16)

    s_gate = Scatter(me, copies, local, p_g, sc_g)
    s_gate.first()
    s_gate.load_fwd()
    writes.append(local.alone(p_g, p_gate))

    @pl.loop(0, 4)
    def _(i):
        p_u[i] = dot_tn(h2[:, strip(i, 256)], g_up[...]).astype(BF16)

    writes.append(local.alone(p_u, p_up))

    @pl.loop(0, 4)
    def _(i):
        p_o[i] = dot_tn(att[:, strip(i, 256)], g_a[...]).astype(BF16)

    writes.append(local.alone(p_o, p_out))
    for j in range(8):
        small[j + 8 : j + 9, :] = 0.5 * gain_sum[0:1, pl.ds(j * 128, 128)]
        small[18:19, :] += 0.5 * loss_row[0:1, pl.ds(j * 128, 128)]
    s_down.finish(sum_d.at[0], sum_d.at[1])
    writes.append(local.alone(sum_d, down_sum))
    s_gate.sum_fwd()
    writes.append(local.alone(sc_g.at[0:2], gate_pass))
    for copy in writes:
        copy.wait()
    for turn in (1, 2, 3):
        other, partner = me.along_z(turn)
        place = g_out.at[pl.ds(pl.multiple_of(other * tokens, tokens), tokens)]
        pltpu.make_async_remote_copy(
            src_ref=place, dst_ref=place, send_sem=send.at[go_base + other],
            recv_sem=recv.at[go_base + other], device_id=partner, device_id_type=MESH,
        ).wait_recv()
    for copy in go_sends:
        copy.wait_send()
    for which, src, dst in ((0, send_1, recv_1), (1, send_2, recv_2), (2, send_3, recv_3)):
        for i in range(4):
            crossing(which, i, src, dst).wait_send()
    s_down.drain()
    s_gate.d_x.wait_send()
    s_gate.d_y.wait_send()


def middle(att, wo, wg, wu, wd, x, t, misc_all, gains_all, count, loss_scale):
    tokens, width = att.shape
    rows = tokens // 2
    hidden = wg.shape[2]

    def bf(*dims):
        return pltpu.VMEM(dims, BF16)

    def held(a):
        return pltpu.VMEM(a.shape, a.dtype)

    def wide(*dims):
        return pltpu.VMEM(dims, F32)

    p_down, p_gate, p_out = (4, hidden // 4, width), (4, width // 4, hidden), (4, width // 4, width)
    return transfer(
        partial(kernel_middle, loss_scale=loss_scale), "middle", 3,
        (att, wo, wg, wu, wd, x.reshape(tokens, width), t.reshape(tokens, width), misc_all, gains_all, count),
        [HBM] * 7 + [VM] * 3,
        [
            shape((rows, width), BF16), shape((4 * tokens, width // 4), BF16),
            shape(p_gate, BF16), shape(p_gate, BF16), shape(p_out, BF16),
            shape((2, hidden // 8, width), BF16), shape((2, width // 8, hidden), BF16),
            shape((rows, width), F32), shape((24, 128), F32),
        ],
        [HBM] * 8 + [VM],
        [held(a) for a in (att, wo, wg, wu, wd)]
        + [bf(tokens, width)] * 2
        + [wide(tokens, width), bf(tokens, width), wide(tokens, hidden), wide(tokens, hidden)]
        + [bf(tokens, hidden)] * 3
        + [bf(tokens, width), wide(tokens, width), bf(tokens, width), bf(tokens, width)]
        + [bf(tokens, width)] * 6
        + [bf(*p_down), bf(*p_gate), bf(*p_gate), bf(*p_out), bf(tokens, width)]
        + [bf(10, hidden // 8, width), bf(2, hidden // 8, width), bf(10, width // 8, hidden)]
        + [wide(8, width), wide(tokens, 128), wide(8, width), wide(8, width)],
        12 + 6 + 4 + 6, 7 + 9 + 4 + 2,
    )


def head_back(g, u, cosine, sine, gain):
    g = g * cosine + half_turn(g * sine)
    r = head_norm(u)
    n = u * r
    g_gain = jnp.sum(g * n, axis=0, keepdims=True)
    g = g * gain
    return r * (g - n * jnp.mean(g * n, axis=-1, keepdims=True)), g_gain


def kernel_backward(
    g_o, gate_pass, down_sum, p_gate, p_up, p_out,
    qkv_in, att_in, lse_in, proj_in, cos_in, sin_in, h_in, w_in,
    x, g_x2, gains_all, small,
    down_tot, gate_tot, up_tot, out_tot, head_tot, grad_in, small_tot,
    g_out, qkv, att, lse, proj, cosines, sines, h_all, w_head, g_proj, g_k, g_v, p_head,
    gh_send, gh_sib, gh_own, gh_in, gain_row, work, plane, pair, line,
    sc_g, sc_u, sc_o, sc_h, own_d, own_g, own_u, own_o, line_d, line_g, line_u, line_o,
    send, recv, lsem,
):
    me = Place()
    z, k, f, c = me.z, me.k, me.f, me.c
    rows = x.shape[0]
    block = 2 * rows
    greet([me.xp, me.yp, me.dp, me.sib] + [me.along_z(step)[1] for step in (1, 2, 3)])
    copies, local = Copies(send, recv), Locals(lsem)
    size, q_size = HEAD_SIZE, GROUP * HEAD_SIZE

    for src, dst in ((g_o, g_out), (qkv_in, qkv), (att_in, att), (lse_in, lse), (proj_in, proj), (cos_in, cosines), (sin_in, sines)):
        local(src, dst)
    late = [local.alone(w_in, w_head)]
    h_base = local.take(4)

    def h_load(i):
        columns = pl.ds(pl.multiple_of(i * rows, rows), rows)
        return pltpu.make_async_copy(h_in.at[:, columns], h_all.at[i % 2], lsem.at[h_base + i])

    h_load(0).start()
    h_load(1).start()
    s_gate = Scatter(me, copies, local, p_gate, sc_g)
    s_up = Scatter(me, copies, local, p_up, sc_u)
    s_out = Scatter(me, copies, local, p_out, sc_o)
    s_head = Scatter(me, copies, local, p_head, sc_h)
    s_gate.resume(gate_pass)
    own_down = local.alone(down_sum, own_d)
    lines = [
        LineSum(me, copies, own, bufs)
        for own, bufs in ((own_d, line_d), (own_g, line_g), (own_u, line_u), (own_o, line_o))
    ]
    l_down, l_gate, l_up, l_out = lines
    totals = (down_tot, gate_tot, up_tot, out_tot)
    swap_base = copies.take(8)
    swaps, writes = [], []

    def finish(i):
        lines[i].arrive()
        half = lines[i].total.shape[1]
        for j in range(2):
            dst = totals[i].at[k, pl.ds(j * half, half)]
            copy = copies.at(swap_base + 2 * i + j, lines[i].total.at[j], dst, me.sib)
            copy.start()
            swaps.append(copy)
            writes.append(local.alone(lines[i].total.at[j], dst))

    def scattered(scatter, entry, own):
        scatter.finish(own.at[0], own.at[1])
        entry.start()

    own_down.wait()
    l_down.start()
    work[...] = small[...]
    for i in range(4):
        for r in range(2):
            gain_row[0:1, pl.ds((2 * i + r) * 128, 128)] = gains_all[i, r : r + 1, :]
    gain_q = (gains_all[0, 4:5, :] + gains_all[1, 4:5, :]) + (gains_all[2, 4:5, :] + gains_all[3, 4:5, :])
    gain_k = (gains_all[0, 5:6, :] + gains_all[1, 5:6, :]) + (gains_all[2, 5:6, :] + gains_all[3, 5:6, :])
    k_at = pl.ds(q_size, size)
    v_at = pl.ds(q_size + size, size)
    g_k[...] = jnp.zeros_like(g_k)
    g_v[...] = jnp.zeros_like(g_v)
    key = lax.broadcasted_iota(jnp.int32, (block, block), 0)
    query = lax.broadcasted_iota(jnp.int32, (block, block), 1)
    def queries(i):
        at = pl.ds(pl.multiple_of(i * block, block), block)
        for g in range(GROUP):
            head = pl.ds(g * size, size)
            q = qkv[at, head]
            go = g_out[at, head]
            product = go.astype(F32) * att[at, head].astype(F32)
            delta = dot_nt(jnp.ones((8, size), F32), product, precision=HIGHEST)[0:1, :]
            log_sum = lse[g, 0:1, at] * LOG2_E

            def part(keys, masked, q=q, go=go, delta=delta, log_sum=log_sum):
                kk, vv = qkv[keys, k_at], qkv[keys, v_at]
                p = jnp.exp2(dot_nt(kk, q) * (SCALE * LOG2_E) - log_sum)
                if masked:
                    p = jnp.where(key <= query, p, 0.0)
                gs = (p * (dot_nt(vv, go) - delta)).astype(BF16)
                g_v[keys, :] += dot_nn(p.astype(BF16), go)
                g_k[keys, :] += dot_nn(gs, q)
                return dot_tn(gs, kk)

            def step(j, acc, part=part):
                return acc + part(pl.ds(pl.multiple_of(j * block, block), block), False)

            acc = lax.fori_loop(0, i, step, jnp.zeros((block, size), F32))
            acc = (acc + part(at, True)) * SCALE
            g_u, g_gain = head_back(acc, proj[at, head], cosines[at, :], sines[at, :], gain_q)
            g_proj[at, head] = g_u.astype(BF16)
            work[16:17, :] += g_gain

    sib_base, right_base, left_base = copies.take(4), copies.take(4), copies.take(4)
    last = (z == 0) | (z == 3)
    inner = (z == 1) | (z == 2)

    def input_part(to, mine, dst):
        at = pl.ds(pl.multiple_of((2 * to + mine) * rows, rows), rows)
        weights = w_head[...].reshape(w_head.shape[0] * w_head.shape[1], w_head.shape[2])
        dst[...] = dot_nt(g_proj[at, :], weights).astype(BF16)

    def crossing(to):
        return copies.at(sib_base + to, gh_send.at[to], gh_sib.at[to], me.sib)

    def rightward(to):
        return copies.at(right_base + to, gh_own.at[to], gh_in.at[to], (f, c + 2))

    def leftward(to):
        there = 1 - (z - to) // 2
        place = gh_in.at[to + (4 - to) * there]
        return copies.at(left_base + to, gh_own.at[to], place, (f, c - 2))

    def onward(to):
        @pl.when(to > z)
        def _():
            rightward(to).start()

        @pl.when(to < z)
        def _():
            leftward(to).start()

    def join(to):
        crossing(to).wait_recv()
        add_rows(gh_own.at[to], [gh_own.at[to], gh_sib.at[to]])

    def end_send(order):
        @pl.when(last)
        def _():
            onward(far_first(order))

    def inner_send(order):
        @pl.when(inner)
        def _():
            to = far_first(order)

            @pl.when(to > z)
            def _():
                rightward(to).wait_recv()

            @pl.when(to < z)
            def _():
                copies.at(left_base + to, gh_own.at[to], gh_in.at[to], (f, c - 2)).wait_recv()

            add_rows(gh_own.at[to], [gh_own.at[to], gh_in.at[to]])
            onward(to)

    def far_first(order):
        return order + (3 - 2 * order) * (z // 2)

    def parts_to(to):
        input_part(to, 1 - k, gh_send.at[to])
        crossing(to).start()
        input_part(to, k, gh_own.at[to])

    spread = Spread(me, copies, head_tot)
    total = SmallSum(me, copies, work, plane, pair, line)
    local.wait()
    s_up.first()
    s_up.second()
    queries(2)
    l_down.meet()
    queries(0)
    queries(1)
    s_gate.finish_resumed(own_g.at[0], own_g.at[1])
    l_gate.start()
    l_down.close()
    queries(3)
    s_up.relay()
    for copy in late:
        copy.wait()
    l_down.spread()
    l_gate.meet()

    @pl.loop(0, 4)
    def _(i):
        at = pl.ds(pl.multiple_of(i * block, block), block)
        g_u, g_gain = head_back(g_k[at, :] * SCALE, proj[at, k_at], cosines[at, :], sines[at, :], gain_k)
        g_proj[at, k_at] = g_u.astype(BF16)
        g_proj[at, v_at] = g_v[at, :].astype(BF16)
        work[17:18, :] += g_gain

    parts_to(far_first(0))
    parts_to(far_first(3))
    l_gate.close()
    parts_to(far_first(1))
    parts_to(far_first(2))
    join(far_first(3))
    end_send(3)
    finish(0)
    inner_send(3)
    join(far_first(0))
    l_gate.spread()
    join(far_first(2))
    s_out.first()
    s_out.second()
    scattered(s_up, l_up, own_u)
    join(far_first(1))

    @pl.loop(0, 4)
    def _(i):
        h_load(i).wait()
        p_head[i] = dot_tn(h_all[i % 2], g_proj[...]).astype(BF16)

        @pl.when(i < 2)
        def _():
            h_load(i + 2).start()

    inner_send(0)
    s_head.first()
    s_head.second()
    s_out.relay()
    l_up.meet()
    scattered(s_out, l_out, own_o)
    s_head.relay()
    l_up.close()
    l_out.meet()
    l_up.spread()
    s_head.finish(head_tot.at[c, 0], head_tot.at[c, 1])
    spread.start()
    end_send(2)
    finish(2)
    end_send(1)
    l_out.close()
    inner_send(2)
    l_out.spread()
    spread.step(1)
    work[0:8, :] = jnp.zeros((8, 128), F32)

    @pl.when(z > 0)
    def _():
        rightward(z).wait_recv()

    @pl.when(z < 3)
    def _():
        copies.at(left_base + z, gh_own.at[z], gh_in.at[4], (f, c - 2)).wait_recv()

    @pl.when(z == 0)
    def _():
        gh_in[0] = jnp.zeros(gh_in.shape[1:], BF16)

    @pl.when(z == 3)
    def _():
        gh_in[4] = jnp.zeros(gh_in.shape[1:], BF16)

    @pl.loop(0, rows // 64)
    def _(i):
        at = pl.ds(pl.multiple_of(i * 64, 64), 64)
        g = gh_own[z, at, :].astype(F32) + gh_in[z, at, :].astype(F32) + gh_in[4, at, :].astype(F32)
        xin = x[at, :].astype(F32)
        r = lax.rsqrt(jnp.mean(xin * xin, axis=-1, keepdims=True) + EPSILON)
        n = xin * r
        g_gain = jnp.sum(g * n, axis=0, keepdims=True)
        for j in range(8):
            work[j : j + 1, :] += g_gain[:, j * 128 : (j + 1) * 128]
        g = g * gain_row[0:1, :]
        grad_in[at, :] = g_x2[at, :] + r * (g - n * jnp.mean(g * n, axis=-1, keepdims=True))


    total.first()
    finish(3)
    finish(1)
    total.second()
    spread.step(2)
    total.third()
    spread.step(3)
    total.finish(small_tot)
    for hop in range(4):
        spread.crossed(hop)
    for i in range(4):
        crossing(i).wait_send()

        @pl.when(i > z)
        def _(i=i):
            rightward(i).wait_send()

        @pl.when(i < z)
        def _(i=i):
            leftward(i).wait_send()

    spread.drain()
    total.drain()
    s_gate.drain_resumed()
    for scatter in (s_up, s_out, s_head):
        scatter.drain()
    for entry in lines:
        entry.drain()
    for copy in swaps:
        copy.wait()
    for copy in writes:
        copy.wait()


def backward(g_o, gate_pass, parts, saved, x, g_x2, gains_all, small):
    rows, width = x.shape
    tokens = 8 * rows
    sizes = [(2 * parts[0].shape[1], width)] + [p.shape[1:] for p in parts[1:]]
    head = (width // 4, HEAD_COLUMNS)

    def held(a):
        return pltpu.VMEM(a.shape, a.dtype)

    pieces = pltpu.VMEM((4, rows, width), BF16)
    scatters = [pltpu.VMEM((10, r // 2, n), BF16) for r, n in sizes[1:] + [head]]
    own = [pltpu.VMEM((2, r // 2, n), BF16) for r, n in sizes]
    line = [pltpu.VMEM((5, r // 2, n), BF16) for r, n in sizes]
    return transfer(
        kernel_backward, "backward", 2,
        (g_o, gate_pass) + tuple(parts) + tuple(saved) + (x, g_x2, gains_all, small),
        [HBM] * 14 + [VM] * 4,
        [shape((2,) + s, BF16) for s in sizes]
        + [
            shape((8, 2, head[0] // 2, head[1]), BF16),
            shape((rows, width), F32),
            shape(small.shape, F32),
        ],
        [HBM] * 4 + [VM] * 3,
        [pltpu.VMEM((tokens, GROUP * HEAD_SIZE), BF16)]
        + [held(a) for a in saved[:6]]
        + [pltpu.VMEM((2, tokens, rows), BF16), held(saved[7])]
        + [
            pltpu.VMEM((tokens, HEAD_COLUMNS), BF16),
            pltpu.VMEM((tokens, HEAD_SIZE), F32),
            pltpu.VMEM((tokens, HEAD_SIZE), F32),
            pltpu.VMEM((4,) + head, BF16),
            pieces, pieces, pieces, pltpu.VMEM((5, rows, width), BF16),
            pltpu.VMEM((8, width), F32),
            pltpu.VMEM(small.shape, F32),
            pltpu.VMEM((4,) + small.shape, F32),
            pltpu.VMEM((2,) + small.shape, F32),
            pltpu.VMEM((4,) + small.shape, F32),
        ]
        + scatters + own + line,
        24 + 32 + 8 + 12 + 7 + 13, 7 + 4 + 1 + 1 + 16 + 8 + 2,
    )


def chip_step(
    hidden_in, teacher, valid, positions, norm_attn, w_query, key_projection, value_projection,
    gain_query, gain_key, w_out, norm_mlp, w_gate, w_up, w_down,
):
    rows = hidden_in.shape[1]
    width = hidden_in.shape[2]
    norms = jnp.concatenate([norm_attn.reshape(-1, 128), norm_mlp.reshape(-1, 128)]).astype(F32)
    gain_heads = jnp.stack([gain_query, gain_key]).astype(F32)
    half_width = HEAD_SIZE // 2
    freq = 1000000.0 ** (-2.0 * np.arange(half_width) / HEAD_SIZE)
    freq = np.broadcast_to(np.concatenate([freq, freq]), (8, HEAD_SIZE)).astype(np.float32)
    (
        x_pair, t_pair, misc_all, gains_all, count, w_head, wo, wg, wu, wd,
        h_all, proj, qkv, att, lse, cosines, sines, att_all,
    ) = forward(
        w_query, key_projection, value_projection, w_out, w_gate, w_up, w_down,
        hidden_in[0], teacher[0], positions, valid, norms, gain_heads, freq,
    )
    loss_scale = rows * lax.axis_size("ctx") * lax.axis_size("fsdp") / 4.0
    output, g_o, p_gate, p_up, p_out, s_down, gate_pass, g_x2, small = middle(
        att_all, wo, wg, wu, wd, x_pair, t_pair, misc_all, gains_all, count, loss_scale
    )
    down, gate, up, out, heads, grad_input, small = backward(
        g_o, gate_pass, (s_down, p_gate, p_up, p_out),
        (qkv, att, lse, proj, cosines, sines, h_all, w_head),
        hidden_in[0], g_x2, gains_all, small,
    )

    g_gate, g_up, g_q, g_k, g_v, g_down, g_out, g_norms, g_gains, loss, output, grad_input = assemble(
        gate, up, heads.reshape(8, -1, HEAD_COLUMNS), down, out, small, count, output, grad_input
    )
    return (
        output[None],
        loss.reshape(()),
        grad_input[None],
        g_norms[0].reshape(-1),
        g_q,
        g_k,
        g_v,
        g_gains[0],
        g_gains[1],
        g_out.reshape(-1, width),
        g_norms[1].reshape(-1),
        g_gate,
        g_up,
        g_down.reshape(-1, width),
    )


def solution(mesh):
    chips = mesh.shape["fsdp"] == 4 and mesh.shape["ctx"] == KEY_VALUE_HEADS
    return jax.shard_map(
        chip_step if chips else per_device,
        mesh=mesh,
        in_specs=(
            P("fsdp", "ctx", None),
            P("fsdp", "ctx", None),
            P("fsdp", "ctx"),
            P("fsdp", "ctx"),
            P("fsdp"),
            P("fsdp", None),
            P("fsdp", None),
            P("fsdp", None),
            P("fsdp"),
            P("fsdp"),
            P("fsdp", None),
            P("fsdp"),
            P("fsdp", None),
            P("fsdp", None),
            P("fsdp", None),
        ),
        out_specs=(
            P("fsdp", "ctx", None),
            P(),
            P("fsdp", "ctx", None),
            P("fsdp"),
            P("fsdp", None),
            P("fsdp", None),
            P("fsdp", None),
            P("fsdp"),
            P("fsdp"),
            P("fsdp", None),
            P("fsdp"),
            P("fsdp", None),
            P("fsdp", None),
            P("fsdp", None),
        ),
        check_vma=False,
    )
```

```python
from functools import partial
import math

import jax
import jax.numpy as jnp
import numpy as np
from jax import lax
from jax.experimental import pallas as pl
from jax.experimental.pallas import tpu as pltpu
from jax.sharding import PartitionSpec as P

QUERY_HEADS = 16
KEY_VALUE_HEADS = 8
HEAD_SIZE = 128


EPSILON = 1e-06


def root_mean_norm(values, norm_gain):
    return (
        values * lax.rsqrt(jnp.mean(values * values, axis=-1, keepdims=True) + EPSILON) * norm_gain
    )


def rope_tables(position_ids):
    half_width = HEAD_SIZE // 2
    freq_table = jnp.exp(
        jnp.arange(half_width, dtype=jnp.float32) * (-2.0 * math.log(1000000.0) / HEAD_SIZE)
    )
    angle_table = position_ids.astype(jnp.float32)[:, None] * freq_table[None, :]
    cosine_table = jnp.cos(angle_table)
    sine_table = jnp.sin(angle_table)
    return (
        jnp.concatenate([cosine_table, cosine_table], -1),
        jnp.concatenate([-sine_table, sine_table], -1),
    )


def apply_rotary(values, cosine_table, sine_table):
    half_width = HEAD_SIZE // 2
    swapped = jnp.concatenate([values[..., half_width:], values[..., :half_width]], -1)
    return values * cosine_table[:, None, :] + swapped * sine_table[:, None, :]


def shape_heads(cosine_table, sine_table, proj_query, projected_key, gain_q, key_gain):
    token_rows = proj_query.shape[0]
    query_rows = apply_rotary(
        root_mean_norm(proj_query.reshape(token_rows, QUERY_HEADS, HEAD_SIZE), gain_q),
        cosine_table,
        sine_table,
    )
    rows_of_keys = apply_rotary(
        root_mean_norm(projected_key.reshape(token_rows, KEY_VALUE_HEADS, HEAD_SIZE), key_gain),
        cosine_table,
        sine_table,
    )
    return (query_rows, rows_of_keys)


def swiglu(gate_proj, up_proj):
    return gate_proj / (1.0 + jnp.exp(-gate_proj)) * up_proj


def contract_rows(left_arr, right_arr):
    return lax.dot_general(
        left_arr, right_arr, (((0,), (0,)), ((), ())), preferred_element_type=jnp.float32
    )


def against(left_arr, right_arr):
    return lax.dot_general(
        left_arr, right_arr, (((1,), (1,)), ((), ())), preferred_element_type=jnp.float32
    )


def in_blocks(block_step, running, shard_portion):
    total_rows = shard_portion.shape[0]
    block_extent = 512
    block_count = total_rows // block_extent
    blocks = shard_portion.reshape((block_count, block_extent) + shard_portion.shape[1:])
    starts = jnp.arange(block_count, dtype=jnp.int32) * block_extent

    def scan_body(state, scan_item):
        return (block_step(state, scan_item[0], scan_item[1]), None)

    running, unused = lax.scan(scan_body, running, (blocks, starts))
    return running


def score_terms(
    query_rows,
    output_gradients,
    lse_heads,
    delta_heads,
    rows_of_keys,
    rows_of_values,
    query_index,
    key_index,
    score_scale,
):
    score_matrix = (
        jnp.einsum("alci,wli->lcaw", query_rows, rows_of_keys, preferred_element_type=jnp.float32)
        * score_scale
    )
    allowed = key_index[None, :] <= query_index[:, None]
    attention_probabilities = jnp.where(allowed, jnp.exp(score_matrix - lse_heads[..., None]), 0.0)
    grad_probs = jnp.einsum(
        "alci,wli->lcaw", output_gradients, rows_of_values, preferred_element_type=jnp.float32
    )
    score_gradient = (
        score_scale * attention_probabilities * (grad_probs - delta_heads[..., None])
    ).astype(jnp.bfloat16)
    return (attention_probabilities, score_gradient)


def per_device(
    hidden_in,
    teacher,
    valid,
    positions,
    norm_attn,
    w_query,
    key_projection,
    value_projection,
    gain_query,
    gain_key,
    w_out,
    norm_mlp,
    w_gate,
    w_up,
    w_down,
):
    gathered = (
        lax.all_gather(norm_attn, "fsdp", axis=0, tiled=True),
        lax.all_gather(w_query, "fsdp", axis=0, tiled=True),
        lax.all_gather(key_projection, "fsdp", axis=0, tiled=True),
        lax.all_gather(value_projection, "fsdp", axis=0, tiled=True),
        lax.all_gather(gain_query, "fsdp", axis=0, tiled=True),
        lax.all_gather(gain_key, "fsdp", axis=0, tiled=True),
        lax.all_gather(w_out, "fsdp", axis=0, tiled=True),
        lax.all_gather(norm_mlp, "fsdp", axis=0, tiled=True),
        lax.all_gather(w_gate, "fsdp", axis=0, tiled=True),
        lax.all_gather(w_up, "fsdp", axis=0, tiled=True),
        lax.all_gather(w_down, "fsdp", axis=0, tiled=True),
    )
    (
        full_norm_attn,
        full_query,
        full_key,
        full_value,
        full_gain_q,
        full_gain_k,
        full_out,
        full_norm_mlp,
        full_gate,
        full_up,
        full_down,
    ) = gathered
    grouped_heads = QUERY_HEADS // KEY_VALUE_HEADS
    score_scale = 1.0 / math.sqrt(HEAD_SIZE)
    residual = hidden_in[0].astype(jnp.float32)
    token_rows = residual.shape[0]
    query_index = lax.axis_index("ctx") * token_rows + jnp.arange(token_rows, dtype=jnp.int32)
    normed_one, norm_one_back = jax.vjp(
        root_mean_norm, residual, full_norm_attn.astype(jnp.float32)
    )
    hidden_one = normed_one.astype(jnp.bfloat16)
    proj_query = jnp.dot(hidden_one, full_query, preferred_element_type=jnp.float32)
    projected_key = jnp.dot(hidden_one, full_key, preferred_element_type=jnp.float32)
    projected_value = jnp.dot(hidden_one, full_value, preferred_element_type=jnp.float32)
    cosine_table, sine_table = rope_tables(positions[0])
    (query_per_head, heads_key), heads_back = jax.vjp(
        partial(shape_heads, cosine_table, sine_table),
        proj_query,
        projected_key,
        full_gain_q.astype(jnp.float32),
        full_gain_k.astype(jnp.float32),
    )
    query_reduced = query_per_head.astype(jnp.bfloat16).reshape(
        token_rows, KEY_VALUE_HEADS, grouped_heads, HEAD_SIZE
    )
    key_reduced = heads_key.astype(jnp.bfloat16)
    value_reduced = projected_value.astype(jnp.bfloat16).reshape(
        token_rows, KEY_VALUE_HEADS, HEAD_SIZE
    )
    key_value = jnp.stack(
        [
            key_reduced.reshape(token_rows, KEY_VALUE_HEADS * HEAD_SIZE),
            value_reduced.reshape(token_rows, KEY_VALUE_HEADS * HEAD_SIZE),
        ],
        axis=1,
    )

    def forward_block(running, shard_portion, first_row):
        run_max, run_total, run_acc = running
        rows_per_block = shard_portion.shape[0]
        rows_of_keys = shard_portion[:, 0].reshape(rows_per_block, KEY_VALUE_HEADS, HEAD_SIZE)
        rows_of_values = shard_portion[:, 1].reshape(rows_per_block, KEY_VALUE_HEADS, HEAD_SIZE)
        key_index = first_row + jnp.arange(rows_per_block, dtype=jnp.int32)
        allowed = key_index[None, :] <= query_index[:, None]
        score_matrix = (
            jnp.einsum(
                "alci,wli->lcaw", query_reduced, rows_of_keys, preferred_element_type=jnp.float32
            )
            * score_scale
        )
        score_matrix = jnp.where(allowed, score_matrix, -1e30)
        new_max = jnp.maximum(run_max, jnp.max(score_matrix, axis=-1))
        weights_part = jnp.where(allowed, jnp.exp(score_matrix - new_max[..., None]), 0.0)
        factor = jnp.exp(run_max - new_max)
        run_total = run_total * factor + jnp.sum(weights_part, axis=-1)
        run_acc = run_acc * factor[..., None] + jnp.einsum(
            "exfw,weq->exfq",
            weights_part.astype(jnp.bfloat16),
            rows_of_values,
            preferred_element_type=jnp.float32,
        )
        return (new_max, run_total, run_acc)

    start_state = (
        jnp.full((KEY_VALUE_HEADS, grouped_heads, token_rows), -1e30, jnp.float32),
        jnp.zeros((KEY_VALUE_HEADS, grouped_heads, token_rows), jnp.float32),
        jnp.zeros((KEY_VALUE_HEADS, grouped_heads, token_rows, HEAD_SIZE), jnp.float32),
    )
    run_max, run_total, run_acc = in_blocks(
        forward_block, start_state, lax.all_gather(key_value, "ctx", axis=0, tiled=True)
    )
    log_total = run_max + jnp.log(run_total)
    attn_rows = jnp.transpose(run_acc / run_total[..., None], (2, 0, 1, 3))
    attn_low = attn_rows.reshape(token_rows, QUERY_HEADS * HEAD_SIZE).astype(jnp.bfloat16)
    mid_resid = residual + jnp.dot(attn_low, full_out, preferred_element_type=jnp.float32)
    normed_two, norm_two_back = jax.vjp(
        root_mean_norm, mid_resid, full_norm_mlp.astype(jnp.float32)
    )
    hidden_two = normed_two.astype(jnp.bfloat16)
    gate_proj = jnp.dot(hidden_two, full_gate, preferred_element_type=jnp.float32)
    up_proj = jnp.dot(hidden_two, full_up, preferred_element_type=jnp.float32)
    gated, gated_back = jax.vjp(swiglu, gate_proj, up_proj)
    gated_low = gated.astype(jnp.bfloat16)
    final_rows = mid_resid + jnp.dot(gated_low, full_down, preferred_element_type=jnp.float32)
    target = teacher[0].astype(jnp.float32)
    weight_rows = valid[0].astype(jnp.float32)
    mismatch = final_rows - target
    sq_local = jnp.sum(weight_rows[:, None] * mismatch * mismatch)
    count_local = jnp.sum(weight_rows)
    sq_total, count_total = lax.psum((sq_local, count_local), ("fsdp", "ctx"))
    loss_value = sq_total / count_total
    loss_scale = token_rows * lax.axis_size("ctx") * lax.axis_size("fsdp") / 4.0
    grad_final = 2.0 * loss_scale / count_total * weight_rows[:, None] * mismatch
    grad_down_in = grad_final.astype(jnp.bfloat16)
    grad_w_down = contract_rows(gated_low, grad_down_in)
    grad_gated = against(grad_down_in, full_down)
    grad_gate_proj, grad_up_proj = gated_back(grad_gated)
    gate_low = grad_gate_proj.astype(jnp.bfloat16)
    up_low = grad_up_proj.astype(jnp.bfloat16)
    grad_w_gate = contract_rows(hidden_two, gate_low)
    grad_w_up = contract_rows(hidden_two, up_low)
    grad_hidden_two = against(gate_low, full_gate) + against(up_low, full_up)
    grad_mid_norm, grad_norm_mlp = norm_two_back(grad_hidden_two)
    grad_mid = grad_final + grad_mid_norm
    grad_branch = grad_mid.astype(jnp.bfloat16)
    grad_w_out = contract_rows(attn_low, grad_branch)
    attention_gradient = against(grad_branch, full_out).astype(jnp.bfloat16)
    attention_head_gradient = attention_gradient.reshape(
        token_rows, KEY_VALUE_HEADS, grouped_heads, HEAD_SIZE
    )
    row_delta = jnp.sum(attention_head_gradient.astype(jnp.float32) * attn_rows, axis=-1)
    delta_heads = jnp.transpose(row_delta, (1, 2, 0))
    row_stats = jnp.stack(
        [
            jnp.transpose(log_total, (2, 0, 1)).reshape(token_rows, QUERY_HEADS),
            row_delta.reshape(token_rows, QUERY_HEADS),
        ],
        axis=1,
    )

    def block_of_queries(grad_query, shard_portion, first_row):
        rows_per_block = shard_portion.shape[0]
        rows_of_keys = shard_portion[:, 0].reshape(rows_per_block, KEY_VALUE_HEADS, HEAD_SIZE)
        rows_of_values = shard_portion[:, 1].reshape(rows_per_block, KEY_VALUE_HEADS, HEAD_SIZE)
        key_index = first_row + jnp.arange(rows_per_block, dtype=jnp.int32)
        attention_probabilities, score_gradient = score_terms(
            query_reduced,
            attention_head_gradient,
            log_total,
            delta_heads,
            rows_of_keys,
            rows_of_values,
            query_index,
            key_index,
            score_scale,
        )
        return grad_query + jnp.einsum(
            "jyux,xji->ujyi", score_gradient, rows_of_keys, preferred_element_type=jnp.float32
        )

    grad_query = in_blocks(
        block_of_queries,
        jnp.zeros((token_rows, KEY_VALUE_HEADS, grouped_heads, HEAD_SIZE), jnp.float32),
        lax.all_gather(key_value, "ctx", axis=0, tiled=True),
    )
    all_stats = lax.all_gather(row_stats.astype(jnp.bfloat16), "ctx", axis=0, tiled=True).astype(
        row_stats.dtype
    )
    query_pair = jnp.stack(
        [query_reduced.reshape(token_rows, QUERY_HEADS * HEAD_SIZE), attention_gradient], axis=1
    )

    def key_block(running, shard_portion, first_row):
        grad_key, value_gradient = running
        rows_per_block = shard_portion.shape[0]
        query_rows = shard_portion[:, 0].reshape(
            rows_per_block, KEY_VALUE_HEADS, grouped_heads, HEAD_SIZE
        )
        output_gradients = shard_portion[:, 1].reshape(
            rows_per_block, KEY_VALUE_HEADS, grouped_heads, HEAD_SIZE
        )
        partial_statistics = lax.dynamic_slice_in_dim(all_stats, first_row, rows_per_block, 0)
        partial_logsumexp = jnp.transpose(
            partial_statistics[:, 0].reshape(rows_per_block, KEY_VALUE_HEADS, grouped_heads),
            (1, 2, 0),
        )
        partial_delta = jnp.transpose(
            partial_statistics[:, 1].reshape(rows_per_block, KEY_VALUE_HEADS, grouped_heads),
            (1, 2, 0),
        )
        part_index = first_row + jnp.arange(rows_per_block, dtype=jnp.int32)
        attention_probabilities, score_gradient = score_terms(
            query_rows,
            output_gradients,
            partial_logsumexp,
            partial_delta,
            key_reduced,
            value_reduced,
            part_index,
            query_index,
            score_scale,
        )
        grad_key = grad_key + jnp.einsum(
            "wzlj,lwzy->jwy", score_gradient, query_rows, preferred_element_type=jnp.float32
        )
        value_gradient = value_gradient + jnp.einsum(
            "wzlj,lwzy->jwy",
            attention_probabilities.astype(jnp.bfloat16),
            output_gradients,
            preferred_element_type=jnp.float32,
        )
        return (grad_key, value_gradient)

    key_state = (
        jnp.zeros((token_rows, KEY_VALUE_HEADS, HEAD_SIZE), jnp.float32),
        jnp.zeros((token_rows, KEY_VALUE_HEADS, HEAD_SIZE), jnp.float32),
    )
    grad_key, value_gradient = in_blocks(
        key_block, key_state, lax.all_gather(query_pair, "ctx", axis=0, tiled=True)
    )
    grad_proj_q, grad_proj_k, grad_gain_q, grad_gain_k = heads_back(
        (grad_query.reshape(token_rows, QUERY_HEADS, HEAD_SIZE), grad_key)
    )
    query_grad_low = grad_proj_q.astype(jnp.bfloat16)
    key_grad_low = grad_proj_k.astype(jnp.bfloat16)
    value_gradient_reduced = value_gradient.reshape(token_rows, KEY_VALUE_HEADS * HEAD_SIZE).astype(
        jnp.bfloat16
    )
    grad_w_query = contract_rows(hidden_one, query_grad_low)
    grad_w_key = contract_rows(hidden_one, key_grad_low)
    grad_w_value = contract_rows(hidden_one, value_gradient_reduced)
    grad_hidden_one = (
        against(query_grad_low, full_query)
        + against(key_grad_low, full_key)
        + against(value_gradient_reduced, full_value)
    )
    grad_resid_norm, grad_norm_attn = norm_one_back(grad_hidden_one)
    grad_input = grad_mid + grad_resid_norm
    grads = (
        grad_norm_attn,
        grad_w_query,
        grad_w_key,
        grad_w_value,
        grad_gain_q,
        grad_gain_k,
        grad_w_out,
        grad_norm_mlp,
        grad_w_gate,
        grad_w_up,
        grad_w_down,
    )
    shares = (
        lax.psum_scatter(grads[0], ("fsdp", "ctx"), scatter_dimension=0, tiled=True),
        lax.psum_scatter(grads[1], ("fsdp", "ctx"), scatter_dimension=0, tiled=True),
        lax.psum_scatter(grads[2], ("fsdp", "ctx"), scatter_dimension=0, tiled=True),
        lax.psum_scatter(grads[3], ("fsdp", "ctx"), scatter_dimension=0, tiled=True),
        lax.psum_scatter(grads[4], ("fsdp", "ctx"), scatter_dimension=0, tiled=True),
        lax.psum_scatter(grads[5], ("fsdp", "ctx"), scatter_dimension=0, tiled=True),
        lax.psum_scatter(grads[6], ("fsdp", "ctx"), scatter_dimension=0, tiled=True),
        lax.psum_scatter(grads[7], ("fsdp", "ctx"), scatter_dimension=0, tiled=True),
        lax.psum_scatter(grads[8], ("fsdp", "ctx"), scatter_dimension=0, tiled=True),
        lax.psum_scatter(grads[9], ("fsdp", "ctx"), scatter_dimension=0, tiled=True),
        lax.psum_scatter(grads[10], ("fsdp", "ctx"), scatter_dimension=0, tiled=True),
    )
    shares = (
        lax.all_gather(shares[0].astype(jnp.bfloat16), "ctx", axis=0, tiled=True).astype(
            jnp.float32
        ),
        lax.all_gather(shares[1].astype(jnp.bfloat16), "ctx", axis=0, tiled=True).astype(
            jnp.float32
        ),
        lax.all_gather(shares[2].astype(jnp.bfloat16), "ctx", axis=0, tiled=True).astype(
            jnp.float32
        ),
        lax.all_gather(shares[3].astype(jnp.bfloat16), "ctx", axis=0, tiled=True).astype(
            jnp.float32
        ),
        lax.all_gather(shares[4].astype(jnp.bfloat16), "ctx", axis=0, tiled=True).astype(
            jnp.float32
        ),
        lax.all_gather(shares[5].astype(jnp.bfloat16), "ctx", axis=0, tiled=True).astype(
            jnp.float32
        ),
        lax.all_gather(shares[6].astype(jnp.bfloat16), "ctx", axis=0, tiled=True).astype(
            jnp.float32
        ),
        lax.all_gather(shares[7].astype(jnp.bfloat16), "ctx", axis=0, tiled=True).astype(
            jnp.float32
        ),
        lax.all_gather(shares[8].astype(jnp.bfloat16), "ctx", axis=0, tiled=True).astype(
            jnp.float32
        ),
        lax.all_gather(shares[9].astype(jnp.bfloat16), "ctx", axis=0, tiled=True).astype(
            jnp.float32
        ),
        lax.all_gather(shares[10].astype(jnp.bfloat16), "ctx", axis=0, tiled=True).astype(
            jnp.float32
        ),
    )
    return (
        final_rows.astype(jnp.bfloat16)[None],
        loss_value,
        grad_input[None],
        shares[0],
        shares[1],
        shares[2],
        shares[3],
        shares[4],
        shares[5],
        shares[6],
        shares[7],
        shares[8],
        shares[9],
        shares[10],
    )


MESH = pl.DeviceIdType.MESH
BF16 = jnp.bfloat16
F32 = jnp.float32
GROUP = QUERY_HEADS // KEY_VALUE_HEADS
HEAD_COLUMNS = (GROUP + 2) * HEAD_SIZE
SCALE = 1.0 / math.sqrt(HEAD_SIZE)
LOG2_E = 1.0 / math.log(2.0)
VMEM_LIMIT = 60 * 1024 * 1024


class Place:
    def __init__(self):
        self.f = lax.axis_index("fsdp")
        self.c = lax.axis_index("ctx")
        self.z = self.c // 2
        self.k = self.c % 2
        self.fx = self.f + 1 - 2 * (self.f % 2)
        self.fy = (self.f + 2) % 4
        self.fd = 3 - self.f
        self.xp = (self.fx, self.c)
        self.yp = (self.fy, self.c)
        self.dp = (self.fd, self.c)
        self.sib = (self.f, self.c + 1 - 2 * self.k)

    def along_z(self, step):
        other = (self.z + step) % 4
        return other, (self.f, 2 * other + self.k)

    def along_ctx(self, step):
        other = (self.c + step) % 8
        return other, (self.f, other)


def greet(partners):
    barrier = pltpu.get_barrier_semaphore()
    for partner in partners:
        pl.semaphore_signal(barrier, inc=1, device_id=partner, device_id_type=MESH)
    pl.semaphore_wait(barrier, len(partners))


class Copies:
    def __init__(self, send, recv):
        self.send, self.recv, self.used = send, recv, 0

    def take(self, count):
        first = self.used
        self.used += count
        return first

    def at(self, index, src, dst, partner):
        return pltpu.make_async_remote_copy(
            src_ref=src,
            dst_ref=dst,
            send_sem=self.send.at[index],
            recv_sem=self.recv.at[index],
            device_id=partner,
            device_id_type=MESH,
        )

    def __call__(self, src, dst, partner):
        return self.at(self.take(1), src, dst, partner)


class Locals:
    def __init__(self, sems):
        self.sems, self.used, self.open = sems, 0, []

    def __call__(self, src, dst):
        copy = pltpu.make_async_copy(src, dst, self.sems.at[self.used])
        self.used += 1
        copy.start()
        self.open.append(copy)
        return copy

    def wait(self):
        for copy in self.open:
            copy.wait()
        self.open = []

    def take(self, count):
        first = self.used
        self.used += count
        return first

    def alone(self, src, dst):
        copy = self(src, dst)
        self.open.pop()
        return copy


def add_rows(dst, sources):
    rows = dst.shape[0]
    step = 32

    @pl.loop(0, rows // step)
    def _(i):
        part = pl.ds(pl.multiple_of(i * step, step), step)
        total = sources[0][part, :].astype(F32)
        for source in sources[1:]:
            total = total + source[part, :].astype(F32)
        dst[part, :] = total.astype(dst.dtype)


class Gather:
    def __init__(self, me, copies, local, own, buf):
        half = buf.shape[1] // 2
        a, b = pl.ds(0, half), pl.ds(half, half)
        own_a, own_b = buf.at[me.f, a], buf.at[me.f, b]
        self.local, self.own, self.slot = local, own, buf.at[me.f]
        self.a_x = copies(own.at[a], own_a, me.xp)
        self.b_y = copies(own.at[b], own_b, me.yp)
        self.b_x = copies(own.at[b], own_b, me.xp)
        self.a_y = copies(own.at[a], own_a, me.yp)
        self.on_y = copies(buf.at[me.fx, a], buf.at[me.fx, a], me.yp)
        self.on_x = copies(buf.at[me.fy, b], buf.at[me.fy, b], me.xp)

    def first(self):
        self.a_x.start()
        self.b_y.start()

    def second(self):
        self.b_x.start()
        self.a_y.start()
        self.kept = self.local.alone(self.own, self.slot)

    def relay(self):
        self.a_x.wait_recv()
        self.on_y.start()
        self.b_y.wait_recv()
        self.on_x.start()

    def finish(self):
        for copy in (self.b_x, self.a_y, self.on_y, self.on_x):
            copy.wait_recv()
        for copy in (self.a_x, self.b_y, self.b_x, self.a_y, self.on_y, self.on_x):
            copy.wait_send()
        self.kept.wait()

    def finish_half(self):
        for copy in (self.a_x, self.b_y, self.b_x, self.a_y):
            copy.wait()
        self.kept.wait()


class GatherEnd:
    def __init__(self, me, copies, local, came, held):
        half = held.shape[1] // 2
        a, b = pl.ds(0, half), pl.ds(half, half)
        self.on_y = copies(came.at[me.fx, a], held.at[me.fx, a], me.yp)
        self.on_x = copies(came.at[me.fy, b], held.at[me.fy, b], me.xp)
        self.me, self.local, self.came, self.held = me, local, came, held

    def start(self):
        self.on_y.start()
        self.on_x.start()

    def load(self):
        me = self.me
        self.loads = [self.local.alone(self.came.at[i], self.held.at[i]) for i in (me.f, me.fx, me.fy)]

    def finish(self):
        for copy in self.loads:
            copy.wait()
        self.on_y.wait()
        self.on_x.wait()


class Scatter:
    def __init__(self, me, copies, local, part, bufs):
        half = part.shape[1] // 2
        a, b = pl.ds(0, half), pl.ds(half, half)
        slot = [bufs.at[i] for i in range(10)]
        self.fwd_a, self.fwd_b, self.own_a, self.own_b = slot[0:4]
        self.rx_own, self.rx_fwd, self.ry_own, self.ry_fwd, self.r2_a, self.r2_b = slot[4:10]
        self.d_x = copies(part.at[me.fd, a], self.rx_fwd, me.xp)
        self.d_y = copies(part.at[me.fd, b], self.ry_fwd, me.yp)
        self.o_x = copies(part.at[me.fx, a], self.rx_own, me.xp)
        self.o_y = copies(part.at[me.fy, b], self.ry_own, me.yp)
        self.to_y = copies(self.fwd_a, self.r2_a, me.yp)
        self.to_x = copies(self.fwd_b, self.r2_b, me.xp)
        self.local, self.me, self.part, self.a, self.b = local, me, part, a, b

    def first(self):
        self.d_x.start()
        self.d_y.start()

    def second(self):
        self.o_x.start()
        self.o_y.start()
        me, part = self.me, self.part
        self.mine = [
            self.local.alone(part.at[me.fy, self.a], self.fwd_a),
            self.local.alone(part.at[me.fx, self.b], self.fwd_b),
            self.local.alone(part.at[me.f, self.a], self.own_a),
            self.local.alone(part.at[me.f, self.b], self.own_b),
        ]

    def relay(self):
        for copy in self.mine:
            copy.wait()
        self.d_x.wait_recv()
        add_rows(self.fwd_a, [self.fwd_a, self.rx_fwd])
        self.to_y.start()
        self.d_y.wait_recv()
        add_rows(self.fwd_b, [self.fwd_b, self.ry_fwd])
        self.to_x.start()

    def load_fwd(self):
        me, part = self.me, self.part
        self.mine = [
            self.local.alone(part.at[me.fy, self.a], self.fwd_a),
            self.local.alone(part.at[me.fx, self.b], self.fwd_b),
        ]

    def sum_fwd(self):
        for copy in self.mine:
            copy.wait()
        self.d_x.wait_recv()
        add_rows(self.fwd_a, [self.fwd_a, self.rx_fwd])
        self.d_y.wait_recv()
        add_rows(self.fwd_b, [self.fwd_b, self.ry_fwd])

    def resume(self, passed):
        me, part = self.me, self.part
        for copy in [self.local.alone(passed.at[0], self.fwd_a), self.local.alone(passed.at[1], self.fwd_b)]:
            copy.wait()
        self.to_y.start()
        self.to_x.start()
        self.o_x.start()
        self.o_y.start()
        self.mine = [
            self.local.alone(part.at[me.f, self.a], self.own_a),
            self.local.alone(part.at[me.f, self.b], self.own_b),
        ]

    def finish_resumed(self, sum_a, sum_b):
        for copy in self.mine:
            copy.wait()
        self.finish(sum_a, sum_b)

    def drain_resumed(self):
        for copy in (self.o_x, self.o_y, self.to_y, self.to_x):
            copy.wait_send()

    def finish(self, sum_a, sum_b):
        self.o_x.wait_recv()
        self.to_y.wait_recv()
        add_rows(sum_a, [self.own_a, self.rx_own, self.r2_a])
        self.o_y.wait_recv()
        self.to_x.wait_recv()
        add_rows(sum_b, [self.own_b, self.ry_own, self.r2_b])

    def drain(self):
        for copy in (self.d_x, self.d_y, self.o_x, self.o_y, self.to_y, self.to_x):
            copy.wait_send()


class LineSum:
    def __init__(self, me, copies, own, bufs):
        z, f, k = me.z, me.f, me.k
        self.z = z
        self.inner = (z == 1) | (z == 2)
        self.outer = (z == 0) | (z == 3)
        self.mine = z - 1
        self.theirs = 2 - z
        self.own, self.from_outer, self.total, self.from_inner = own, bufs.at[0:2], bufs.at[2:4], bufs.at[4]
        self.copies = copies
        self.base = copies.take(8)
        self.inner_of = (f, 2 * (1 + z // 3) + k)
        self.outer_of = (f, 2 * (3 * (z - 1)) + k)
        self.partner = (f, 2 * (3 - z) + k)

    def inward(self, half):
        return self.copies.at(
            self.base + half, self.own.at[half], self.from_outer.at[half], self.inner_of
        )

    def across(self, half):
        return self.copies.at(
            self.base + 2 + half, self.own.at[half], self.from_inner, self.partner
        )

    def back_across(self, half):
        return self.copies.at(
            self.base + 4 + half, self.total.at[half], self.total.at[half], self.partner
        )

    def outward(self, half):
        return self.copies.at(
            self.base + 6 + half, self.total.at[half], self.total.at[half], self.outer_of
        )

    def start(self):
        @pl.when(self.outer)
        def _():
            first = 1 - self.z // 3
            self.inward(first).start()
            self.inward(1 - first).start()

    def meet(self):
        @pl.when(self.inner)
        def _():
            t, m = self.theirs, self.mine
            self.inward(t).wait_recv()
            add_rows(self.own.at[t], [self.own.at[t], self.from_outer.at[t]])
            self.across(t).start()

    def close(self):
        @pl.when(self.inner)
        def _():
            m = self.mine
            self.inward(m).wait_recv()
            self.across(m).wait_recv()
            add_rows(
                self.total.at[m], [self.own.at[m], self.from_outer.at[m], self.from_inner]
            )
            self.back_across(m).start()
            self.outward(m).start()

    def spread(self):
        @pl.when(self.inner)
        def _():
            t = self.theirs
            self.back_across(t).wait_recv()
            self.outward(t).start()

    def arrive(self):
        @pl.when(self.outer)
        def _():
            self.outward(0).wait_recv()
            self.outward(1).wait_recv()

    def drain(self):
        @pl.when(self.outer)
        def _():
            self.inward(0).wait_send()
            self.inward(1).wait_send()

        @pl.when(self.inner)
        def _():
            self.across(self.theirs).wait_send()
            self.back_across(self.mine).wait_send()
            self.outward(0).wait_send()
            self.outward(1).wait_send()


HBM = pl.BlockSpec(memory_space=pl.ANY)
VM = pl.BlockSpec(memory_space=pltpu.VMEM)


def transfer(kernel, name, number, args, in_specs, outs, out_specs, scratch, copies, local):
    return pl.pallas_call(
        kernel,
        out_shape=outs,
        in_specs=in_specs,
        out_specs=out_specs,
        scratch_shapes=scratch
        + [
            pltpu.SemaphoreType.DMA((copies,)),
            pltpu.SemaphoreType.DMA((copies,)),
            pltpu.SemaphoreType.DMA((local,)),
        ],
        compiler_params=pltpu.CompilerParams(
            collective_id=number, has_side_effects=True, vmem_limit_bytes=VMEM_LIMIT
        ),
        name=name,
    )(*args)


def shape(dims, dtype):
    return jax.ShapeDtypeStruct(dims, dtype)


def assemble_kernel(
    gate, up, heads, down, out, small, count, tokens_out, tokens_grad,
    g_gate, g_up, g_q, g_k, g_v, g_down, g_out, g_norm_a, g_norm_m, g_gain_q, g_gain_k, loss, output, grad_in,
):
    for src, dst in ((gate, g_gate), (up, g_up)):
        width = src.shape[2] // 4
        for i in range(4):
            for j in range(2):
                dst[:, pl.ds((2 * i + j) * width, width)] = src[j, :, pl.ds(i * width, width)].astype(F32)
    q_size, size = GROUP * HEAD_SIZE, HEAD_SIZE
    for head in range(KEY_VALUE_HEADS):
        g_q[:, pl.ds(head * q_size, q_size)] = heads[head, :, pl.ds(0, q_size)].astype(F32)
        g_k[:, pl.ds(head * size, size)] = heads[head, :, pl.ds(q_size, size)].astype(F32)
        g_v[:, pl.ds(head * size, size)] = heads[head, :, pl.ds(q_size + size, size)].astype(F32)
    f = lax.axis_index("fsdp")
    output[...] = tokens_out[...]
    grad_in[...] = tokens_grad[...]
    g_norm_a[...] = small[pl.ds(2 * f, 2), :]
    g_norm_m[...] = small[pl.ds(8 + 2 * f, 2), :]
    part = g_gain_q.shape[1]
    lane = lax.broadcasted_iota(jnp.int32, (HEAD_SIZE, part), 0)
    column = lax.broadcasted_iota(jnp.int32, (HEAD_SIZE, part), 1)
    pick = jnp.where(lane == column + part * f, 1.0, 0.0)
    both = lax.dot_general(
        small[16:24, :], pick, (((1,), (0,)), ((), ())), preferred_element_type=F32, precision=lax.Precision.HIGHEST
    )
    g_gain_q[...] = both[0:1, :]
    g_gain_k[...] = both[1:2, :]
    loss[...] = jnp.sum(small[18:19, :], axis=1, keepdims=True) / count[0:1, 0:1]
    g_down[...] = down[...].astype(F32)
    g_out[...] = out[...].astype(F32)


def assemble(gate, up, heads, down, out, small, count, tokens_out, tokens_grad):
    steps = 4

    def cut(dims):
        return pl.BlockSpec((dims[0], dims[1] // steps, dims[2]), lambda i: (0, i, 0))

    def whole(dims):
        return pl.BlockSpec(dims, lambda i: (0,) * len(dims))

    def rows_of(a):
        return pl.BlockSpec((a.shape[0] // steps, a.shape[1]), lambda i: (i, 0))

    def flat(rows, columns):
        return pl.BlockSpec((rows // steps, columns), lambda i: (i, 0)), shape((rows, columns), F32)

    rows, width = gate.shape[1], 2 * gate.shape[2]
    all_heads = KEY_VALUE_HEADS * HEAD_SIZE
    outs = [
        flat(rows, width), flat(rows, width), flat(rows, GROUP * all_heads), flat(rows, all_heads), flat(rows, all_heads),
        (cut(down.shape), shape(down.shape, F32)), (cut(out.shape), shape(out.shape, F32)),
        (whole((2, 128)), shape((2, 128), F32)), (whole((2, 128)), shape((2, 128), F32)),
        (whole((1, 32)), shape((1, 32), F32)), (whole((1, 32)), shape((1, 32), F32)),
        (whole((1, 1)), shape((1, 1), F32)),
    ] + [(rows_of(a), shape(a.shape, a.dtype)) for a in (tokens_out, tokens_grad)]
    return pl.pallas_call(
        assemble_kernel,
        grid=(steps,),
        out_shape=[s for _, s in outs],
        in_specs=[cut(a.shape) for a in (gate, up, heads, down, out)]
        + [whole(small.shape), whole(count.shape), rows_of(tokens_out), rows_of(tokens_grad)],
        out_specs=[b for b, _ in outs],
        compiler_params=pltpu.CompilerParams(vmem_limit_bytes=VMEM_LIMIT),
        name="assemble",
    )(gate, up, heads, down, out, small, count, tokens_out, tokens_grad)


def dot_nt(a, b, **kw):
    return lax.dot_general(a, b, (((1,), (1,)), ((), ())), preferred_element_type=F32, **kw)


def dot_nn(a, b):
    return lax.dot_general(a, b, (((1,), (0,)), ((), ())), preferred_element_type=F32)


def dot_tn(a, b):
    return lax.dot_general(a, b, (((0,), (0,)), ((), ())), preferred_element_type=F32)


HIGHEST = lax.Precision.HIGHEST


class SmallSum:
    def __init__(self, me, copies, own, plane, pair, line):
        self.me, self.own, self.plane, self.pair, self.line = me, own, plane, pair, line
        self.one = [copies(own, plane.at[me.f], partner) for partner in (me.xp, me.yp, me.dp)]
        self.two = [copies(pair.at[me.k], pair.at[me.k], me.sib)]
        self.three = [
            copies(line.at[me.z], line.at[me.z], me.along_z(step)[1]) for step in (1, 2, 3)
        ]

    def first(self):
        for copy in self.one:
            copy.start()
        self.plane[self.me.f] = self.own[...]

    def second(self):
        for copy in self.one:
            copy.wait_recv()
        plane = self.plane
        self.pair[self.me.k] = (plane[0] + plane[1]) + (plane[2] + plane[3])
        self.two[0].start()

    def third(self):
        self.two[0].wait_recv()
        self.line[self.me.z] = self.pair[0] + self.pair[1]
        for copy in self.three:
            copy.start()

    def finish(self, dst):
        for copy in self.three:
            copy.wait_recv()
        line = self.line
        dst[...] = (line[0] + line[1]) + (line[2] + line[3])

    def drain(self):
        for copy in self.one + self.two + self.three:
            copy.wait_send()


class Spread:
    def __init__(self, me, copies, held, cross=True):
        self.me, self.held, self.copies, self.cross = me, held, copies, cross
        self.here, self.stride = (me.c, 2) if cross else (me.z, 1)
        self.up, self.down = copies.take(3), copies.take(3)
        if cross:
            self.cross_own, self.cross_up, self.cross_down = copies.take(1), copies.take(3), copies.take(3)

    def hop(self, base, hop, block, partner):
        ref = self.held.at[block]
        return self.copies.at(base + hop - 1, ref, ref, partner)

    def rise(self, hop):
        me = self.me
        return self.hop(self.up, hop, self.here - self.stride * (hop - 1), (me.f, me.c + 2))

    def fall(self, hop):
        me = self.me
        return self.hop(self.down, hop, self.here + self.stride * (hop - 1), (me.f, me.c - 2))

    def across(self, base, hop, block):
        return self.hop(base, hop, block, self.me.sib)

    def start(self):
        z = self.me.z

        @pl.when(z < 3)
        def _():
            self.rise(1).start()

        @pl.when(z > 0)
        def _():
            self.fall(1).start()

        if self.cross:
            self.across(self.cross_own, 1, self.me.c).start()

    def step(self, hop):
        z, c = self.me.z, self.me.c

        @pl.when(z >= hop)
        def _():
            self.rise(hop).wait_recv()
            if hop < 3:

                @pl.when(z < 3)
                def _():
                    self.rise(hop + 1).start()

            if self.cross:
                self.across(self.cross_up, hop, c - 2 * hop).start()

        @pl.when(z + hop <= 3)
        def _():
            self.fall(hop).wait_recv()
            if hop < 3:

                @pl.when(z > 0)
                def _():
                    self.fall(hop + 1).start()

            if self.cross:
                self.across(self.cross_down, hop, c + 2 * hop).start()

    def crossed(self, hop):
        z, c = self.me.z, self.me.c
        if hop == 0:
            self.across(self.cross_own, 1, c).wait_recv()
            return

        @pl.when(z >= hop)
        def _():
            self.across(self.cross_up, hop, c - 2 * hop).wait_recv()

        @pl.when(z + hop <= 3)
        def _():
            self.across(self.cross_down, hop, c + 2 * hop).wait_recv()

    def drain(self):
        z, c = self.me.z, self.me.c
        if self.cross:
            self.across(self.cross_own, 1, c).wait_send()
        for hop in (1, 2, 3):

            @pl.when((z >= hop - 1) & (z < 3))
            def _(hop=hop):
                self.rise(hop).wait_send()

            @pl.when((z + hop - 1 <= 3) & (z > 0))
            def _(hop=hop):
                self.fall(hop).wait_send()

            if not self.cross:
                continue

            @pl.when(z >= hop)
            def _(hop=hop):
                self.across(self.cross_up, hop, c - 2 * hop).wait_send()

            @pl.when(z + hop <= 3)
            def _(hop=hop):
                self.across(self.cross_down, hop, c + 2 * hop).wait_send()


def half_turn(values):
    return pltpu.roll(values, HEAD_SIZE // 2, 1)


def rotary_tables(position_rows, freq, cosines, sines, at):
    columns = jnp.transpose(position_rows)
    lane = lax.broadcasted_iota(jnp.int32, (HEAD_SIZE, HEAD_SIZE), 1)
    first = lane < HEAD_SIZE // 2
    for r in range(2):
        angle = columns[:, r : r + 1] * freq
        turns = jnp.floor(angle * (2.0 / math.pi) + 0.5)
        rest = ((angle - turns * 1.5703125) - turns * 4.837512969970703125e-04) - turns * 7.549789954891882e-08
        square = rest * rest
        sine = rest + rest * square * (
            -1.6666654611e-01 + square * (8.3321608736e-03 - square * 1.9515295891e-04)
        )
        cosine = 1.0 + square * (
            -0.5 + square * (4.166664568298827e-02 + square * (-1.388731625493765e-03 + square * 2.443315711809948e-05))
        )
        quarter = (turns.astype(jnp.int32) + jnp.where(first, 0, 3)) & 3
        odd = (quarter & 1) == 1
        value = jnp.where(odd, sine, cosine)
        value = jnp.where((quarter == 1) | (quarter == 2), -value, value)
        other = half_turn(value)
        rows = pl.ds(pl.multiple_of(at + r * 128, 128), 128)
        cosines[rows, :] = jnp.where(first, value, other)
        sines[rows, :] = jnp.where(first, -other, value)


def head_norm(u):
    return lax.rsqrt(jnp.mean(u * u, axis=-1, keepdims=True) + EPSILON)


def small_arguments(f, positions, valid, norm_a, norm_m, gain_q, gain_k, misc, gains, count):
    misc[...] = jnp.zeros_like(misc)
    for r in range(2):
        misc[r : r + 1, :] = positions[0:1, pl.ds(r * 128, 128)].astype(F32)
        misc[r + 2 : r + 3, :] = valid[0:1, pl.ds(r * 128, 128)].astype(F32)
    gains[...] = jnp.zeros_like(gains)
    for i, norm in enumerate((norm_a, norm_m)):
        gains[2 * i : 2 * i + 2, :] = norm[...].astype(F32).reshape(2, 128)
    size = gain_q.shape[0]
    lane = lax.broadcasted_iota(jnp.int32, (1, HEAD_SIZE), 1)
    for r, gain in enumerate((gain_q, gain_k)):
        wide = jnp.concatenate([gain[...].astype(F32).reshape(1, size)] * (HEAD_SIZE // size), axis=1)
        gains[r + 4 : r + 5, :] = jnp.where(lane // size == f, wide, 0.0)
    count[...] = jnp.broadcast_to(jnp.sum(valid[...].astype(F32), axis=1, keepdims=True), count.shape)


def kernel_forward(
    wq, wk, wv, wo, wg, wu, wd, x, t, positions, valid, norm_a, norm_m, gain_qs, gain_ks, freq,
    x_pair, t_pair, misc_all, gains_all, count_out,
    w_head_out, wo_all, wg_all, wu_all, wd_all,
    h_out, proj_out, qkv_out, att_out, lse_out, cos_out, sin_out, att_all,
    w_head, h_all, proj, qkv, att, lse, cosines, sines, x_all, values, own_h, own_o, own_g, own_u, own_d, gain_row, misc, gains, count, plane, pair, line,
    send, recv, lsem,
):
    me = Place()
    z, k, f, c = me.z, me.k, me.f, me.c
    rows = x.shape[0]
    small_arguments(f, positions, valid, norm_a, norm_m, gain_qs, gain_ks, misc, gains, count)
    greet([me.xp, me.yp, me.dp, me.sib] + [me.along_z(step)[1] for step in (1, 2, 3)])
    copies, local = Copies(send, recv), Locals(lsem)
    q_size = GROUP * HEAD_SIZE
    head_loads = [
        local.alone(wq.at[:, pl.ds(pl.multiple_of(c * q_size, 128), q_size)], own_h.at[:, pl.ds(0, q_size)]),
        local.alone(wk.at[:, pl.ds(pl.multiple_of(c * HEAD_SIZE, 128), HEAD_SIZE)], own_h.at[:, pl.ds(q_size, HEAD_SIZE)]),
        local.alone(
            wv.at[:, pl.ds(pl.multiple_of(c * HEAD_SIZE, 128), HEAD_SIZE)],
            own_h.at[:, pl.ds(q_size + HEAD_SIZE, HEAD_SIZE)],
        ),
    ]
    width = wg.shape[1] // 8
    for src, own in ((wo, own_o), (wd, own_d)):
        local(src.at[pl.ds(pl.multiple_of(k * own.shape[0], 16), own.shape[0])], own)
    for src, own in ((wg, own_g), (wu, own_u)):
        for i in range(4):
            at = pl.ds(pl.multiple_of((2 * i + k) * width, 128), width)
            local(src.at[:, at], own.at[:, pl.ds(i * width, width)])
    small = SmallSum(me, copies, count, plane, pair, line)
    small.first()
    gain_sends = [copies(gains, gains_all.at[f], partner) for partner in (me.xp, me.yp, me.dp)]
    misc_sends = [
        copies(misc, misc_all.at[k, z], me.along_z(step)[1]) for step in (1, 2, 3)
    ]
    for copy in misc_sends + gain_sends:
        copy.start()
    x_all[c] = x[...]
    spread = Spread(me, copies, x_all)
    spread.start()
    pair_sends = [copies(t, t_pair.at[k], me.sib)]
    pair_sends[0].start()
    for copy in head_loads:
        copy.wait()
    head = Gather(me, copies, local, own_h, w_head)
    head.first()
    head.second()
    out = Gather(me, copies, local, own_o, wo_all)
    gate = Gather(me, copies, local, own_g, wg_all)
    up = Gather(me, copies, local, own_u, wu_all)
    down = Gather(me, copies, local, own_d, wd_all)
    keep = [local.alone(t, t_pair.at[k])]
    for copy in misc_sends:
        copy.wait_recv()
    misc_all[k, z] = misc[...]
    gains_all[f] = gains[...]
    misc_pass = copies(misc_all.at[k], misc_all.at[k], me.sib)
    misc_pass.start()
    small.second()
    for copy in gain_sends:
        copy.wait_recv()
    for i in range(4):
        for r in range(2):
            gain_row[0:1, pl.ds((2 * i + r) * 128, 128)] = gains_all[i, r : r + 1, :]
    gain_q = (gains_all[0, 4:5, :] + gains_all[1, 4:5, :]) + (gains_all[2, 4:5, :] + gains_all[3, 4:5, :])
    gain_k = (gains_all[0, 5:6, :] + gains_all[1, 5:6, :]) + (gains_all[2, 5:6, :] + gains_all[3, 5:6, :])
    head.relay()
    local.wait()
    for gather in (out, gate, up, down):
        gather.first()
    for gather in (out, gate, up, down):
        gather.second()
    misc_pass.wait_recv()
    small.third()

    @pl.loop(0, 8)
    def _(i):
        rotary_tables(
            misc_all[i % 2, i // 2], freq[0:1, :], cosines, sines, pl.multiple_of(i * 256, 256)
        )

    head.finish()
    spread.step(1)
    out.relay()

    def project(block):
        @pl.loop(0, 2)
        def _(u):
            piece = 2 * block + u
            at = pl.ds(pl.multiple_of(piece * rows, rows), rows)
            xin = x_all[piece].astype(F32)
            r = lax.rsqrt(jnp.mean(xin * xin, axis=-1, keepdims=True) + EPSILON)
            h = (xin * r * gain_row[0:1, :]).astype(BF16)
            h_all[at, :] = h
            p = dot_nn(h, w_head[...].reshape(w_head.shape[0] * w_head.shape[1], w_head.shape[2]))
            cosine, sine = cosines[at, :], sines[at, :]
            for g in range(GROUP + 1):
                lanes = slice(g * HEAD_SIZE, (g + 1) * HEAD_SIZE)
                one = p[:, lanes]
                proj[at, lanes] = one
                one = one * head_norm(one) * (gain_q if g < GROUP else gain_k)
                qkv[at, lanes] = (one * cosine + half_turn(one) * sine).astype(BF16)
            qkv[at, (GROUP + 1) * HEAD_SIZE :] = p[:, (GROUP + 1) * HEAD_SIZE :].astype(BF16)

    way = 1 - 2 * (z // 2)
    spread.crossed(0)
    project(z)
    spread.step(2)
    spread.crossed(1)
    spread.step(3)
    gate.relay()
    spread.crossed(2)
    spread.crossed(3)

    @pl.loop(1, 4)
    def _(step):
        project((z + way * step + 4) % 4)

    for src, dst in (
        (w_head, w_head_out), (h_all, h_out), (proj, proj_out), (qkv, qkv_out), (cosines, cos_out), (sines, sin_out)
    ):
        keep.append(local.alone(src, dst))
    values[:, 0:HEAD_SIZE] = qkv[:, (GROUP + 1) * HEAD_SIZE :]
    values[:, HEAD_SIZE:] = jnp.ones((qkv.shape[0], HEAD_SIZE), BF16)
    base = copies.take(4)
    block = 2 * rows
    for step in (1, 2, 3, 0):
        to, partner = me.along_z(step)
        attend_rows(qkv, values, att, lse, to, block)
        piece = att.at[pl.ds(pl.multiple_of(to * block, block), block)]
        keep.append(local.alone(piece, att_out.at[pl.ds(pl.multiple_of(to * block, block), block)]))
        place = att_all.at[:, pl.ds(pl.multiple_of(z * q_size, 128), q_size)]
        if step:
            copy = pltpu.make_async_remote_copy(
                src_ref=piece, dst_ref=place, send_sem=send.at[base + step], recv_sem=recv.at[base + step],
                device_id=partner, device_id_type=MESH,
            )
            copy.start()
            keep.append(copy)
        else:
            keep.append(local.alone(piece, place))
    small.finish(count_out)
    keep.append(local.alone(lse, lse_out))
    for i in range(2):
        keep.append(local.alone(x_all.at[2 * z + i], x_pair.at[i]))
    for gather in (out, gate):
        gather.finish()
    for gather in (up, down):
        gather.finish_half()
    for copy in pair_sends + [misc_pass]:
        copy.wait_send()
    pair_sends[0].wait_recv()
    for copy in misc_sends + gain_sends:
        copy.wait_send()
    for copy in keep:
        copy.wait()
    spread.drain()
    small.drain()


def forward(wq, wk, wv, wo, wg, wu, wd, x, t, *small):
    rows, width = x.shape
    tokens = 8 * rows
    row = wq.shape[0]
    half_ff = wg.shape[1] // 2
    out_rows, down_rows = wo.shape[0] // 2, wd.shape[0] // 2
    return transfer(
        kernel_forward, "forward", 1,
        (wq, wk, wv, wo, wg, wu, wd, x, t) + small,
        [HBM] * 7 + [VM] * 9,
        [
            shape((2, rows, width), BF16),
            shape((2, rows, width), BF16),
            shape((2, 4, 8, 128), F32),
            shape((4, 8, 128), F32),
            shape((8, 128), F32),
            shape((4, row, HEAD_COLUMNS), BF16),
            shape((4, out_rows, width), BF16),
            shape((4, row, half_ff), BF16),
            shape((4, row, half_ff), BF16),
            shape((4, down_rows, width), BF16),
            shape((tokens, width), BF16),
            shape((tokens, (GROUP + 1) * HEAD_SIZE), F32),
            shape((tokens, HEAD_COLUMNS), BF16),
            shape((tokens, GROUP * HEAD_SIZE), BF16),
            shape((GROUP, 8, tokens), F32),
            shape((tokens, HEAD_SIZE), F32),
            shape((tokens, HEAD_SIZE), F32),
            shape((2 * rows, 4 * GROUP * HEAD_SIZE), BF16),
        ],
        [HBM] * 2 + [VM] * 3 + [HBM] * 13,
        [
            pltpu.VMEM((4, row, HEAD_COLUMNS), BF16),
            pltpu.VMEM((tokens, width), BF16),
            pltpu.VMEM((tokens, (GROUP + 1) * HEAD_SIZE), F32),
            pltpu.VMEM((tokens, HEAD_COLUMNS), BF16),
            pltpu.VMEM((tokens, GROUP * HEAD_SIZE), BF16),
            pltpu.VMEM((GROUP, 8, tokens), F32),
            pltpu.VMEM((tokens, HEAD_SIZE), F32),
            pltpu.VMEM((tokens, HEAD_SIZE), F32),
            pltpu.VMEM((8, rows, width), BF16),
            pltpu.VMEM((tokens, 2 * HEAD_SIZE), BF16),
            pltpu.VMEM((row, HEAD_COLUMNS), BF16),
            pltpu.VMEM((out_rows, width), BF16),
            pltpu.VMEM((row, half_ff), BF16),
            pltpu.VMEM((row, half_ff), BF16),
            pltpu.VMEM((down_rows, width), BF16),
            pltpu.VMEM((8, width), F32),
            pltpu.VMEM((8, 128), F32),
            pltpu.VMEM((8, 128), F32),
            pltpu.VMEM((8, 128), F32),
            pltpu.VMEM((4, 8, 128), F32),
            pltpu.VMEM((2, 8, 128), F32),
            pltpu.VMEM((4, 8, 128), F32),
        ],
        7 + 3 + 3 + 13 + 1 + 30 + 1 + 4, 3 + 2 + 8 + 5 + 1 + 1 + 2 + 6 + 4 + 1,
    )


def attend_rows(qkv, values, att, lse, i, block):
    rows = pl.ds(pl.multiple_of(i * block, block), block)
    k_at = pl.ds(GROUP * HEAD_SIZE, HEAD_SIZE)
    row = lax.broadcasted_iota(jnp.int32, (block, block), 0)
    column = lax.broadcasted_iota(jnp.int32, (block, block), 1)
    for g in range(GROUP):
        q = qkv[rows, pl.ds(g * HEAD_SIZE, HEAD_SIZE)]

        def part(j, acc, q=q):
            keys = pl.ds(pl.multiple_of(j * block, block), block)
            e = jnp.exp2(dot_nt(q, qkv[keys, k_at]) * (SCALE * LOG2_E))
            return acc + dot_nn(e.astype(BF16), values[keys, :])

        acc = lax.fori_loop(0, i, part, jnp.zeros((block, 2 * HEAD_SIZE), F32))
        e = jnp.exp2(dot_nt(q, qkv[rows, k_at]) * (SCALE * LOG2_E))
        acc = acc + dot_nn(jnp.where(column <= row, e, 0.0).astype(BF16), values[rows, :])
        total = acc[:, HEAD_SIZE:]
        att[rows, pl.ds(g * HEAD_SIZE, HEAD_SIZE)] = (acc[:, :HEAD_SIZE] / total).astype(BF16)
        mean = jnp.full((8, HEAD_SIZE), 1.0 / HEAD_SIZE, F32)
        lse[g, :, rows] = dot_nt(mean, jnp.log(total), precision=HIGHEST)


def kernel_middle(
    att_in, wo_in, wg_in, wu_in, wd_in, x_in, t_in, misc_all, gains_all, count,
    output, g_out, p_gate, p_up, p_out, down_sum, gate_pass, g_x2_own, small,
    att, wo, wg, wu, wd, x, t, x2, h2, gate, up, mid, g_gate, g_up, fin, g_fin, g_dn, g_a,
    send_1, recv_1, send_2, recv_2, send_3, recv_3, p_down, p_g, p_u, p_o, g_ob, sc_d, sum_d, sc_g,
    gain_row, valid, loss_row, gain_sum,
    send, recv, lsem, loss_scale,
):
    me = Place()
    z, k = me.z, me.k
    tokens, width = att.shape
    rows = tokens // 2
    greet([me.xp, me.yp, me.sib] + [me.along_z(step)[1] for step in (1, 2, 3)])
    copies, local = Copies(send, recv), Locals(lsem)
    loads = [
        local.alone(src, dst)
        for src, dst in (
            (att_in, att), (wo_in, wo), (x_in, x), (wg_in, wg), (t_in, t)
        )
    ]
    ends = [GatherEnd(me, copies, local, wu_in, wu), GatherEnd(me, copies, local, wd_in, wd)]
    for entry in ends:
        entry.start()
    for entry in ends:
        entry.load()
    for i in range(4):
        for r in range(2):
            gain_row[0:1, pl.ds((2 * i + r) * 128, 128)] = gains_all[i, r + 2 : r + 3, :]
    for u in range(2):
        columns = jnp.transpose(misc_all[u, z])
        for r in range(2):
            valid[pl.ds(u * rows + r * 128, 128), :] = jnp.broadcast_to(columns[:, r + 2 : r + 3], (128, 128))
    small[...] = jnp.zeros_like(small)
    loss_row[...] = jnp.zeros_like(loss_row)
    gain_sum[...] = jnp.zeros_like(gain_sum)
    step = 64
    bases = [copies.take(4) for _ in range(3)]

    def crossing(which, i, src, dst):
        at = pl.ds(pl.multiple_of(i * 256, 256), 256)
        return copies.at(bases[which] + i, src.at[:, at], dst.at[:, at], me.sib)

    def flat(ref, at):
        value = ref[:, :, at]
        return value.reshape(value.shape[0] * value.shape[1], value.shape[2])

    def strip(i, size):
        return pl.ds(pl.multiple_of(i * size, size), size)

    for copy in loads[0:2]:
        copy.wait()

    @pl.loop(0, 4)
    def _(i):
        at = strip(i, 256)
        send_1[:, at] = dot_nn(att[...], flat(wo, at)).astype(BF16)
        crossing(0, i, send_1, recv_1).start()

    for copy in loads[2:4]:
        copy.wait()
    for i in range(4):
        crossing(0, i, send_1, recv_1).wait_recv()

    @pl.loop(0, tokens // step)
    def _(i):
        at = strip(i, step)
        value = x[at, :].astype(F32) + (send_1[at, :].astype(F32) + recv_1[at, :].astype(F32))
        x2[at, :] = value
        r = lax.rsqrt(jnp.mean(value * value, axis=-1, keepdims=True) + EPSILON)
        h2[at, :] = (value * r * gain_row[0:1, :]).astype(BF16)

    @pl.loop(0, gate.shape[1] // 256)
    def _(i):
        at = strip(i, 256)
        gate[:, at] = dot_nn(h2[...], flat(wg, at))

    ends[0].finish()

    @pl.loop(0, gate.shape[1] // 256)
    def _(i):
        at = strip(i, 256)
        a = gate[:, at]
        b = dot_nn(h2[...], flat(wu, at))
        up[:, at] = b
        mid[:, at] = (a / (1.0 + jnp.exp(-a)) * b).astype(BF16)

    ends[1].finish()
    loads[4].wait()

    @pl.loop(0, 4)
    def _(i):
        at = strip(i, 256)
        send_2[:, at] = dot_nn(mid[...], flat(wd, at)).astype(BF16)
        crossing(1, i, send_2, recv_2).start()

    for i in range(4):
        crossing(1, i, send_2, recv_2).wait_recv()
    factor = 2.0 * loss_scale / count[0:1, 0:1]

    @pl.loop(0, tokens // step)
    def _(i):
        at = strip(i, step)
        value = x2[at, :] + (send_2[at, :].astype(F32) + recv_2[at, :].astype(F32))
        fin[at, :] = value.astype(BF16)
        miss = value - t[at, :].astype(F32)
        weighted = valid[at, 0:1] * miss
        loss_row[0:1, :] += jnp.sum(weighted * miss, axis=0, keepdims=True)
        g = factor * weighted
        g_fin[at, :] = g
        g_dn[at, :] = g.astype(BF16)

    writes = [local.alone(fin.at[pl.ds(pl.multiple_of(k * rows, rows), rows)], output)]
    down_rows = p_down.shape[1]

    @pl.loop(0, 4)
    def _(i):
        p_down[i] = dot_tn(mid[:, strip(i, down_rows)], g_dn[...]).astype(BF16)

    s_down = Scatter(me, copies, local, p_down, sc_d)
    s_down.first()
    s_down.second()

    @pl.loop(0, 4)
    def _(i):
        at = strip(i, down_rows)
        g = dot_nt(g_dn[...], wd[i])
        a, b = gate[:, at], up[:, at]
        s = 1.0 / (1.0 + jnp.exp(-a))
        g_gate[:, at] = (g * b * s * (1.0 + a * (1.0 - s))).astype(BF16)
        g_up[:, at] = (g * a * s).astype(BF16)

    @pl.loop(0, 4)
    def _(i):
        at = strip(i, 256)
        send_3[:, at] = (dot_nt(g_gate[...], wg[i]) + dot_nt(g_up[...], wu[i])).astype(BF16)
        crossing(2, i, send_3, recv_3).start()

    for i in range(4):
        crossing(2, i, send_3, recv_3).wait_recv()

    @pl.loop(0, tokens // step)
    def _(i):
        at = strip(i, step)
        g = send_3[at, :].astype(F32) + recv_3[at, :].astype(F32)
        value = x2[at, :]
        r = lax.rsqrt(jnp.mean(value * value, axis=-1, keepdims=True) + EPSILON)
        n = value * r
        gain_sum[0:1, :] += jnp.sum(g * n, axis=0, keepdims=True)
        g = g * gain_row[0:1, :]
        g = g_fin[at, :] + r * (g - n * jnp.mean(g * n, axis=-1, keepdims=True))
        g_fin[at, :] = g
        g_a[at, :] = g.astype(BF16)

    writes.append(local.alone(g_fin.at[pl.ds(pl.multiple_of(k * rows, rows), rows)], g_x2_own))
    go_base = copies.take(4)
    go_sends = []
    for turn in (2, 1, 3, 0):
        to, partner = me.along_z(turn)
        at = strip(to, 256)
        g_ob[:, at] = dot_nt(g_a[...], wo[to]).astype(BF16)
        place = g_out.at[pl.ds(pl.multiple_of(z * tokens, tokens), tokens)]
        if turn:
            go_sends.append(
                pltpu.make_async_remote_copy(
                    src_ref=g_ob.at[:, at], dst_ref=place, send_sem=send.at[go_base + to],
                    recv_sem=recv.at[go_base + z], device_id=partner, device_id_type=MESH,
                )
            )
            go_sends[-1].start()
        else:
            writes.append(local.alone(g_ob.at[:, at], place))
    s_down.relay()

    @pl.loop(0, 4)
    def _(i):
        p_g[i] = dot_tn(h2[:, strip(i, 256)], g_gate[...]).astype(BF16)

    s_gate = Scatter(me, copies, local, p_g, sc_g)
    s_gate.first()
    s_gate.load_fwd()
    writes.append(local.alone(p_g, p_gate))

    @pl.loop(0, 4)
    def _(i):
        p_u[i] = dot_tn(h2[:, strip(i, 256)], g_up[...]).astype(BF16)

    writes.append(local.alone(p_u, p_up))

    @pl.loop(0, 4)
    def _(i):
        p_o[i] = dot_tn(att[:, strip(i, 256)], g_a[...]).astype(BF16)

    writes.append(local.alone(p_o, p_out))
    for j in range(8):
        small[j + 8 : j + 9, :] = 0.5 * gain_sum[0:1, pl.ds(j * 128, 128)]
        small[18:19, :] += 0.5 * loss_row[0:1, pl.ds(j * 128, 128)]
    s_down.finish(sum_d.at[0], sum_d.at[1])
    writes.append(local.alone(sum_d, down_sum))
    s_gate.sum_fwd()
    writes.append(local.alone(sc_g.at[0:2], gate_pass))
    for copy in writes:
        copy.wait()
    for turn in (1, 2, 3):
        other, partner = me.along_z(turn)
        place = g_out.at[pl.ds(pl.multiple_of(other * tokens, tokens), tokens)]
        pltpu.make_async_remote_copy(
            src_ref=place, dst_ref=place, send_sem=send.at[go_base + other],
            recv_sem=recv.at[go_base + other], device_id=partner, device_id_type=MESH,
        ).wait_recv()
    for copy in go_sends:
        copy.wait_send()
    for which, src, dst in ((0, send_1, recv_1), (1, send_2, recv_2), (2, send_3, recv_3)):
        for i in range(4):
            crossing(which, i, src, dst).wait_send()
    s_down.drain()
    s_gate.d_x.wait_send()
    s_gate.d_y.wait_send()


def middle(att, wo, wg, wu, wd, x, t, misc_all, gains_all, count, loss_scale):
    tokens, width = att.shape
    rows = tokens // 2
    hidden = wg.shape[2]

    def bf(*dims):
        return pltpu.VMEM(dims, BF16)

    def held(a):
        return pltpu.VMEM(a.shape, a.dtype)

    def wide(*dims):
        return pltpu.VMEM(dims, F32)

    p_down, p_gate, p_out = (4, hidden // 4, width), (4, width // 4, hidden), (4, width // 4, width)
    return transfer(
        partial(kernel_middle, loss_scale=loss_scale), "middle", 3,
        (att, wo, wg, wu, wd, x.reshape(tokens, width), t.reshape(tokens, width), misc_all, gains_all, count),
        [HBM] * 7 + [VM] * 3,
        [
            shape((rows, width), BF16), shape((4 * tokens, width // 4), BF16),
            shape(p_gate, BF16), shape(p_gate, BF16), shape(p_out, BF16),
            shape((2, hidden // 8, width), BF16), shape((2, width // 8, hidden), BF16),
            shape((rows, width), F32), shape((24, 128), F32),
        ],
        [HBM] * 8 + [VM],
        [held(a) for a in (att, wo, wg, wu, wd)]
        + [bf(tokens, width)] * 2
        + [wide(tokens, width), bf(tokens, width), wide(tokens, hidden), wide(tokens, hidden)]
        + [bf(tokens, hidden)] * 3
        + [bf(tokens, width), wide(tokens, width), bf(tokens, width), bf(tokens, width)]
        + [bf(tokens, width)] * 6
        + [bf(*p_down), bf(*p_gate), bf(*p_gate), bf(*p_out), bf(tokens, width)]
        + [bf(10, hidden // 8, width), bf(2, hidden // 8, width), bf(10, width // 8, hidden)]
        + [wide(8, width), wide(tokens, 128), wide(8, width), wide(8, width)],
        12 + 6 + 4 + 6 + 4, 5 + 6 + 9 + 4 + 2,
    )


def head_back(g, u, cosine, sine, gain):
    g = g * cosine + half_turn(g * sine)
    r = head_norm(u)
    n = u * r
    g_gain = jnp.sum(g * n, axis=0, keepdims=True)
    g = g * gain
    return r * (g - n * jnp.mean(g * n, axis=-1, keepdims=True)), g_gain


def kernel_backward(
    g_o, gate_pass, down_sum, p_gate, p_up, p_out,
    qkv_in, att_in, lse_in, proj_in, cos_in, sin_in, h_in, w_in,
    x, g_x2, gains_all, small,
    down_tot, gate_tot, up_tot, out_tot, head_tot, grad_in, small_tot,
    g_out, qkv, att, lse, proj, cosines, sines, h_all, w_head, g_proj, g_k, g_v, p_head,
    gh_send, gh_sib, gh_own, gh_in, gain_row, work, plane, pair, line,
    sc_g, sc_u, sc_o, sc_h, own_d, own_g, own_u, own_o, line_d, line_g, line_u, line_o,
    send, recv, lsem,
):
    me = Place()
    z, k, f, c = me.z, me.k, me.f, me.c
    rows = x.shape[0]
    block = 2 * rows
    greet([me.xp, me.yp, me.dp, me.sib] + [me.along_z(step)[1] for step in (1, 2, 3)])
    copies, local = Copies(send, recv), Locals(lsem)
    size, q_size = HEAD_SIZE, GROUP * HEAD_SIZE

    for src, dst in ((g_o, g_out), (qkv_in, qkv), (att_in, att), (lse_in, lse), (proj_in, proj), (cos_in, cosines), (sin_in, sines)):
        local(src, dst)
    late = [local.alone(w_in, w_head)]
    h_base = local.take(4)

    def h_load(i):
        columns = pl.ds(pl.multiple_of(i * rows, rows), rows)
        return pltpu.make_async_copy(h_in.at[:, columns], h_all.at[i % 2], lsem.at[h_base + i])

    h_load(0).start()
    h_load(1).start()
    s_gate = Scatter(me, copies, local, p_gate, sc_g)
    s_up = Scatter(me, copies, local, p_up, sc_u)
    s_out = Scatter(me, copies, local, p_out, sc_o)
    s_head = Scatter(me, copies, local, p_head, sc_h)
    s_gate.resume(gate_pass)
    own_down = local.alone(down_sum, own_d)
    lines = [
        LineSum(me, copies, own, bufs)
        for own, bufs in ((own_d, line_d), (own_g, line_g), (own_u, line_u), (own_o, line_o))
    ]
    l_down, l_gate, l_up, l_out = lines
    totals = (down_tot, gate_tot, up_tot, out_tot)
    swap_base = copies.take(8)
    swaps, writes = [], []

    def finish(i):
        lines[i].arrive()
        half = lines[i].total.shape[1]
        for j in range(2):
            dst = totals[i].at[k, pl.ds(j * half, half)]
            copy = copies.at(swap_base + 2 * i + j, lines[i].total.at[j], dst, me.sib)
            copy.start()
            swaps.append(copy)
            writes.append(local.alone(lines[i].total.at[j], dst))

    def scattered(scatter, entry, own):
        scatter.finish(own.at[0], own.at[1])
        entry.start()

    own_down.wait()
    l_down.start()
    work[...] = small[...]
    for i in range(4):
        for r in range(2):
            gain_row[0:1, pl.ds((2 * i + r) * 128, 128)] = gains_all[i, r : r + 1, :]
    gain_q = (gains_all[0, 4:5, :] + gains_all[1, 4:5, :]) + (gains_all[2, 4:5, :] + gains_all[3, 4:5, :])
    gain_k = (gains_all[0, 5:6, :] + gains_all[1, 5:6, :]) + (gains_all[2, 5:6, :] + gains_all[3, 5:6, :])
    k_at = pl.ds(q_size, size)
    v_at = pl.ds(q_size + size, size)
    g_k[...] = jnp.zeros_like(g_k)
    g_v[...] = jnp.zeros_like(g_v)
    key = lax.broadcasted_iota(jnp.int32, (block, block), 0)
    query = lax.broadcasted_iota(jnp.int32, (block, block), 1)
    def queries(i):
        at = pl.ds(pl.multiple_of(i * block, block), block)
        for g in range(GROUP):
            head = pl.ds(g * size, size)
            q = qkv[at, head]
            go = g_out[at, head]
            product = go.astype(F32) * att[at, head].astype(F32)
            delta = dot_nt(jnp.ones((8, size), F32), product, precision=HIGHEST)[0:1, :]
            log_sum = lse[g, 0:1, at] * LOG2_E

            def part(keys, masked, q=q, go=go, delta=delta, log_sum=log_sum):
                kk, vv = qkv[keys, k_at], qkv[keys, v_at]
                p = jnp.exp2(dot_nt(kk, q) * (SCALE * LOG2_E) - log_sum)
                if masked:
                    p = jnp.where(key <= query, p, 0.0)
                gs = (p * (dot_nt(vv, go) - delta)).astype(BF16)
                g_v[keys, :] += dot_nn(p.astype(BF16), go)
                g_k[keys, :] += dot_nn(gs, q)
                return dot_tn(gs, kk)

            def step(j, acc, part=part):
                return acc + part(pl.ds(pl.multiple_of(j * block, block), block), False)

            acc = lax.fori_loop(0, i, step, jnp.zeros((block, size), F32))
            acc = (acc + part(at, True)) * SCALE
            g_u, g_gain = head_back(acc, proj[at, head], cosines[at, :], sines[at, :], gain_q)
            g_proj[at, head] = g_u.astype(BF16)
            work[16:17, :] += g_gain

    sib_base, right_base, left_base = copies.take(4), copies.take(4), copies.take(4)
    last = (z == 0) | (z == 3)
    inner = (z == 1) | (z == 2)

    def input_part(to, mine, dst):
        at = pl.ds(pl.multiple_of((2 * to + mine) * rows, rows), rows)
        weights = w_head[...].reshape(w_head.shape[0] * w_head.shape[1], w_head.shape[2])
        dst[...] = dot_nt(g_proj[at, :], weights).astype(BF16)

    def crossing(to):
        return copies.at(sib_base + to, gh_send.at[to], gh_sib.at[to], me.sib)

    def rightward(to):
        return copies.at(right_base + to, gh_own.at[to], gh_in.at[to], (f, c + 2))

    def leftward(to):
        there = 1 - (z - to) // 2
        place = gh_in.at[to + (4 - to) * there]
        return copies.at(left_base + to, gh_own.at[to], place, (f, c - 2))

    def onward(to):
        @pl.when(to > z)
        def _():
            rightward(to).start()

        @pl.when(to < z)
        def _():
            leftward(to).start()

    def join(to):
        crossing(to).wait_recv()
        add_rows(gh_own.at[to], [gh_own.at[to], gh_sib.at[to]])

    def end_send(order):
        @pl.when(last)
        def _():
            onward(far_first(order))

    def inner_send(order):
        @pl.when(inner)
        def _():
            to = far_first(order)

            @pl.when(to > z)
            def _():
                rightward(to).wait_recv()

            @pl.when(to < z)
            def _():
                copies.at(left_base + to, gh_own.at[to], gh_in.at[to], (f, c - 2)).wait_recv()

            add_rows(gh_own.at[to], [gh_own.at[to], gh_in.at[to]])
            onward(to)

    def far_first(order):
        return order + (3 - 2 * order) * (z // 2)

    def parts_to(to):
        input_part(to, 1 - k, gh_send.at[to])
        crossing(to).start()
        input_part(to, k, gh_own.at[to])

    spread = Spread(me, copies, head_tot)
    total = SmallSum(me, copies, work, plane, pair, line)
    local.wait()
    s_up.first()
    s_up.second()
    queries(2)
    l_down.meet()
    queries(0)
    queries(1)
    s_gate.finish_resumed(own_g.at[0], own_g.at[1])
    l_gate.start()
    l_down.close()
    queries(3)
    s_up.relay()
    for copy in late:
        copy.wait()
    l_down.spread()
    l_gate.meet()

    @pl.loop(0, 4)
    def _(i):
        at = pl.ds(pl.multiple_of(i * block, block), block)
        g_u, g_gain = head_back(g_k[at, :] * SCALE, proj[at, k_at], cosines[at, :], sines[at, :], gain_k)
        g_proj[at, k_at] = g_u.astype(BF16)
        g_proj[at, v_at] = g_v[at, :].astype(BF16)
        work[17:18, :] += g_gain

    parts_to(far_first(0))
    parts_to(far_first(3))
    l_gate.close()
    parts_to(far_first(1))
    parts_to(far_first(2))
    join(far_first(3))
    end_send(3)
    finish(0)
    inner_send(3)
    join(far_first(0))
    l_gate.spread()
    join(far_first(2))
    s_out.first()
    s_out.second()
    scattered(s_up, l_up, own_u)
    join(far_first(1))

    @pl.loop(0, 4)
    def _(i):
        h_load(i).wait()
        p_head[i] = dot_tn(h_all[i % 2], g_proj[...]).astype(BF16)

        @pl.when(i < 2)
        def _():
            h_load(i + 2).start()

    inner_send(0)
    s_head.first()
    s_head.second()
    s_out.relay()
    l_up.meet()
    scattered(s_out, l_out, own_o)
    s_head.relay()
    l_up.close()
    l_out.meet()
    l_up.spread()
    s_head.finish(head_tot.at[c, 0], head_tot.at[c, 1])
    spread.start()
    end_send(2)
    finish(2)
    end_send(1)
    l_out.close()
    inner_send(2)
    l_out.spread()
    spread.step(1)
    work[0:8, :] = jnp.zeros((8, 128), F32)

    @pl.when(z > 0)
    def _():
        rightward(z).wait_recv()

    @pl.when(z < 3)
    def _():
        copies.at(left_base + z, gh_own.at[z], gh_in.at[4], (f, c - 2)).wait_recv()

    @pl.when(z == 0)
    def _():
        gh_in[0] = jnp.zeros(gh_in.shape[1:], BF16)

    @pl.when(z == 3)
    def _():
        gh_in[4] = jnp.zeros(gh_in.shape[1:], BF16)

    @pl.loop(0, rows // 64)
    def _(i):
        at = pl.ds(pl.multiple_of(i * 64, 64), 64)
        g = gh_own[z, at, :].astype(F32) + gh_in[z, at, :].astype(F32) + gh_in[4, at, :].astype(F32)
        xin = x[at, :].astype(F32)
        r = lax.rsqrt(jnp.mean(xin * xin, axis=-1, keepdims=True) + EPSILON)
        n = xin * r
        g_gain = jnp.sum(g * n, axis=0, keepdims=True)
        for j in range(8):
            work[j : j + 1, :] += g_gain[:, j * 128 : (j + 1) * 128]
        g = g * gain_row[0:1, :]
        grad_in[at, :] = g_x2[at, :] + r * (g - n * jnp.mean(g * n, axis=-1, keepdims=True))


    total.first()
    finish(3)
    finish(1)
    total.second()
    spread.step(2)
    total.third()
    spread.step(3)
    total.finish(small_tot)
    for hop in range(4):
        spread.crossed(hop)
    for i in range(4):
        crossing(i).wait_send()

        @pl.when(i > z)
        def _(i=i):
            rightward(i).wait_send()

        @pl.when(i < z)
        def _(i=i):
            leftward(i).wait_send()

    spread.drain()
    total.drain()
    s_gate.drain_resumed()
    for scatter in (s_up, s_out, s_head):
        scatter.drain()
    for entry in lines:
        entry.drain()
    for copy in swaps:
        copy.wait()
    for copy in writes:
        copy.wait()


def backward(g_o, gate_pass, parts, saved, x, g_x2, gains_all, small):
    rows, width = x.shape
    tokens = 8 * rows
    sizes = [(2 * parts[0].shape[1], width)] + [p.shape[1:] for p in parts[1:]]
    head = (width // 4, HEAD_COLUMNS)

    def held(a):
        return pltpu.VMEM(a.shape, a.dtype)

    pieces = pltpu.VMEM((4, rows, width), BF16)
    scatters = [pltpu.VMEM((10, r // 2, n), BF16) for r, n in sizes[1:] + [head]]
    own = [pltpu.VMEM((2, r // 2, n), BF16) for r, n in sizes]
    line = [pltpu.VMEM((5, r // 2, n), BF16) for r, n in sizes]
    return transfer(
        kernel_backward, "backward", 2,
        (g_o, gate_pass) + tuple(parts) + tuple(saved) + (x, g_x2, gains_all, small),
        [HBM] * 14 + [VM] * 4,
        [shape((2,) + s, BF16) for s in sizes]
        + [
            shape((8, 2, head[0] // 2, head[1]), BF16),
            shape((rows, width), F32),
            shape(small.shape, F32),
        ],
        [HBM] * 4 + [VM] * 3,
        [pltpu.VMEM((tokens, GROUP * HEAD_SIZE), BF16)]
        + [held(a) for a in saved[:6]]
        + [pltpu.VMEM((2, tokens, rows), BF16), held(saved[7])]
        + [
            pltpu.VMEM((tokens, HEAD_COLUMNS), BF16),
            pltpu.VMEM((tokens, HEAD_SIZE), F32),
            pltpu.VMEM((tokens, HEAD_SIZE), F32),
            pltpu.VMEM((4,) + head, BF16),
            pieces, pieces, pieces, pltpu.VMEM((5, rows, width), BF16),
            pltpu.VMEM((8, width), F32),
            pltpu.VMEM(small.shape, F32),
            pltpu.VMEM((4,) + small.shape, F32),
            pltpu.VMEM((2,) + small.shape, F32),
            pltpu.VMEM((4,) + small.shape, F32),
        ]
        + scatters + own + line,
        24 + 32 + 8 + 12 + 7 + 13, 7 + 4 + 1 + 1 + 16 + 8 + 2,
    )


def chip_step(
    hidden_in, teacher, valid, positions, norm_attn, w_query, key_projection, value_projection,
    gain_query, gain_key, w_out, norm_mlp, w_gate, w_up, w_down,
):
    rows = hidden_in.shape[1]
    width = hidden_in.shape[2]
    half_width = HEAD_SIZE // 2
    freq = 1000000.0 ** (-2.0 * np.arange(half_width) / HEAD_SIZE)
    freq = np.broadcast_to(np.concatenate([freq, freq]), (8, HEAD_SIZE)).astype(np.float32)
    (
        x_pair, t_pair, misc_all, gains_all, count, w_head, wo, wg, wu, wd,
        h_all, proj, qkv, att, lse, cosines, sines, att_all,
    ) = forward(
        w_query, key_projection, value_projection, w_out, w_gate, w_up, w_down,
        hidden_in[0], teacher[0], positions, valid, norm_attn, norm_mlp, gain_query, gain_key, freq,
    )
    loss_scale = rows * lax.axis_size("ctx") * lax.axis_size("fsdp") / 4.0
    output, g_o, p_gate, p_up, p_out, s_down, gate_pass, g_x2, small = middle(
        att_all, wo, wg, wu, wd, x_pair, t_pair, misc_all, gains_all, count, loss_scale
    )
    down, gate, up, out, heads, grad_input, small = backward(
        g_o, gate_pass, (s_down, p_gate, p_up, p_out),
        (qkv, att, lse, proj, cosines, sines, h_all, w_head),
        hidden_in[0], g_x2, gains_all, small,
    )

    g_gate, g_up, g_q, g_k, g_v, g_down, g_out, g_norm_a, g_norm_m, g_gain_q, g_gain_k, loss, output, grad_input = assemble(
        gate, up, heads.reshape(8, -1, HEAD_COLUMNS), down, out, small, count, output, grad_input
    )
    return (
        output[None],
        loss.reshape(()),
        grad_input[None],
        g_norm_a.reshape(-1),
        g_q,
        g_k,
        g_v,
        g_gain_q.reshape(-1),
        g_gain_k.reshape(-1),
        g_out.reshape(-1, width),
        g_norm_m.reshape(-1),
        g_gate,
        g_up,
        g_down.reshape(-1, width),
    )


def solution(mesh):
    chips = mesh.shape["fsdp"] == 4 and mesh.shape["ctx"] == KEY_VALUE_HEADS
    return jax.shard_map(
        chip_step if chips else per_device,
        mesh=mesh,
        in_specs=(
            P("fsdp", "ctx", None),
            P("fsdp", "ctx", None),
            P("fsdp", "ctx"),
            P("fsdp", "ctx"),
            P("fsdp"),
            P("fsdp", None),
            P("fsdp", None),
            P("fsdp", None),
            P("fsdp"),
            P("fsdp"),
            P("fsdp", None),
            P("fsdp"),
            P("fsdp", None),
            P("fsdp", None),
            P("fsdp", None),
        ),
        out_specs=(
            P("fsdp", "ctx", None),
            P(),
            P("fsdp", "ctx", None),
            P("fsdp"),
            P("fsdp", None),
            P("fsdp", None),
            P("fsdp", None),
            P("fsdp"),
            P("fsdp"),
            P("fsdp", None),
            P("fsdp"),
            P("fsdp", None),
            P("fsdp", None),
            P("fsdp", None),
        ),
        check_vma=False,
    )
```

```python
from functools import partial
import math

import jax
import jax.numpy as jnp
import numpy as np
from jax import lax
from jax.experimental import pallas as pl
from jax.experimental.pallas import tpu as pltpu
from jax.sharding import PartitionSpec as P

QUERY_HEADS = 16
KEY_VALUE_HEADS = 8
HEAD_SIZE = 128


EPSILON = 1e-06


def root_mean_norm(values, norm_gain):
    return (
        values * lax.rsqrt(jnp.mean(values * values, axis=-1, keepdims=True) + EPSILON) * norm_gain
    )


def rope_tables(position_ids):
    half_width = HEAD_SIZE // 2
    freq_table = jnp.exp(
        jnp.arange(half_width, dtype=jnp.float32) * (-2.0 * math.log(1000000.0) / HEAD_SIZE)
    )
    angle_table = position_ids.astype(jnp.float32)[:, None] * freq_table[None, :]
    cosine_table = jnp.cos(angle_table)
    sine_table = jnp.sin(angle_table)
    return (
        jnp.concatenate([cosine_table, cosine_table], -1),
        jnp.concatenate([-sine_table, sine_table], -1),
    )


def apply_rotary(values, cosine_table, sine_table):
    half_width = HEAD_SIZE // 2
    swapped = jnp.concatenate([values[..., half_width:], values[..., :half_width]], -1)
    return values * cosine_table[:, None, :] + swapped * sine_table[:, None, :]


def shape_heads(cosine_table, sine_table, proj_query, projected_key, gain_q, key_gain):
    token_rows = proj_query.shape[0]
    query_rows = apply_rotary(
        root_mean_norm(proj_query.reshape(token_rows, QUERY_HEADS, HEAD_SIZE), gain_q),
        cosine_table,
        sine_table,
    )
    rows_of_keys = apply_rotary(
        root_mean_norm(projected_key.reshape(token_rows, KEY_VALUE_HEADS, HEAD_SIZE), key_gain),
        cosine_table,
        sine_table,
    )
    return (query_rows, rows_of_keys)


def swiglu(gate_proj, up_proj):
    return gate_proj / (1.0 + jnp.exp(-gate_proj)) * up_proj


def contract_rows(left_arr, right_arr):
    return lax.dot_general(
        left_arr, right_arr, (((0,), (0,)), ((), ())), preferred_element_type=jnp.float32
    )


def against(left_arr, right_arr):
    return lax.dot_general(
        left_arr, right_arr, (((1,), (1,)), ((), ())), preferred_element_type=jnp.float32
    )


def in_blocks(block_step, running, shard_portion):
    total_rows = shard_portion.shape[0]
    block_extent = 512
    block_count = total_rows // block_extent
    blocks = shard_portion.reshape((block_count, block_extent) + shard_portion.shape[1:])
    starts = jnp.arange(block_count, dtype=jnp.int32) * block_extent

    def scan_body(state, scan_item):
        return (block_step(state, scan_item[0], scan_item[1]), None)

    running, unused = lax.scan(scan_body, running, (blocks, starts))
    return running


def score_terms(
    query_rows,
    output_gradients,
    lse_heads,
    delta_heads,
    rows_of_keys,
    rows_of_values,
    query_index,
    key_index,
    score_scale,
):
    score_matrix = (
        jnp.einsum("alci,wli->lcaw", query_rows, rows_of_keys, preferred_element_type=jnp.float32)
        * score_scale
    )
    allowed = key_index[None, :] <= query_index[:, None]
    attention_probabilities = jnp.where(allowed, jnp.exp(score_matrix - lse_heads[..., None]), 0.0)
    grad_probs = jnp.einsum(
        "alci,wli->lcaw", output_gradients, rows_of_values, preferred_element_type=jnp.float32
    )
    score_gradient = (
        score_scale * attention_probabilities * (grad_probs - delta_heads[..., None])
    ).astype(jnp.bfloat16)
    return (attention_probabilities, score_gradient)


def per_device(
    hidden_in,
    teacher,
    valid,
    positions,
    norm_attn,
    w_query,
    key_projection,
    value_projection,
    gain_query,
    gain_key,
    w_out,
    norm_mlp,
    w_gate,
    w_up,
    w_down,
):
    gathered = (
        lax.all_gather(norm_attn, "fsdp", axis=0, tiled=True),
        lax.all_gather(w_query, "fsdp", axis=0, tiled=True),
        lax.all_gather(key_projection, "fsdp", axis=0, tiled=True),
        lax.all_gather(value_projection, "fsdp", axis=0, tiled=True),
        lax.all_gather(gain_query, "fsdp", axis=0, tiled=True),
        lax.all_gather(gain_key, "fsdp", axis=0, tiled=True),
        lax.all_gather(w_out, "fsdp", axis=0, tiled=True),
        lax.all_gather(norm_mlp, "fsdp", axis=0, tiled=True),
        lax.all_gather(w_gate, "fsdp", axis=0, tiled=True),
        lax.all_gather(w_up, "fsdp", axis=0, tiled=True),
        lax.all_gather(w_down, "fsdp", axis=0, tiled=True),
    )
    (
        full_norm_attn,
        full_query,
        full_key,
        full_value,
        full_gain_q,
        full_gain_k,
        full_out,
        full_norm_mlp,
        full_gate,
        full_up,
        full_down,
    ) = gathered
    grouped_heads = QUERY_HEADS // KEY_VALUE_HEADS
    score_scale = 1.0 / math.sqrt(HEAD_SIZE)
    residual = hidden_in[0].astype(jnp.float32)
    token_rows = residual.shape[0]
    query_index = lax.axis_index("ctx") * token_rows + jnp.arange(token_rows, dtype=jnp.int32)
    normed_one, norm_one_back = jax.vjp(
        root_mean_norm, residual, full_norm_attn.astype(jnp.float32)
    )
    hidden_one = normed_one.astype(jnp.bfloat16)
    proj_query = jnp.dot(hidden_one, full_query, preferred_element_type=jnp.float32)
    projected_key = jnp.dot(hidden_one, full_key, preferred_element_type=jnp.float32)
    projected_value = jnp.dot(hidden_one, full_value, preferred_element_type=jnp.float32)
    cosine_table, sine_table = rope_tables(positions[0])
    (query_per_head, heads_key), heads_back = jax.vjp(
        partial(shape_heads, cosine_table, sine_table),
        proj_query,
        projected_key,
        full_gain_q.astype(jnp.float32),
        full_gain_k.astype(jnp.float32),
    )
    query_reduced = query_per_head.astype(jnp.bfloat16).reshape(
        token_rows, KEY_VALUE_HEADS, grouped_heads, HEAD_SIZE
    )
    key_reduced = heads_key.astype(jnp.bfloat16)
    value_reduced = projected_value.astype(jnp.bfloat16).reshape(
        token_rows, KEY_VALUE_HEADS, HEAD_SIZE
    )
    key_value = jnp.stack(
        [
            key_reduced.reshape(token_rows, KEY_VALUE_HEADS * HEAD_SIZE),
            value_reduced.reshape(token_rows, KEY_VALUE_HEADS * HEAD_SIZE),
        ],
        axis=1,
    )

    def forward_block(running, shard_portion, first_row):
        run_max, run_total, run_acc = running
        rows_per_block = shard_portion.shape[0]
        rows_of_keys = shard_portion[:, 0].reshape(rows_per_block, KEY_VALUE_HEADS, HEAD_SIZE)
        rows_of_values = shard_portion[:, 1].reshape(rows_per_block, KEY_VALUE_HEADS, HEAD_SIZE)
        key_index = first_row + jnp.arange(rows_per_block, dtype=jnp.int32)
        allowed = key_index[None, :] <= query_index[:, None]
        score_matrix = (
            jnp.einsum(
                "alci,wli->lcaw", query_reduced, rows_of_keys, preferred_element_type=jnp.float32
            )
            * score_scale
        )
        score_matrix = jnp.where(allowed, score_matrix, -1e30)
        new_max = jnp.maximum(run_max, jnp.max(score_matrix, axis=-1))
        weights_part = jnp.where(allowed, jnp.exp(score_matrix - new_max[..., None]), 0.0)
        factor = jnp.exp(run_max - new_max)
        run_total = run_total * factor + jnp.sum(weights_part, axis=-1)
        run_acc = run_acc * factor[..., None] + jnp.einsum(
            "exfw,weq->exfq",
            weights_part.astype(jnp.bfloat16),
            rows_of_values,
            preferred_element_type=jnp.float32,
        )
        return (new_max, run_total, run_acc)

    start_state = (
        jnp.full((KEY_VALUE_HEADS, grouped_heads, token_rows), -1e30, jnp.float32),
        jnp.zeros((KEY_VALUE_HEADS, grouped_heads, token_rows), jnp.float32),
        jnp.zeros((KEY_VALUE_HEADS, grouped_heads, token_rows, HEAD_SIZE), jnp.float32),
    )
    run_max, run_total, run_acc = in_blocks(
        forward_block, start_state, lax.all_gather(key_value, "ctx", axis=0, tiled=True)
    )
    log_total = run_max + jnp.log(run_total)
    attn_rows = jnp.transpose(run_acc / run_total[..., None], (2, 0, 1, 3))
    attn_low = attn_rows.reshape(token_rows, QUERY_HEADS * HEAD_SIZE).astype(jnp.bfloat16)
    mid_resid = residual + jnp.dot(attn_low, full_out, preferred_element_type=jnp.float32)
    normed_two, norm_two_back = jax.vjp(
        root_mean_norm, mid_resid, full_norm_mlp.astype(jnp.float32)
    )
    hidden_two = normed_two.astype(jnp.bfloat16)
    gate_proj = jnp.dot(hidden_two, full_gate, preferred_element_type=jnp.float32)
    up_proj = jnp.dot(hidden_two, full_up, preferred_element_type=jnp.float32)
    gated, gated_back = jax.vjp(swiglu, gate_proj, up_proj)
    gated_low = gated.astype(jnp.bfloat16)
    final_rows = mid_resid + jnp.dot(gated_low, full_down, preferred_element_type=jnp.float32)
    target = teacher[0].astype(jnp.float32)
    weight_rows = valid[0].astype(jnp.float32)
    mismatch = final_rows - target
    sq_local = jnp.sum(weight_rows[:, None] * mismatch * mismatch)
    count_local = jnp.sum(weight_rows)
    sq_total, count_total = lax.psum((sq_local, count_local), ("fsdp", "ctx"))
    loss_value = sq_total / count_total
    loss_scale = token_rows * lax.axis_size("ctx") * lax.axis_size("fsdp") / 4.0
    grad_final = 2.0 * loss_scale / count_total * weight_rows[:, None] * mismatch
    grad_down_in = grad_final.astype(jnp.bfloat16)
    grad_w_down = contract_rows(gated_low, grad_down_in)
    grad_gated = against(grad_down_in, full_down)
    grad_gate_proj, grad_up_proj = gated_back(grad_gated)
    gate_low = grad_gate_proj.astype(jnp.bfloat16)
    up_low = grad_up_proj.astype(jnp.bfloat16)
    grad_w_gate = contract_rows(hidden_two, gate_low)
    grad_w_up = contract_rows(hidden_two, up_low)
    grad_hidden_two = against(gate_low, full_gate) + against(up_low, full_up)
    grad_mid_norm, grad_norm_mlp = norm_two_back(grad_hidden_two)
    grad_mid = grad_final + grad_mid_norm
    grad_branch = grad_mid.astype(jnp.bfloat16)
    grad_w_out = contract_rows(attn_low, grad_branch)
    attention_gradient = against(grad_branch, full_out).astype(jnp.bfloat16)
    attention_head_gradient = attention_gradient.reshape(
        token_rows, KEY_VALUE_HEADS, grouped_heads, HEAD_SIZE
    )
    row_delta = jnp.sum(attention_head_gradient.astype(jnp.float32) * attn_rows, axis=-1)
    delta_heads = jnp.transpose(row_delta, (1, 2, 0))
    row_stats = jnp.stack(
        [
            jnp.transpose(log_total, (2, 0, 1)).reshape(token_rows, QUERY_HEADS),
            row_delta.reshape(token_rows, QUERY_HEADS),
        ],
        axis=1,
    )

    def block_of_queries(grad_query, shard_portion, first_row):
        rows_per_block = shard_portion.shape[0]
        rows_of_keys = shard_portion[:, 0].reshape(rows_per_block, KEY_VALUE_HEADS, HEAD_SIZE)
        rows_of_values = shard_portion[:, 1].reshape(rows_per_block, KEY_VALUE_HEADS, HEAD_SIZE)
        key_index = first_row + jnp.arange(rows_per_block, dtype=jnp.int32)
        attention_probabilities, score_gradient = score_terms(
            query_reduced,
            attention_head_gradient,
            log_total,
            delta_heads,
            rows_of_keys,
            rows_of_values,
            query_index,
            key_index,
            score_scale,
        )
        return grad_query + jnp.einsum(
            "jyux,xji->ujyi", score_gradient, rows_of_keys, preferred_element_type=jnp.float32
        )

    grad_query = in_blocks(
        block_of_queries,
        jnp.zeros((token_rows, KEY_VALUE_HEADS, grouped_heads, HEAD_SIZE), jnp.float32),
        lax.all_gather(key_value, "ctx", axis=0, tiled=True),
    )
    all_stats = lax.all_gather(row_stats.astype(jnp.bfloat16), "ctx", axis=0, tiled=True).astype(
        row_stats.dtype
    )
    query_pair = jnp.stack(
        [query_reduced.reshape(token_rows, QUERY_HEADS * HEAD_SIZE), attention_gradient], axis=1
    )

    def key_block(running, shard_portion, first_row):
        grad_key, value_gradient = running
        rows_per_block = shard_portion.shape[0]
        query_rows = shard_portion[:, 0].reshape(
            rows_per_block, KEY_VALUE_HEADS, grouped_heads, HEAD_SIZE
        )
        output_gradients = shard_portion[:, 1].reshape(
            rows_per_block, KEY_VALUE_HEADS, grouped_heads, HEAD_SIZE
        )
        partial_statistics = lax.dynamic_slice_in_dim(all_stats, first_row, rows_per_block, 0)
        partial_logsumexp = jnp.transpose(
            partial_statistics[:, 0].reshape(rows_per_block, KEY_VALUE_HEADS, grouped_heads),
            (1, 2, 0),
        )
        partial_delta = jnp.transpose(
            partial_statistics[:, 1].reshape(rows_per_block, KEY_VALUE_HEADS, grouped_heads),
            (1, 2, 0),
        )
        part_index = first_row + jnp.arange(rows_per_block, dtype=jnp.int32)
        attention_probabilities, score_gradient = score_terms(
            query_rows,
            output_gradients,
            partial_logsumexp,
            partial_delta,
            key_reduced,
            value_reduced,
            part_index,
            query_index,
            score_scale,
        )
        grad_key = grad_key + jnp.einsum(
            "wzlj,lwzy->jwy", score_gradient, query_rows, preferred_element_type=jnp.float32
        )
        value_gradient = value_gradient + jnp.einsum(
            "wzlj,lwzy->jwy",
            attention_probabilities.astype(jnp.bfloat16),
            output_gradients,
            preferred_element_type=jnp.float32,
        )
        return (grad_key, value_gradient)

    key_state = (
        jnp.zeros((token_rows, KEY_VALUE_HEADS, HEAD_SIZE), jnp.float32),
        jnp.zeros((token_rows, KEY_VALUE_HEADS, HEAD_SIZE), jnp.float32),
    )
    grad_key, value_gradient = in_blocks(
        key_block, key_state, lax.all_gather(query_pair, "ctx", axis=0, tiled=True)
    )
    grad_proj_q, grad_proj_k, grad_gain_q, grad_gain_k = heads_back(
        (grad_query.reshape(token_rows, QUERY_HEADS, HEAD_SIZE), grad_key)
    )
    query_grad_low = grad_proj_q.astype(jnp.bfloat16)
    key_grad_low = grad_proj_k.astype(jnp.bfloat16)
    value_gradient_reduced = value_gradient.reshape(token_rows, KEY_VALUE_HEADS * HEAD_SIZE).astype(
        jnp.bfloat16
    )
    grad_w_query = contract_rows(hidden_one, query_grad_low)
    grad_w_key = contract_rows(hidden_one, key_grad_low)
    grad_w_value = contract_rows(hidden_one, value_gradient_reduced)
    grad_hidden_one = (
        against(query_grad_low, full_query)
        + against(key_grad_low, full_key)
        + against(value_gradient_reduced, full_value)
    )
    grad_resid_norm, grad_norm_attn = norm_one_back(grad_hidden_one)
    grad_input = grad_mid + grad_resid_norm
    grads = (
        grad_norm_attn,
        grad_w_query,
        grad_w_key,
        grad_w_value,
        grad_gain_q,
        grad_gain_k,
        grad_w_out,
        grad_norm_mlp,
        grad_w_gate,
        grad_w_up,
        grad_w_down,
    )
    shares = (
        lax.psum_scatter(grads[0], ("fsdp", "ctx"), scatter_dimension=0, tiled=True),
        lax.psum_scatter(grads[1], ("fsdp", "ctx"), scatter_dimension=0, tiled=True),
        lax.psum_scatter(grads[2], ("fsdp", "ctx"), scatter_dimension=0, tiled=True),
        lax.psum_scatter(grads[3], ("fsdp", "ctx"), scatter_dimension=0, tiled=True),
        lax.psum_scatter(grads[4], ("fsdp", "ctx"), scatter_dimension=0, tiled=True),
        lax.psum_scatter(grads[5], ("fsdp", "ctx"), scatter_dimension=0, tiled=True),
        lax.psum_scatter(grads[6], ("fsdp", "ctx"), scatter_dimension=0, tiled=True),
        lax.psum_scatter(grads[7], ("fsdp", "ctx"), scatter_dimension=0, tiled=True),
        lax.psum_scatter(grads[8], ("fsdp", "ctx"), scatter_dimension=0, tiled=True),
        lax.psum_scatter(grads[9], ("fsdp", "ctx"), scatter_dimension=0, tiled=True),
        lax.psum_scatter(grads[10], ("fsdp", "ctx"), scatter_dimension=0, tiled=True),
    )
    shares = (
        lax.all_gather(shares[0].astype(jnp.bfloat16), "ctx", axis=0, tiled=True).astype(
            jnp.float32
        ),
        lax.all_gather(shares[1].astype(jnp.bfloat16), "ctx", axis=0, tiled=True).astype(
            jnp.float32
        ),
        lax.all_gather(shares[2].astype(jnp.bfloat16), "ctx", axis=0, tiled=True).astype(
            jnp.float32
        ),
        lax.all_gather(shares[3].astype(jnp.bfloat16), "ctx", axis=0, tiled=True).astype(
            jnp.float32
        ),
        lax.all_gather(shares[4].astype(jnp.bfloat16), "ctx", axis=0, tiled=True).astype(
            jnp.float32
        ),
        lax.all_gather(shares[5].astype(jnp.bfloat16), "ctx", axis=0, tiled=True).astype(
            jnp.float32
        ),
        lax.all_gather(shares[6].astype(jnp.bfloat16), "ctx", axis=0, tiled=True).astype(
            jnp.float32
        ),
        lax.all_gather(shares[7].astype(jnp.bfloat16), "ctx", axis=0, tiled=True).astype(
            jnp.float32
        ),
        lax.all_gather(shares[8].astype(jnp.bfloat16), "ctx", axis=0, tiled=True).astype(
            jnp.float32
        ),
        lax.all_gather(shares[9].astype(jnp.bfloat16), "ctx", axis=0, tiled=True).astype(
            jnp.float32
        ),
        lax.all_gather(shares[10].astype(jnp.bfloat16), "ctx", axis=0, tiled=True).astype(
            jnp.float32
        ),
    )
    return (
        final_rows.astype(jnp.bfloat16)[None],
        loss_value,
        grad_input[None],
        shares[0],
        shares[1],
        shares[2],
        shares[3],
        shares[4],
        shares[5],
        shares[6],
        shares[7],
        shares[8],
        shares[9],
        shares[10],
    )


MESH = pl.DeviceIdType.MESH
BF16 = jnp.bfloat16
F32 = jnp.float32
GROUP = QUERY_HEADS // KEY_VALUE_HEADS
HEAD_COLUMNS = (GROUP + 2) * HEAD_SIZE
SCALE = 1.0 / math.sqrt(HEAD_SIZE)
LOG2_E = 1.0 / math.log(2.0)
VMEM_LIMIT = 60 * 1024 * 1024


class Place:
    def __init__(self):
        self.f = lax.axis_index("fsdp")
        self.c = lax.axis_index("ctx")
        self.z = self.c // 2
        self.k = self.c % 2
        self.fx = self.f + 1 - 2 * (self.f % 2)
        self.fy = (self.f + 2) % 4
        self.fd = 3 - self.f
        self.xp = (self.fx, self.c)
        self.yp = (self.fy, self.c)
        self.dp = (self.fd, self.c)
        self.sib = (self.f, self.c + 1 - 2 * self.k)

    def along_z(self, step):
        other = (self.z + step) % 4
        return other, (self.f, 2 * other + self.k)

    def along_ctx(self, step):
        other = (self.c + step) % 8
        return other, (self.f, other)


def greet(partners):
    barrier = pltpu.get_barrier_semaphore()
    for partner in partners:
        pl.semaphore_signal(barrier, inc=1, device_id=partner, device_id_type=MESH)
    pl.semaphore_wait(barrier, len(partners))


class Copies:
    def __init__(self, send, recv):
        self.send, self.recv, self.used = send, recv, 0

    def take(self, count):
        first = self.used
        self.used += count
        return first

    def at(self, index, src, dst, partner):
        return pltpu.make_async_remote_copy(
            src_ref=src,
            dst_ref=dst,
            send_sem=self.send.at[index],
            recv_sem=self.recv.at[index],
            device_id=partner,
            device_id_type=MESH,
        )

    def __call__(self, src, dst, partner):
        return self.at(self.take(1), src, dst, partner)


class Locals:
    def __init__(self, sems):
        self.sems, self.used, self.open = sems, 0, []

    def __call__(self, src, dst):
        copy = pltpu.make_async_copy(src, dst, self.sems.at[self.used])
        self.used += 1
        copy.start()
        self.open.append(copy)
        return copy

    def wait(self):
        for copy in self.open:
            copy.wait()
        self.open = []

    def take(self, count):
        first = self.used
        self.used += count
        return first

    def alone(self, src, dst):
        copy = self(src, dst)
        self.open.pop()
        return copy


def add_rows(dst, sources):
    rows = dst.shape[0]
    step = 32

    @pl.loop(0, rows // step)
    def _(i):
        part = pl.ds(pl.multiple_of(i * step, step), step)
        total = sources[0][part, :].astype(F32)
        for source in sources[1:]:
            total = total + source[part, :].astype(F32)
        dst[part, :] = total.astype(dst.dtype)


class Gather:
    def __init__(self, me, copies, local, own, buf):
        half = buf.shape[1] // 2
        a, b = pl.ds(0, half), pl.ds(half, half)
        own_a, own_b = buf.at[me.f, a], buf.at[me.f, b]
        self.local, self.own, self.slot = local, own, buf.at[me.f]
        self.a_x = copies(own.at[a], own_a, me.xp)
        self.b_y = copies(own.at[b], own_b, me.yp)
        self.b_x = copies(own.at[b], own_b, me.xp)
        self.a_y = copies(own.at[a], own_a, me.yp)
        self.on_y = copies(buf.at[me.fx, a], buf.at[me.fx, a], me.yp)
        self.on_x = copies(buf.at[me.fy, b], buf.at[me.fy, b], me.xp)

    def first(self):
        self.a_x.start()
        self.b_y.start()

    def second(self):
        self.b_x.start()
        self.a_y.start()
        self.kept = self.local.alone(self.own, self.slot)

    def relay(self):
        self.a_x.wait_recv()
        self.on_y.start()
        self.b_y.wait_recv()
        self.on_x.start()

    def finish(self):
        for copy in (self.b_x, self.a_y, self.on_y, self.on_x):
            copy.wait_recv()
        for copy in (self.a_x, self.b_y, self.b_x, self.a_y, self.on_y, self.on_x):
            copy.wait_send()
        self.kept.wait()

    def finish_half(self):
        for copy in (self.a_x, self.b_y, self.b_x, self.a_y):
            copy.wait()
        self.kept.wait()


class GatherEnd:
    def __init__(self, me, copies, local, came, held):
        half = held.shape[1] // 2
        a, b = pl.ds(0, half), pl.ds(half, half)
        self.on_y = copies(came.at[me.fx, a], held.at[me.fx, a], me.yp)
        self.on_x = copies(came.at[me.fy, b], held.at[me.fy, b], me.xp)
        self.me, self.local, self.came, self.held = me, local, came, held

    def start(self):
        self.on_y.start()
        self.on_x.start()

    def load(self):
        me = self.me
        self.loads = [self.local.alone(self.came.at[i], self.held.at[i]) for i in (me.f, me.fx, me.fy)]

    def finish(self):
        for copy in self.loads:
            copy.wait()
        self.on_y.wait()
        self.on_x.wait()


class Scatter:
    def __init__(self, me, copies, local, part, bufs):
        half = part.shape[1] // 2
        a, b = pl.ds(0, half), pl.ds(half, half)
        slot = [bufs.at[i] for i in range(10)]
        self.fwd_a, self.fwd_b, self.own_a, self.own_b = slot[0:4]
        self.rx_own, self.rx_fwd, self.ry_own, self.ry_fwd, self.r2_a, self.r2_b = slot[4:10]
        self.d_x = copies(part.at[me.fd, a], self.rx_fwd, me.xp)
        self.d_y = copies(part.at[me.fd, b], self.ry_fwd, me.yp)
        self.o_x = copies(part.at[me.fx, a], self.rx_own, me.xp)
        self.o_y = copies(part.at[me.fy, b], self.ry_own, me.yp)
        self.to_y = copies(self.fwd_a, self.r2_a, me.yp)
        self.to_x = copies(self.fwd_b, self.r2_b, me.xp)
        self.local, self.me, self.part, self.a, self.b = local, me, part, a, b

    def first(self):
        self.d_x.start()
        self.d_y.start()

    def second(self):
        self.o_x.start()
        self.o_y.start()
        me, part = self.me, self.part
        self.mine = [
            self.local.alone(part.at[me.fy, self.a], self.fwd_a),
            self.local.alone(part.at[me.fx, self.b], self.fwd_b),
            self.local.alone(part.at[me.f, self.a], self.own_a),
            self.local.alone(part.at[me.f, self.b], self.own_b),
        ]

    def relay(self):
        for copy in self.mine:
            copy.wait()
        self.d_x.wait_recv()
        add_rows(self.fwd_a, [self.fwd_a, self.rx_fwd])
        self.to_y.start()
        self.d_y.wait_recv()
        add_rows(self.fwd_b, [self.fwd_b, self.ry_fwd])
        self.to_x.start()

    def load_fwd(self):
        me, part = self.me, self.part
        self.mine = [
            self.local.alone(part.at[me.fy, self.a], self.fwd_a),
            self.local.alone(part.at[me.fx, self.b], self.fwd_b),
        ]

    def sum_fwd(self):
        for copy in self.mine:
            copy.wait()
        self.d_x.wait_recv()
        add_rows(self.fwd_a, [self.fwd_a, self.rx_fwd])
        self.d_y.wait_recv()
        add_rows(self.fwd_b, [self.fwd_b, self.ry_fwd])

    def resume(self, passed):
        me, part = self.me, self.part
        for copy in [self.local.alone(passed.at[0], self.fwd_a), self.local.alone(passed.at[1], self.fwd_b)]:
            copy.wait()
        self.to_y.start()
        self.to_x.start()
        self.o_x.start()
        self.o_y.start()
        self.mine = [
            self.local.alone(part.at[me.f, self.a], self.own_a),
            self.local.alone(part.at[me.f, self.b], self.own_b),
        ]

    def finish_resumed(self, sum_a, sum_b):
        for copy in self.mine:
            copy.wait()
        self.finish(sum_a, sum_b)

    def drain_resumed(self):
        for copy in (self.o_x, self.o_y, self.to_y, self.to_x):
            copy.wait_send()

    def finish(self, sum_a, sum_b):
        self.o_x.wait_recv()
        self.to_y.wait_recv()
        add_rows(sum_a, [self.own_a, self.rx_own, self.r2_a])
        self.o_y.wait_recv()
        self.to_x.wait_recv()
        add_rows(sum_b, [self.own_b, self.ry_own, self.r2_b])

    def drain(self):
        for copy in (self.d_x, self.d_y, self.o_x, self.o_y, self.to_y, self.to_x):
            copy.wait_send()


class LineSum:
    def __init__(self, me, copies, own, bufs):
        z, f, k = me.z, me.f, me.k
        self.z = z
        self.inner = (z == 1) | (z == 2)
        self.outer = (z == 0) | (z == 3)
        self.mine = z - 1
        self.theirs = 2 - z
        self.own, self.from_outer, self.total, self.from_inner = own, bufs.at[0:2], bufs.at[2:4], bufs.at[4]
        self.copies = copies
        self.base = copies.take(8)
        self.inner_of = (f, 2 * (1 + z // 3) + k)
        self.outer_of = (f, 2 * (3 * (z - 1)) + k)
        self.partner = (f, 2 * (3 - z) + k)

    def inward(self, half):
        return self.copies.at(
            self.base + half, self.own.at[half], self.from_outer.at[half], self.inner_of
        )

    def across(self, half):
        return self.copies.at(
            self.base + 2 + half, self.own.at[half], self.from_inner, self.partner
        )

    def back_across(self, half):
        return self.copies.at(
            self.base + 4 + half, self.total.at[half], self.total.at[half], self.partner
        )

    def outward(self, half):
        return self.copies.at(
            self.base + 6 + half, self.total.at[half], self.total.at[half], self.outer_of
        )

    def start(self):
        @pl.when(self.outer)
        def _():
            first = 1 - self.z // 3
            self.inward(first).start()
            self.inward(1 - first).start()

    def meet(self):
        @pl.when(self.inner)
        def _():
            t, m = self.theirs, self.mine
            self.inward(t).wait_recv()
            add_rows(self.own.at[t], [self.own.at[t], self.from_outer.at[t]])
            self.across(t).start()

    def close(self):
        @pl.when(self.inner)
        def _():
            m = self.mine
            self.inward(m).wait_recv()
            self.across(m).wait_recv()
            add_rows(
                self.total.at[m], [self.own.at[m], self.from_outer.at[m], self.from_inner]
            )
            self.back_across(m).start()
            self.outward(m).start()

    def spread(self):
        @pl.when(self.inner)
        def _():
            t = self.theirs
            self.back_across(t).wait_recv()
            self.outward(t).start()

    def arrive(self):
        @pl.when(self.outer)
        def _():
            self.outward(0).wait_recv()
            self.outward(1).wait_recv()

    def drain(self):
        @pl.when(self.outer)
        def _():
            self.inward(0).wait_send()
            self.inward(1).wait_send()

        @pl.when(self.inner)
        def _():
            self.across(self.theirs).wait_send()
            self.back_across(self.mine).wait_send()
            self.outward(0).wait_send()
            self.outward(1).wait_send()


HBM = pl.BlockSpec(memory_space=pl.ANY)
VM = pl.BlockSpec(memory_space=pltpu.VMEM)


def transfer(kernel, name, number, args, in_specs, outs, out_specs, scratch, copies, local):
    return pl.pallas_call(
        kernel,
        out_shape=outs,
        in_specs=in_specs,
        out_specs=out_specs,
        scratch_shapes=scratch
        + [
            pltpu.SemaphoreType.DMA((copies,)),
            pltpu.SemaphoreType.DMA((copies,)),
            pltpu.SemaphoreType.DMA((local,)),
        ],
        compiler_params=pltpu.CompilerParams(
            collective_id=number, has_side_effects=True, vmem_limit_bytes=VMEM_LIMIT
        ),
        name=name,
    )(*args)


def shape(dims, dtype):
    return jax.ShapeDtypeStruct(dims, dtype)


def assemble_kernel(
    gate, up, heads, down, out, small, count, tokens_out, tokens_grad,
    g_gate, g_up, g_q, g_k, g_v, g_down, g_out, g_norm_a, g_norm_m, g_gain_q, g_gain_k, loss, output, grad_in,
):
    for src, dst in ((gate, g_gate), (up, g_up)):
        width = src.shape[2] // 4
        for i in range(4):
            for j in range(2):
                dst[:, pl.ds((2 * i + j) * width, width)] = src[j, :, pl.ds(i * width, width)].astype(F32)
    q_size, size = GROUP * HEAD_SIZE, HEAD_SIZE
    for head in range(KEY_VALUE_HEADS):
        g_q[:, pl.ds(head * q_size, q_size)] = heads[head, :, pl.ds(0, q_size)].astype(F32)
        g_k[:, pl.ds(head * size, size)] = heads[head, :, pl.ds(q_size, size)].astype(F32)
        g_v[:, pl.ds(head * size, size)] = heads[head, :, pl.ds(q_size + size, size)].astype(F32)
    f = lax.axis_index("fsdp")
    output[...] = tokens_out[...]
    grad_in[...] = tokens_grad[...]
    g_norm_a[...] = small[pl.ds(2 * f, 2), :]
    g_norm_m[...] = small[pl.ds(8 + 2 * f, 2), :]
    part = g_gain_q.shape[1]
    lane = lax.broadcasted_iota(jnp.int32, (HEAD_SIZE, part), 0)
    column = lax.broadcasted_iota(jnp.int32, (HEAD_SIZE, part), 1)
    pick = jnp.where(lane == column + part * f, 1.0, 0.0)
    both = lax.dot_general(
        small[16:24, :], pick, (((1,), (0,)), ((), ())), preferred_element_type=F32, precision=lax.Precision.HIGHEST
    )
    g_gain_q[...] = both[0:1, :]
    g_gain_k[...] = both[1:2, :]
    loss[...] = jnp.sum(small[18:19, :], axis=1, keepdims=True) / count[0:1, 0:1]
    g_down[...] = down[...].astype(F32)
    g_out[...] = out[...].astype(F32)


def assemble(gate, up, heads, down, out, small, count, tokens_out, tokens_grad):
    steps = 4

    def cut(dims):
        return pl.BlockSpec((dims[0], dims[1] // steps, dims[2]), lambda i: (0, i, 0))

    def whole(dims):
        return pl.BlockSpec(dims, lambda i: (0,) * len(dims))

    def rows_of(a):
        return pl.BlockSpec((a.shape[0] // steps, a.shape[1]), lambda i: (i, 0))

    def flat(rows, columns):
        return pl.BlockSpec((rows // steps, columns), lambda i: (i, 0)), shape((rows, columns), F32)

    rows, width = gate.shape[1], 2 * gate.shape[2]
    all_heads = KEY_VALUE_HEADS * HEAD_SIZE
    outs = [
        flat(rows, width), flat(rows, width), flat(rows, GROUP * all_heads), flat(rows, all_heads), flat(rows, all_heads),
        (cut(down.shape), shape(down.shape, F32)), (cut(out.shape), shape(out.shape, F32)),
        (whole((2, 128)), shape((2, 128), F32)), (whole((2, 128)), shape((2, 128), F32)),
        (whole((1, 32)), shape((1, 32), F32)), (whole((1, 32)), shape((1, 32), F32)),
        (whole((1, 1)), shape((1, 1), F32)),
    ] + [(rows_of(a), shape(a.shape, a.dtype)) for a in (tokens_out, tokens_grad)]
    return pl.pallas_call(
        assemble_kernel,
        grid=(steps,),
        out_shape=[s for _, s in outs],
        in_specs=[cut(a.shape) for a in (gate, up, heads, down, out)]
        + [whole(small.shape), whole(count.shape), rows_of(tokens_out), rows_of(tokens_grad)],
        out_specs=[b for b, _ in outs],
        compiler_params=pltpu.CompilerParams(vmem_limit_bytes=VMEM_LIMIT),
        name="assemble",
    )(gate, up, heads, down, out, small, count, tokens_out, tokens_grad)


def dot_nt(a, b, **kw):
    return lax.dot_general(a, b, (((1,), (1,)), ((), ())), preferred_element_type=F32, **kw)


def dot_nn(a, b):
    return lax.dot_general(a, b, (((1,), (0,)), ((), ())), preferred_element_type=F32)


def dot_tn(a, b):
    return lax.dot_general(a, b, (((0,), (0,)), ((), ())), preferred_element_type=F32)


HIGHEST = lax.Precision.HIGHEST


class SmallSum:
    def __init__(self, me, copies, own, plane, pair, line):
        self.me, self.own, self.plane, self.pair, self.line = me, own, plane, pair, line
        self.one = [copies(own, plane.at[me.f], partner) for partner in (me.xp, me.yp, me.dp)]
        self.two = [copies(pair.at[me.k], pair.at[me.k], me.sib)]
        self.three = [
            copies(line.at[me.z], line.at[me.z], me.along_z(step)[1]) for step in (1, 2, 3)
        ]

    def first(self):
        for copy in self.one:
            copy.start()
        self.plane[self.me.f] = self.own[...]

    def second(self):
        for copy in self.one:
            copy.wait_recv()
        plane = self.plane
        self.pair[self.me.k] = (plane[0] + plane[1]) + (plane[2] + plane[3])
        self.two[0].start()

    def third(self):
        self.two[0].wait_recv()
        self.line[self.me.z] = self.pair[0] + self.pair[1]
        for copy in self.three:
            copy.start()

    def finish(self, dst):
        for copy in self.three:
            copy.wait_recv()
        line = self.line
        dst[...] = (line[0] + line[1]) + (line[2] + line[3])

    def drain(self):
        for copy in self.one + self.two + self.three:
            copy.wait_send()


class Spread:
    def __init__(self, me, copies, held, cross=True):
        self.me, self.held, self.copies, self.cross = me, held, copies, cross
        self.here, self.stride = (me.c, 2) if cross else (me.z, 1)
        self.up, self.down = copies.take(3), copies.take(3)
        if cross:
            self.cross_own, self.cross_up, self.cross_down = copies.take(1), copies.take(3), copies.take(3)

    def hop(self, base, hop, block, partner):
        ref = self.held.at[block]
        return self.copies.at(base + hop - 1, ref, ref, partner)

    def rise(self, hop):
        me = self.me
        return self.hop(self.up, hop, self.here - self.stride * (hop - 1), (me.f, me.c + 2))

    def fall(self, hop):
        me = self.me
        return self.hop(self.down, hop, self.here + self.stride * (hop - 1), (me.f, me.c - 2))

    def across(self, base, hop, block):
        return self.hop(base, hop, block, self.me.sib)

    def start(self):
        z = self.me.z

        @pl.when(z < 3)
        def _():
            self.rise(1).start()

        @pl.when(z > 0)
        def _():
            self.fall(1).start()

        if self.cross:
            self.across(self.cross_own, 1, self.me.c).start()

    def step(self, hop):
        z, c = self.me.z, self.me.c

        @pl.when(z >= hop)
        def _():
            self.rise(hop).wait_recv()
            if hop < 3:

                @pl.when(z < 3)
                def _():
                    self.rise(hop + 1).start()

            if self.cross:
                self.across(self.cross_up, hop, c - 2 * hop).start()

        @pl.when(z + hop <= 3)
        def _():
            self.fall(hop).wait_recv()
            if hop < 3:

                @pl.when(z > 0)
                def _():
                    self.fall(hop + 1).start()

            if self.cross:
                self.across(self.cross_down, hop, c + 2 * hop).start()

    def crossed(self, hop):
        z, c = self.me.z, self.me.c
        if hop == 0:
            self.across(self.cross_own, 1, c).wait_recv()
            return

        @pl.when(z >= hop)
        def _():
            self.across(self.cross_up, hop, c - 2 * hop).wait_recv()

        @pl.when(z + hop <= 3)
        def _():
            self.across(self.cross_down, hop, c + 2 * hop).wait_recv()

    def drain(self):
        z, c = self.me.z, self.me.c
        if self.cross:
            self.across(self.cross_own, 1, c).wait_send()
        for hop in (1, 2, 3):

            @pl.when((z >= hop - 1) & (z < 3))
            def _(hop=hop):
                self.rise(hop).wait_send()

            @pl.when((z + hop - 1 <= 3) & (z > 0))
            def _(hop=hop):
                self.fall(hop).wait_send()

            if not self.cross:
                continue

            @pl.when(z >= hop)
            def _(hop=hop):
                self.across(self.cross_up, hop, c - 2 * hop).wait_send()

            @pl.when(z + hop <= 3)
            def _(hop=hop):
                self.across(self.cross_down, hop, c + 2 * hop).wait_send()


def half_turn(values):
    return pltpu.roll(values, HEAD_SIZE // 2, 1)


def rotary_tables(position_rows, freq, cosines, sines, at):
    columns = jnp.transpose(position_rows)
    lane = lax.broadcasted_iota(jnp.int32, (HEAD_SIZE, HEAD_SIZE), 1)
    first = lane < HEAD_SIZE // 2
    for r in range(2):
        angle = columns[:, r : r + 1] * freq
        turns = jnp.floor(angle * (2.0 / math.pi) + 0.5)
        rest = ((angle - turns * 1.5703125) - turns * 4.837512969970703125e-04) - turns * 7.549789954891882e-08
        square = rest * rest
        sine = rest + rest * square * (
            -1.6666654611e-01 + square * (8.3321608736e-03 - square * 1.9515295891e-04)
        )
        cosine = 1.0 + square * (
            -0.5 + square * (4.166664568298827e-02 + square * (-1.388731625493765e-03 + square * 2.443315711809948e-05))
        )
        quarter = (turns.astype(jnp.int32) + jnp.where(first, 0, 3)) & 3
        odd = (quarter & 1) == 1
        value = jnp.where(odd, sine, cosine)
        value = jnp.where((quarter == 1) | (quarter == 2), -value, value)
        other = half_turn(value)
        rows = pl.ds(pl.multiple_of(at + r * 128, 128), 128)
        cosines[rows, :] = jnp.where(first, value, other)
        sines[rows, :] = jnp.where(first, -other, value)


def head_norm(u):
    return lax.rsqrt(jnp.mean(u * u, axis=-1, keepdims=True) + EPSILON)


def small_arguments(f, positions, valid, norm_a, norm_m, gain_q, gain_k, misc, gains, count):
    misc[...] = jnp.zeros_like(misc)
    for r in range(2):
        misc[r : r + 1, :] = positions[0:1, pl.ds(r * 128, 128)].astype(F32)
        misc[r + 2 : r + 3, :] = valid[0:1, pl.ds(r * 128, 128)].astype(F32)
    gains[...] = jnp.zeros_like(gains)
    for i, norm in enumerate((norm_a, norm_m)):
        gains[2 * i : 2 * i + 2, :] = norm[...].astype(F32).reshape(2, 128)
    size = gain_q.shape[0]
    lane = lax.broadcasted_iota(jnp.int32, (1, HEAD_SIZE), 1)
    for r, gain in enumerate((gain_q, gain_k)):
        wide = jnp.concatenate([gain[...].astype(F32).reshape(1, size)] * (HEAD_SIZE // size), axis=1)
        gains[r + 4 : r + 5, :] = jnp.where(lane // size == f, wide, 0.0)
    count[...] = jnp.broadcast_to(jnp.sum(valid[...].astype(F32), axis=1, keepdims=True), count.shape)


def kernel_forward(
    wq, wk, wv, wo, wg, wu, wd, x, t, positions, valid, norm_a, norm_m, gain_qs, gain_ks, freq,
    x_pair, t_pair, misc_all, gains_all, count_out,
    w_head_out, wo_all, wo_rest, wg_all, wu_all, wd_all,
    h_out, proj_out, qkv_out, att_out, lse_out, cos_out, sin_out, att_all,
    w_head, h_all, proj, qkv, att, lse, cosines, sines, x_all, values, own_h, own_o, own_p, own_g, own_u, own_d, gain_row, misc, gains, count, plane, pair, line,
    send, recv, lsem,
):
    me = Place()
    z, k, f, c = me.z, me.k, me.f, me.c
    rows = x.shape[0]
    small_arguments(f, positions, valid, norm_a, norm_m, gain_qs, gain_ks, misc, gains, count)
    greet([me.xp, me.yp, me.dp, me.sib] + [me.along_z(step)[1] for step in (1, 2, 3)])
    copies, local = Copies(send, recv), Locals(lsem)
    q_size = GROUP * HEAD_SIZE
    head_loads = [
        local.alone(wq.at[:, pl.ds(pl.multiple_of(c * q_size, 128), q_size)], own_h.at[:, pl.ds(0, q_size)]),
        local.alone(wk.at[:, pl.ds(pl.multiple_of(c * HEAD_SIZE, 128), HEAD_SIZE)], own_h.at[:, pl.ds(q_size, HEAD_SIZE)]),
        local.alone(
            wv.at[:, pl.ds(pl.multiple_of(c * HEAD_SIZE, 128), HEAD_SIZE)],
            own_h.at[:, pl.ds(q_size + HEAD_SIZE, HEAD_SIZE)],
        ),
    ]
    width = wg.shape[1] // 8
    local(wd.at[pl.ds(pl.multiple_of(k * own_d.shape[0], 16), own_d.shape[0])], own_d)
    part, quarter = own_o.shape[0], own_p.shape[0]
    first_row = k * (part + 4 * quarter)
    local(wo.at[pl.ds(pl.multiple_of(first_row, 16), part)], own_o)
    local(wo.at[pl.ds(pl.multiple_of(first_row + part + z * quarter, 16), quarter)], own_p)
    for src, own in ((wg, own_g), (wu, own_u)):
        for i in range(4):
            at = pl.ds(pl.multiple_of((2 * i + k) * width, 128), width)
            local(src.at[:, at], own.at[:, pl.ds(i * width, width)])
    small = SmallSum(me, copies, count, plane, pair, line)
    small.first()
    gain_sends = [copies(gains, gains_all.at[f], partner) for partner in (me.xp, me.yp, me.dp)]
    misc_sends = [
        copies(misc, misc_all.at[k, z], me.along_z(step)[1]) for step in (1, 2, 3)
    ]
    for copy in misc_sends + gain_sends:
        copy.start()
    x_all[c] = x[...]
    spread = Spread(me, copies, x_all)
    spread.start()
    pair_sends = [copies(t, t_pair.at[k], me.sib)]
    pair_sends[0].start()
    for copy in head_loads:
        copy.wait()
    head = Gather(me, copies, local, own_h, w_head)
    piece = Gather(me, copies, local, own_p, wo_rest.at[z])
    chain = Spread(me, copies, wo_rest, False)
    head.first()
    head.second()
    local.wait()
    piece.first()
    piece.second()
    out = Gather(me, copies, local, own_o, wo_all)
    gate = Gather(me, copies, local, own_g, wg_all)
    up = Gather(me, copies, local, own_u, wu_all)
    down = Gather(me, copies, local, own_d, wd_all)
    keep = [local.alone(t, t_pair.at[k])]
    for copy in misc_sends:
        copy.wait_recv()
    misc_all[k, z] = misc[...]
    gains_all[f] = gains[...]
    misc_pass = copies(misc_all.at[k], misc_all.at[k], me.sib)
    misc_pass.start()
    small.second()
    for copy in gain_sends:
        copy.wait_recv()
    for i in range(4):
        for r in range(2):
            gain_row[0:1, pl.ds((2 * i + r) * 128, 128)] = gains_all[i, r : r + 1, :]
    gain_q = (gains_all[0, 4:5, :] + gains_all[1, 4:5, :]) + (gains_all[2, 4:5, :] + gains_all[3, 4:5, :])
    gain_k = (gains_all[0, 5:6, :] + gains_all[1, 5:6, :]) + (gains_all[2, 5:6, :] + gains_all[3, 5:6, :])
    head.relay()
    piece.relay()
    for gather in (out, gate, up, down):
        gather.first()
    for gather in (out, gate, up, down):
        gather.second()
    misc_pass.wait_recv()
    small.third()

    @pl.loop(0, 8)
    def _(i):
        rotary_tables(
            misc_all[i % 2, i // 2], freq[0:1, :], cosines, sines, pl.multiple_of(i * 256, 256)
        )

    head.finish()
    spread.step(1)

    def project(block):
        @pl.loop(0, 2)
        def _(u):
            piece = 2 * block + u
            at = pl.ds(pl.multiple_of(piece * rows, rows), rows)
            xin = x_all[piece].astype(F32)
            r = lax.rsqrt(jnp.mean(xin * xin, axis=-1, keepdims=True) + EPSILON)
            h = (xin * r * gain_row[0:1, :]).astype(BF16)
            h_all[at, :] = h
            p = dot_nn(h, w_head[...].reshape(w_head.shape[0] * w_head.shape[1], w_head.shape[2]))
            cosine, sine = cosines[at, :], sines[at, :]
            for g in range(GROUP + 1):
                lanes = slice(g * HEAD_SIZE, (g + 1) * HEAD_SIZE)
                one = p[:, lanes]
                proj[at, lanes] = one
                one = one * head_norm(one) * (gain_q if g < GROUP else gain_k)
                qkv[at, lanes] = (one * cosine + half_turn(one) * sine).astype(BF16)
            qkv[at, (GROUP + 1) * HEAD_SIZE :] = p[:, (GROUP + 1) * HEAD_SIZE :].astype(BF16)

    way = 1 - 2 * (z // 2)
    spread.crossed(0)
    project(z)
    spread.step(2)
    piece.finish()
    chain.start()
    out.relay()
    spread.crossed(1)
    spread.step(3)
    gate.relay()
    spread.crossed(2)
    spread.crossed(3)

    @pl.loop(1, 4)
    def _(step):
        project((z + way * step + 4) % 4)

    chain.step(1)
    for src, dst in (
        (w_head, w_head_out), (h_all, h_out), (proj, proj_out), (qkv, qkv_out), (cosines, cos_out), (sines, sin_out)
    ):
        keep.append(local.alone(src, dst))
    values[:, 0:HEAD_SIZE] = qkv[:, (GROUP + 1) * HEAD_SIZE :]
    values[:, HEAD_SIZE:] = jnp.ones((qkv.shape[0], HEAD_SIZE), BF16)
    base = copies.take(4)
    block = 2 * rows
    for step in (1, 2, 3, 0):
        to, partner = me.along_z(step)
        attend_rows(qkv, values, att, lse, to, block)
        block_rows = att.at[pl.ds(pl.multiple_of(to * block, block), block)]
        keep.append(local.alone(block_rows, att_out.at[pl.ds(pl.multiple_of(to * block, block), block)]))
        place = att_all.at[:, pl.ds(pl.multiple_of(z * q_size, 128), q_size)]
        if step:
            copy = pltpu.make_async_remote_copy(
                src_ref=block_rows, dst_ref=place, send_sem=send.at[base + step], recv_sem=recv.at[base + step],
                device_id=partner, device_id_type=MESH,
            )
            copy.start()
            keep.append(copy)
        else:
            keep.append(local.alone(block_rows, place))
        if step in (1, 2):
            chain.step(step + 1)
    small.finish(count_out)
    keep.append(local.alone(lse, lse_out))
    for i in range(2):
        keep.append(local.alone(x_all.at[2 * z + i], x_pair.at[i]))
    for gather in (out, gate):
        gather.finish()
    chain.drain()
    for gather in (up, down):
        gather.finish_half()
    for copy in pair_sends + [misc_pass]:
        copy.wait_send()
    pair_sends[0].wait_recv()
    for copy in misc_sends + gain_sends:
        copy.wait_send()
    for copy in keep:
        copy.wait()
    spread.drain()
    small.drain()


def forward(wq, wk, wv, wo, wg, wu, wd, x, t, *small):
    rows, width = x.shape
    tokens = 8 * rows
    row = wq.shape[0]
    half_ff = wg.shape[1] // 2
    out_rows, down_rows = wo.shape[0] // 2, wd.shape[0] // 2
    return transfer(
        kernel_forward, "forward", 1,
        (wq, wk, wv, wo, wg, wu, wd, x, t) + small,
        [HBM] * 7 + [VM] * 9,
        [
            shape((2, rows, width), BF16),
            shape((2, rows, width), BF16),
            shape((2, 4, 8, 128), F32),
            shape((4, 8, 128), F32),
            shape((8, 128), F32),
            shape((4, row, HEAD_COLUMNS), BF16),
            shape((4, out_rows // 2, width), BF16),
            shape((4, 4, out_rows // 8, width), BF16),
            shape((4, row, half_ff), BF16),
            shape((4, row, half_ff), BF16),
            shape((4, down_rows, width), BF16),
            shape((tokens, width), BF16),
            shape((tokens, (GROUP + 1) * HEAD_SIZE), F32),
            shape((tokens, HEAD_COLUMNS), BF16),
            shape((tokens, GROUP * HEAD_SIZE), BF16),
            shape((GROUP, 8, tokens), F32),
            shape((tokens, HEAD_SIZE), F32),
            shape((tokens, HEAD_SIZE), F32),
            shape((2 * rows, 4 * GROUP * HEAD_SIZE), BF16),
        ],
        [HBM] * 2 + [VM] * 3 + [HBM] * 14,
        [
            pltpu.VMEM((4, row, HEAD_COLUMNS), BF16),
            pltpu.VMEM((tokens, width), BF16),
            pltpu.VMEM((tokens, (GROUP + 1) * HEAD_SIZE), F32),
            pltpu.VMEM((tokens, HEAD_COLUMNS), BF16),
            pltpu.VMEM((tokens, GROUP * HEAD_SIZE), BF16),
            pltpu.VMEM((GROUP, 8, tokens), F32),
            pltpu.VMEM((tokens, HEAD_SIZE), F32),
            pltpu.VMEM((tokens, HEAD_SIZE), F32),
            pltpu.VMEM((8, rows, width), BF16),
            pltpu.VMEM((tokens, 2 * HEAD_SIZE), BF16),
            pltpu.VMEM((row, HEAD_COLUMNS), BF16),
            pltpu.VMEM((out_rows // 2, width), BF16),
            pltpu.VMEM((out_rows // 8, width), BF16),
            pltpu.VMEM((row, half_ff), BF16),
            pltpu.VMEM((row, half_ff), BF16),
            pltpu.VMEM((down_rows, width), BF16),
            pltpu.VMEM((8, width), F32),
            pltpu.VMEM((8, 128), F32),
            pltpu.VMEM((8, 128), F32),
            pltpu.VMEM((8, 128), F32),
            pltpu.VMEM((4, 8, 128), F32),
            pltpu.VMEM((2, 8, 128), F32),
            pltpu.VMEM((4, 8, 128), F32),
        ],
        7 + 3 + 3 + 13 + 1 + 30 + 6 + 6 + 1 + 4, 3 + 3 + 8 + 6 + 1 + 1 + 2 + 6 + 4 + 1,
    )


def attend_rows(qkv, values, att, lse, i, block):
    rows = pl.ds(pl.multiple_of(i * block, block), block)
    k_at = pl.ds(GROUP * HEAD_SIZE, HEAD_SIZE)
    row = lax.broadcasted_iota(jnp.int32, (block, block), 0)
    column = lax.broadcasted_iota(jnp.int32, (block, block), 1)
    for g in range(GROUP):
        q = qkv[rows, pl.ds(g * HEAD_SIZE, HEAD_SIZE)]

        def part(j, acc, q=q):
            keys = pl.ds(pl.multiple_of(j * block, block), block)
            e = jnp.exp2(dot_nt(q, qkv[keys, k_at]) * (SCALE * LOG2_E))
            return acc + dot_nn(e.astype(BF16), values[keys, :])

        acc = lax.fori_loop(0, i, part, jnp.zeros((block, 2 * HEAD_SIZE), F32))
        e = jnp.exp2(dot_nt(q, qkv[rows, k_at]) * (SCALE * LOG2_E))
        acc = acc + dot_nn(jnp.where(column <= row, e, 0.0).astype(BF16), values[rows, :])
        total = acc[:, HEAD_SIZE:]
        att[rows, pl.ds(g * HEAD_SIZE, HEAD_SIZE)] = (acc[:, :HEAD_SIZE] / total).astype(BF16)
        mean = jnp.full((8, HEAD_SIZE), 1.0 / HEAD_SIZE, F32)
        lse[g, :, rows] = dot_nt(mean, jnp.log(total), precision=HIGHEST)


def kernel_middle(
    att_in, wo_in, wo_more, wg_in, wu_in, wd_in, x_in, t_in, misc_all, gains_all, count,
    output, g_out, p_gate, p_up, p_out, down_sum, gate_pass, g_x2_own, small,
    att, wo, wg, wu, wd, x, t, x2, h2, gate, up, mid, g_gate, g_up, fin, g_fin, g_dn, g_a,
    send_1, recv_1, send_2, recv_2, send_3, recv_3, p_down, p_g, p_u, p_o, g_ob, sc_d, sum_d, sc_g,
    gain_row, valid, loss_row, gain_sum,
    send, recv, lsem, loss_scale,
):
    me = Place()
    z, k = me.z, me.k
    tokens, width = att.shape
    rows = tokens // 2
    greet([me.xp, me.yp, me.sib] + [me.along_z(step)[1] for step in (1, 2, 3)])
    copies, local = Copies(send, recv), Locals(lsem)
    loads = [
        local.alone(src, dst)
        for src, dst in (
            (att_in, att), (x_in, x), (wg_in, wg), (t_in, t)
        )
    ]
    part, quarter = wo_in.shape[1], wo_more.shape[2]
    local(wo_in, wo.at[:, pl.ds(0, part)])
    for i in range(4):
        local(wo_more.at[i], wo.at[:, pl.ds(part + i * quarter, quarter)])
    ends = [GatherEnd(me, copies, local, wu_in, wu), GatherEnd(me, copies, local, wd_in, wd)]
    for entry in ends:
        entry.start()
    for entry in ends:
        entry.load()
    for i in range(4):
        for r in range(2):
            gain_row[0:1, pl.ds((2 * i + r) * 128, 128)] = gains_all[i, r + 2 : r + 3, :]
    for u in range(2):
        columns = jnp.transpose(misc_all[u, z])
        for r in range(2):
            valid[pl.ds(u * rows + r * 128, 128), :] = jnp.broadcast_to(columns[:, r + 2 : r + 3], (128, 128))
    small[...] = jnp.zeros_like(small)
    loss_row[...] = jnp.zeros_like(loss_row)
    gain_sum[...] = jnp.zeros_like(gain_sum)
    step = 64
    bases = [copies.take(4) for _ in range(3)]

    def crossing(which, i, src, dst):
        at = pl.ds(pl.multiple_of(i * 256, 256), 256)
        return copies.at(bases[which] + i, src.at[:, at], dst.at[:, at], me.sib)

    def flat(ref, at):
        value = ref[:, :, at]
        return value.reshape(value.shape[0] * value.shape[1], value.shape[2])

    def strip(i, size):
        return pl.ds(pl.multiple_of(i * size, size), size)

    loads[0].wait()
    local.wait()

    @pl.loop(0, 4)
    def _(i):
        at = strip(i, 256)
        send_1[:, at] = dot_nn(att[...], flat(wo, at)).astype(BF16)
        crossing(0, i, send_1, recv_1).start()

    for copy in loads[1:3]:
        copy.wait()
    for i in range(4):
        crossing(0, i, send_1, recv_1).wait_recv()

    @pl.loop(0, tokens // step)
    def _(i):
        at = strip(i, step)
        value = x[at, :].astype(F32) + (send_1[at, :].astype(F32) + recv_1[at, :].astype(F32))
        x2[at, :] = value
        r = lax.rsqrt(jnp.mean(value * value, axis=-1, keepdims=True) + EPSILON)
        h2[at, :] = (value * r * gain_row[0:1, :]).astype(BF16)

    @pl.loop(0, gate.shape[1] // 512)
    def _(i):
        at = strip(i, 512)
        gate[:, at] = dot_nn(h2[...], flat(wg, at))

    ends[0].finish()

    @pl.loop(0, gate.shape[1] // 512)
    def _(i):
        at = strip(i, 512)
        a = gate[:, at]
        b = dot_nn(h2[...], flat(wu, at))
        up[:, at] = b
        mid[:, at] = (a / (1.0 + jnp.exp(-a)) * b).astype(BF16)

    ends[1].finish()
    loads[3].wait()

    @pl.loop(0, 4)
    def _(i):
        at = strip(i, 256)
        send_2[:, at] = dot_nn(mid[...], flat(wd, at)).astype(BF16)
        crossing(1, i, send_2, recv_2).start()

    for i in range(4):
        crossing(1, i, send_2, recv_2).wait_recv()
    factor = 2.0 * loss_scale / count[0:1, 0:1]

    @pl.loop(0, tokens // step)
    def _(i):
        at = strip(i, step)
        value = x2[at, :] + (send_2[at, :].astype(F32) + recv_2[at, :].astype(F32))
        fin[at, :] = value.astype(BF16)
        miss = value - t[at, :].astype(F32)
        weighted = valid[at, 0:1] * miss
        loss_row[0:1, :] += jnp.sum(weighted * miss, axis=0, keepdims=True)
        g = factor * weighted
        g_fin[at, :] = g
        g_dn[at, :] = g.astype(BF16)

    writes = [local.alone(fin.at[pl.ds(pl.multiple_of(k * rows, rows), rows)], output)]
    down_rows = p_down.shape[1]

    @pl.loop(0, 4)
    def _(i):
        p_down[i] = dot_tn(mid[:, strip(i, down_rows)], g_dn[...]).astype(BF16)

    s_down = Scatter(me, copies, local, p_down, sc_d)
    s_down.first()
    s_down.second()

    @pl.loop(0, 4)
    def _(i):
        at = strip(i, down_rows)
        g = dot_nt(g_dn[...], wd[i])
        a, b = gate[:, at], up[:, at]
        s = 1.0 / (1.0 + jnp.exp(-a))
        g_gate[:, at] = (g * b * s * (1.0 + a * (1.0 - s))).astype(BF16)
        g_up[:, at] = (g * a * s).astype(BF16)

    @pl.loop(0, 4)
    def _(i):
        at = strip(i, 256)
        send_3[:, at] = (dot_nt(g_gate[...], wg[i]) + dot_nt(g_up[...], wu[i])).astype(BF16)
        crossing(2, i, send_3, recv_3).start()

    for i in range(4):
        crossing(2, i, send_3, recv_3).wait_recv()

    @pl.loop(0, tokens // step)
    def _(i):
        at = strip(i, step)
        g = send_3[at, :].astype(F32) + recv_3[at, :].astype(F32)
        value = x2[at, :]
        r = lax.rsqrt(jnp.mean(value * value, axis=-1, keepdims=True) + EPSILON)
        n = value * r
        gain_sum[0:1, :] += jnp.sum(g * n, axis=0, keepdims=True)
        g = g * gain_row[0:1, :]
        g = g_fin[at, :] + r * (g - n * jnp.mean(g * n, axis=-1, keepdims=True))
        g_fin[at, :] = g
        g_a[at, :] = g.astype(BF16)

    writes.append(local.alone(g_fin.at[pl.ds(pl.multiple_of(k * rows, rows), rows)], g_x2_own))
    go_base = copies.take(4)
    go_sends = []
    for turn in (2, 1, 3, 0):
        to, partner = me.along_z(turn)
        at = strip(to, 256)
        g_ob[:, at] = dot_nt(g_a[...], wo[to]).astype(BF16)
        place = g_out.at[pl.ds(pl.multiple_of(z * tokens, tokens), tokens)]
        if turn:
            go_sends.append(
                pltpu.make_async_remote_copy(
                    src_ref=g_ob.at[:, at], dst_ref=place, send_sem=send.at[go_base + to],
                    recv_sem=recv.at[go_base + z], device_id=partner, device_id_type=MESH,
                )
            )
            go_sends[-1].start()
        else:
            writes.append(local.alone(g_ob.at[:, at], place))
    s_down.relay()

    @pl.loop(0, 4)
    def _(i):
        p_g[i] = dot_tn(h2[:, strip(i, 256)], g_gate[...]).astype(BF16)

    s_gate = Scatter(me, copies, local, p_g, sc_g)
    s_gate.first()
    s_gate.load_fwd()
    writes.append(local.alone(p_g, p_gate))

    @pl.loop(0, 4)
    def _(i):
        p_u[i] = dot_tn(h2[:, strip(i, 256)], g_up[...]).astype(BF16)

    writes.append(local.alone(p_u, p_up))

    @pl.loop(0, 4)
    def _(i):
        p_o[i] = dot_tn(att[:, strip(i, 256)], g_a[...]).astype(BF16)

    writes.append(local.alone(p_o, p_out))
    for j in range(8):
        small[j + 8 : j + 9, :] = 0.5 * gain_sum[0:1, pl.ds(j * 128, 128)]
        small[18:19, :] += 0.5 * loss_row[0:1, pl.ds(j * 128, 128)]
    s_down.finish(sum_d.at[0], sum_d.at[1])
    writes.append(local.alone(sum_d, down_sum))
    s_gate.sum_fwd()
    writes.append(local.alone(sc_g.at[0:2], gate_pass))
    for copy in writes:
        copy.wait()
    for turn in (1, 2, 3):
        other, partner = me.along_z(turn)
        place = g_out.at[pl.ds(pl.multiple_of(other * tokens, tokens), tokens)]
        pltpu.make_async_remote_copy(
            src_ref=place, dst_ref=place, send_sem=send.at[go_base + other],
            recv_sem=recv.at[go_base + other], device_id=partner, device_id_type=MESH,
        ).wait_recv()
    for copy in go_sends:
        copy.wait_send()
    for which, src, dst in ((0, send_1, recv_1), (1, send_2, recv_2), (2, send_3, recv_3)):
        for i in range(4):
            crossing(which, i, src, dst).wait_send()
    s_down.drain()
    s_gate.d_x.wait_send()
    s_gate.d_y.wait_send()


def middle(att, wo, wo_more, wg, wu, wd, x, t, misc_all, gains_all, count, loss_scale):
    tokens, width = att.shape
    rows = tokens // 2
    hidden = wg.shape[2]

    def bf(*dims):
        return pltpu.VMEM(dims, BF16)

    def held(a):
        return pltpu.VMEM(a.shape, a.dtype)

    def wide(*dims):
        return pltpu.VMEM(dims, F32)

    p_down, p_gate, p_out = (4, hidden // 4, width), (4, width // 4, hidden), (4, width // 4, width)
    return transfer(
        partial(kernel_middle, loss_scale=loss_scale), "middle", 3,
        (att, wo, wo_more, wg, wu, wd, x.reshape(tokens, width), t.reshape(tokens, width), misc_all, gains_all, count),
        [HBM] * 8 + [VM] * 3,
        [
            shape((rows, width), BF16), shape((4 * tokens, width // 4), BF16),
            shape(p_gate, BF16), shape(p_gate, BF16), shape(p_out, BF16),
            shape((2, hidden // 8, width), BF16), shape((2, width // 8, hidden), BF16),
            shape((rows, width), F32), shape((24, 128), F32),
        ],
        [HBM] * 8 + [VM],
        [held(att), bf(wo.shape[0], 2 * wo.shape[1], width)] + [held(a) for a in (wg, wu, wd)]
        + [bf(tokens, width)] * 2
        + [wide(tokens, width), bf(tokens, width), wide(tokens, hidden), wide(tokens, hidden)]
        + [bf(tokens, hidden)] * 3
        + [bf(tokens, width), wide(tokens, width), bf(tokens, width), bf(tokens, width)]
        + [bf(tokens, width)] * 6
        + [bf(*p_down), bf(*p_gate), bf(*p_gate), bf(*p_out), bf(tokens, width)]
        + [bf(10, hidden // 8, width), bf(2, hidden // 8, width), bf(10, width // 8, hidden)]
        + [wide(8, width), wide(tokens, 128), wide(8, width), wide(8, width)],
        12 + 6 + 4 + 6 + 4, 4 + 5 + 6 + 9 + 4 + 2,
    )


def head_back(g, u, cosine, sine, gain):
    g = g * cosine + half_turn(g * sine)
    r = head_norm(u)
    n = u * r
    g_gain = jnp.sum(g * n, axis=0, keepdims=True)
    g = g * gain
    return r * (g - n * jnp.mean(g * n, axis=-1, keepdims=True)), g_gain


def kernel_backward(
    g_o, gate_pass, down_sum, p_gate, p_up, p_out,
    qkv_in, att_in, lse_in, proj_in, cos_in, sin_in, h_in, w_in,
    x, g_x2, gains_all, small,
    down_tot, gate_tot, up_tot, out_tot, head_tot, grad_in, small_tot,
    g_out, qkv, att, lse, proj, cosines, sines, h_all, w_head, g_proj, g_k, g_v, p_head,
    gh_send, gh_sib, gh_own, gh_in, gain_row, work, plane, pair, line,
    sc_g, sc_u, sc_o, sc_h, own_d, own_g, own_u, own_o, line_d, line_g, line_u, line_o,
    send, recv, lsem,
):
    me = Place()
    z, k, f, c = me.z, me.k, me.f, me.c
    rows = x.shape[0]
    block = 2 * rows
    greet([me.xp, me.yp, me.dp, me.sib] + [me.along_z(step)[1] for step in (1, 2, 3)])
    copies, local = Copies(send, recv), Locals(lsem)
    size, q_size = HEAD_SIZE, GROUP * HEAD_SIZE

    for src, dst in ((g_o, g_out), (qkv_in, qkv), (att_in, att), (lse_in, lse), (proj_in, proj), (cos_in, cosines), (sin_in, sines)):
        local(src, dst)
    late = [local.alone(w_in, w_head)]
    h_base = local.take(4)

    def h_load(i):
        columns = pl.ds(pl.multiple_of(i * rows, rows), rows)
        return pltpu.make_async_copy(h_in.at[:, columns], h_all.at[i % 2], lsem.at[h_base + i])

    h_load(0).start()
    h_load(1).start()
    s_gate = Scatter(me, copies, local, p_gate, sc_g)
    s_up = Scatter(me, copies, local, p_up, sc_u)
    s_out = Scatter(me, copies, local, p_out, sc_o)
    s_head = Scatter(me, copies, local, p_head, sc_h)
    s_gate.resume(gate_pass)
    own_down = local.alone(down_sum, own_d)
    lines = [
        LineSum(me, copies, own, bufs)
        for own, bufs in ((own_d, line_d), (own_g, line_g), (own_u, line_u), (own_o, line_o))
    ]
    l_down, l_gate, l_up, l_out = lines
    totals = (down_tot, gate_tot, up_tot, out_tot)
    swap_base = copies.take(8)
    swaps, writes = [], []

    def finish(i):
        lines[i].arrive()
        half = lines[i].total.shape[1]
        for j in range(2):
            dst = totals[i].at[k, pl.ds(j * half, half)]
            copy = copies.at(swap_base + 2 * i + j, lines[i].total.at[j], dst, me.sib)
            copy.start()
            swaps.append(copy)
            writes.append(local.alone(lines[i].total.at[j], dst))

    def scattered(scatter, entry, own):
        scatter.finish(own.at[0], own.at[1])
        entry.start()

    own_down.wait()
    l_down.start()
    work[...] = small[...]
    for i in range(4):
        for r in range(2):
            gain_row[0:1, pl.ds((2 * i + r) * 128, 128)] = gains_all[i, r : r + 1, :]
    gain_q = (gains_all[0, 4:5, :] + gains_all[1, 4:5, :]) + (gains_all[2, 4:5, :] + gains_all[3, 4:5, :])
    gain_k = (gains_all[0, 5:6, :] + gains_all[1, 5:6, :]) + (gains_all[2, 5:6, :] + gains_all[3, 5:6, :])
    k_at = pl.ds(q_size, size)
    v_at = pl.ds(q_size + size, size)
    g_k[...] = jnp.zeros_like(g_k)
    g_v[...] = jnp.zeros_like(g_v)
    key = lax.broadcasted_iota(jnp.int32, (block, block), 0)
    query = lax.broadcasted_iota(jnp.int32, (block, block), 1)
    def queries(i):
        at = pl.ds(pl.multiple_of(i * block, block), block)
        for g in range(GROUP):
            head = pl.ds(g * size, size)
            q = qkv[at, head]
            go = g_out[at, head]
            product = go.astype(F32) * att[at, head].astype(F32)
            delta = dot_nt(jnp.ones((8, size), F32), product, precision=HIGHEST)[0:1, :]
            log_sum = lse[g, 0:1, at] * LOG2_E

            def part(keys, masked, q=q, go=go, delta=delta, log_sum=log_sum):
                kk, vv = qkv[keys, k_at], qkv[keys, v_at]
                p = jnp.exp2(dot_nt(kk, q) * (SCALE * LOG2_E) - log_sum)
                if masked:
                    p = jnp.where(key <= query, p, 0.0)
                gs = (p * (dot_nt(vv, go) - delta)).astype(BF16)
                g_v[keys, :] += dot_nn(p.astype(BF16), go)
                g_k[keys, :] += dot_nn(gs, q)
                return dot_tn(gs, kk)

            def step(j, acc, part=part):
                return acc + part(pl.ds(pl.multiple_of(j * block, block), block), False)

            acc = lax.fori_loop(0, i, step, jnp.zeros((block, size), F32))
            acc = (acc + part(at, True)) * SCALE
            g_u, g_gain = head_back(acc, proj[at, head], cosines[at, :], sines[at, :], gain_q)
            g_proj[at, head] = g_u.astype(BF16)
            work[16:17, :] += g_gain

    sib_base, right_base, left_base = copies.take(4), copies.take(4), copies.take(4)
    last = (z == 0) | (z == 3)
    inner = (z == 1) | (z == 2)

    def input_part(to, mine, dst):
        at = pl.ds(pl.multiple_of((2 * to + mine) * rows, rows), rows)
        weights = w_head[...].reshape(w_head.shape[0] * w_head.shape[1], w_head.shape[2])
        dst[...] = dot_nt(g_proj[at, :], weights).astype(BF16)

    def crossing(to):
        return copies.at(sib_base + to, gh_send.at[to], gh_sib.at[to], me.sib)

    def rightward(to):
        return copies.at(right_base + to, gh_own.at[to], gh_in.at[to], (f, c + 2))

    def leftward(to):
        there = 1 - (z - to) // 2
        place = gh_in.at[to + (4 - to) * there]
        return copies.at(left_base + to, gh_own.at[to], place, (f, c - 2))

    def onward(to):
        @pl.when(to > z)
        def _():
            rightward(to).start()

        @pl.when(to < z)
        def _():
            leftward(to).start()

    def join(to):
        crossing(to).wait_recv()
        add_rows(gh_own.at[to], [gh_own.at[to], gh_sib.at[to]])

    def end_send(order):
        @pl.when(last)
        def _():
            onward(far_first(order))

    def inner_send(order):
        @pl.when(inner)
        def _():
            to = far_first(order)

            @pl.when(to > z)
            def _():
                rightward(to).wait_recv()

            @pl.when(to < z)
            def _():
                copies.at(left_base + to, gh_own.at[to], gh_in.at[to], (f, c - 2)).wait_recv()

            add_rows(gh_own.at[to], [gh_own.at[to], gh_in.at[to]])
            onward(to)

    def far_first(order):
        return order + (3 - 2 * order) * (z // 2)

    def parts_to(to):
        input_part(to, 1 - k, gh_send.at[to])
        crossing(to).start()
        input_part(to, k, gh_own.at[to])

    spread = Spread(me, copies, head_tot)
    total = SmallSum(me, copies, work, plane, pair, line)
    local.wait()
    queries(0)
    l_down.meet()
    s_up.first()
    s_up.second()
    queries(3)
    l_down.close()
    s_gate.finish_resumed(own_g.at[0], own_g.at[1])
    l_gate.start()
    queries(2)
    for copy in late:
        copy.wait()
    l_gate.meet()
    l_down.spread()
    queries(1)

    @pl.loop(0, 4)
    def _(i):
        at = pl.ds(pl.multiple_of(i * block, block), block)
        g_u, g_gain = head_back(g_k[at, :] * SCALE, proj[at, k_at], cosines[at, :], sines[at, :], gain_k)
        g_proj[at, k_at] = g_u.astype(BF16)
        g_proj[at, v_at] = g_v[at, :].astype(BF16)
        work[17:18, :] += g_gain

    parts_to(far_first(3))
    s_up.relay()
    parts_to(far_first(2))
    l_gate.close()
    s_out.first()
    s_out.second()

    @pl.loop(0, 4)
    def _(i):
        h_load(i).wait()
        p_head[i] = dot_tn(h_all[i % 2], g_proj[...]).astype(BF16)

        @pl.when(i < 2)
        def _():
            h_load(i + 2).start()

    join(far_first(3))
    end_send(3)
    parts_to(far_first(0))
    inner_send(3)
    l_gate.spread()
    scattered(s_up, l_up, own_u)
    l_up.meet()
    join(far_first(2))
    parts_to(far_first(1))
    s_head.first()
    s_head.second()
    join(far_first(0))
    inner_send(0)
    s_head.relay()
    s_head.finish(head_tot.at[c, 0], head_tot.at[c, 1])
    spread.start()
    end_send(2)
    l_up.close()
    s_out.relay()
    finish(1)
    spread.step(1)
    scattered(s_out, l_out, own_o)
    l_out.meet()
    join(far_first(1))
    l_up.spread()
    inner_send(2)
    spread.step(2)
    l_out.close()
    finish(0)
    work[0:8, :] = jnp.zeros((8, 128), F32)

    @pl.when(z > 0)
    def _():
        rightward(z).wait_recv()

    @pl.when(z < 3)
    def _():
        copies.at(left_base + z, gh_own.at[z], gh_in.at[4], (f, c - 2)).wait_recv()

    @pl.when(z == 0)
    def _():
        gh_in[0] = jnp.zeros(gh_in.shape[1:], BF16)

    @pl.when(z == 3)
    def _():
        gh_in[4] = jnp.zeros(gh_in.shape[1:], BF16)

    @pl.loop(0, rows // 64)
    def _(i):
        at = pl.ds(pl.multiple_of(i * 64, 64), 64)
        g = gh_own[z, at, :].astype(F32) + gh_in[z, at, :].astype(F32) + gh_in[4, at, :].astype(F32)
        xin = x[at, :].astype(F32)
        r = lax.rsqrt(jnp.mean(xin * xin, axis=-1, keepdims=True) + EPSILON)
        n = xin * r
        g_gain = jnp.sum(g * n, axis=0, keepdims=True)
        for j in range(8):
            work[j : j + 1, :] += g_gain[:, j * 128 : (j + 1) * 128]
        g = g * gain_row[0:1, :]
        grad_in[at, :] = g_x2[at, :] + r * (g - n * jnp.mean(g * n, axis=-1, keepdims=True))


    total.first()
    end_send(1)
    spread.step(3)
    l_out.spread()
    finish(2)
    total.second()
    total.third()
    finish(3)
    total.finish(small_tot)
    for hop in range(4):
        spread.crossed(hop)
    for i in range(4):
        crossing(i).wait_send()

        @pl.when(i > z)
        def _(i=i):
            rightward(i).wait_send()

        @pl.when(i < z)
        def _(i=i):
            leftward(i).wait_send()

    spread.drain()
    total.drain()
    s_gate.drain_resumed()
    for scatter in (s_up, s_out, s_head):
        scatter.drain()
    for entry in lines:
        entry.drain()
    for copy in swaps:
        copy.wait()
    for copy in writes:
        copy.wait()


def backward(g_o, gate_pass, parts, saved, x, g_x2, gains_all, small):
    rows, width = x.shape
    tokens = 8 * rows
    sizes = [(2 * parts[0].shape[1], width)] + [p.shape[1:] for p in parts[1:]]
    head = (width // 4, HEAD_COLUMNS)

    def held(a):
        return pltpu.VMEM(a.shape, a.dtype)

    pieces = pltpu.VMEM((4, rows, width), BF16)
    scatters = [pltpu.VMEM((10, r // 2, n), BF16) for r, n in sizes[1:] + [head]]
    own = [pltpu.VMEM((2, r // 2, n), BF16) for r, n in sizes]
    line = [pltpu.VMEM((5, r // 2, n), BF16) for r, n in sizes]
    return transfer(
        kernel_backward, "backward", 2,
        (g_o, gate_pass) + tuple(parts) + tuple(saved) + (x, g_x2, gains_all, small),
        [HBM] * 14 + [VM] * 4,
        [shape((2,) + s, BF16) for s in sizes]
        + [
            shape((8, 2, head[0] // 2, head[1]), BF16),
            shape((rows, width), F32),
            shape(small.shape, F32),
        ],
        [HBM] * 4 + [VM] * 3,
        [pltpu.VMEM((tokens, GROUP * HEAD_SIZE), BF16)]
        + [held(a) for a in saved[:6]]
        + [pltpu.VMEM((2, tokens, rows), BF16), held(saved[7])]
        + [
            pltpu.VMEM((tokens, HEAD_COLUMNS), BF16),
            pltpu.VMEM((tokens, HEAD_SIZE), F32),
            pltpu.VMEM((tokens, HEAD_SIZE), F32),
            pltpu.VMEM((4,) + head, BF16),
            pieces, pieces, pieces, pltpu.VMEM((5, rows, width), BF16),
            pltpu.VMEM((8, width), F32),
            pltpu.VMEM(small.shape, F32),
            pltpu.VMEM((4,) + small.shape, F32),
            pltpu.VMEM((2,) + small.shape, F32),
            pltpu.VMEM((4,) + small.shape, F32),
        ]
        + scatters + own + line,
        24 + 32 + 8 + 12 + 7 + 13, 7 + 4 + 1 + 1 + 16 + 8 + 2,
    )


def chip_step(
    hidden_in, teacher, valid, positions, norm_attn, w_query, key_projection, value_projection,
    gain_query, gain_key, w_out, norm_mlp, w_gate, w_up, w_down,
):
    rows = hidden_in.shape[1]
    width = hidden_in.shape[2]
    half_width = HEAD_SIZE // 2
    freq = 1000000.0 ** (-2.0 * np.arange(half_width) / HEAD_SIZE)
    freq = np.broadcast_to(np.concatenate([freq, freq]), (8, HEAD_SIZE)).astype(np.float32)
    (
        x_pair, t_pair, misc_all, gains_all, count, w_head, wo, wo_more, wg, wu, wd,
        h_all, proj, qkv, att, lse, cosines, sines, att_all,
    ) = forward(
        w_query, key_projection, value_projection, w_out, w_gate, w_up, w_down,
        hidden_in[0], teacher[0], positions, valid, norm_attn, norm_mlp, gain_query, gain_key, freq,
    )
    loss_scale = rows * lax.axis_size("ctx") * lax.axis_size("fsdp") / 4.0
    output, g_o, p_gate, p_up, p_out, s_down, gate_pass, g_x2, small = middle(
        att_all, wo, wo_more, wg, wu, wd, x_pair, t_pair, misc_all, gains_all, count, loss_scale
    )
    down, gate, up, out, heads, grad_input, small = backward(
        g_o, gate_pass, (s_down, p_gate, p_up, p_out),
        (qkv, att, lse, proj, cosines, sines, h_all, w_head),
        hidden_in[0], g_x2, gains_all, small,
    )

    g_gate, g_up, g_q, g_k, g_v, g_down, g_out, g_norm_a, g_norm_m, g_gain_q, g_gain_k, loss, output, grad_input = assemble(
        gate, up, heads.reshape(8, -1, HEAD_COLUMNS), down, out, small, count, output, grad_input
    )
    return (
        output[None],
        loss.reshape(()),
        grad_input[None],
        g_norm_a.reshape(-1),
        g_q,
        g_k,
        g_v,
        g_gain_q.reshape(-1),
        g_gain_k.reshape(-1),
        g_out.reshape(-1, width),
        g_norm_m.reshape(-1),
        g_gate,
        g_up,
        g_down.reshape(-1, width),
    )


def solution(mesh):
    chips = mesh.shape["fsdp"] == 4 and mesh.shape["ctx"] == KEY_VALUE_HEADS
    return jax.shard_map(
        chip_step if chips else per_device,
        mesh=mesh,
        in_specs=(
            P("fsdp", "ctx", None),
            P("fsdp", "ctx", None),
            P("fsdp", "ctx"),
            P("fsdp", "ctx"),
            P("fsdp"),
            P("fsdp", None),
            P("fsdp", None),
            P("fsdp", None),
            P("fsdp"),
            P("fsdp"),
            P("fsdp", None),
            P("fsdp"),
            P("fsdp", None),
            P("fsdp", None),
            P("fsdp", None),
        ),
        out_specs=(
            P("fsdp", "ctx", None),
            P(),
            P("fsdp", "ctx", None),
            P("fsdp"),
            P("fsdp", None),
            P("fsdp", None),
            P("fsdp", None),
            P("fsdp"),
            P("fsdp"),
            P("fsdp", None),
            P("fsdp"),
            P("fsdp", None),
            P("fsdp", None),
            P("fsdp", None),
        ),
        check_vma=False,
    )
```

```python
from functools import partial
import math

import jax
import jax.numpy as jnp
import numpy as np
from jax import lax
from jax.experimental import pallas as pl
from jax.experimental.pallas import tpu as pltpu
from jax.sharding import PartitionSpec as P

QUERY_HEADS = 16
KEY_VALUE_HEADS = 8
HEAD_SIZE = 128


EPSILON = 1e-06


def root_mean_norm(values, norm_gain):
    return (
        values * lax.rsqrt(jnp.mean(values * values, axis=-1, keepdims=True) + EPSILON) * norm_gain
    )


def rope_tables(position_ids):
    half_width = HEAD_SIZE // 2
    freq_table = jnp.exp(
        jnp.arange(half_width, dtype=jnp.float32) * (-2.0 * math.log(1000000.0) / HEAD_SIZE)
    )
    angle_table = position_ids.astype(jnp.float32)[:, None] * freq_table[None, :]
    cosine_table = jnp.cos(angle_table)
    sine_table = jnp.sin(angle_table)
    return (
        jnp.concatenate([cosine_table, cosine_table], -1),
        jnp.concatenate([-sine_table, sine_table], -1),
    )


def apply_rotary(values, cosine_table, sine_table):
    half_width = HEAD_SIZE // 2
    swapped = jnp.concatenate([values[..., half_width:], values[..., :half_width]], -1)
    return values * cosine_table[:, None, :] + swapped * sine_table[:, None, :]


def shape_heads(cosine_table, sine_table, proj_query, projected_key, gain_q, key_gain):
    token_rows = proj_query.shape[0]
    query_rows = apply_rotary(
        root_mean_norm(proj_query.reshape(token_rows, QUERY_HEADS, HEAD_SIZE), gain_q),
        cosine_table,
        sine_table,
    )
    rows_of_keys = apply_rotary(
        root_mean_norm(projected_key.reshape(token_rows, KEY_VALUE_HEADS, HEAD_SIZE), key_gain),
        cosine_table,
        sine_table,
    )
    return (query_rows, rows_of_keys)


def swiglu(gate_proj, up_proj):
    return gate_proj / (1.0 + jnp.exp(-gate_proj)) * up_proj


def contract_rows(left_arr, right_arr):
    return lax.dot_general(
        left_arr, right_arr, (((0,), (0,)), ((), ())), preferred_element_type=jnp.float32
    )


def against(left_arr, right_arr):
    return lax.dot_general(
        left_arr, right_arr, (((1,), (1,)), ((), ())), preferred_element_type=jnp.float32
    )


def in_blocks(block_step, running, shard_portion):
    total_rows = shard_portion.shape[0]
    block_extent = 512
    block_count = total_rows // block_extent
    blocks = shard_portion.reshape((block_count, block_extent) + shard_portion.shape[1:])
    starts = jnp.arange(block_count, dtype=jnp.int32) * block_extent

    def scan_body(state, scan_item):
        return (block_step(state, scan_item[0], scan_item[1]), None)

    running, unused = lax.scan(scan_body, running, (blocks, starts))
    return running


def score_terms(
    query_rows,
    output_gradients,
    lse_heads,
    delta_heads,
    rows_of_keys,
    rows_of_values,
    query_index,
    key_index,
    score_scale,
):
    score_matrix = (
        jnp.einsum("alci,wli->lcaw", query_rows, rows_of_keys, preferred_element_type=jnp.float32)
        * score_scale
    )
    allowed = key_index[None, :] <= query_index[:, None]
    attention_probabilities = jnp.where(allowed, jnp.exp(score_matrix - lse_heads[..., None]), 0.0)
    grad_probs = jnp.einsum(
        "alci,wli->lcaw", output_gradients, rows_of_values, preferred_element_type=jnp.float32
    )
    score_gradient = (
        score_scale * attention_probabilities * (grad_probs - delta_heads[..., None])
    ).astype(jnp.bfloat16)
    return (attention_probabilities, score_gradient)


def per_device(
    hidden_in,
    teacher,
    valid,
    positions,
    norm_attn,
    w_query,
    key_projection,
    value_projection,
    gain_query,
    gain_key,
    w_out,
    norm_mlp,
    w_gate,
    w_up,
    w_down,
):
    gathered = (
        lax.all_gather(norm_attn, "fsdp", axis=0, tiled=True),
        lax.all_gather(w_query, "fsdp", axis=0, tiled=True),
        lax.all_gather(key_projection, "fsdp", axis=0, tiled=True),
        lax.all_gather(value_projection, "fsdp", axis=0, tiled=True),
        lax.all_gather(gain_query, "fsdp", axis=0, tiled=True),
        lax.all_gather(gain_key, "fsdp", axis=0, tiled=True),
        lax.all_gather(w_out, "fsdp", axis=0, tiled=True),
        lax.all_gather(norm_mlp, "fsdp", axis=0, tiled=True),
        lax.all_gather(w_gate, "fsdp", axis=0, tiled=True),
        lax.all_gather(w_up, "fsdp", axis=0, tiled=True),
        lax.all_gather(w_down, "fsdp", axis=0, tiled=True),
    )
    (
        full_norm_attn,
        full_query,
        full_key,
        full_value,
        full_gain_q,
        full_gain_k,
        full_out,
        full_norm_mlp,
        full_gate,
        full_up,
        full_down,
    ) = gathered
    grouped_heads = QUERY_HEADS // KEY_VALUE_HEADS
    score_scale = 1.0 / math.sqrt(HEAD_SIZE)
    residual = hidden_in[0].astype(jnp.float32)
    token_rows = residual.shape[0]
    query_index = lax.axis_index("ctx") * token_rows + jnp.arange(token_rows, dtype=jnp.int32)
    normed_one, norm_one_back = jax.vjp(
        root_mean_norm, residual, full_norm_attn.astype(jnp.float32)
    )
    hidden_one = normed_one.astype(jnp.bfloat16)
    proj_query = jnp.dot(hidden_one, full_query, preferred_element_type=jnp.float32)
    projected_key = jnp.dot(hidden_one, full_key, preferred_element_type=jnp.float32)
    projected_value = jnp.dot(hidden_one, full_value, preferred_element_type=jnp.float32)
    cosine_table, sine_table = rope_tables(positions[0])
    (query_per_head, heads_key), heads_back = jax.vjp(
        partial(shape_heads, cosine_table, sine_table),
        proj_query,
        projected_key,
        full_gain_q.astype(jnp.float32),
        full_gain_k.astype(jnp.float32),
    )
    query_reduced = query_per_head.astype(jnp.bfloat16).reshape(
        token_rows, KEY_VALUE_HEADS, grouped_heads, HEAD_SIZE
    )
    key_reduced = heads_key.astype(jnp.bfloat16)
    value_reduced = projected_value.astype(jnp.bfloat16).reshape(
        token_rows, KEY_VALUE_HEADS, HEAD_SIZE
    )
    key_value = jnp.stack(
        [
            key_reduced.reshape(token_rows, KEY_VALUE_HEADS * HEAD_SIZE),
            value_reduced.reshape(token_rows, KEY_VALUE_HEADS * HEAD_SIZE),
        ],
        axis=1,
    )

    def forward_block(running, shard_portion, first_row):
        run_max, run_total, run_acc = running
        rows_per_block = shard_portion.shape[0]
        rows_of_keys = shard_portion[:, 0].reshape(rows_per_block, KEY_VALUE_HEADS, HEAD_SIZE)
        rows_of_values = shard_portion[:, 1].reshape(rows_per_block, KEY_VALUE_HEADS, HEAD_SIZE)
        key_index = first_row + jnp.arange(rows_per_block, dtype=jnp.int32)
        allowed = key_index[None, :] <= query_index[:, None]
        score_matrix = (
            jnp.einsum(
                "alci,wli->lcaw", query_reduced, rows_of_keys, preferred_element_type=jnp.float32
            )
            * score_scale
        )
        score_matrix = jnp.where(allowed, score_matrix, -1e30)
        new_max = jnp.maximum(run_max, jnp.max(score_matrix, axis=-1))
        weights_part = jnp.where(allowed, jnp.exp(score_matrix - new_max[..., None]), 0.0)
        factor = jnp.exp(run_max - new_max)
        run_total = run_total * factor + jnp.sum(weights_part, axis=-1)
        run_acc = run_acc * factor[..., None] + jnp.einsum(
            "exfw,weq->exfq",
            weights_part.astype(jnp.bfloat16),
            rows_of_values,
            preferred_element_type=jnp.float32,
        )
        return (new_max, run_total, run_acc)

    start_state = (
        jnp.full((KEY_VALUE_HEADS, grouped_heads, token_rows), -1e30, jnp.float32),
        jnp.zeros((KEY_VALUE_HEADS, grouped_heads, token_rows), jnp.float32),
        jnp.zeros((KEY_VALUE_HEADS, grouped_heads, token_rows, HEAD_SIZE), jnp.float32),
    )
    run_max, run_total, run_acc = in_blocks(
        forward_block, start_state, lax.all_gather(key_value, "ctx", axis=0, tiled=True)
    )
    log_total = run_max + jnp.log(run_total)
    attn_rows = jnp.transpose(run_acc / run_total[..., None], (2, 0, 1, 3))
    attn_low = attn_rows.reshape(token_rows, QUERY_HEADS * HEAD_SIZE).astype(jnp.bfloat16)
    mid_resid = residual + jnp.dot(attn_low, full_out, preferred_element_type=jnp.float32)
    normed_two, norm_two_back = jax.vjp(
        root_mean_norm, mid_resid, full_norm_mlp.astype(jnp.float32)
    )
    hidden_two = normed_two.astype(jnp.bfloat16)
    gate_proj = jnp.dot(hidden_two, full_gate, preferred_element_type=jnp.float32)
    up_proj = jnp.dot(hidden_two, full_up, preferred_element_type=jnp.float32)
    gated, gated_back = jax.vjp(swiglu, gate_proj, up_proj)
    gated_low = gated.astype(jnp.bfloat16)
    final_rows = mid_resid + jnp.dot(gated_low, full_down, preferred_element_type=jnp.float32)
    target = teacher[0].astype(jnp.float32)
    weight_rows = valid[0].astype(jnp.float32)
    mismatch = final_rows - target
    sq_local = jnp.sum(weight_rows[:, None] * mismatch * mismatch)
    count_local = jnp.sum(weight_rows)
    sq_total, count_total = lax.psum((sq_local, count_local), ("fsdp", "ctx"))
    loss_value = sq_total / count_total
    loss_scale = token_rows * lax.axis_size("ctx") * lax.axis_size("fsdp") / 4.0
    grad_final = 2.0 * loss_scale / count_total * weight_rows[:, None] * mismatch
    grad_down_in = grad_final.astype(jnp.bfloat16)
    grad_w_down = contract_rows(gated_low, grad_down_in)
    grad_gated = against(grad_down_in, full_down)
    grad_gate_proj, grad_up_proj = gated_back(grad_gated)
    gate_low = grad_gate_proj.astype(jnp.bfloat16)
    up_low = grad_up_proj.astype(jnp.bfloat16)
    grad_w_gate = contract_rows(hidden_two, gate_low)
    grad_w_up = contract_rows(hidden_two, up_low)
    grad_hidden_two = against(gate_low, full_gate) + against(up_low, full_up)
    grad_mid_norm, grad_norm_mlp = norm_two_back(grad_hidden_two)
    grad_mid = grad_final + grad_mid_norm
    grad_branch = grad_mid.astype(jnp.bfloat16)
    grad_w_out = contract_rows(attn_low, grad_branch)
    attention_gradient = against(grad_branch, full_out).astype(jnp.bfloat16)
    attention_head_gradient = attention_gradient.reshape(
        token_rows, KEY_VALUE_HEADS, grouped_heads, HEAD_SIZE
    )
    row_delta = jnp.sum(attention_head_gradient.astype(jnp.float32) * attn_rows, axis=-1)
    delta_heads = jnp.transpose(row_delta, (1, 2, 0))
    row_stats = jnp.stack(
        [
            jnp.transpose(log_total, (2, 0, 1)).reshape(token_rows, QUERY_HEADS),
            row_delta.reshape(token_rows, QUERY_HEADS),
        ],
        axis=1,
    )

    def block_of_queries(grad_query, shard_portion, first_row):
        rows_per_block = shard_portion.shape[0]
        rows_of_keys = shard_portion[:, 0].reshape(rows_per_block, KEY_VALUE_HEADS, HEAD_SIZE)
        rows_of_values = shard_portion[:, 1].reshape(rows_per_block, KEY_VALUE_HEADS, HEAD_SIZE)
        key_index = first_row + jnp.arange(rows_per_block, dtype=jnp.int32)
        attention_probabilities, score_gradient = score_terms(
            query_reduced,
            attention_head_gradient,
            log_total,
            delta_heads,
            rows_of_keys,
            rows_of_values,
            query_index,
            key_index,
            score_scale,
        )
        return grad_query + jnp.einsum(
            "jyux,xji->ujyi", score_gradient, rows_of_keys, preferred_element_type=jnp.float32
        )

    grad_query = in_blocks(
        block_of_queries,
        jnp.zeros((token_rows, KEY_VALUE_HEADS, grouped_heads, HEAD_SIZE), jnp.float32),
        lax.all_gather(key_value, "ctx", axis=0, tiled=True),
    )
    all_stats = lax.all_gather(row_stats.astype(jnp.bfloat16), "ctx", axis=0, tiled=True).astype(
        row_stats.dtype
    )
    query_pair = jnp.stack(
        [query_reduced.reshape(token_rows, QUERY_HEADS * HEAD_SIZE), attention_gradient], axis=1
    )

    def key_block(running, shard_portion, first_row):
        grad_key, value_gradient = running
        rows_per_block = shard_portion.shape[0]
        query_rows = shard_portion[:, 0].reshape(
            rows_per_block, KEY_VALUE_HEADS, grouped_heads, HEAD_SIZE
        )
        output_gradients = shard_portion[:, 1].reshape(
            rows_per_block, KEY_VALUE_HEADS, grouped_heads, HEAD_SIZE
        )
        partial_statistics = lax.dynamic_slice_in_dim(all_stats, first_row, rows_per_block, 0)
        partial_logsumexp = jnp.transpose(
            partial_statistics[:, 0].reshape(rows_per_block, KEY_VALUE_HEADS, grouped_heads),
            (1, 2, 0),
        )
        partial_delta = jnp.transpose(
            partial_statistics[:, 1].reshape(rows_per_block, KEY_VALUE_HEADS, grouped_heads),
            (1, 2, 0),
        )
        part_index = first_row + jnp.arange(rows_per_block, dtype=jnp.int32)
        attention_probabilities, score_gradient = score_terms(
            query_rows,
            output_gradients,
            partial_logsumexp,
            partial_delta,
            key_reduced,
            value_reduced,
            part_index,
            query_index,
            score_scale,
        )
        grad_key = grad_key + jnp.einsum(
            "wzlj,lwzy->jwy", score_gradient, query_rows, preferred_element_type=jnp.float32
        )
        value_gradient = value_gradient + jnp.einsum(
            "wzlj,lwzy->jwy",
            attention_probabilities.astype(jnp.bfloat16),
            output_gradients,
            preferred_element_type=jnp.float32,
        )
        return (grad_key, value_gradient)

    key_state = (
        jnp.zeros((token_rows, KEY_VALUE_HEADS, HEAD_SIZE), jnp.float32),
        jnp.zeros((token_rows, KEY_VALUE_HEADS, HEAD_SIZE), jnp.float32),
    )
    grad_key, value_gradient = in_blocks(
        key_block, key_state, lax.all_gather(query_pair, "ctx", axis=0, tiled=True)
    )
    grad_proj_q, grad_proj_k, grad_gain_q, grad_gain_k = heads_back(
        (grad_query.reshape(token_rows, QUERY_HEADS, HEAD_SIZE), grad_key)
    )
    query_grad_low = grad_proj_q.astype(jnp.bfloat16)
    key_grad_low = grad_proj_k.astype(jnp.bfloat16)
    value_gradient_reduced = value_gradient.reshape(token_rows, KEY_VALUE_HEADS * HEAD_SIZE).astype(
        jnp.bfloat16
    )
    grad_w_query = contract_rows(hidden_one, query_grad_low)
    grad_w_key = contract_rows(hidden_one, key_grad_low)
    grad_w_value = contract_rows(hidden_one, value_gradient_reduced)
    grad_hidden_one = (
        against(query_grad_low, full_query)
        + against(key_grad_low, full_key)
        + against(value_gradient_reduced, full_value)
    )
    grad_resid_norm, grad_norm_attn = norm_one_back(grad_hidden_one)
    grad_input = grad_mid + grad_resid_norm
    grads = (
        grad_norm_attn,
        grad_w_query,
        grad_w_key,
        grad_w_value,
        grad_gain_q,
        grad_gain_k,
        grad_w_out,
        grad_norm_mlp,
        grad_w_gate,
        grad_w_up,
        grad_w_down,
    )
    shares = (
        lax.psum_scatter(grads[0], ("fsdp", "ctx"), scatter_dimension=0, tiled=True),
        lax.psum_scatter(grads[1], ("fsdp", "ctx"), scatter_dimension=0, tiled=True),
        lax.psum_scatter(grads[2], ("fsdp", "ctx"), scatter_dimension=0, tiled=True),
        lax.psum_scatter(grads[3], ("fsdp", "ctx"), scatter_dimension=0, tiled=True),
        lax.psum_scatter(grads[4], ("fsdp", "ctx"), scatter_dimension=0, tiled=True),
        lax.psum_scatter(grads[5], ("fsdp", "ctx"), scatter_dimension=0, tiled=True),
        lax.psum_scatter(grads[6], ("fsdp", "ctx"), scatter_dimension=0, tiled=True),
        lax.psum_scatter(grads[7], ("fsdp", "ctx"), scatter_dimension=0, tiled=True),
        lax.psum_scatter(grads[8], ("fsdp", "ctx"), scatter_dimension=0, tiled=True),
        lax.psum_scatter(grads[9], ("fsdp", "ctx"), scatter_dimension=0, tiled=True),
        lax.psum_scatter(grads[10], ("fsdp", "ctx"), scatter_dimension=0, tiled=True),
    )
    shares = (
        lax.all_gather(shares[0].astype(jnp.bfloat16), "ctx", axis=0, tiled=True).astype(
            jnp.float32
        ),
        lax.all_gather(shares[1].astype(jnp.bfloat16), "ctx", axis=0, tiled=True).astype(
            jnp.float32
        ),
        lax.all_gather(shares[2].astype(jnp.bfloat16), "ctx", axis=0, tiled=True).astype(
            jnp.float32
        ),
        lax.all_gather(shares[3].astype(jnp.bfloat16), "ctx", axis=0, tiled=True).astype(
            jnp.float32
        ),
        lax.all_gather(shares[4].astype(jnp.bfloat16), "ctx", axis=0, tiled=True).astype(
            jnp.float32
        ),
        lax.all_gather(shares[5].astype(jnp.bfloat16), "ctx", axis=0, tiled=True).astype(
            jnp.float32
        ),
        lax.all_gather(shares[6].astype(jnp.bfloat16), "ctx", axis=0, tiled=True).astype(
            jnp.float32
        ),
        lax.all_gather(shares[7].astype(jnp.bfloat16), "ctx", axis=0, tiled=True).astype(
            jnp.float32
        ),
        lax.all_gather(shares[8].astype(jnp.bfloat16), "ctx", axis=0, tiled=True).astype(
            jnp.float32
        ),
        lax.all_gather(shares[9].astype(jnp.bfloat16), "ctx", axis=0, tiled=True).astype(
            jnp.float32
        ),
        lax.all_gather(shares[10].astype(jnp.bfloat16), "ctx", axis=0, tiled=True).astype(
            jnp.float32
        ),
    )
    return (
        final_rows.astype(jnp.bfloat16)[None],
        loss_value,
        grad_input[None],
        shares[0],
        shares[1],
        shares[2],
        shares[3],
        shares[4],
        shares[5],
        shares[6],
        shares[7],
        shares[8],
        shares[9],
        shares[10],
    )


MESH = pl.DeviceIdType.MESH
BF16 = jnp.bfloat16
F32 = jnp.float32
GROUP = QUERY_HEADS // KEY_VALUE_HEADS
HEAD_COLUMNS = (GROUP + 2) * HEAD_SIZE
SCALE = 1.0 / math.sqrt(HEAD_SIZE)
LOG2_E = 1.0 / math.log(2.0)
VMEM_LIMIT = 60 * 1024 * 1024


class Place:
    def __init__(self):
        self.f = lax.axis_index("fsdp")
        self.c = lax.axis_index("ctx")
        self.z = self.c // 2
        self.k = self.c % 2
        self.fx = self.f + 1 - 2 * (self.f % 2)
        self.fy = (self.f + 2) % 4
        self.fd = 3 - self.f
        self.xp = (self.fx, self.c)
        self.yp = (self.fy, self.c)
        self.dp = (self.fd, self.c)
        self.sib = (self.f, self.c + 1 - 2 * self.k)

    def along_z(self, step):
        other = (self.z + step) % 4
        return other, (self.f, 2 * other + self.k)

    def along_ctx(self, step):
        other = (self.c + step) % 8
        return other, (self.f, other)


def greet(partners):
    barrier = pltpu.get_barrier_semaphore()
    for partner in partners:
        pl.semaphore_signal(barrier, inc=1, device_id=partner, device_id_type=MESH)
    pl.semaphore_wait(barrier, len(partners))


class Copies:
    def __init__(self, send, recv):
        self.send, self.recv, self.used = send, recv, 0

    def take(self, count):
        first = self.used
        self.used += count
        return first

    def at(self, index, src, dst, partner):
        return pltpu.make_async_remote_copy(
            src_ref=src,
            dst_ref=dst,
            send_sem=self.send.at[index],
            recv_sem=self.recv.at[index],
            device_id=partner,
            device_id_type=MESH,
        )

    def __call__(self, src, dst, partner):
        return self.at(self.take(1), src, dst, partner)


class Locals:
    def __init__(self, sems):
        self.sems, self.used, self.open = sems, 0, []

    def __call__(self, src, dst):
        copy = pltpu.make_async_copy(src, dst, self.sems.at[self.used])
        self.used += 1
        copy.start()
        self.open.append(copy)
        return copy

    def wait(self):
        for copy in self.open:
            copy.wait()
        self.open = []

    def take(self, count):
        first = self.used
        self.used += count
        return first

    def alone(self, src, dst):
        copy = self(src, dst)
        self.open.pop()
        return copy


def add_rows(dst, sources):
    rows = dst.shape[0]
    step = 32

    @pl.loop(0, rows // step)
    def _(i):
        part = pl.ds(pl.multiple_of(i * step, step), step)
        total = sources[0][part, :].astype(F32)
        for source in sources[1:]:
            total = total + source[part, :].astype(F32)
        dst[part, :] = total.astype(dst.dtype)


class Gather:
    def __init__(self, me, copies, local, own, buf):
        half = buf.shape[1] // 2
        a, b = pl.ds(0, half), pl.ds(half, half)
        own_a, own_b = buf.at[me.f, a], buf.at[me.f, b]
        self.local, self.own, self.slot = local, own, buf.at[me.f]
        self.a_x = copies(own.at[a], own_a, me.xp)
        self.b_y = copies(own.at[b], own_b, me.yp)
        self.b_x = copies(own.at[b], own_b, me.xp)
        self.a_y = copies(own.at[a], own_a, me.yp)
        self.on_y = copies(buf.at[me.fx, a], buf.at[me.fx, a], me.yp)
        self.on_x = copies(buf.at[me.fy, b], buf.at[me.fy, b], me.xp)

    def first(self):
        self.a_x.start()
        self.b_y.start()

    def second(self):
        self.b_x.start()
        self.a_y.start()
        self.kept = self.local.alone(self.own, self.slot)

    def relay(self):
        self.a_x.wait_recv()
        self.on_y.start()
        self.b_y.wait_recv()
        self.on_x.start()

    def finish(self):
        for copy in (self.b_x, self.a_y, self.on_y, self.on_x):
            copy.wait_recv()
        for copy in (self.a_x, self.b_y, self.b_x, self.a_y, self.on_y, self.on_x):
            copy.wait_send()
        self.kept.wait()

    def finish_half(self):
        for copy in (self.a_x, self.b_y, self.b_x, self.a_y):
            copy.wait()
        self.kept.wait()


class GatherEnd:
    def __init__(self, me, copies, local, came, held):
        half = held.shape[1] // 2
        a, b = pl.ds(0, half), pl.ds(half, half)
        self.on_y = copies(came.at[me.fx, a], held.at[me.fx, a], me.yp)
        self.on_x = copies(came.at[me.fy, b], held.at[me.fy, b], me.xp)
        self.me, self.local, self.came, self.held = me, local, came, held

    def start(self):
        self.on_y.start()
        self.on_x.start()

    def load(self):
        me = self.me
        self.loads = [self.local.alone(self.came.at[i], self.held.at[i]) for i in (me.f, me.fx, me.fy)]

    def finish(self):
        for copy in self.loads:
            copy.wait()
        self.on_y.wait()
        self.on_x.wait()


class Scatter:
    def __init__(self, me, copies, local, part, bufs):
        half = part.shape[1] // 2
        a, b = pl.ds(0, half), pl.ds(half, half)
        slot = [bufs.at[i] for i in range(10)]
        self.fwd_a, self.fwd_b, self.own_a, self.own_b = slot[0:4]
        self.rx_own, self.rx_fwd, self.ry_own, self.ry_fwd, self.r2_a, self.r2_b = slot[4:10]
        self.d_x = copies(part.at[me.fd, a], self.rx_fwd, me.xp)
        self.d_y = copies(part.at[me.fd, b], self.ry_fwd, me.yp)
        self.o_x = copies(part.at[me.fx, a], self.rx_own, me.xp)
        self.o_y = copies(part.at[me.fy, b], self.ry_own, me.yp)
        self.to_y = copies(self.fwd_a, self.r2_a, me.yp)
        self.to_x = copies(self.fwd_b, self.r2_b, me.xp)
        self.local, self.me, self.part, self.a, self.b = local, me, part, a, b

    def first(self):
        self.d_x.start()
        self.d_y.start()

    def second(self):
        self.o_x.start()
        self.o_y.start()
        me, part = self.me, self.part
        self.mine = [
            self.local.alone(part.at[me.fy, self.a], self.fwd_a),
            self.local.alone(part.at[me.fx, self.b], self.fwd_b),
            self.local.alone(part.at[me.f, self.a], self.own_a),
            self.local.alone(part.at[me.f, self.b], self.own_b),
        ]

    def relay(self):
        for copy in self.mine:
            copy.wait()
        self.d_x.wait_recv()
        add_rows(self.fwd_a, [self.fwd_a, self.rx_fwd])
        self.to_y.start()
        self.d_y.wait_recv()
        add_rows(self.fwd_b, [self.fwd_b, self.ry_fwd])
        self.to_x.start()

    def load_fwd(self):
        me, part = self.me, self.part
        self.mine = [
            self.local.alone(part.at[me.fy, self.a], self.fwd_a),
            self.local.alone(part.at[me.fx, self.b], self.fwd_b),
        ]

    def sum_fwd(self):
        for copy in self.mine:
            copy.wait()
        self.d_x.wait_recv()
        add_rows(self.fwd_a, [self.fwd_a, self.rx_fwd])
        self.d_y.wait_recv()
        add_rows(self.fwd_b, [self.fwd_b, self.ry_fwd])

    def load_passed(self, passed):
        self.passed = [
            self.local.alone(passed.at[0], self.fwd_a), self.local.alone(passed.at[1], self.fwd_b)
        ]

    def resume(self):
        me, part = self.me, self.part
        for copy in self.passed:
            copy.wait()
        self.to_y.start()
        self.to_x.start()
        self.o_x.start()
        self.o_y.start()
        self.mine = [
            self.local.alone(part.at[me.f, self.a], self.own_a),
            self.local.alone(part.at[me.f, self.b], self.own_b),
        ]

    def finish_resumed(self, sum_a, sum_b):
        for copy in self.mine:
            copy.wait()
        self.finish(sum_a, sum_b)

    def drain_resumed(self):
        for copy in (self.o_x, self.o_y, self.to_y, self.to_x):
            copy.wait_send()

    def finish(self, sum_a, sum_b):
        self.o_x.wait_recv()
        self.to_y.wait_recv()
        add_rows(sum_a, [self.own_a, self.rx_own, self.r2_a])
        self.o_y.wait_recv()
        self.to_x.wait_recv()
        add_rows(sum_b, [self.own_b, self.ry_own, self.r2_b])

    def drain(self):
        for copy in (self.d_x, self.d_y, self.o_x, self.o_y, self.to_y, self.to_x):
            copy.wait_send()


class LineSum:
    def __init__(self, me, copies, own, bufs):
        z, f, k = me.z, me.f, me.k
        self.z = z
        self.inner = (z == 1) | (z == 2)
        self.outer = (z == 0) | (z == 3)
        self.mine = z - 1
        self.theirs = 2 - z
        self.own, self.from_outer, self.total, self.from_inner = own, bufs.at[0:2], bufs.at[2:4], bufs.at[4]
        self.copies = copies
        self.base = copies.take(8)
        self.inner_of = (f, 2 * (1 + z // 3) + k)
        self.outer_of = (f, 2 * (3 * (z - 1)) + k)
        self.partner = (f, 2 * (3 - z) + k)

    def inward(self, half):
        return self.copies.at(
            self.base + half, self.own.at[half], self.from_outer.at[half], self.inner_of
        )

    def across(self, half):
        return self.copies.at(
            self.base + 2 + half, self.own.at[half], self.from_inner, self.partner
        )

    def back_across(self, half):
        return self.copies.at(
            self.base + 4 + half, self.total.at[half], self.total.at[half], self.partner
        )

    def outward(self, half):
        return self.copies.at(
            self.base + 6 + half, self.total.at[half], self.total.at[half], self.outer_of
        )

    def start(self):
        @pl.when(self.outer)
        def _():
            first = 1 - self.z // 3
            self.inward(first).start()
            self.inward(1 - first).start()

    def meet(self):
        @pl.when(self.inner)
        def _():
            t, m = self.theirs, self.mine
            self.inward(t).wait_recv()
            add_rows(self.own.at[t], [self.own.at[t], self.from_outer.at[t]])
            self.across(t).start()

    def close(self):
        @pl.when(self.inner)
        def _():
            m = self.mine
            self.inward(m).wait_recv()
            self.across(m).wait_recv()
            add_rows(
                self.total.at[m], [self.own.at[m], self.from_outer.at[m], self.from_inner]
            )
            self.back_across(m).start()
            self.outward(m).start()

    def spread(self):
        @pl.when(self.inner)
        def _():
            t = self.theirs
            self.back_across(t).wait_recv()
            self.outward(t).start()

    def arrive(self):
        @pl.when(self.outer)
        def _():
            self.outward(0).wait_recv()
            self.outward(1).wait_recv()

    def drain(self):
        @pl.when(self.outer)
        def _():
            self.inward(0).wait_send()
            self.inward(1).wait_send()

        @pl.when(self.inner)
        def _():
            self.across(self.theirs).wait_send()
            self.back_across(self.mine).wait_send()
            self.outward(0).wait_send()
            self.outward(1).wait_send()


HBM = pl.BlockSpec(memory_space=pl.ANY)
VM = pl.BlockSpec(memory_space=pltpu.VMEM)


def transfer(kernel, name, number, args, in_specs, outs, out_specs, scratch, copies, local):
    return pl.pallas_call(
        kernel,
        out_shape=outs,
        in_specs=in_specs,
        out_specs=out_specs,
        scratch_shapes=scratch
        + [
            pltpu.SemaphoreType.DMA((copies,)),
            pltpu.SemaphoreType.DMA((copies,)),
            pltpu.SemaphoreType.DMA((local,)),
        ],
        compiler_params=pltpu.CompilerParams(
            collective_id=number, has_side_effects=True, vmem_limit_bytes=VMEM_LIMIT
        ),
        name=name,
    )(*args)


def shape(dims, dtype):
    return jax.ShapeDtypeStruct(dims, dtype)


def assemble_kernel(
    gate, up, heads, down, out, small, count, tokens_out, tokens_grad,
    g_gate, g_up, g_q, g_k, g_v, g_down, g_out, g_norm_a, g_norm_m, g_gain_q, g_gain_k, loss, output, grad_in,
):
    for src, dst in ((gate, g_gate), (up, g_up)):
        width = src.shape[2] // 4
        for i in range(4):
            for j in range(2):
                dst[:, pl.ds((2 * i + j) * width, width)] = src[j, :, pl.ds(i * width, width)].astype(F32)
    q_size, size = GROUP * HEAD_SIZE, HEAD_SIZE
    for head in range(KEY_VALUE_HEADS):
        g_q[:, pl.ds(head * q_size, q_size)] = heads[head, :, pl.ds(0, q_size)].astype(F32)
        g_k[:, pl.ds(head * size, size)] = heads[head, :, pl.ds(q_size, size)].astype(F32)
        g_v[:, pl.ds(head * size, size)] = heads[head, :, pl.ds(q_size + size, size)].astype(F32)
    f = lax.axis_index("fsdp")
    output[...] = tokens_out[...]
    grad_in[...] = tokens_grad[...]
    g_norm_a[...] = small[pl.ds(2 * f, 2), :]
    g_norm_m[...] = small[pl.ds(8 + 2 * f, 2), :]
    part = g_gain_q.shape[1]
    lane = lax.broadcasted_iota(jnp.int32, (HEAD_SIZE, part), 0)
    column = lax.broadcasted_iota(jnp.int32, (HEAD_SIZE, part), 1)
    pick = jnp.where(lane == column + part * f, 1.0, 0.0)
    both = lax.dot_general(
        small[16:24, :], pick, (((1,), (0,)), ((), ())), preferred_element_type=F32, precision=lax.Precision.HIGHEST
    )
    g_gain_q[...] = both[0:1, :]
    g_gain_k[...] = both[1:2, :]
    loss[...] = jnp.sum(small[18:19, :], axis=1, keepdims=True) / count[0:1, 0:1]
    g_down[...] = down[...].astype(F32)
    g_out[...] = out[...].astype(F32)


def assemble(gate, up, heads, down, out, small, count, tokens_out, tokens_grad):
    steps = 4

    def cut(dims):
        return pl.BlockSpec((dims[0], dims[1] // steps, dims[2]), lambda i: (0, i, 0))

    def whole(dims):
        return pl.BlockSpec(dims, lambda i: (0,) * len(dims))

    def rows_of(a):
        return pl.BlockSpec((a.shape[0] // steps, a.shape[1]), lambda i: (i, 0))

    def flat(rows, columns):
        return pl.BlockSpec((rows // steps, columns), lambda i: (i, 0)), shape((rows, columns), F32)

    rows, width = gate.shape[1], 2 * gate.shape[2]
    all_heads = KEY_VALUE_HEADS * HEAD_SIZE
    outs = [
        flat(rows, width), flat(rows, width), flat(rows, GROUP * all_heads), flat(rows, all_heads), flat(rows, all_heads),
        (cut(down.shape), shape(down.shape, F32)), (cut(out.shape), shape(out.shape, F32)),
        (whole((2, 128)), shape((2, 128), F32)), (whole((2, 128)), shape((2, 128), F32)),
        (whole((1, 32)), shape((1, 32), F32)), (whole((1, 32)), shape((1, 32), F32)),
        (whole((1, 1)), shape((1, 1), F32)),
    ] + [(rows_of(a), shape(a.shape, a.dtype)) for a in (tokens_out, tokens_grad)]
    return pl.pallas_call(
        assemble_kernel,
        grid=(steps,),
        out_shape=[s for _, s in outs],
        in_specs=[cut(a.shape) for a in (gate, up, heads, down, out)]
        + [whole(small.shape), whole(count.shape), rows_of(tokens_out), rows_of(tokens_grad)],
        out_specs=[b for b, _ in outs],
        compiler_params=pltpu.CompilerParams(vmem_limit_bytes=VMEM_LIMIT),
        name="assemble",
    )(gate, up, heads, down, out, small, count, tokens_out, tokens_grad)


def dot_nt(a, b, **kw):
    return lax.dot_general(a, b, (((1,), (1,)), ((), ())), preferred_element_type=F32, **kw)


def dot_nn(a, b):
    return lax.dot_general(a, b, (((1,), (0,)), ((), ())), preferred_element_type=F32)


def dot_tn(a, b):
    return lax.dot_general(a, b, (((0,), (0,)), ((), ())), preferred_element_type=F32)


HIGHEST = lax.Precision.HIGHEST


class SmallSum:
    def __init__(self, me, copies, own, plane, pair, line):
        self.me, self.own, self.plane, self.pair, self.line = me, own, plane, pair, line
        self.one = [copies(own, plane.at[me.f], partner) for partner in (me.xp, me.yp, me.dp)]
        self.two = [copies(pair.at[me.k], pair.at[me.k], me.sib)]
        self.three = [
            copies(line.at[me.z], line.at[me.z], me.along_z(step)[1]) for step in (1, 2, 3)
        ]

    def first(self):
        for copy in self.one:
            copy.start()
        self.plane[self.me.f] = self.own[...]

    def second(self):
        for copy in self.one:
            copy.wait_recv()
        plane = self.plane
        self.pair[self.me.k] = (plane[0] + plane[1]) + (plane[2] + plane[3])
        self.two[0].start()

    def third(self):
        self.two[0].wait_recv()
        self.line[self.me.z] = self.pair[0] + self.pair[1]
        for copy in self.three:
            copy.start()

    def finish(self, dst):
        for copy in self.three:
            copy.wait_recv()
        line = self.line
        dst[...] = (line[0] + line[1]) + (line[2] + line[3])

    def drain(self):
        for copy in self.one + self.two + self.three:
            copy.wait_send()


class Spread:
    def __init__(self, me, copies, held, cross=True):
        self.me, self.held, self.copies, self.cross = me, held, copies, cross
        self.here, self.stride = (me.c, 2) if cross else (me.z, 1)
        self.up, self.down = copies.take(3), copies.take(3)
        if cross:
            self.cross_own, self.cross_up, self.cross_down = copies.take(1), copies.take(3), copies.take(3)

    def hop(self, base, hop, block, partner):
        ref = self.held.at[block]
        return self.copies.at(base + hop - 1, ref, ref, partner)

    def rise(self, hop):
        me = self.me
        return self.hop(self.up, hop, self.here - self.stride * (hop - 1), (me.f, me.c + 2))

    def fall(self, hop):
        me = self.me
        return self.hop(self.down, hop, self.here + self.stride * (hop - 1), (me.f, me.c - 2))

    def across(self, base, hop, block):
        return self.hop(base, hop, block, self.me.sib)

    def start(self):
        z = self.me.z

        @pl.when(z < 3)
        def _():
            self.rise(1).start()

        @pl.when(z > 0)
        def _():
            self.fall(1).start()

        if self.cross:
            self.across(self.cross_own, 1, self.me.c).start()

    def step(self, hop):
        z, c = self.me.z, self.me.c

        @pl.when(z >= hop)
        def _():
            self.rise(hop).wait_recv()
            if hop < 3:

                @pl.when(z < 3)
                def _():
                    self.rise(hop + 1).start()

            if self.cross:
                self.across(self.cross_up, hop, c - 2 * hop).start()

        @pl.when(z + hop <= 3)
        def _():
            self.fall(hop).wait_recv()
            if hop < 3:

                @pl.when(z > 0)
                def _():
                    self.fall(hop + 1).start()

            if self.cross:
                self.across(self.cross_down, hop, c + 2 * hop).start()

    def crossed(self, hop):
        z, c = self.me.z, self.me.c
        if hop == 0:
            self.across(self.cross_own, 1, c).wait_recv()
            return

        @pl.when(z >= hop)
        def _():
            self.across(self.cross_up, hop, c - 2 * hop).wait_recv()

        @pl.when(z + hop <= 3)
        def _():
            self.across(self.cross_down, hop, c + 2 * hop).wait_recv()

    def drain(self):
        z, c = self.me.z, self.me.c
        if self.cross:
            self.across(self.cross_own, 1, c).wait_send()
        for hop in (1, 2, 3):

            @pl.when((z >= hop - 1) & (z < 3))
            def _(hop=hop):
                self.rise(hop).wait_send()

            @pl.when((z + hop - 1 <= 3) & (z > 0))
            def _(hop=hop):
                self.fall(hop).wait_send()

            if not self.cross:
                continue

            @pl.when(z >= hop)
            def _(hop=hop):
                self.across(self.cross_up, hop, c - 2 * hop).wait_send()

            @pl.when(z + hop <= 3)
            def _(hop=hop):
                self.across(self.cross_down, hop, c + 2 * hop).wait_send()


def half_turn(values):
    return pltpu.roll(values, HEAD_SIZE // 2, 1)


def rotary_tables(position_rows, freq, cosines, sines, at):
    columns = jnp.transpose(position_rows)
    lane = lax.broadcasted_iota(jnp.int32, (HEAD_SIZE, HEAD_SIZE), 1)
    first = lane < HEAD_SIZE // 2
    for r in range(2):
        angle = columns[:, r : r + 1] * freq
        turns = jnp.floor(angle * (2.0 / math.pi) + 0.5)
        rest = ((angle - turns * 1.5703125) - turns * 4.837512969970703125e-04) - turns * 7.549789954891882e-08
        square = rest * rest
        sine = rest + rest * square * (
            -1.6666654611e-01 + square * (8.3321608736e-03 - square * 1.9515295891e-04)
        )
        cosine = 1.0 + square * (
            -0.5 + square * (4.166664568298827e-02 + square * (-1.388731625493765e-03 + square * 2.443315711809948e-05))
        )
        quarter = (turns.astype(jnp.int32) + jnp.where(first, 0, 3)) & 3
        odd = (quarter & 1) == 1
        value = jnp.where(odd, sine, cosine)
        value = jnp.where((quarter == 1) | (quarter == 2), -value, value)
        other = half_turn(value)
        rows = pl.ds(pl.multiple_of(at + r * 128, 128), 128)
        cosines[rows, :] = jnp.where(first, value, other)
        sines[rows, :] = jnp.where(first, -other, value)


def head_norm(u):
    return lax.rsqrt(jnp.mean(u * u, axis=-1, keepdims=True) + EPSILON)


def small_arguments(f, positions, valid, norm_a, norm_m, gain_q, gain_k, misc, gains, count):
    misc[...] = jnp.zeros_like(misc)
    for r in range(2):
        misc[r : r + 1, :] = positions[0:1, pl.ds(r * 128, 128)].astype(F32)
        misc[r + 2 : r + 3, :] = valid[0:1, pl.ds(r * 128, 128)].astype(F32)
    gains[...] = jnp.zeros_like(gains)
    for i, norm in enumerate((norm_a, norm_m)):
        gains[2 * i : 2 * i + 2, :] = norm[...].astype(F32).reshape(2, 128)
    size = gain_q.shape[0]
    lane = lax.broadcasted_iota(jnp.int32, (1, HEAD_SIZE), 1)
    for r, gain in enumerate((gain_q, gain_k)):
        wide = jnp.concatenate([gain[...].astype(F32).reshape(1, size)] * (HEAD_SIZE // size), axis=1)
        gains[r + 4 : r + 5, :] = jnp.where(lane // size == f, wide, 0.0)
    count[...] = jnp.broadcast_to(jnp.sum(valid[...].astype(F32), axis=1, keepdims=True), count.shape)


def kernel_forward(
    wq, wk, wv, wo, wg, wu, wd, x, t, positions, valid, norm_a, norm_m, gain_qs, gain_ks, freq,
    x_pair, t_pair, misc_all, gains_all, count_out,
    w_head_out, wo_all, wo_rest, wg_all, wu_all, wd_all,
    h_out, proj_out, qkv_out, att_out, lse_out, cos_out, sin_out, att_all,
    w_head, h_all, proj, qkv, att, lse, cosines, sines, x_all, values, own_h, own_o, own_p, own_g, own_u, own_d, gain_row, misc, gains, count, plane, pair, line,
    send, recv, lsem,
):
    me = Place()
    z, k, f, c = me.z, me.k, me.f, me.c
    rows = x.shape[0]
    small_arguments(f, positions, valid, norm_a, norm_m, gain_qs, gain_ks, misc, gains, count)
    greet([me.xp, me.yp, me.dp, me.sib] + [me.along_z(step)[1] for step in (1, 2, 3)])
    copies, local = Copies(send, recv), Locals(lsem)
    q_size = GROUP * HEAD_SIZE
    head_loads = [
        local.alone(wq.at[:, pl.ds(pl.multiple_of(c * q_size, 128), q_size)], own_h.at[:, pl.ds(0, q_size)]),
        local.alone(wk.at[:, pl.ds(pl.multiple_of(c * HEAD_SIZE, 128), HEAD_SIZE)], own_h.at[:, pl.ds(q_size, HEAD_SIZE)]),
        local.alone(
            wv.at[:, pl.ds(pl.multiple_of(c * HEAD_SIZE, 128), HEAD_SIZE)],
            own_h.at[:, pl.ds(q_size + HEAD_SIZE, HEAD_SIZE)],
        ),
    ]
    width = wg.shape[1] // 8
    local(wd.at[pl.ds(pl.multiple_of(k * own_d.shape[0], 16), own_d.shape[0])], own_d)
    part, quarter = own_o.shape[0], own_p.shape[0]
    first_row = k * (part + 4 * quarter)
    local(wo.at[pl.ds(pl.multiple_of(first_row, 16), part)], own_o)
    local(wo.at[pl.ds(pl.multiple_of(first_row + part + z * quarter, 16), quarter)], own_p)
    for src, own in ((wg, own_g), (wu, own_u)):
        for i in range(4):
            at = pl.ds(pl.multiple_of((2 * i + k) * width, 128), width)
            local(src.at[:, at], own.at[:, pl.ds(i * width, width)])
    small = SmallSum(me, copies, count, plane, pair, line)
    small.first()
    gain_sends = [copies(gains, gains_all.at[f], partner) for partner in (me.xp, me.yp, me.dp)]
    misc_sends = [
        copies(misc, misc_all.at[k, z], me.along_z(step)[1]) for step in (1, 2, 3)
    ]
    for copy in misc_sends + gain_sends:
        copy.start()
    x_all[c] = x[...]
    spread = Spread(me, copies, x_all)
    spread.start()
    pair_sends = [copies(t, t_pair.at[k], me.sib)]
    pair_sends[0].start()
    for copy in head_loads:
        copy.wait()
    head = Gather(me, copies, local, own_h, w_head)
    piece = Gather(me, copies, local, own_p, wo_rest.at[z])
    chain = Spread(me, copies, wo_rest, False)
    head.first()
    head.second()
    local.wait()
    piece.first()
    piece.second()
    out = Gather(me, copies, local, own_o, wo_all)
    gate = Gather(me, copies, local, own_g, wg_all)
    up = Gather(me, copies, local, own_u, wu_all)
    down = Gather(me, copies, local, own_d, wd_all)
    keep = [local.alone(t, t_pair.at[k])]
    for copy in misc_sends:
        copy.wait_recv()
    misc_all[k, z] = misc[...]
    gains_all[f] = gains[...]
    misc_pass = copies(misc_all.at[k], misc_all.at[k], me.sib)
    misc_pass.start()
    small.second()
    for copy in gain_sends:
        copy.wait_recv()
    for i in range(4):
        for r in range(2):
            gain_row[0:1, pl.ds((2 * i + r) * 128, 128)] = gains_all[i, r : r + 1, :]
    gain_q = (gains_all[0, 4:5, :] + gains_all[1, 4:5, :]) + (gains_all[2, 4:5, :] + gains_all[3, 4:5, :])
    gain_k = (gains_all[0, 5:6, :] + gains_all[1, 5:6, :]) + (gains_all[2, 5:6, :] + gains_all[3, 5:6, :])
    head.relay()
    piece.relay()
    for gather in (out, gate, up, down):
        gather.first()
    for gather in (out, gate, up, down):
        gather.second()
    misc_pass.wait_recv()
    small.third()

    @pl.loop(0, 8)
    def _(i):
        rotary_tables(
            misc_all[i % 2, i // 2], freq[0:1, :], cosines, sines, pl.multiple_of(i * 256, 256)
        )

    head.finish()
    spread.step(1)

    def project(block):
        @pl.loop(0, 2)
        def _(u):
            piece = 2 * block + u
            at = pl.ds(pl.multiple_of(piece * rows, rows), rows)
            xin = x_all[piece].astype(F32)
            r = lax.rsqrt(jnp.mean(xin * xin, axis=-1, keepdims=True) + EPSILON)
            h = (xin * r * gain_row[0:1, :]).astype(BF16)
            h_all[at, :] = h
            p = dot_nn(h, w_head[...].reshape(w_head.shape[0] * w_head.shape[1], w_head.shape[2]))
            cosine, sine = cosines[at, :], sines[at, :]
            for g in range(GROUP + 1):
                lanes = slice(g * HEAD_SIZE, (g + 1) * HEAD_SIZE)
                one = p[:, lanes]
                proj[at, lanes] = one
                one = one * head_norm(one) * (gain_q if g < GROUP else gain_k)
                qkv[at, lanes] = (one * cosine + half_turn(one) * sine).astype(BF16)
            qkv[at, (GROUP + 1) * HEAD_SIZE :] = p[:, (GROUP + 1) * HEAD_SIZE :].astype(BF16)

    way = 1 - 2 * (z // 2)
    spread.crossed(0)
    project(z)
    spread.step(2)
    piece.finish()
    chain.start()
    out.relay()
    spread.crossed(1)
    spread.step(3)
    gate.relay()
    spread.crossed(2)
    spread.crossed(3)

    @pl.loop(1, 4)
    def _(step):
        project((z + way * step + 4) % 4)

    chain.step(1)
    for src, dst in (
        (w_head, w_head_out), (h_all, h_out), (proj, proj_out), (qkv, qkv_out), (cosines, cos_out), (sines, sin_out)
    ):
        keep.append(local.alone(src, dst))
    values[:, 0:HEAD_SIZE] = qkv[:, (GROUP + 1) * HEAD_SIZE :]
    values[:, HEAD_SIZE:] = jnp.ones((qkv.shape[0], HEAD_SIZE), BF16)
    base = copies.take(4)
    block = 2 * rows
    for step in (1, 2, 3, 0):
        to, partner = me.along_z(step)
        attend_rows(qkv, values, att, lse, to, block)
        block_rows = att.at[pl.ds(pl.multiple_of(to * block, block), block)]
        keep.append(local.alone(block_rows, att_out.at[pl.ds(pl.multiple_of(to * block, block), block)]))
        place = att_all.at[:, pl.ds(pl.multiple_of(z * q_size, 128), q_size)]
        if step:
            copy = pltpu.make_async_remote_copy(
                src_ref=block_rows, dst_ref=place, send_sem=send.at[base + step], recv_sem=recv.at[base + step],
                device_id=partner, device_id_type=MESH,
            )
            copy.start()
            keep.append(copy)
        else:
            keep.append(local.alone(block_rows, place))
        if step in (1, 2):
            chain.step(step + 1)
    small.finish(count_out)
    keep.append(local.alone(lse, lse_out))
    for i in range(2):
        keep.append(local.alone(x_all.at[2 * z + i], x_pair.at[i]))
    for gather in (out, gate):
        gather.finish()
    chain.drain()
    for gather in (up, down):
        gather.finish_half()
    for copy in pair_sends + [misc_pass]:
        copy.wait_send()
    pair_sends[0].wait_recv()
    for copy in misc_sends + gain_sends:
        copy.wait_send()
    for copy in keep:
        copy.wait()
    spread.drain()
    small.drain()


def forward(wq, wk, wv, wo, wg, wu, wd, x, t, *small):
    rows, width = x.shape
    tokens = 8 * rows
    row = wq.shape[0]
    half_ff = wg.shape[1] // 2
    out_rows, down_rows = wo.shape[0] // 2, wd.shape[0] // 2
    return transfer(
        kernel_forward, "forward", 1,
        (wq, wk, wv, wo, wg, wu, wd, x, t) + small,
        [HBM] * 7 + [VM] * 9,
        [
            shape((2, rows, width), BF16),
            shape((2, rows, width), BF16),
            shape((2, 4, 8, 128), F32),
            shape((4, 8, 128), F32),
            shape((8, 128), F32),
            shape((4, row, HEAD_COLUMNS), BF16),
            shape((4, out_rows // 2, width), BF16),
            shape((4, 4, out_rows // 8, width), BF16),
            shape((4, row, half_ff), BF16),
            shape((4, row, half_ff), BF16),
            shape((4, down_rows, width), BF16),
            shape((tokens, width), BF16),
            shape((tokens, (GROUP + 1) * HEAD_SIZE), F32),
            shape((tokens, HEAD_COLUMNS), BF16),
            shape((tokens, GROUP * HEAD_SIZE), BF16),
            shape((GROUP, 8, tokens), F32),
            shape((tokens, HEAD_SIZE), F32),
            shape((tokens, HEAD_SIZE), F32),
            shape((2 * rows, 4 * GROUP * HEAD_SIZE), BF16),
        ],
        [HBM] * 2 + [VM] * 3 + [HBM] * 14,
        [
            pltpu.VMEM((4, row, HEAD_COLUMNS), BF16),
            pltpu.VMEM((tokens, width), BF16),
            pltpu.VMEM((tokens, (GROUP + 1) * HEAD_SIZE), F32),
            pltpu.VMEM((tokens, HEAD_COLUMNS), BF16),
            pltpu.VMEM((tokens, GROUP * HEAD_SIZE), BF16),
            pltpu.VMEM((GROUP, 8, tokens), F32),
            pltpu.VMEM((tokens, HEAD_SIZE), F32),
            pltpu.VMEM((tokens, HEAD_SIZE), F32),
            pltpu.VMEM((8, rows, width), BF16),
            pltpu.VMEM((tokens, 2 * HEAD_SIZE), BF16),
            pltpu.VMEM((row, HEAD_COLUMNS), BF16),
            pltpu.VMEM((out_rows // 2, width), BF16),
            pltpu.VMEM((out_rows // 8, width), BF16),
            pltpu.VMEM((row, half_ff), BF16),
            pltpu.VMEM((row, half_ff), BF16),
            pltpu.VMEM((down_rows, width), BF16),
            pltpu.VMEM((8, width), F32),
            pltpu.VMEM((8, 128), F32),
            pltpu.VMEM((8, 128), F32),
            pltpu.VMEM((8, 128), F32),
            pltpu.VMEM((4, 8, 128), F32),
            pltpu.VMEM((2, 8, 128), F32),
            pltpu.VMEM((4, 8, 128), F32),
        ],
        7 + 3 + 3 + 13 + 1 + 30 + 6 + 6 + 1 + 4, 3 + 3 + 8 + 6 + 1 + 1 + 2 + 6 + 4 + 1,
    )


def attend_rows(qkv, values, att, lse, i, block):
    rows = pl.ds(pl.multiple_of(i * block, block), block)
    k_at = pl.ds(GROUP * HEAD_SIZE, HEAD_SIZE)
    row = lax.broadcasted_iota(jnp.int32, (block, block), 0)
    column = lax.broadcasted_iota(jnp.int32, (block, block), 1)
    for g in range(GROUP):
        q = qkv[rows, pl.ds(g * HEAD_SIZE, HEAD_SIZE)]

        def part(j, acc, q=q):
            keys = pl.ds(pl.multiple_of(j * block, block), block)
            e = jnp.exp2(dot_nt(q, qkv[keys, k_at]) * (SCALE * LOG2_E))
            return acc + dot_nn(e.astype(BF16), values[keys, :])

        acc = lax.fori_loop(0, i, part, jnp.zeros((block, 2 * HEAD_SIZE), F32))
        e = jnp.exp2(dot_nt(q, qkv[rows, k_at]) * (SCALE * LOG2_E))
        acc = acc + dot_nn(jnp.where(column <= row, e, 0.0).astype(BF16), values[rows, :])
        total = acc[:, HEAD_SIZE:]
        att[rows, pl.ds(g * HEAD_SIZE, HEAD_SIZE)] = (acc[:, :HEAD_SIZE] / total).astype(BF16)
        mean = jnp.full((8, HEAD_SIZE), 1.0 / HEAD_SIZE, F32)
        lse[g, :, rows] = dot_nt(mean, jnp.log(total), precision=HIGHEST)


def kernel_middle(
    att_in, wo_in, wo_more, wg_in, wu_in, wd_in, x_in, t_in, misc_all, gains_all, count,
    output, g_out, p_gate, p_up, p_out, down_sum, gate_pass, g_x2_own, small,
    att, wo, wg, wu, wd, x, t, x2, h2, gate, up, mid, g_gate, g_up, fin, g_fin, g_dn, g_a,
    send_1, recv_1, send_2, recv_2, send_3, recv_3, p_down, p_g, p_u, p_o, g_ob, sc_d, sum_d, sc_g,
    gain_row, valid, loss_row, gain_sum,
    send, recv, lsem, loss_scale,
):
    me = Place()
    z, k = me.z, me.k
    tokens, width = att.shape
    rows = tokens // 2
    greet([me.xp, me.yp, me.sib] + [me.along_z(step)[1] for step in (1, 2, 3)])
    copies, local = Copies(send, recv), Locals(lsem)
    part, quarter = wo_in.shape[1], wo_more.shape[2]
    local(att_in, att)
    local(wo_in, wo.at[:, pl.ds(0, part)])
    for i in range(4):
        local(wo_more.at[i], wo.at[:, pl.ds(part + i * quarter, quarter)])
    loads = [
        local.alone(src, dst)
        for src, dst in (
            (x_in, x), (wg_in, wg), (t_in, t)
        )
    ]
    ends = [GatherEnd(me, copies, local, wu_in, wu), GatherEnd(me, copies, local, wd_in, wd)]
    for entry in ends:
        entry.start()
    for entry in ends:
        entry.load()
    for i in range(4):
        for r in range(2):
            gain_row[0:1, pl.ds((2 * i + r) * 128, 128)] = gains_all[i, r + 2 : r + 3, :]
    for u in range(2):
        columns = jnp.transpose(misc_all[u, z])
        for r in range(2):
            valid[pl.ds(u * rows + r * 128, 128), :] = jnp.broadcast_to(columns[:, r + 2 : r + 3], (128, 128))
    small[...] = jnp.zeros_like(small)
    loss_row[...] = jnp.zeros_like(loss_row)
    gain_sum[...] = jnp.zeros_like(gain_sum)
    step = 64
    bases = [copies.take(4) for _ in range(3)]

    def crossing(which, i, src, dst):
        at = pl.ds(pl.multiple_of(i * 256, 256), 256)
        return copies.at(bases[which] + i, src.at[:, at], dst.at[:, at], me.sib)

    def flat(ref, at):
        value = ref[:, :, at]
        return value.reshape(value.shape[0] * value.shape[1], value.shape[2])

    def strip(i, size):
        return pl.ds(pl.multiple_of(i * size, size), size)

    local.wait()

    @pl.loop(0, 4)
    def _(i):
        at = strip(i, 256)
        send_1[:, at] = dot_nn(att[...], flat(wo, at)).astype(BF16)
        crossing(0, i, send_1, recv_1).start()

    for copy in loads[0:2]:
        copy.wait()
    for i in range(4):
        crossing(0, i, send_1, recv_1).wait_recv()

    @pl.loop(0, tokens // step)
    def _(i):
        at = strip(i, step)
        value = x[at, :].astype(F32) + (send_1[at, :].astype(F32) + recv_1[at, :].astype(F32))
        x2[at, :] = value
        r = lax.rsqrt(jnp.mean(value * value, axis=-1, keepdims=True) + EPSILON)
        h2[at, :] = (value * r * gain_row[0:1, :]).astype(BF16)

    @pl.loop(0, gate.shape[1] // 512)
    def _(i):
        at = strip(i, 512)
        gate[:, at] = dot_nn(h2[...], flat(wg, at))

    ends[0].finish()

    @pl.loop(0, gate.shape[1] // 512)
    def _(i):
        at = strip(i, 512)
        a = gate[:, at]
        b = dot_nn(h2[...], flat(wu, at))
        up[:, at] = b
        mid[:, at] = (a / (1.0 + jnp.exp(-a)) * b).astype(BF16)

    ends[1].finish()
    loads[2].wait()

    @pl.loop(0, 4)
    def _(i):
        at = strip(i, 256)
        send_2[:, at] = dot_nn(mid[...], flat(wd, at)).astype(BF16)
        crossing(1, i, send_2, recv_2).start()

    for i in range(4):
        crossing(1, i, send_2, recv_2).wait_recv()
    factor = 2.0 * loss_scale / count[0:1, 0:1]

    @pl.loop(0, tokens // step)
    def _(i):
        at = strip(i, step)
        value = x2[at, :] + (send_2[at, :].astype(F32) + recv_2[at, :].astype(F32))
        fin[at, :] = value.astype(BF16)
        miss = value - t[at, :].astype(F32)
        weighted = valid[at, 0:1] * miss
        loss_row[0:1, :] += jnp.sum(weighted * miss, axis=0, keepdims=True)
        g = factor * weighted
        g_fin[at, :] = g
        g_dn[at, :] = g.astype(BF16)

    writes = [local.alone(fin.at[pl.ds(pl.multiple_of(k * rows, rows), rows)], output)]
    down_rows = p_down.shape[1]

    @pl.loop(0, 4)
    def _(i):
        p_down[i] = dot_tn(mid[:, strip(i, down_rows)], g_dn[...]).astype(BF16)

    s_down = Scatter(me, copies, local, p_down, sc_d)
    s_down.first()
    s_down.second()

    @pl.loop(0, 4)
    def _(i):
        at = strip(i, down_rows)
        g = dot_nt(g_dn[...], wd[i])
        a, b = gate[:, at], up[:, at]
        s = 1.0 / (1.0 + jnp.exp(-a))
        g_gate[:, at] = (g * b * s * (1.0 + a * (1.0 - s))).astype(BF16)
        g_up[:, at] = (g * a * s).astype(BF16)

    @pl.loop(0, 4)
    def _(i):
        at = strip(i, 256)
        send_3[:, at] = (dot_nt(g_gate[...], wg[i]) + dot_nt(g_up[...], wu[i])).astype(BF16)
        crossing(2, i, send_3, recv_3).start()

    for i in range(4):
        crossing(2, i, send_3, recv_3).wait_recv()

    @pl.loop(0, tokens // step)
    def _(i):
        at = strip(i, step)
        g = send_3[at, :].astype(F32) + recv_3[at, :].astype(F32)
        value = x2[at, :]
        r = lax.rsqrt(jnp.mean(value * value, axis=-1, keepdims=True) + EPSILON)
        n = value * r
        gain_sum[0:1, :] += jnp.sum(g * n, axis=0, keepdims=True)
        g = g * gain_row[0:1, :]
        g = g_fin[at, :] + r * (g - n * jnp.mean(g * n, axis=-1, keepdims=True))
        g_fin[at, :] = g
        g_a[at, :] = g.astype(BF16)

    writes.append(local.alone(g_fin.at[pl.ds(pl.multiple_of(k * rows, rows), rows)], g_x2_own))
    go_base = copies.take(4)
    go_sends = []
    for turn in (2, 1, 3, 0):
        to, partner = me.along_z(turn)
        at = strip(to, 256)
        g_ob[:, at] = dot_nt(g_a[...], wo[to]).astype(BF16)
        place = g_out.at[pl.ds(pl.multiple_of(z * tokens, tokens), tokens)]
        if turn:
            go_sends.append(
                pltpu.make_async_remote_copy(
                    src_ref=g_ob.at[:, at], dst_ref=place, send_sem=send.at[go_base + to],
                    recv_sem=recv.at[go_base + z], device_id=partner, device_id_type=MESH,
                )
            )
            go_sends[-1].start()
        else:
            writes.append(local.alone(g_ob.at[:, at], place))
    s_down.relay()

    @pl.loop(0, 4)
    def _(i):
        p_g[i] = dot_tn(h2[:, strip(i, 256)], g_gate[...]).astype(BF16)

    s_gate = Scatter(me, copies, local, p_g, sc_g)
    s_gate.first()
    s_gate.load_fwd()
    writes.append(local.alone(p_g, p_gate))

    @pl.loop(0, 4)
    def _(i):
        p_u[i] = dot_tn(h2[:, strip(i, 256)], g_up[...]).astype(BF16)

    writes.append(local.alone(p_u, p_up))

    @pl.loop(0, 4)
    def _(i):
        p_o[i] = dot_tn(att[:, strip(i, 256)], g_a[...]).astype(BF16)

    writes.append(local.alone(p_o, p_out))
    for j in range(8):
        small[j + 8 : j + 9, :] = 0.5 * gain_sum[0:1, pl.ds(j * 128, 128)]
        small[18:19, :] += 0.5 * loss_row[0:1, pl.ds(j * 128, 128)]
    s_down.finish(sum_d.at[0], sum_d.at[1])
    writes.append(local.alone(sum_d, down_sum))
    s_gate.sum_fwd()
    writes.append(local.alone(sc_g.at[0:2], gate_pass))
    for copy in writes:
        copy.wait()
    for turn in (1, 2, 3):
        other, partner = me.along_z(turn)
        place = g_out.at[pl.ds(pl.multiple_of(other * tokens, tokens), tokens)]
        pltpu.make_async_remote_copy(
            src_ref=place, dst_ref=place, send_sem=send.at[go_base + other],
            recv_sem=recv.at[go_base + other], device_id=partner, device_id_type=MESH,
        ).wait_recv()
    for copy in go_sends:
        copy.wait_send()
    for which, src, dst in ((0, send_1, recv_1), (1, send_2, recv_2), (2, send_3, recv_3)):
        for i in range(4):
            crossing(which, i, src, dst).wait_send()
    s_down.drain()
    s_gate.d_x.wait_send()
    s_gate.d_y.wait_send()


def middle(att, wo, wo_more, wg, wu, wd, x, t, misc_all, gains_all, count, loss_scale):
    tokens, width = att.shape
    rows = tokens // 2
    hidden = wg.shape[2]

    def bf(*dims):
        return pltpu.VMEM(dims, BF16)

    def held(a):
        return pltpu.VMEM(a.shape, a.dtype)

    def wide(*dims):
        return pltpu.VMEM(dims, F32)

    p_down, p_gate, p_out = (4, hidden // 4, width), (4, width // 4, hidden), (4, width // 4, width)
    return transfer(
        partial(kernel_middle, loss_scale=loss_scale), "middle", 3,
        (att, wo, wo_more, wg, wu, wd, x.reshape(tokens, width), t.reshape(tokens, width), misc_all, gains_all, count),
        [HBM] * 8 + [VM] * 3,
        [
            shape((rows, width), BF16), shape((4 * tokens, width // 4), BF16),
            shape(p_gate, BF16), shape(p_gate, BF16), shape(p_out, BF16),
            shape((2, hidden // 8, width), BF16), shape((2, width // 8, hidden), BF16),
            shape((rows, width), F32), shape((24, 128), F32),
        ],
        [HBM] * 8 + [VM],
        [held(att), bf(wo.shape[0], 2 * wo.shape[1], width)] + [held(a) for a in (wg, wu, wd)]
        + [bf(tokens, width)] * 2
        + [wide(tokens, width), bf(tokens, width), wide(tokens, hidden), wide(tokens, hidden)]
        + [bf(tokens, hidden)] * 3
        + [bf(tokens, width), wide(tokens, width), bf(tokens, width), bf(tokens, width)]
        + [bf(tokens, width)] * 6
        + [bf(*p_down), bf(*p_gate), bf(*p_gate), bf(*p_out), bf(tokens, width)]
        + [bf(10, hidden // 8, width), bf(2, hidden // 8, width), bf(10, width // 8, hidden)]
        + [wide(8, width), wide(tokens, 128), wide(8, width), wide(8, width)],
        12 + 6 + 4 + 6 + 4, 4 + 5 + 6 + 9 + 4 + 2,
    )


def head_back(g, u, cosine, sine, gain):
    g = g * cosine + half_turn(g * sine)
    r = head_norm(u)
    n = u * r
    g_gain = jnp.sum(g * n, axis=0, keepdims=True)
    g = g * gain
    return r * (g - n * jnp.mean(g * n, axis=-1, keepdims=True)), g_gain


def kernel_backward(
    g_o, gate_pass, down_sum, p_gate, p_up, p_out,
    qkv_in, att_in, lse_in, proj_in, cos_in, sin_in, h_in, w_in,
    x, g_x2, gains_all, small,
    down_tot, gate_tot, up_tot, out_tot, head_tot, grad_in, small_tot,
    g_out, qkv, att, lse, proj, cosines, sines, h_all, w_head, g_proj, g_k, g_v, p_head,
    gh_send, gh_sib, gh_own, gh_in, gain_row, work, plane, pair, line,
    sc_g, sc_u, sc_o, sc_h, own_d, own_g, own_u, own_o, line_d, line_g, line_u, line_o,
    send, recv, lsem,
):
    me = Place()
    z, k, f, c = me.z, me.k, me.f, me.c
    rows = x.shape[0]
    block = 2 * rows
    greet([me.xp, me.yp, me.dp, me.sib] + [me.along_z(step)[1] for step in (1, 2, 3)])
    copies, local = Copies(send, recv), Locals(lsem)
    size, q_size = HEAD_SIZE, GROUP * HEAD_SIZE

    own_down = local.alone(down_sum, own_d)
    s_gate = Scatter(me, copies, local, p_gate, sc_g)
    s_gate.load_passed(gate_pass)
    for src, dst in ((g_o, g_out), (qkv_in, qkv), (att_in, att), (lse_in, lse), (proj_in, proj), (cos_in, cosines), (sin_in, sines)):
        local(src, dst)
    late = [local.alone(w_in, w_head)]
    h_base = local.take(4)

    def h_load(i):
        columns = pl.ds(pl.multiple_of(i * rows, rows), rows)
        return pltpu.make_async_copy(h_in.at[:, columns], h_all.at[i % 2], lsem.at[h_base + i])

    h_load(0).start()
    h_load(1).start()
    s_up = Scatter(me, copies, local, p_up, sc_u)
    s_out = Scatter(me, copies, local, p_out, sc_o)
    s_head = Scatter(me, copies, local, p_head, sc_h)
    s_gate.resume()
    lines = [
        LineSum(me, copies, own, bufs)
        for own, bufs in ((own_d, line_d), (own_g, line_g), (own_u, line_u), (own_o, line_o))
    ]
    l_down, l_gate, l_up, l_out = lines
    totals = (down_tot, gate_tot, up_tot, out_tot)
    swap_base = copies.take(8)
    swaps, writes = [], []

    def finish(i):
        lines[i].arrive()
        half = lines[i].total.shape[1]
        for j in range(2):
            dst = totals[i].at[k, pl.ds(j * half, half)]
            copy = copies.at(swap_base + 2 * i + j, lines[i].total.at[j], dst, me.sib)
            copy.start()
            swaps.append(copy)
            writes.append(local.alone(lines[i].total.at[j], dst))

    def scattered(scatter, entry, own):
        scatter.finish(own.at[0], own.at[1])
        entry.start()

    own_down.wait()
    l_down.start()
    work[...] = small[...]
    for i in range(4):
        for r in range(2):
            gain_row[0:1, pl.ds((2 * i + r) * 128, 128)] = gains_all[i, r : r + 1, :]
    gain_q = (gains_all[0, 4:5, :] + gains_all[1, 4:5, :]) + (gains_all[2, 4:5, :] + gains_all[3, 4:5, :])
    gain_k = (gains_all[0, 5:6, :] + gains_all[1, 5:6, :]) + (gains_all[2, 5:6, :] + gains_all[3, 5:6, :])
    k_at = pl.ds(q_size, size)
    v_at = pl.ds(q_size + size, size)
    g_k[...] = jnp.zeros_like(g_k)
    g_v[...] = jnp.zeros_like(g_v)
    key = lax.broadcasted_iota(jnp.int32, (block, block), 0)
    query = lax.broadcasted_iota(jnp.int32, (block, block), 1)
    def queries(i):
        at = pl.ds(pl.multiple_of(i * block, block), block)
        for g in range(GROUP):
            head = pl.ds(g * size, size)
            q = qkv[at, head]
            go = g_out[at, head]
            product = go.astype(F32) * att[at, head].astype(F32)
            delta = dot_nt(jnp.ones((8, size), F32), product, precision=HIGHEST)[0:1, :]
            log_sum = lse[g, 0:1, at] * LOG2_E

            def part(keys, masked, q=q, go=go, delta=delta, log_sum=log_sum):
                kk, vv = qkv[keys, k_at], qkv[keys, v_at]
                p = jnp.exp2(dot_nt(kk, q) * (SCALE * LOG2_E) - log_sum)
                if masked:
                    p = jnp.where(key <= query, p, 0.0)
                gs = (p * (dot_nt(vv, go) - delta)).astype(BF16)
                g_v[keys, :] += dot_nn(p.astype(BF16), go)
                g_k[keys, :] += dot_nn(gs, q)
                return dot_tn(gs, kk)

            def step(j, acc, part=part):
                return acc + part(pl.ds(pl.multiple_of(j * block, block), block), False)

            acc = lax.fori_loop(0, i, step, jnp.zeros((block, size), F32))
            acc = (acc + part(at, True)) * SCALE
            g_u, g_gain = head_back(acc, proj[at, head], cosines[at, :], sines[at, :], gain_q)
            g_proj[at, head] = g_u.astype(BF16)
            work[16:17, :] += g_gain

    sib_base, right_base, left_base = copies.take(4), copies.take(4), copies.take(4)
    last = (z == 0) | (z == 3)
    inner = (z == 1) | (z == 2)

    def input_part(to, mine, dst):
        at = pl.ds(pl.multiple_of((2 * to + mine) * rows, rows), rows)
        weights = w_head[...].reshape(w_head.shape[0] * w_head.shape[1], w_head.shape[2])
        dst[...] = dot_nt(g_proj[at, :], weights).astype(BF16)

    def crossing(to):
        return copies.at(sib_base + to, gh_send.at[to], gh_sib.at[to], me.sib)

    def rightward(to):
        return copies.at(right_base + to, gh_own.at[to], gh_in.at[to], (f, c + 2))

    def leftward(to):
        there = 1 - (z - to) // 2
        place = gh_in.at[to + (4 - to) * there]
        return copies.at(left_base + to, gh_own.at[to], place, (f, c - 2))

    def onward(to):
        @pl.when(to > z)
        def _():
            rightward(to).start()

        @pl.when(to < z)
        def _():
            leftward(to).start()

    def join(to):
        crossing(to).wait_recv()
        add_rows(gh_own.at[to], [gh_own.at[to], gh_sib.at[to]])

    def end_send(order):
        @pl.when(last)
        def _():
            onward(far_first(order))

    def inner_send(order):
        @pl.when(inner)
        def _():
            to = far_first(order)

            @pl.when(to > z)
            def _():
                rightward(to).wait_recv()

            @pl.when(to < z)
            def _():
                copies.at(left_base + to, gh_own.at[to], gh_in.at[to], (f, c - 2)).wait_recv()

            add_rows(gh_own.at[to], [gh_own.at[to], gh_in.at[to]])
            onward(to)

    def far_first(order):
        return order + (3 - 2 * order) * (z // 2)

    def parts_to(to):
        input_part(to, 1 - k, gh_send.at[to])
        crossing(to).start()
        input_part(to, k, gh_own.at[to])

    spread = Spread(me, copies, head_tot)
    total = SmallSum(me, copies, work, plane, pair, line)
    local.wait()
    s_up.first()
    s_up.second()
    queries(1)
    l_down.meet()
    queries(3)
    l_down.close()
    for copy in late:
        copy.wait()
    s_gate.finish_resumed(own_g.at[0], own_g.at[1])
    l_gate.start()
    queries(2)
    l_gate.meet()
    l_down.spread()
    queries(0)
    s_up.relay()

    @pl.loop(0, 4)
    def _(i):
        at = pl.ds(pl.multiple_of(i * block, block), block)
        g_u, g_gain = head_back(g_k[at, :] * SCALE, proj[at, k_at], cosines[at, :], sines[at, :], gain_k)
        g_proj[at, k_at] = g_u.astype(BF16)
        g_proj[at, v_at] = g_v[at, :].astype(BF16)
        work[17:18, :] += g_gain

    l_gate.close()
    parts_to(far_first(3))

    @pl.loop(0, 4)
    def _(i):
        h_load(i).wait()
        product = dot_tn(h_all[i % 2], g_proj[...])
        p_head[i] = product.astype(BF16)
        with_weights = product * w_head[i].astype(F32)
        sums = dot_nt(jnp.ones((8, with_weights.shape[1]), F32), with_weights, precision=HIGHEST)[0:1, :]
        sums = sums / gain_row[0:1, pl.ds(pl.multiple_of(i * rows, rows), rows)]
        for j in range(2):
            work[pl.ds(2 * i + j, 1), :] = sums[:, j * 128 : (j + 1) * 128]

        @pl.when(i < 2)
        def _():
            h_load(i + 2).start()

    s_head.first()
    s_head.second()
    parts_to(far_first(1))
    parts_to(far_first(0))
    join(far_first(3))
    total.first()
    end_send(3)
    l_gate.spread()
    inner_send(3)
    s_head.relay()
    scattered(s_up, l_up, own_u)
    join(far_first(0))
    parts_to(far_first(2))
    s_out.first()
    s_out.second()
    s_head.finish(head_tot.at[c, 0], head_tot.at[c, 1])
    spread.start()
    finish(0)
    inner_send(0)
    l_up.meet()
    s_out.relay()
    scattered(s_out, l_out, own_o)
    finish(1)
    spread.step(1)
    l_up.close()
    l_out.meet()
    l_up.spread()
    l_out.close()
    join(far_first(2))
    join(far_first(1))
    l_out.spread()
    end_send(2)
    inner_send(2)
    spread.step(2)
    finish(2)
    total.second()
    total.third()
    end_send(1)
    finish(3)
    spread.step(3)

    @pl.when(z > 0)
    def _():
        rightward(z).wait_recv()

    @pl.when(z < 3)
    def _():
        copies.at(left_base + z, gh_own.at[z], gh_in.at[4], (f, c - 2)).wait_recv()

    @pl.when(z == 0)
    def _():
        gh_in[0] = jnp.zeros(gh_in.shape[1:], BF16)

    @pl.when(z == 3)
    def _():
        gh_in[4] = jnp.zeros(gh_in.shape[1:], BF16)

    @pl.loop(0, rows // 64)
    def _(i):
        at = pl.ds(pl.multiple_of(i * 64, 64), 64)
        g = gh_own[z, at, :].astype(F32) + gh_in[z, at, :].astype(F32) + gh_in[4, at, :].astype(F32)
        xin = x[at, :].astype(F32)
        r = lax.rsqrt(jnp.mean(xin * xin, axis=-1, keepdims=True) + EPSILON)
        n = xin * r
        g = g * gain_row[0:1, :]
        grad_in[at, :] = g_x2[at, :] + r * (g - n * jnp.mean(g * n, axis=-1, keepdims=True))


    total.finish(small_tot)
    for hop in range(4):
        spread.crossed(hop)
    for i in range(4):
        crossing(i).wait_send()

        @pl.when(i > z)
        def _(i=i):
            rightward(i).wait_send()

        @pl.when(i < z)
        def _(i=i):
            leftward(i).wait_send()

    spread.drain()
    total.drain()
    s_gate.drain_resumed()
    for scatter in (s_up, s_out, s_head):
        scatter.drain()
    for entry in lines:
        entry.drain()
    for copy in swaps:
        copy.wait()
    for copy in writes:
        copy.wait()


def backward(g_o, gate_pass, parts, saved, x, g_x2, gains_all, small):
    rows, width = x.shape
    tokens = 8 * rows
    sizes = [(2 * parts[0].shape[1], width)] + [p.shape[1:] for p in parts[1:]]
    head = (width // 4, HEAD_COLUMNS)

    def held(a):
        return pltpu.VMEM(a.shape, a.dtype)

    pieces = pltpu.VMEM((4, rows, width), BF16)
    scatters = [pltpu.VMEM((10, r // 2, n), BF16) for r, n in sizes[1:] + [head]]
    own = [pltpu.VMEM((2, r // 2, n), BF16) for r, n in sizes]
    line = [pltpu.VMEM((5, r // 2, n), BF16) for r, n in sizes]
    return transfer(
        kernel_backward, "backward", 2,
        (g_o, gate_pass) + tuple(parts) + tuple(saved) + (x, g_x2, gains_all, small),
        [HBM] * 14 + [VM] * 4,
        [shape((2,) + s, BF16) for s in sizes]
        + [
            shape((8, 2, head[0] // 2, head[1]), BF16),
            shape((rows, width), F32),
            shape(small.shape, F32),
        ],
        [HBM] * 4 + [VM] * 3,
        [pltpu.VMEM((tokens, GROUP * HEAD_SIZE), BF16)]
        + [held(a) for a in saved[:6]]
        + [pltpu.VMEM((2, tokens, rows), BF16), held(saved[7])]
        + [
            pltpu.VMEM((tokens, HEAD_COLUMNS), BF16),
            pltpu.VMEM((tokens, HEAD_SIZE), F32),
            pltpu.VMEM((tokens, HEAD_SIZE), F32),
            pltpu.VMEM((4,) + head, BF16),
            pieces, pieces, pieces, pltpu.VMEM((5, rows, width), BF16),
            pltpu.VMEM((8, width), F32),
            pltpu.VMEM(small.shape, F32),
            pltpu.VMEM((4,) + small.shape, F32),
            pltpu.VMEM((2,) + small.shape, F32),
            pltpu.VMEM((4,) + small.shape, F32),
        ]
        + scatters + own + line,
        24 + 32 + 8 + 12 + 7 + 13, 7 + 4 + 1 + 1 + 16 + 8 + 2,
    )


def chip_step(
    hidden_in, teacher, valid, positions, norm_attn, w_query, key_projection, value_projection,
    gain_query, gain_key, w_out, norm_mlp, w_gate, w_up, w_down,
):
    rows = hidden_in.shape[1]
    width = hidden_in.shape[2]
    half_width = HEAD_SIZE // 2
    freq = 1000000.0 ** (-2.0 * np.arange(half_width) / HEAD_SIZE)
    freq = np.broadcast_to(np.concatenate([freq, freq]), (8, HEAD_SIZE)).astype(np.float32)
    (
        x_pair, t_pair, misc_all, gains_all, count, w_head, wo, wo_more, wg, wu, wd,
        h_all, proj, qkv, att, lse, cosines, sines, att_all,
    ) = forward(
        w_query, key_projection, value_projection, w_out, w_gate, w_up, w_down,
        hidden_in[0], teacher[0], positions, valid, norm_attn, norm_mlp, gain_query, gain_key, freq,
    )
    loss_scale = rows * lax.axis_size("ctx") * lax.axis_size("fsdp") / 4.0
    output, g_o, p_gate, p_up, p_out, s_down, gate_pass, g_x2, small = middle(
        att_all, wo, wo_more, wg, wu, wd, x_pair, t_pair, misc_all, gains_all, count, loss_scale
    )
    down, gate, up, out, heads, grad_input, small = backward(
        g_o, gate_pass, (s_down, p_gate, p_up, p_out),
        (qkv, att, lse, proj, cosines, sines, h_all, w_head),
        hidden_in[0], g_x2, gains_all, small,
    )

    g_gate, g_up, g_q, g_k, g_v, g_down, g_out, g_norm_a, g_norm_m, g_gain_q, g_gain_k, loss, output, grad_input = assemble(
        gate, up, heads.reshape(8, -1, HEAD_COLUMNS), down, out, small, count, output, grad_input
    )
    return (
        output[None],
        loss.reshape(()),
        grad_input[None],
        g_norm_a.reshape(-1),
        g_q,
        g_k,
        g_v,
        g_gain_q.reshape(-1),
        g_gain_k.reshape(-1),
        g_out.reshape(-1, width),
        g_norm_m.reshape(-1),
        g_gate,
        g_up,
        g_down.reshape(-1, width),
    )


def solution(mesh):
    chips = mesh.shape["fsdp"] == 4 and mesh.shape["ctx"] == KEY_VALUE_HEADS
    return jax.shard_map(
        chip_step if chips else per_device,
        mesh=mesh,
        in_specs=(
            P("fsdp", "ctx", None),
            P("fsdp", "ctx", None),
            P("fsdp", "ctx"),
            P("fsdp", "ctx"),
            P("fsdp"),
            P("fsdp", None),
            P("fsdp", None),
            P("fsdp", None),
            P("fsdp"),
            P("fsdp"),
            P("fsdp", None),
            P("fsdp"),
            P("fsdp", None),
            P("fsdp", None),
            P("fsdp", None),
        ),
        out_specs=(
            P("fsdp", "ctx", None),
            P(),
            P("fsdp", "ctx", None),
            P("fsdp"),
            P("fsdp", None),
            P("fsdp", None),
            P("fsdp", None),
            P("fsdp"),
            P("fsdp"),
            P("fsdp", None),
            P("fsdp"),
            P("fsdp", None),
            P("fsdp", None),
            P("fsdp", None),
        ),
        check_vma=False,
    )
```

```python
from functools import partial
import math

import jax
import jax.numpy as jnp
import numpy as np
from jax import lax
from jax.experimental import pallas as pl
from jax.experimental.pallas import tpu as pltpu
from jax.sharding import PartitionSpec as P

QUERY_HEADS = 16
KEY_VALUE_HEADS = 8
HEAD_SIZE = 128


EPSILON = 1e-06


def root_mean_norm(values, norm_gain):
    return (
        values * lax.rsqrt(jnp.mean(values * values, axis=-1, keepdims=True) + EPSILON) * norm_gain
    )


def rope_tables(position_ids):
    half_width = HEAD_SIZE // 2
    freq_table = jnp.exp(
        jnp.arange(half_width, dtype=jnp.float32) * (-2.0 * math.log(1000000.0) / HEAD_SIZE)
    )
    angle_table = position_ids.astype(jnp.float32)[:, None] * freq_table[None, :]
    cosine_table = jnp.cos(angle_table)
    sine_table = jnp.sin(angle_table)
    return (
        jnp.concatenate([cosine_table, cosine_table], -1),
        jnp.concatenate([-sine_table, sine_table], -1),
    )


def apply_rotary(values, cosine_table, sine_table):
    half_width = HEAD_SIZE // 2
    swapped = jnp.concatenate([values[..., half_width:], values[..., :half_width]], -1)
    return values * cosine_table[:, None, :] + swapped * sine_table[:, None, :]


def shape_heads(cosine_table, sine_table, proj_query, projected_key, gain_q, key_gain):
    token_rows = proj_query.shape[0]
    query_rows = apply_rotary(
        root_mean_norm(proj_query.reshape(token_rows, QUERY_HEADS, HEAD_SIZE), gain_q),
        cosine_table,
        sine_table,
    )
    rows_of_keys = apply_rotary(
        root_mean_norm(projected_key.reshape(token_rows, KEY_VALUE_HEADS, HEAD_SIZE), key_gain),
        cosine_table,
        sine_table,
    )
    return (query_rows, rows_of_keys)


def swiglu(gate_proj, up_proj):
    return gate_proj / (1.0 + jnp.exp(-gate_proj)) * up_proj


def contract_rows(left_arr, right_arr):
    return lax.dot_general(
        left_arr, right_arr, (((0,), (0,)), ((), ())), preferred_element_type=jnp.float32
    )


def against(left_arr, right_arr):
    return lax.dot_general(
        left_arr, right_arr, (((1,), (1,)), ((), ())), preferred_element_type=jnp.float32
    )


def in_blocks(block_step, running, shard_portion):
    total_rows = shard_portion.shape[0]
    block_extent = 512
    block_count = total_rows // block_extent
    blocks = shard_portion.reshape((block_count, block_extent) + shard_portion.shape[1:])
    starts = jnp.arange(block_count, dtype=jnp.int32) * block_extent

    def scan_body(state, scan_item):
        return (block_step(state, scan_item[0], scan_item[1]), None)

    running, unused = lax.scan(scan_body, running, (blocks, starts))
    return running


def score_terms(
    query_rows,
    output_gradients,
    lse_heads,
    delta_heads,
    rows_of_keys,
    rows_of_values,
    query_index,
    key_index,
    score_scale,
):
    score_matrix = (
        jnp.einsum("alci,wli->lcaw", query_rows, rows_of_keys, preferred_element_type=jnp.float32)
        * score_scale
    )
    allowed = key_index[None, :] <= query_index[:, None]
    attention_probabilities = jnp.where(allowed, jnp.exp(score_matrix - lse_heads[..., None]), 0.0)
    grad_probs = jnp.einsum(
        "alci,wli->lcaw", output_gradients, rows_of_values, preferred_element_type=jnp.float32
    )
    score_gradient = (
        score_scale * attention_probabilities * (grad_probs - delta_heads[..., None])
    ).astype(jnp.bfloat16)
    return (attention_probabilities, score_gradient)


def per_device(
    hidden_in,
    teacher,
    valid,
    positions,
    norm_attn,
    w_query,
    key_projection,
    value_projection,
    gain_query,
    gain_key,
    w_out,
    norm_mlp,
    w_gate,
    w_up,
    w_down,
):
    gathered = (
        lax.all_gather(norm_attn, "fsdp", axis=0, tiled=True),
        lax.all_gather(w_query, "fsdp", axis=0, tiled=True),
        lax.all_gather(key_projection, "fsdp", axis=0, tiled=True),
        lax.all_gather(value_projection, "fsdp", axis=0, tiled=True),
        lax.all_gather(gain_query, "fsdp", axis=0, tiled=True),
        lax.all_gather(gain_key, "fsdp", axis=0, tiled=True),
        lax.all_gather(w_out, "fsdp", axis=0, tiled=True),
        lax.all_gather(norm_mlp, "fsdp", axis=0, tiled=True),
        lax.all_gather(w_gate, "fsdp", axis=0, tiled=True),
        lax.all_gather(w_up, "fsdp", axis=0, tiled=True),
        lax.all_gather(w_down, "fsdp", axis=0, tiled=True),
    )
    (
        full_norm_attn,
        full_query,
        full_key,
        full_value,
        full_gain_q,
        full_gain_k,
        full_out,
        full_norm_mlp,
        full_gate,
        full_up,
        full_down,
    ) = gathered
    grouped_heads = QUERY_HEADS // KEY_VALUE_HEADS
    score_scale = 1.0 / math.sqrt(HEAD_SIZE)
    residual = hidden_in[0].astype(jnp.float32)
    token_rows = residual.shape[0]
    query_index = lax.axis_index("ctx") * token_rows + jnp.arange(token_rows, dtype=jnp.int32)
    normed_one, norm_one_back = jax.vjp(
        root_mean_norm, residual, full_norm_attn.astype(jnp.float32)
    )
    hidden_one = normed_one.astype(jnp.bfloat16)
    proj_query = jnp.dot(hidden_one, full_query, preferred_element_type=jnp.float32)
    projected_key = jnp.dot(hidden_one, full_key, preferred_element_type=jnp.float32)
    projected_value = jnp.dot(hidden_one, full_value, preferred_element_type=jnp.float32)
    cosine_table, sine_table = rope_tables(positions[0])
    (query_per_head, heads_key), heads_back = jax.vjp(
        partial(shape_heads, cosine_table, sine_table),
        proj_query,
        projected_key,
        full_gain_q.astype(jnp.float32),
        full_gain_k.astype(jnp.float32),
    )
    query_reduced = query_per_head.astype(jnp.bfloat16).reshape(
        token_rows, KEY_VALUE_HEADS, grouped_heads, HEAD_SIZE
    )
    key_reduced = heads_key.astype(jnp.bfloat16)
    value_reduced = projected_value.astype(jnp.bfloat16).reshape(
        token_rows, KEY_VALUE_HEADS, HEAD_SIZE
    )
    key_value = jnp.stack(
        [
            key_reduced.reshape(token_rows, KEY_VALUE_HEADS * HEAD_SIZE),
            value_reduced.reshape(token_rows, KEY_VALUE_HEADS * HEAD_SIZE),
        ],
        axis=1,
    )

    def forward_block(running, shard_portion, first_row):
        run_max, run_total, run_acc = running
        rows_per_block = shard_portion.shape[0]
        rows_of_keys = shard_portion[:, 0].reshape(rows_per_block, KEY_VALUE_HEADS, HEAD_SIZE)
        rows_of_values = shard_portion[:, 1].reshape(rows_per_block, KEY_VALUE_HEADS, HEAD_SIZE)
        key_index = first_row + jnp.arange(rows_per_block, dtype=jnp.int32)
        allowed = key_index[None, :] <= query_index[:, None]
        score_matrix = (
            jnp.einsum(
                "alci,wli->lcaw", query_reduced, rows_of_keys, preferred_element_type=jnp.float32
            )
            * score_scale
        )
        score_matrix = jnp.where(allowed, score_matrix, -1e30)
        new_max = jnp.maximum(run_max, jnp.max(score_matrix, axis=-1))
        weights_part = jnp.where(allowed, jnp.exp(score_matrix - new_max[..., None]), 0.0)
        factor = jnp.exp(run_max - new_max)
        run_total = run_total * factor + jnp.sum(weights_part, axis=-1)
        run_acc = run_acc * factor[..., None] + jnp.einsum(
            "exfw,weq->exfq",
            weights_part.astype(jnp.bfloat16),
            rows_of_values,
            preferred_element_type=jnp.float32,
        )
        return (new_max, run_total, run_acc)

    start_state = (
        jnp.full((KEY_VALUE_HEADS, grouped_heads, token_rows), -1e30, jnp.float32),
        jnp.zeros((KEY_VALUE_HEADS, grouped_heads, token_rows), jnp.float32),
        jnp.zeros((KEY_VALUE_HEADS, grouped_heads, token_rows, HEAD_SIZE), jnp.float32),
    )
    run_max, run_total, run_acc = in_blocks(
        forward_block, start_state, lax.all_gather(key_value, "ctx", axis=0, tiled=True)
    )
    log_total = run_max + jnp.log(run_total)
    attn_rows = jnp.transpose(run_acc / run_total[..., None], (2, 0, 1, 3))
    attn_low = attn_rows.reshape(token_rows, QUERY_HEADS * HEAD_SIZE).astype(jnp.bfloat16)
    mid_resid = residual + jnp.dot(attn_low, full_out, preferred_element_type=jnp.float32)
    normed_two, norm_two_back = jax.vjp(
        root_mean_norm, mid_resid, full_norm_mlp.astype(jnp.float32)
    )
    hidden_two = normed_two.astype(jnp.bfloat16)
    gate_proj = jnp.dot(hidden_two, full_gate, preferred_element_type=jnp.float32)
    up_proj = jnp.dot(hidden_two, full_up, preferred_element_type=jnp.float32)
    gated, gated_back = jax.vjp(swiglu, gate_proj, up_proj)
    gated_low = gated.astype(jnp.bfloat16)
    final_rows = mid_resid + jnp.dot(gated_low, full_down, preferred_element_type=jnp.float32)
    target = teacher[0].astype(jnp.float32)
    weight_rows = valid[0].astype(jnp.float32)
    mismatch = final_rows - target
    sq_local = jnp.sum(weight_rows[:, None] * mismatch * mismatch)
    count_local = jnp.sum(weight_rows)
    sq_total, count_total = lax.psum((sq_local, count_local), ("fsdp", "ctx"))
    loss_value = sq_total / count_total
    loss_scale = token_rows * lax.axis_size("ctx") * lax.axis_size("fsdp") / 4.0
    grad_final = 2.0 * loss_scale / count_total * weight_rows[:, None] * mismatch
    grad_down_in = grad_final.astype(jnp.bfloat16)
    grad_w_down = contract_rows(gated_low, grad_down_in)
    grad_gated = against(grad_down_in, full_down)
    grad_gate_proj, grad_up_proj = gated_back(grad_gated)
    gate_low = grad_gate_proj.astype(jnp.bfloat16)
    up_low = grad_up_proj.astype(jnp.bfloat16)
    grad_w_gate = contract_rows(hidden_two, gate_low)
    grad_w_up = contract_rows(hidden_two, up_low)
    grad_hidden_two = against(gate_low, full_gate) + against(up_low, full_up)
    grad_mid_norm, grad_norm_mlp = norm_two_back(grad_hidden_two)
    grad_mid = grad_final + grad_mid_norm
    grad_branch = grad_mid.astype(jnp.bfloat16)
    grad_w_out = contract_rows(attn_low, grad_branch)
    attention_gradient = against(grad_branch, full_out).astype(jnp.bfloat16)
    attention_head_gradient = attention_gradient.reshape(
        token_rows, KEY_VALUE_HEADS, grouped_heads, HEAD_SIZE
    )
    row_delta = jnp.sum(attention_head_gradient.astype(jnp.float32) * attn_rows, axis=-1)
    delta_heads = jnp.transpose(row_delta, (1, 2, 0))
    row_stats = jnp.stack(
        [
            jnp.transpose(log_total, (2, 0, 1)).reshape(token_rows, QUERY_HEADS),
            row_delta.reshape(token_rows, QUERY_HEADS),
        ],
        axis=1,
    )

    def block_of_queries(grad_query, shard_portion, first_row):
        rows_per_block = shard_portion.shape[0]
        rows_of_keys = shard_portion[:, 0].reshape(rows_per_block, KEY_VALUE_HEADS, HEAD_SIZE)
        rows_of_values = shard_portion[:, 1].reshape(rows_per_block, KEY_VALUE_HEADS, HEAD_SIZE)
        key_index = first_row + jnp.arange(rows_per_block, dtype=jnp.int32)
        attention_probabilities, score_gradient = score_terms(
            query_reduced,
            attention_head_gradient,
            log_total,
            delta_heads,
            rows_of_keys,
            rows_of_values,
            query_index,
            key_index,
            score_scale,
        )
        return grad_query + jnp.einsum(
            "jyux,xji->ujyi", score_gradient, rows_of_keys, preferred_element_type=jnp.float32
        )

    grad_query = in_blocks(
        block_of_queries,
        jnp.zeros((token_rows, KEY_VALUE_HEADS, grouped_heads, HEAD_SIZE), jnp.float32),
        lax.all_gather(key_value, "ctx", axis=0, tiled=True),
    )
    all_stats = lax.all_gather(row_stats.astype(jnp.bfloat16), "ctx", axis=0, tiled=True).astype(
        row_stats.dtype
    )
    query_pair = jnp.stack(
        [query_reduced.reshape(token_rows, QUERY_HEADS * HEAD_SIZE), attention_gradient], axis=1
    )

    def key_block(running, shard_portion, first_row):
        grad_key, value_gradient = running
        rows_per_block = shard_portion.shape[0]
        query_rows = shard_portion[:, 0].reshape(
            rows_per_block, KEY_VALUE_HEADS, grouped_heads, HEAD_SIZE
        )
        output_gradients = shard_portion[:, 1].reshape(
            rows_per_block, KEY_VALUE_HEADS, grouped_heads, HEAD_SIZE
        )
        partial_statistics = lax.dynamic_slice_in_dim(all_stats, first_row, rows_per_block, 0)
        partial_logsumexp = jnp.transpose(
            partial_statistics[:, 0].reshape(rows_per_block, KEY_VALUE_HEADS, grouped_heads),
            (1, 2, 0),
        )
        partial_delta = jnp.transpose(
            partial_statistics[:, 1].reshape(rows_per_block, KEY_VALUE_HEADS, grouped_heads),
            (1, 2, 0),
        )
        part_index = first_row + jnp.arange(rows_per_block, dtype=jnp.int32)
        attention_probabilities, score_gradient = score_terms(
            query_rows,
            output_gradients,
            partial_logsumexp,
            partial_delta,
            key_reduced,
            value_reduced,
            part_index,
            query_index,
            score_scale,
        )
        grad_key = grad_key + jnp.einsum(
            "wzlj,lwzy->jwy", score_gradient, query_rows, preferred_element_type=jnp.float32
        )
        value_gradient = value_gradient + jnp.einsum(
            "wzlj,lwzy->jwy",
            attention_probabilities.astype(jnp.bfloat16),
            output_gradients,
            preferred_element_type=jnp.float32,
        )
        return (grad_key, value_gradient)

    key_state = (
        jnp.zeros((token_rows, KEY_VALUE_HEADS, HEAD_SIZE), jnp.float32),
        jnp.zeros((token_rows, KEY_VALUE_HEADS, HEAD_SIZE), jnp.float32),
    )
    grad_key, value_gradient = in_blocks(
        key_block, key_state, lax.all_gather(query_pair, "ctx", axis=0, tiled=True)
    )
    grad_proj_q, grad_proj_k, grad_gain_q, grad_gain_k = heads_back(
        (grad_query.reshape(token_rows, QUERY_HEADS, HEAD_SIZE), grad_key)
    )
    query_grad_low = grad_proj_q.astype(jnp.bfloat16)
    key_grad_low = grad_proj_k.astype(jnp.bfloat16)
    value_gradient_reduced = value_gradient.reshape(token_rows, KEY_VALUE_HEADS * HEAD_SIZE).astype(
        jnp.bfloat16
    )
    grad_w_query = contract_rows(hidden_one, query_grad_low)
    grad_w_key = contract_rows(hidden_one, key_grad_low)
    grad_w_value = contract_rows(hidden_one, value_gradient_reduced)
    grad_hidden_one = (
        against(query_grad_low, full_query)
        + against(key_grad_low, full_key)
        + against(value_gradient_reduced, full_value)
    )
    grad_resid_norm, grad_norm_attn = norm_one_back(grad_hidden_one)
    grad_input = grad_mid + grad_resid_norm
    grads = (
        grad_norm_attn,
        grad_w_query,
        grad_w_key,
        grad_w_value,
        grad_gain_q,
        grad_gain_k,
        grad_w_out,
        grad_norm_mlp,
        grad_w_gate,
        grad_w_up,
        grad_w_down,
    )
    shares = (
        lax.psum_scatter(grads[0], ("fsdp", "ctx"), scatter_dimension=0, tiled=True),
        lax.psum_scatter(grads[1], ("fsdp", "ctx"), scatter_dimension=0, tiled=True),
        lax.psum_scatter(grads[2], ("fsdp", "ctx"), scatter_dimension=0, tiled=True),
        lax.psum_scatter(grads[3], ("fsdp", "ctx"), scatter_dimension=0, tiled=True),
        lax.psum_scatter(grads[4], ("fsdp", "ctx"), scatter_dimension=0, tiled=True),
        lax.psum_scatter(grads[5], ("fsdp", "ctx"), scatter_dimension=0, tiled=True),
        lax.psum_scatter(grads[6], ("fsdp", "ctx"), scatter_dimension=0, tiled=True),
        lax.psum_scatter(grads[7], ("fsdp", "ctx"), scatter_dimension=0, tiled=True),
        lax.psum_scatter(grads[8], ("fsdp", "ctx"), scatter_dimension=0, tiled=True),
        lax.psum_scatter(grads[9], ("fsdp", "ctx"), scatter_dimension=0, tiled=True),
        lax.psum_scatter(grads[10], ("fsdp", "ctx"), scatter_dimension=0, tiled=True),
    )
    shares = (
        lax.all_gather(shares[0].astype(jnp.bfloat16), "ctx", axis=0, tiled=True).astype(
            jnp.float32
        ),
        lax.all_gather(shares[1].astype(jnp.bfloat16), "ctx", axis=0, tiled=True).astype(
            jnp.float32
        ),
        lax.all_gather(shares[2].astype(jnp.bfloat16), "ctx", axis=0, tiled=True).astype(
            jnp.float32
        ),
        lax.all_gather(shares[3].astype(jnp.bfloat16), "ctx", axis=0, tiled=True).astype(
            jnp.float32
        ),
        lax.all_gather(shares[4].astype(jnp.bfloat16), "ctx", axis=0, tiled=True).astype(
            jnp.float32
        ),
        lax.all_gather(shares[5].astype(jnp.bfloat16), "ctx", axis=0, tiled=True).astype(
            jnp.float32
        ),
        lax.all_gather(shares[6].astype(jnp.bfloat16), "ctx", axis=0, tiled=True).astype(
            jnp.float32
        ),
        lax.all_gather(shares[7].astype(jnp.bfloat16), "ctx", axis=0, tiled=True).astype(
            jnp.float32
        ),
        lax.all_gather(shares[8].astype(jnp.bfloat16), "ctx", axis=0, tiled=True).astype(
            jnp.float32
        ),
        lax.all_gather(shares[9].astype(jnp.bfloat16), "ctx", axis=0, tiled=True).astype(
            jnp.float32
        ),
        lax.all_gather(shares[10].astype(jnp.bfloat16), "ctx", axis=0, tiled=True).astype(
            jnp.float32
        ),
    )
    return (
        final_rows.astype(jnp.bfloat16)[None],
        loss_value,
        grad_input[None],
        shares[0],
        shares[1],
        shares[2],
        shares[3],
        shares[4],
        shares[5],
        shares[6],
        shares[7],
        shares[8],
        shares[9],
        shares[10],
    )


MESH = pl.DeviceIdType.MESH
BF16 = jnp.bfloat16
F32 = jnp.float32
GROUP = QUERY_HEADS // KEY_VALUE_HEADS
HEAD_COLUMNS = (GROUP + 2) * HEAD_SIZE
SCALE = 1.0 / math.sqrt(HEAD_SIZE)
LOG2_E = 1.0 / math.log(2.0)
VMEM_LIMIT = 60 * 1024 * 1024


class Place:
    def __init__(self):
        self.f = lax.axis_index("fsdp")
        self.c = lax.axis_index("ctx")
        self.z = self.c // 2
        self.k = self.c % 2
        self.fx = self.f + 1 - 2 * (self.f % 2)
        self.fy = (self.f + 2) % 4
        self.fd = 3 - self.f
        self.xp = (self.fx, self.c)
        self.yp = (self.fy, self.c)
        self.dp = (self.fd, self.c)
        self.sib = (self.f, self.c + 1 - 2 * self.k)

    def along_z(self, step):
        other = (self.z + step) % 4
        return other, (self.f, 2 * other + self.k)

    def along_ctx(self, step):
        other = (self.c + step) % 8
        return other, (self.f, other)


def greet(partners):
    barrier = pltpu.get_barrier_semaphore()
    for partner in partners:
        pl.semaphore_signal(barrier, inc=1, device_id=partner, device_id_type=MESH)
    pl.semaphore_wait(barrier, len(partners))


class Copies:
    def __init__(self, send, recv):
        self.send, self.recv, self.used = send, recv, 0

    def take(self, count):
        first = self.used
        self.used += count
        return first

    def at(self, index, src, dst, partner):
        return pltpu.make_async_remote_copy(
            src_ref=src,
            dst_ref=dst,
            send_sem=self.send.at[index],
            recv_sem=self.recv.at[index],
            device_id=partner,
            device_id_type=MESH,
        )

    def __call__(self, src, dst, partner):
        return self.at(self.take(1), src, dst, partner)


class Locals:
    def __init__(self, sems):
        self.sems, self.used, self.open = sems, 0, []

    def __call__(self, src, dst):
        copy = pltpu.make_async_copy(src, dst, self.sems.at[self.used])
        self.used += 1
        copy.start()
        self.open.append(copy)
        return copy

    def wait(self):
        for copy in self.open:
            copy.wait()
        self.open = []

    def take(self, count):
        first = self.used
        self.used += count
        return first

    def alone(self, src, dst):
        copy = self(src, dst)
        self.open.pop()
        return copy


def add_rows(dst, sources):
    rows = dst.shape[0]
    step = 32

    @pl.loop(0, rows // step)
    def _(i):
        part = pl.ds(pl.multiple_of(i * step, step), step)
        total = sources[0][part, :].astype(F32)
        for source in sources[1:]:
            total = total + source[part, :].astype(F32)
        dst[part, :] = total.astype(dst.dtype)


class Gather:
    def __init__(self, me, copies, local, own, buf):
        half = buf.shape[1] // 2
        a, b = pl.ds(0, half), pl.ds(half, half)
        own_a, own_b = buf.at[me.f, a], buf.at[me.f, b]
        self.local, self.own, self.slot = local, own, buf.at[me.f]
        self.a_x = copies(own.at[a], own_a, me.xp)
        self.b_y = copies(own.at[b], own_b, me.yp)
        self.b_x = copies(own.at[b], own_b, me.xp)
        self.a_y = copies(own.at[a], own_a, me.yp)
        self.on_y = copies(buf.at[me.fx, a], buf.at[me.fx, a], me.yp)
        self.on_x = copies(buf.at[me.fy, b], buf.at[me.fy, b], me.xp)

    def first(self):
        self.a_x.start()
        self.b_y.start()

    def second(self):
        self.b_x.start()
        self.a_y.start()
        self.kept = self.local.alone(self.own, self.slot)

    def relay(self):
        self.a_x.wait_recv()
        self.on_y.start()
        self.b_y.wait_recv()
        self.on_x.start()

    def finish(self):
        for copy in (self.b_x, self.a_y, self.on_y, self.on_x):
            copy.wait_recv()
        for copy in (self.a_x, self.b_y, self.b_x, self.a_y, self.on_y, self.on_x):
            copy.wait_send()
        self.kept.wait()

    def finish_half(self):
        for copy in (self.a_x, self.b_y, self.b_x, self.a_y):
            copy.wait()
        self.kept.wait()


class GatherEnd:
    def __init__(self, me, copies, local, came, held):
        half = held.shape[1] // 2
        a, b = pl.ds(0, half), pl.ds(half, half)
        self.on_y = copies(came.at[me.fx, a], held.at[me.fx, a], me.yp)
        self.on_x = copies(came.at[me.fy, b], held.at[me.fy, b], me.xp)
        self.me, self.local, self.came, self.held = me, local, came, held

    def start(self):
        self.on_y.start()
        self.on_x.start()

    def load(self):
        me = self.me
        self.loads = [self.local.alone(self.came.at[i], self.held.at[i]) for i in (me.f, me.fx, me.fy)]

    def finish(self):
        for copy in self.loads:
            copy.wait()
        self.on_y.wait()
        self.on_x.wait()


class Scatter:
    def __init__(self, me, copies, local, part, bufs):
        half = part.shape[1] // 2
        a, b = pl.ds(0, half), pl.ds(half, half)
        slot = [bufs.at[i] for i in range(bufs.shape[0])]
        slot = slot + slot[0:1] * (10 - len(slot))
        self.fwd_a, self.fwd_b, self.rx_fwd, self.ry_fwd = slot[0:4]
        self.own_a, self.own_b, self.rx_own, self.ry_own, self.r2_a, self.r2_b = slot[4:10]
        self.d_x = copies(part.at[me.fd, a], self.rx_fwd, me.xp)
        self.d_y = copies(part.at[me.fd, b], self.ry_fwd, me.yp)
        self.o_x = copies(part.at[me.fx, a], self.rx_own, me.xp)
        self.o_y = copies(part.at[me.fy, b], self.ry_own, me.yp)
        self.to_y = copies(self.fwd_a, self.r2_a, me.yp)
        self.to_x = copies(self.fwd_b, self.r2_b, me.xp)
        self.local, self.me, self.part, self.a, self.b = local, me, part, a, b

    def first(self):
        self.d_x.start()
        self.d_y.start()

    def second(self):
        self.o_x.start()
        self.o_y.start()
        me, part = self.me, self.part
        self.mine = [
            self.local.alone(part.at[me.fy, self.a], self.fwd_a),
            self.local.alone(part.at[me.fx, self.b], self.fwd_b),
            self.local.alone(part.at[me.f, self.a], self.own_a),
            self.local.alone(part.at[me.f, self.b], self.own_b),
        ]

    def relay(self):
        for copy in self.mine:
            copy.wait()
        self.d_x.wait_recv()
        add_rows(self.fwd_a, [self.fwd_a, self.rx_fwd])
        self.to_y.start()
        self.d_y.wait_recv()
        add_rows(self.fwd_b, [self.fwd_b, self.ry_fwd])
        self.to_x.start()

    def load_fwd(self):
        me, part = self.me, self.part
        self.mine = [
            self.local.alone(part.at[me.fy, self.a], self.fwd_a),
            self.local.alone(part.at[me.fx, self.b], self.fwd_b),
        ]

    def sum_fwd(self):
        for copy in self.mine:
            copy.wait()
        self.d_x.wait_recv()
        add_rows(self.fwd_a, [self.fwd_a, self.rx_fwd])
        self.d_y.wait_recv()
        add_rows(self.fwd_b, [self.fwd_b, self.ry_fwd])

    def load_passed(self, passed):
        self.passed = [
            self.local.alone(passed.at[0], self.fwd_a), self.local.alone(passed.at[1], self.fwd_b)
        ]

    def resume(self):
        me, part = self.me, self.part
        for copy in self.passed:
            copy.wait()
        self.to_y.start()
        self.to_x.start()
        self.o_x.start()
        self.o_y.start()
        self.mine = [
            self.local.alone(part.at[me.f, self.a], self.own_a),
            self.local.alone(part.at[me.f, self.b], self.own_b),
        ]

    def finish_resumed(self, sum_a, sum_b):
        for copy in self.mine:
            copy.wait()
        self.finish(sum_a, sum_b)

    def drain_resumed(self):
        for copy in (self.o_x, self.o_y, self.to_y, self.to_x):
            copy.wait_send()

    def finish(self, sum_a, sum_b):
        self.o_x.wait_recv()
        self.to_y.wait_recv()
        add_rows(sum_a, [self.own_a, self.rx_own, self.r2_a])
        self.o_y.wait_recv()
        self.to_x.wait_recv()
        add_rows(sum_b, [self.own_b, self.ry_own, self.r2_b])

    def drain(self):
        for copy in (self.d_x, self.d_y, self.o_x, self.o_y, self.to_y, self.to_x):
            copy.wait_send()


class LineSum:
    def __init__(self, me, copies, own, bufs):
        z, f, k = me.z, me.f, me.k
        self.z = z
        self.inner = (z == 1) | (z == 2)
        self.outer = (z == 0) | (z == 3)
        self.mine = z - 1
        self.theirs = 2 - z
        self.own, self.from_outer, self.total, self.from_inner = own, bufs.at[0:2], bufs.at[2:4], bufs.at[4]
        self.copies = copies
        self.base = copies.take(8)
        self.inner_of = (f, 2 * (1 + z // 3) + k)
        self.outer_of = (f, 2 * (3 * (z - 1)) + k)
        self.partner = (f, 2 * (3 - z) + k)

    def inward(self, half):
        return self.copies.at(
            self.base + half, self.own.at[half], self.from_outer.at[half], self.inner_of
        )

    def across(self, half):
        return self.copies.at(
            self.base + 2 + half, self.own.at[half], self.from_inner, self.partner
        )

    def back_across(self, half):
        return self.copies.at(
            self.base + 4 + half, self.total.at[half], self.total.at[half], self.partner
        )

    def outward(self, half):
        return self.copies.at(
            self.base + 6 + half, self.total.at[half], self.total.at[half], self.outer_of
        )

    def start(self):
        @pl.when(self.outer)
        def _():
            first = 1 - self.z // 3
            self.inward(first).start()
            self.inward(1 - first).start()

    def meet(self):
        @pl.when(self.inner)
        def _():
            t, m = self.theirs, self.mine
            self.inward(t).wait_recv()
            add_rows(self.own.at[t], [self.own.at[t], self.from_outer.at[t]])
            self.across(t).start()

    def close(self):
        @pl.when(self.inner)
        def _():
            m = self.mine
            self.inward(m).wait_recv()
            self.across(m).wait_recv()
            add_rows(
                self.total.at[m], [self.own.at[m], self.from_outer.at[m], self.from_inner]
            )
            self.back_across(m).start()
            self.outward(m).start()

    def spread(self):
        @pl.when(self.inner)
        def _():
            t = self.theirs
            self.back_across(t).wait_recv()
            self.outward(t).start()

    def arrive(self):
        @pl.when(self.outer)
        def _():
            self.outward(0).wait_recv()
            self.outward(1).wait_recv()

    def drain(self):
        @pl.when(self.outer)
        def _():
            self.inward(0).wait_send()
            self.inward(1).wait_send()

        @pl.when(self.inner)
        def _():
            self.across(self.theirs).wait_send()
            self.back_across(self.mine).wait_send()
            self.outward(0).wait_send()
            self.outward(1).wait_send()


HBM = pl.BlockSpec(memory_space=pl.ANY)
VM = pl.BlockSpec(memory_space=pltpu.VMEM)


def transfer(kernel, name, number, args, in_specs, outs, out_specs, scratch, copies, local):
    return pl.pallas_call(
        kernel,
        out_shape=outs,
        in_specs=in_specs,
        out_specs=out_specs,
        scratch_shapes=scratch
        + [
            pltpu.SemaphoreType.DMA((copies,)),
            pltpu.SemaphoreType.DMA((copies,)),
            pltpu.SemaphoreType.DMA((local,)),
        ],
        compiler_params=pltpu.CompilerParams(
            collective_id=number, has_side_effects=True, vmem_limit_bytes=VMEM_LIMIT
        ),
        name=name,
    )(*args)


def shape(dims, dtype):
    return jax.ShapeDtypeStruct(dims, dtype)


def assemble_kernel(
    gate, up, heads, down, out, small, count, tokens_out, tokens_grad,
    g_gate, g_up, g_q, g_k, g_v, g_down, g_out, g_norm_a, g_norm_m, g_gain_q, g_gain_k, loss, output, grad_in,
):
    for src, dst in ((gate, g_gate), (up, g_up)):
        width = src.shape[2] // 4
        for i in range(4):
            for j in range(2):
                dst[:, pl.ds((2 * i + j) * width, width)] = src[j, :, pl.ds(i * width, width)].astype(F32)
    q_size, size = GROUP * HEAD_SIZE, HEAD_SIZE
    for head in range(KEY_VALUE_HEADS):
        g_q[:, pl.ds(head * q_size, q_size)] = heads[head, :, pl.ds(0, q_size)].astype(F32)
        g_k[:, pl.ds(head * size, size)] = heads[head, :, pl.ds(q_size, size)].astype(F32)
        g_v[:, pl.ds(head * size, size)] = heads[head, :, pl.ds(q_size + size, size)].astype(F32)
    f = lax.axis_index("fsdp")
    output[...] = tokens_out[...]
    grad_in[...] = tokens_grad[...]
    g_norm_a[...] = small[pl.ds(2 * f, 2), :]
    g_norm_m[...] = small[pl.ds(8 + 2 * f, 2), :]
    part = g_gain_q.shape[1]
    lane = lax.broadcasted_iota(jnp.int32, (HEAD_SIZE, part), 0)
    column = lax.broadcasted_iota(jnp.int32, (HEAD_SIZE, part), 1)
    pick = jnp.where(lane == column + part * f, 1.0, 0.0)
    both = lax.dot_general(
        small[16:24, :], pick, (((1,), (0,)), ((), ())), preferred_element_type=F32, precision=lax.Precision.HIGHEST
    )
    g_gain_q[...] = both[0:1, :]
    g_gain_k[...] = both[1:2, :]
    loss[...] = jnp.sum(small[18:19, :], axis=1, keepdims=True) / count[0:1, 0:1]
    g_down[...] = down[...].astype(F32)
    g_out[...] = out[...].astype(F32)


def assemble(gate, up, heads, down, out, small, count, tokens_out, tokens_grad):
    steps = 4

    def cut(dims):
        return pl.BlockSpec((dims[0], dims[1] // steps, dims[2]), lambda i: (0, i, 0))

    def whole(dims):
        return pl.BlockSpec(dims, lambda i: (0,) * len(dims))

    def rows_of(a):
        return pl.BlockSpec((a.shape[0] // steps, a.shape[1]), lambda i: (i, 0))

    def flat(rows, columns):
        return pl.BlockSpec((rows // steps, columns), lambda i: (i, 0)), shape((rows, columns), F32)

    rows, width = gate.shape[1], 2 * gate.shape[2]
    all_heads = KEY_VALUE_HEADS * HEAD_SIZE
    outs = [
        flat(rows, width), flat(rows, width), flat(rows, GROUP * all_heads), flat(rows, all_heads), flat(rows, all_heads),
        (cut(down.shape), shape(down.shape, F32)), (cut(out.shape), shape(out.shape, F32)),
        (whole((2, 128)), shape((2, 128), F32)), (whole((2, 128)), shape((2, 128), F32)),
        (whole((1, 32)), shape((1, 32), F32)), (whole((1, 32)), shape((1, 32), F32)),
        (whole((1, 1)), shape((1, 1), F32)),
    ] + [(rows_of(a), shape(a.shape, a.dtype)) for a in (tokens_out, tokens_grad)]
    return pl.pallas_call(
        assemble_kernel,
        grid=(steps,),
        out_shape=[s for _, s in outs],
        in_specs=[cut(a.shape) for a in (gate, up, heads, down, out)]
        + [whole(small.shape), whole(count.shape), rows_of(tokens_out), rows_of(tokens_grad)],
        out_specs=[b for b, _ in outs],
        compiler_params=pltpu.CompilerParams(vmem_limit_bytes=VMEM_LIMIT),
        name="assemble",
    )(gate, up, heads, down, out, small, count, tokens_out, tokens_grad)


def dot_nt(a, b, **kw):
    return lax.dot_general(a, b, (((1,), (1,)), ((), ())), preferred_element_type=F32, **kw)


def dot_nn(a, b):
    return lax.dot_general(a, b, (((1,), (0,)), ((), ())), preferred_element_type=F32)


def dot_tn(a, b):
    return lax.dot_general(a, b, (((0,), (0,)), ((), ())), preferred_element_type=F32)


HIGHEST = lax.Precision.HIGHEST


class SmallSum:
    def __init__(self, me, copies, own, plane, pair, line):
        self.me, self.own, self.plane, self.pair, self.line = me, own, plane, pair, line
        self.one = [copies(own, plane.at[me.f], partner) for partner in (me.xp, me.yp, me.dp)]
        self.two = [copies(pair.at[me.k], pair.at[me.k], me.sib)]
        self.three = [
            copies(line.at[me.z], line.at[me.z], me.along_z(step)[1]) for step in (1, 2, 3)
        ]

    def first(self):
        for copy in self.one:
            copy.start()
        self.plane[self.me.f] = self.own[...]

    def second(self):
        for copy in self.one:
            copy.wait_recv()
        plane = self.plane
        self.pair[self.me.k] = (plane[0] + plane[1]) + (plane[2] + plane[3])
        self.two[0].start()

    def third(self):
        self.two[0].wait_recv()
        self.line[self.me.z] = self.pair[0] + self.pair[1]
        for copy in self.three:
            copy.start()

    def finish(self, dst):
        for copy in self.three:
            copy.wait_recv()
        line = self.line
        dst[...] = (line[0] + line[1]) + (line[2] + line[3])

    def drain(self):
        for copy in self.one + self.two + self.three:
            copy.wait_send()


class Spread:
    def __init__(self, me, copies, held, cross=True):
        self.me, self.held, self.copies, self.cross = me, held, copies, cross
        self.here, self.stride = (me.c, 2) if cross else (me.z, 1)
        self.up, self.down = copies.take(3), copies.take(3)
        if cross:
            self.cross_own, self.cross_up, self.cross_down = copies.take(1), copies.take(3), copies.take(3)

    def hop(self, base, hop, block, partner):
        ref = self.held.at[block]
        return self.copies.at(base + hop - 1, ref, ref, partner)

    def rise(self, hop):
        me = self.me
        return self.hop(self.up, hop, self.here - self.stride * (hop - 1), (me.f, me.c + 2))

    def fall(self, hop):
        me = self.me
        return self.hop(self.down, hop, self.here + self.stride * (hop - 1), (me.f, me.c - 2))

    def across(self, base, hop, block):
        return self.hop(base, hop, block, self.me.sib)

    def start(self):
        z = self.me.z

        @pl.when(z < 3)
        def _():
            self.rise(1).start()

        @pl.when(z > 0)
        def _():
            self.fall(1).start()

        if self.cross:
            self.across(self.cross_own, 1, self.me.c).start()

    def step(self, hop):
        z, c = self.me.z, self.me.c

        @pl.when(z >= hop)
        def _():
            self.rise(hop).wait_recv()
            if hop < 3:

                @pl.when(z < 3)
                def _():
                    self.rise(hop + 1).start()

            if self.cross:
                self.across(self.cross_up, hop, c - 2 * hop).start()

        @pl.when(z + hop <= 3)
        def _():
            self.fall(hop).wait_recv()
            if hop < 3:

                @pl.when(z > 0)
                def _():
                    self.fall(hop + 1).start()

            if self.cross:
                self.across(self.cross_down, hop, c + 2 * hop).start()

    def crossed(self, hop):
        z, c = self.me.z, self.me.c
        if hop == 0:
            self.across(self.cross_own, 1, c).wait_recv()
            return

        @pl.when(z >= hop)
        def _():
            self.across(self.cross_up, hop, c - 2 * hop).wait_recv()

        @pl.when(z + hop <= 3)
        def _():
            self.across(self.cross_down, hop, c + 2 * hop).wait_recv()

    def drain(self):
        z, c = self.me.z, self.me.c
        if self.cross:
            self.across(self.cross_own, 1, c).wait_send()
        for hop in (1, 2, 3):

            @pl.when((z >= hop - 1) & (z < 3))
            def _(hop=hop):
                self.rise(hop).wait_send()

            @pl.when((z + hop - 1 <= 3) & (z > 0))
            def _(hop=hop):
                self.fall(hop).wait_send()

            if not self.cross:
                continue

            @pl.when(z >= hop)
            def _(hop=hop):
                self.across(self.cross_up, hop, c - 2 * hop).wait_send()

            @pl.when(z + hop <= 3)
            def _(hop=hop):
                self.across(self.cross_down, hop, c + 2 * hop).wait_send()


def half_turn(values):
    return pltpu.roll(values, HEAD_SIZE // 2, 1)


def rotary_tables(position_rows, freq, cosines, sines, at):
    columns = jnp.transpose(position_rows)
    lane = lax.broadcasted_iota(jnp.int32, (HEAD_SIZE, HEAD_SIZE), 1)
    first = lane < HEAD_SIZE // 2
    for r in range(2):
        angle = columns[:, r : r + 1] * freq
        turns = jnp.floor(angle * (2.0 / math.pi) + 0.5)
        rest = ((angle - turns * 1.5703125) - turns * 4.837512969970703125e-04) - turns * 7.549789954891882e-08
        square = rest * rest
        sine = rest + rest * square * (
            -1.6666654611e-01 + square * (8.3321608736e-03 - square * 1.9515295891e-04)
        )
        cosine = 1.0 + square * (
            -0.5 + square * (4.166664568298827e-02 + square * (-1.388731625493765e-03 + square * 2.443315711809948e-05))
        )
        quarter = (turns.astype(jnp.int32) + jnp.where(first, 0, 3)) & 3
        odd = (quarter & 1) == 1
        value = jnp.where(odd, sine, cosine)
        value = jnp.where((quarter == 1) | (quarter == 2), -value, value)
        other = half_turn(value)
        rows = pl.ds(pl.multiple_of(at + r * 128, 128), 128)
        cosines[rows, :] = jnp.where(first, value, other)
        sines[rows, :] = jnp.where(first, -other, value)


def head_norm(u):
    return lax.rsqrt(jnp.mean(u * u, axis=-1, keepdims=True) + EPSILON)


def small_arguments(f, positions, valid, norm_a, norm_m, gain_q, gain_k, misc, gains, count):
    misc[...] = jnp.zeros_like(misc)
    for r in range(2):
        misc[r : r + 1, :] = positions[0:1, pl.ds(r * 128, 128)].astype(F32)
        misc[r + 2 : r + 3, :] = valid[0:1, pl.ds(r * 128, 128)].astype(F32)
    gains[...] = jnp.zeros_like(gains)
    for i, norm in enumerate((norm_a, norm_m)):
        gains[2 * i : 2 * i + 2, :] = norm[...].astype(F32).reshape(2, 128)
    size = gain_q.shape[0]
    lane = lax.broadcasted_iota(jnp.int32, (1, HEAD_SIZE), 1)
    for r, gain in enumerate((gain_q, gain_k)):
        wide = jnp.concatenate([gain[...].astype(F32).reshape(1, size)] * (HEAD_SIZE // size), axis=1)
        gains[r + 4 : r + 5, :] = jnp.where(lane // size == f, wide, 0.0)
    count[...] = jnp.broadcast_to(jnp.sum(valid[...].astype(F32), axis=1, keepdims=True), count.shape)


def kernel_forward(
    wq, wk, wv, wo, wg, wu, wd, x, t, positions, valid, norm_a, norm_m, gain_qs, gain_ks, freq,
    x_pair, t_pair, misc_all, gains_all, count_out,
    w_head_out, wo_all, wo_rest, wg_all, wu_all, wd_all,
    h_out, proj_out, qkv_out, att_out, lse_out, cos_out, sin_out, att_all,
    w_head, h_all, proj, qkv, att, lse, cosines, sines, x_all, values, own_h, own_o, own_p, own_g, own_u, own_d, gain_row, misc, gains, count, plane, pair, line,
    send, recv, lsem,
):
    me = Place()
    z, k, f, c = me.z, me.k, me.f, me.c
    rows = x.shape[0]
    small_arguments(f, positions, valid, norm_a, norm_m, gain_qs, gain_ks, misc, gains, count)
    greet([me.xp, me.yp, me.dp, me.sib] + [me.along_z(step)[1] for step in (1, 2, 3)])
    copies, local = Copies(send, recv), Locals(lsem)
    q_size = GROUP * HEAD_SIZE
    head_loads = [
        local.alone(wq.at[:, pl.ds(pl.multiple_of(c * q_size, 128), q_size)], own_h.at[:, pl.ds(0, q_size)]),
        local.alone(wk.at[:, pl.ds(pl.multiple_of(c * HEAD_SIZE, 128), HEAD_SIZE)], own_h.at[:, pl.ds(q_size, HEAD_SIZE)]),
        local.alone(
            wv.at[:, pl.ds(pl.multiple_of(c * HEAD_SIZE, 128), HEAD_SIZE)],
            own_h.at[:, pl.ds(q_size + HEAD_SIZE, HEAD_SIZE)],
        ),
    ]
    width = wg.shape[1] // 8
    local(wd.at[pl.ds(pl.multiple_of(k * own_d.shape[0], 16), own_d.shape[0])], own_d)
    part, quarter = own_o.shape[0], own_p.shape[0]
    first_row = k * (part + 4 * quarter)
    local(wo.at[pl.ds(pl.multiple_of(first_row, 16), part)], own_o)
    local(wo.at[pl.ds(pl.multiple_of(first_row + part + z * quarter, 16), quarter)], own_p)
    for src, own in ((wg, own_g), (wu, own_u)):
        for i in range(4):
            at = pl.ds(pl.multiple_of((2 * i + k) * width, 128), width)
            local(src.at[:, at], own.at[:, pl.ds(i * width, width)])
    small = SmallSum(me, copies, count, plane, pair, line)
    small.first()
    gain_sends = [copies(gains, gains_all.at[f], partner) for partner in (me.xp, me.yp, me.dp)]
    misc_sends = [
        copies(misc, misc_all.at[k, z], me.along_z(step)[1]) for step in (1, 2, 3)
    ]
    for copy in misc_sends + gain_sends:
        copy.start()
    x_all[c] = x[...]
    spread = Spread(me, copies, x_all)
    spread.start()
    pair_sends = [copies(t, t_pair.at[k], me.sib)]
    pair_sends[0].start()
    for copy in head_loads:
        copy.wait()
    head = Gather(me, copies, local, own_h, w_head)
    piece = Gather(me, copies, local, own_p, wo_rest.at[z])
    chain = Spread(me, copies, wo_rest, False)
    head.first()
    head.second()
    local.wait()
    piece.first()
    piece.second()
    out = Gather(me, copies, local, own_o, wo_all)
    gate = Gather(me, copies, local, own_g, wg_all)
    up = Gather(me, copies, local, own_u, wu_all)
    down = Gather(me, copies, local, own_d, wd_all)
    keep = [local.alone(t, t_pair.at[k])]
    for copy in misc_sends:
        copy.wait_recv()
    misc_all[k, z] = misc[...]
    gains_all[f] = gains[...]
    misc_pass = copies(misc_all.at[k], misc_all.at[k], me.sib)
    misc_pass.start()
    small.second()
    for copy in gain_sends:
        copy.wait_recv()
    for i in range(4):
        for r in range(2):
            gain_row[0:1, pl.ds((2 * i + r) * 128, 128)] = gains_all[i, r : r + 1, :]
    gain_q = (gains_all[0, 4:5, :] + gains_all[1, 4:5, :]) + (gains_all[2, 4:5, :] + gains_all[3, 4:5, :])
    gain_k = (gains_all[0, 5:6, :] + gains_all[1, 5:6, :]) + (gains_all[2, 5:6, :] + gains_all[3, 5:6, :])
    head.relay()
    piece.relay()
    for gather in (out, gate, up, down):
        gather.first()
    for gather in (out, gate, up, down):
        gather.second()
    misc_pass.wait_recv()
    small.third()

    @pl.loop(0, 8)
    def _(i):
        rotary_tables(
            misc_all[i % 2, i // 2], freq[0:1, :], cosines, sines, pl.multiple_of(i * 256, 256)
        )

    head.finish()
    spread.step(1)

    def project(block):
        @pl.loop(0, 2)
        def _(u):
            piece = 2 * block + u
            at = pl.ds(pl.multiple_of(piece * rows, rows), rows)
            xin = x_all[piece].astype(F32)
            r = lax.rsqrt(jnp.mean(xin * xin, axis=-1, keepdims=True) + EPSILON)
            h = (xin * r * gain_row[0:1, :]).astype(BF16)
            h_all[at, :] = h
            p = dot_nn(h, w_head[...].reshape(w_head.shape[0] * w_head.shape[1], w_head.shape[2]))
            cosine, sine = cosines[at, :], sines[at, :]
            for g in range(GROUP + 1):
                lanes = slice(g * HEAD_SIZE, (g + 1) * HEAD_SIZE)
                one = p[:, lanes]
                proj[at, lanes] = one
                one = one * head_norm(one) * (gain_q if g < GROUP else gain_k)
                qkv[at, lanes] = (one * cosine + half_turn(one) * sine).astype(BF16)
            qkv[at, (GROUP + 1) * HEAD_SIZE :] = p[:, (GROUP + 1) * HEAD_SIZE :].astype(BF16)

    way = 1 - 2 * (z // 2)
    spread.crossed(0)
    project(z)
    spread.step(2)
    piece.finish()
    chain.start()
    out.relay()
    spread.crossed(1)
    spread.step(3)
    gate.relay()
    spread.crossed(2)
    spread.crossed(3)

    @pl.loop(1, 4)
    def _(step):
        project((z + way * step + 4) % 4)

    chain.step(1)
    for src, dst in (
        (w_head, w_head_out), (h_all, h_out), (proj, proj_out), (qkv, qkv_out), (cosines, cos_out), (sines, sin_out)
    ):
        keep.append(local.alone(src, dst))
    values[:, 0:HEAD_SIZE] = qkv[:, (GROUP + 1) * HEAD_SIZE :]
    values[:, HEAD_SIZE:] = jnp.ones((qkv.shape[0], HEAD_SIZE), BF16)
    base = copies.take(4)
    block = 2 * rows
    for step in (1, 2, 3, 0):
        to, partner = me.along_z(step)
        attend_rows(qkv, values, att, lse, to, block)
        block_rows = att.at[pl.ds(pl.multiple_of(to * block, block), block)]
        keep.append(local.alone(block_rows, att_out.at[pl.ds(pl.multiple_of(to * block, block), block)]))
        place = att_all.at[:, pl.ds(pl.multiple_of(z * q_size, 128), q_size)]
        if step:
            copy = pltpu.make_async_remote_copy(
                src_ref=block_rows, dst_ref=place, send_sem=send.at[base + step], recv_sem=recv.at[base + step],
                device_id=partner, device_id_type=MESH,
            )
            copy.start()
            keep.append(copy)
        else:
            keep.append(local.alone(block_rows, place))
        if step in (1, 2):
            chain.step(step + 1)
    small.finish(count_out)
    keep.append(local.alone(lse, lse_out))
    for i in range(2):
        keep.append(local.alone(x_all.at[2 * z + i], x_pair.at[i]))
    for gather in (out, gate):
        gather.finish()
    chain.drain()
    for gather in (up, down):
        gather.finish_half()
    for copy in pair_sends + [misc_pass]:
        copy.wait_send()
    pair_sends[0].wait_recv()
    for copy in misc_sends + gain_sends:
        copy.wait_send()
    for copy in keep:
        copy.wait()
    spread.drain()
    small.drain()


def forward(wq, wk, wv, wo, wg, wu, wd, x, t, *small):
    rows, width = x.shape
    tokens = 8 * rows
    row = wq.shape[0]
    half_ff = wg.shape[1] // 2
    out_rows, down_rows = wo.shape[0] // 2, wd.shape[0] // 2
    return transfer(
        kernel_forward, "forward", 1,
        (wq, wk, wv, wo, wg, wu, wd, x, t) + small,
        [HBM] * 7 + [VM] * 9,
        [
            shape((2, rows, width), BF16),
            shape((2, rows, width), BF16),
            shape((2, 4, 8, 128), F32),
            shape((4, 8, 128), F32),
            shape((8, 128), F32),
            shape((4, row, HEAD_COLUMNS), BF16),
            shape((4, out_rows // 2, width), BF16),
            shape((4, 4, out_rows // 8, width), BF16),
            shape((4, row, half_ff), BF16),
            shape((4, row, half_ff), BF16),
            shape((4, down_rows, width), BF16),
            shape((tokens, width), BF16),
            shape((tokens, (GROUP + 1) * HEAD_SIZE), F32),
            shape((tokens, HEAD_COLUMNS), BF16),
            shape((tokens, GROUP * HEAD_SIZE), BF16),
            shape((GROUP, 8, tokens), F32),
            shape((tokens, HEAD_SIZE), F32),
            shape((tokens, HEAD_SIZE), F32),
            shape((2 * rows, 4 * GROUP * HEAD_SIZE), BF16),
        ],
        [HBM] * 2 + [VM] * 3 + [HBM] * 14,
        [
            pltpu.VMEM((4, row, HEAD_COLUMNS), BF16),
            pltpu.VMEM((tokens, width), BF16),
            pltpu.VMEM((tokens, (GROUP + 1) * HEAD_SIZE), F32),
            pltpu.VMEM((tokens, HEAD_COLUMNS), BF16),
            pltpu.VMEM((tokens, GROUP * HEAD_SIZE), BF16),
            pltpu.VMEM((GROUP, 8, tokens), F32),
            pltpu.VMEM((tokens, HEAD_SIZE), F32),
            pltpu.VMEM((tokens, HEAD_SIZE), F32),
            pltpu.VMEM((8, rows, width), BF16),
            pltpu.VMEM((tokens, 2 * HEAD_SIZE), BF16),
            pltpu.VMEM((row, HEAD_COLUMNS), BF16),
            pltpu.VMEM((out_rows // 2, width), BF16),
            pltpu.VMEM((out_rows // 8, width), BF16),
            pltpu.VMEM((row, half_ff), BF16),
            pltpu.VMEM((row, half_ff), BF16),
            pltpu.VMEM((down_rows, width), BF16),
            pltpu.VMEM((8, width), F32),
            pltpu.VMEM((8, 128), F32),
            pltpu.VMEM((8, 128), F32),
            pltpu.VMEM((8, 128), F32),
            pltpu.VMEM((4, 8, 128), F32),
            pltpu.VMEM((2, 8, 128), F32),
            pltpu.VMEM((4, 8, 128), F32),
        ],
        7 + 3 + 3 + 13 + 1 + 30 + 6 + 6 + 1 + 4, 3 + 3 + 8 + 6 + 1 + 1 + 2 + 6 + 4 + 1,
    )


def attend_rows(qkv, values, att, lse, i, block):
    rows = pl.ds(pl.multiple_of(i * block, block), block)
    k_at = pl.ds(GROUP * HEAD_SIZE, HEAD_SIZE)
    row = lax.broadcasted_iota(jnp.int32, (block, block), 0)
    column = lax.broadcasted_iota(jnp.int32, (block, block), 1)
    for g in range(GROUP):
        q = qkv[rows, pl.ds(g * HEAD_SIZE, HEAD_SIZE)]

        def part(j, acc, q=q):
            keys = pl.ds(pl.multiple_of(j * block, block), block)
            e = jnp.exp2(dot_nt(q, qkv[keys, k_at]) * (SCALE * LOG2_E))
            return acc + dot_nn(e.astype(BF16), values[keys, :])

        acc = lax.fori_loop(0, i, part, jnp.zeros((block, 2 * HEAD_SIZE), F32))
        e = jnp.exp2(dot_nt(q, qkv[rows, k_at]) * (SCALE * LOG2_E))
        acc = acc + dot_nn(jnp.where(column <= row, e, 0.0).astype(BF16), values[rows, :])
        total = acc[:, HEAD_SIZE:]
        att[rows, pl.ds(g * HEAD_SIZE, HEAD_SIZE)] = (acc[:, :HEAD_SIZE] / total).astype(BF16)
        mean = jnp.full((8, HEAD_SIZE), 1.0 / HEAD_SIZE, F32)
        lse[g, :, rows] = dot_nt(mean, jnp.log(total), precision=HIGHEST)


def kernel_middle(
    att_in, wo_in, wo_more, wg_in, wu_in, wd_in, x_in, t_in, misc_all, gains_all, count,
    output, g_out, p_gate, p_up, p_out, down_sum, gate_pass, g_x2_own, small,
    att, wo, wg, wu, wd, x, t, x2, h2, gate, up, mid, g_gate, g_up, fin, g_fin, g_dn, g_a,
    send_1, recv_1, send_2, recv_2, send_3, recv_3, p_down, p_g, p_u, p_o, g_ob, sc_d, sum_d, sc_g,
    gain_row, valid, loss_row, gain_sum,
    send, recv, lsem, loss_scale,
):
    me = Place()
    z, k = me.z, me.k
    tokens, width = att.shape
    rows = tokens // 2
    greet([me.xp, me.yp, me.sib] + [me.along_z(step)[1] for step in (1, 2, 3)])
    copies, local = Copies(send, recv), Locals(lsem)
    part, quarter = wo_in.shape[1], wo_more.shape[2]
    local(att_in, att)
    local(wo_in, wo.at[:, pl.ds(0, part)])
    for i in range(4):
        local(wo_more.at[i], wo.at[:, pl.ds(part + i * quarter, quarter)])
    loads = [
        local.alone(src, dst)
        for src, dst in (
            (x_in, x), (wg_in, wg), (t_in, t)
        )
    ]
    ends = [GatherEnd(me, copies, local, wu_in, wu), GatherEnd(me, copies, local, wd_in, wd)]
    for entry in ends:
        entry.start()
    for entry in ends:
        entry.load()
    for i in range(4):
        for r in range(2):
            gain_row[0:1, pl.ds((2 * i + r) * 128, 128)] = gains_all[i, r + 2 : r + 3, :]
    for u in range(2):
        columns = jnp.transpose(misc_all[u, z])
        for r in range(2):
            valid[pl.ds(u * rows + r * 128, 128), :] = jnp.broadcast_to(columns[:, r + 2 : r + 3], (128, 128))
    small[...] = jnp.zeros_like(small)
    loss_row[...] = jnp.zeros_like(loss_row)
    gain_sum[...] = jnp.zeros_like(gain_sum)
    step = 64
    bases = [copies.take(4) for _ in range(3)]

    def crossing(which, i, src, dst):
        at = pl.ds(pl.multiple_of(i * 256, 256), 256)
        return copies.at(bases[which] + i, src.at[:, at], dst.at[:, at], me.sib)

    def flat(ref, at):
        value = ref[:, :, at]
        return value.reshape(value.shape[0] * value.shape[1], value.shape[2])

    def strip(i, size):
        return pl.ds(pl.multiple_of(i * size, size), size)

    local.wait()

    @pl.loop(0, 4)
    def _(i):
        at = strip(i, 256)
        send_1[:, at] = dot_nn(att[...], flat(wo, at)).astype(BF16)
        crossing(0, i, send_1, recv_1).start()

    for copy in loads[0:2]:
        copy.wait()
    for i in range(4):
        crossing(0, i, send_1, recv_1).wait_recv()

    @pl.loop(0, tokens // step)
    def _(i):
        at = strip(i, step)
        value = x[at, :].astype(F32) + (send_1[at, :].astype(F32) + recv_1[at, :].astype(F32))
        x2[at, :] = value
        r = lax.rsqrt(jnp.mean(value * value, axis=-1, keepdims=True) + EPSILON)
        h2[at, :] = (value * r * gain_row[0:1, :]).astype(BF16)

    @pl.loop(0, gate.shape[1] // 512)
    def _(i):
        at = strip(i, 512)
        gate[:, at] = dot_nn(h2[...], flat(wg, at))

    ends[0].finish()

    @pl.loop(0, gate.shape[1] // 512)
    def _(i):
        at = strip(i, 512)
        a = gate[:, at]
        b = dot_nn(h2[...], flat(wu, at))
        up[:, at] = b
        mid[:, at] = (a / (1.0 + jnp.exp(-a)) * b).astype(BF16)

    ends[1].finish()
    loads[2].wait()

    @pl.loop(0, 4)
    def _(i):
        at = strip(i, 256)
        send_2[:, at] = dot_nn(mid[...], flat(wd, at)).astype(BF16)
        crossing(1, i, send_2, recv_2).start()

    factor = 2.0 * loss_scale / count[0:1, 0:1]

    @pl.loop(0, 4)
    def _(i):
        crossing(1, i, send_2, recv_2).wait_recv()
        across = strip(i, 256)

        @pl.loop(0, tokens // 128)
        def _(j):
            at = strip(j, 128)
            value = x2[at, across] + (send_2[at, across].astype(F32) + recv_2[at, across].astype(F32))
            fin[at, across] = value.astype(BF16)
            miss = value - t[at, across].astype(F32)
            weighted = valid[at, 0:1] * miss
            loss_row[0:1, across] += jnp.sum(weighted * miss, axis=0, keepdims=True)
            g = factor * weighted
            g_fin[at, across] = g
            g_dn[at, across] = g.astype(BF16)

    writes = [local.alone(fin.at[pl.ds(pl.multiple_of(k * rows, rows), rows)], output)]
    down_rows = p_down.shape[1]

    s_down = Scatter(me, copies, local, p_down, sc_d)

    def down_part(i):
        p_down[i] = dot_tn(mid[:, strip(i, down_rows)], g_dn[...]).astype(BF16)

    down_part(me.fd)
    s_down.first()

    @pl.loop(1, 4)
    def _(i):
        down_part((me.fd + i) % 4)

    s_down.second()

    @pl.loop(0, 4)
    def _(i):
        at = strip(i, down_rows)
        g = dot_nt(g_dn[...], wd[i])
        a, b = gate[:, at], up[:, at]
        s = 1.0 / (1.0 + jnp.exp(-a))
        g_gate[:, at] = (g * b * s * (1.0 + a * (1.0 - s))).astype(BF16)
        g_up[:, at] = (g * a * s).astype(BF16)

    @pl.loop(0, 4)
    def _(i):
        at = strip(i, 256)
        send_3[:, at] = (dot_nt(g_gate[...], wg[i]) + dot_nt(g_up[...], wu[i])).astype(BF16)
        crossing(2, i, send_3, recv_3).start()

    for i in range(4):
        crossing(2, i, send_3, recv_3).wait_recv()

    @pl.loop(0, tokens // step)
    def _(i):
        at = strip(i, step)
        g = send_3[at, :].astype(F32) + recv_3[at, :].astype(F32)
        value = x2[at, :]
        r = lax.rsqrt(jnp.mean(value * value, axis=-1, keepdims=True) + EPSILON)
        n = value * r
        gain_sum[0:1, :] += jnp.sum(g * n, axis=0, keepdims=True)
        g = g * gain_row[0:1, :]
        g = g_fin[at, :] + r * (g - n * jnp.mean(g * n, axis=-1, keepdims=True))
        g_fin[at, :] = g
        g_a[at, :] = g.astype(BF16)

    writes.append(local.alone(g_fin.at[pl.ds(pl.multiple_of(k * rows, rows), rows)], g_x2_own))
    go_base = copies.take(4)
    go_sends = []
    for turn in (2, 1, 3, 0):
        to, partner = me.along_z(turn)
        at = strip(to, 256)
        g_ob[:, at] = dot_nt(g_a[...], wo[to]).astype(BF16)
        place = g_out.at[pl.ds(pl.multiple_of(z * tokens, tokens), tokens)]
        if turn:
            go_sends.append(
                pltpu.make_async_remote_copy(
                    src_ref=g_ob.at[:, at], dst_ref=place, send_sem=send.at[go_base + to],
                    recv_sem=recv.at[go_base + z], device_id=partner, device_id_type=MESH,
                )
            )
            go_sends[-1].start()
        else:
            writes.append(local.alone(g_ob.at[:, at], place))
    s_down.relay()

    @pl.loop(0, 4)
    def _(i):
        p_g[i] = dot_tn(h2[:, strip(i, 256)], g_gate[...]).astype(BF16)

    s_gate = Scatter(me, copies, local, p_g, sc_g)
    s_gate.first()
    s_gate.load_fwd()
    writes.append(local.alone(p_g, p_gate))

    @pl.loop(0, 4)
    def _(i):
        p_u[i] = dot_tn(h2[:, strip(i, 256)], g_up[...]).astype(BF16)

    writes.append(local.alone(p_u, p_up))

    @pl.loop(0, 4)
    def _(i):
        p_o[i] = dot_tn(att[:, strip(i, 256)], g_a[...]).astype(BF16)

    writes.append(local.alone(p_o, p_out))
    for j in range(8):
        small[j + 8 : j + 9, :] = 0.5 * gain_sum[0:1, pl.ds(j * 128, 128)]
        small[18:19, :] += 0.5 * loss_row[0:1, pl.ds(j * 128, 128)]
    s_down.finish(sum_d.at[0], sum_d.at[1])
    writes.append(local.alone(sum_d, down_sum))
    s_gate.sum_fwd()
    writes.append(local.alone(sc_g.at[0:2], gate_pass))
    for copy in writes:
        copy.wait()
    for turn in (1, 2, 3):
        other, partner = me.along_z(turn)
        place = g_out.at[pl.ds(pl.multiple_of(other * tokens, tokens), tokens)]
        pltpu.make_async_remote_copy(
            src_ref=place, dst_ref=place, send_sem=send.at[go_base + other],
            recv_sem=recv.at[go_base + other], device_id=partner, device_id_type=MESH,
        ).wait_recv()
    for copy in go_sends:
        copy.wait_send()
    for which, src, dst in ((0, send_1, recv_1), (1, send_2, recv_2), (2, send_3, recv_3)):
        for i in range(4):
            crossing(which, i, src, dst).wait_send()
    s_down.drain()
    s_gate.d_x.wait_send()
    s_gate.d_y.wait_send()


def middle(att, wo, wo_more, wg, wu, wd, x, t, misc_all, gains_all, count, loss_scale):
    tokens, width = att.shape
    rows = tokens // 2
    hidden = wg.shape[2]

    def bf(*dims):
        return pltpu.VMEM(dims, BF16)

    def held(a):
        return pltpu.VMEM(a.shape, a.dtype)

    def wide(*dims):
        return pltpu.VMEM(dims, F32)

    p_down, p_gate, p_out = (4, hidden // 4, width), (4, width // 4, hidden), (4, width // 4, width)
    return transfer(
        partial(kernel_middle, loss_scale=loss_scale), "middle", 3,
        (att, wo, wo_more, wg, wu, wd, x.reshape(tokens, width), t.reshape(tokens, width), misc_all, gains_all, count),
        [HBM] * 8 + [VM] * 3,
        [
            shape((rows, width), BF16), shape((4 * tokens, width // 4), BF16),
            shape(p_gate, BF16), shape(p_gate, BF16), shape(p_out, BF16),
            shape((2, hidden // 8, width), BF16), shape((2, width // 8, hidden), BF16),
            shape((rows, width), F32), shape((24, 128), F32),
        ],
        [HBM] * 8 + [VM],
        [held(att), bf(wo.shape[0], 2 * wo.shape[1], width)] + [held(a) for a in (wg, wu, wd)]
        + [bf(tokens, width)] * 2
        + [wide(tokens, width), bf(tokens, width), wide(tokens, hidden), wide(tokens, hidden)]
        + [bf(tokens, hidden)] * 3
        + [bf(tokens, width), wide(tokens, width), bf(tokens, width), bf(tokens, width)]
        + [bf(tokens, width)] * 6
        + [bf(*p_down), bf(*p_gate), bf(*p_gate), bf(*p_out), bf(tokens, width)]
        + [bf(10, hidden // 8, width), bf(2, hidden // 8, width), bf(4, width // 8, hidden)]
        + [wide(8, width), wide(tokens, 128), wide(8, width), wide(8, width)],
        12 + 6 + 4 + 6 + 4, 4 + 5 + 6 + 9 + 4 + 2,
    )


def head_back(g, u, cosine, sine, gain):
    g = g * cosine + half_turn(g * sine)
    r = head_norm(u)
    n = u * r
    g_gain = jnp.sum(g * n, axis=0, keepdims=True)
    g = g * gain
    return r * (g - n * jnp.mean(g * n, axis=-1, keepdims=True)), g_gain


def kernel_backward(
    g_o, gate_pass, down_sum, p_gate, p_up, p_out,
    qkv_in, att_in, lse_in, proj_in, cos_in, sin_in, h_in, w_in,
    x_in, g_x2_in, gains_all, small,
    down_tot, gate_tot, up_tot, out_tot, head_out, grad_out, small_tot,
    g_out, qkv, att, lse, proj, cosines, sines, h_all, w_head, g_proj, g_k, g_v, p_head,
    head_tot, x, g_x2, grad_in, gh_send, gh_sib, gh_own, gh_in, gain_row, work, plane, pair, line,
    sc_g, sc_u, sc_o, sc_h, own_d, own_g, own_u, own_o, line_d, line_g, line_u, line_o,
    send, recv, lsem,
):
    me = Place()
    z, k, f, c = me.z, me.k, me.f, me.c
    rows = x.shape[0]
    block = 2 * rows
    greet([me.xp, me.yp, me.dp, me.sib] + [me.along_z(step)[1] for step in (1, 2, 3)])
    copies, local = Copies(send, recv), Locals(lsem)
    size, q_size = HEAD_SIZE, GROUP * HEAD_SIZE

    own_down = local.alone(down_sum, own_d)
    s_gate = Scatter(me, copies, local, p_gate, sc_g)
    s_gate.load_passed(gate_pass)
    for src, dst in ((g_o, g_out), (qkv_in, qkv), (att_in, att), (lse_in, lse), (proj_in, proj), (cos_in, cosines), (sin_in, sines)):
        local(src, dst)
    late = [local.alone(w_in, w_head), local.alone(x_in, x), local.alone(g_x2_in, g_x2)]
    h_base = local.take(4)

    def h_load(i):
        columns = pl.ds(pl.multiple_of(i * rows, rows), rows)
        return pltpu.make_async_copy(h_in.at[:, columns], h_all.at[i % 2], lsem.at[h_base + i])

    h_load(0).start()
    h_load(1).start()
    s_up = Scatter(me, copies, local, p_up, sc_u)
    s_out = Scatter(me, copies, local, p_out, sc_o)
    s_head = Scatter(me, copies, local, p_head, sc_h)
    s_gate.resume()
    lines = [
        LineSum(me, copies, own, bufs)
        for own, bufs in ((own_d, line_d), (own_g, line_g), (own_u, line_u), (own_o, line_o))
    ]
    l_down, l_gate, l_up, l_out = lines
    totals = (down_tot, gate_tot, up_tot, out_tot)
    swap_base = copies.take(8)
    swaps, writes = [], []

    def finish(i):
        lines[i].arrive()
        half = lines[i].total.shape[1]
        for j in range(2):
            dst = totals[i].at[k, pl.ds(j * half, half)]
            copy = copies.at(swap_base + 2 * i + j, lines[i].total.at[j], dst, me.sib)
            copy.start()
            swaps.append(copy)
            writes.append(local.alone(lines[i].total.at[j], dst))

    def scattered(scatter, entry, own):
        scatter.finish(own.at[0], own.at[1])
        entry.start()

    own_down.wait()
    l_down.start()
    work[...] = small[...]
    for i in range(4):
        for r in range(2):
            gain_row[0:1, pl.ds((2 * i + r) * 128, 128)] = gains_all[i, r : r + 1, :]
    gain_q = (gains_all[0, 4:5, :] + gains_all[1, 4:5, :]) + (gains_all[2, 4:5, :] + gains_all[3, 4:5, :])
    gain_k = (gains_all[0, 5:6, :] + gains_all[1, 5:6, :]) + (gains_all[2, 5:6, :] + gains_all[3, 5:6, :])
    k_at = pl.ds(q_size, size)
    v_at = pl.ds(q_size + size, size)
    g_k[...] = jnp.zeros_like(g_k)
    g_v[...] = jnp.zeros_like(g_v)
    key = lax.broadcasted_iota(jnp.int32, (block, block), 0)
    query = lax.broadcasted_iota(jnp.int32, (block, block), 1)
    def queries(i):
        at = pl.ds(pl.multiple_of(i * block, block), block)
        for g in range(GROUP):
            head = pl.ds(g * size, size)
            q = qkv[at, head]
            go = g_out[at, head]
            product = go.astype(F32) * att[at, head].astype(F32)
            delta = dot_nt(jnp.ones((8, size), F32), product, precision=HIGHEST)[0:1, :]
            log_sum = lse[g, 0:1, at] * LOG2_E

            def part(keys, masked, q=q, go=go, delta=delta, log_sum=log_sum):
                kk, vv = qkv[keys, k_at], qkv[keys, v_at]
                p = jnp.exp2(dot_nt(kk, q) * (SCALE * LOG2_E) - log_sum)
                if masked:
                    p = jnp.where(key <= query, p, 0.0)
                gs = (p * (dot_nt(vv, go) - delta)).astype(BF16)
                g_v[keys, :] += dot_nn(p.astype(BF16), go)
                g_k[keys, :] += dot_nn(gs, q)
                return dot_tn(gs, kk)

            def step(j, acc, part=part):
                return acc + part(pl.ds(pl.multiple_of(j * block, block), block), False)

            acc = lax.fori_loop(0, i, step, jnp.zeros((block, size), F32))
            acc = (acc + part(at, True)) * SCALE
            g_u, g_gain = head_back(acc, proj[at, head], cosines[at, :], sines[at, :], gain_q)
            g_proj[at, head] = g_u.astype(BF16)
            work[16:17, :] += g_gain

    sib_base, right_base, left_base = copies.take(4), copies.take(4), copies.take(4)
    last = (z == 0) | (z == 3)
    inner = (z == 1) | (z == 2)

    def input_part(to, mine, dst):
        at = pl.ds(pl.multiple_of((2 * to + mine) * rows, rows), rows)
        weights = w_head[...].reshape(w_head.shape[0] * w_head.shape[1], w_head.shape[2])
        dst[...] = dot_nt(g_proj[at, :], weights).astype(BF16)

    def crossing(to):
        return copies.at(sib_base + to, gh_send.at[to], gh_sib.at[to], me.sib)

    def rightward(to):
        return copies.at(right_base + to, gh_own.at[to], gh_in.at[to], (f, c + 2))

    def leftward(to):
        there = 1 - (z - to) // 2
        place = gh_in.at[to + (4 - to) * there]
        return copies.at(left_base + to, gh_own.at[to], place, (f, c - 2))

    def onward(to):
        @pl.when(to > z)
        def _():
            rightward(to).start()

        @pl.when(to < z)
        def _():
            leftward(to).start()

    def join(to):
        crossing(to).wait_recv()
        add_rows(gh_own.at[to], [gh_own.at[to], gh_sib.at[to]])

    def end_send(order):
        @pl.when(last)
        def _():
            onward(far_first(order))

    def inner_send(order):
        @pl.when(inner)
        def _():
            to = far_first(order)

            @pl.when(to > z)
            def _():
                rightward(to).wait_recv()

            @pl.when(to < z)
            def _():
                copies.at(left_base + to, gh_own.at[to], gh_in.at[to], (f, c - 2)).wait_recv()

            add_rows(gh_own.at[to], [gh_own.at[to], gh_in.at[to]])
            onward(to)

    def far_first(order):
        return order + (3 - 2 * order) * (z // 2)

    def parts_to(to):
        input_part(to, 1 - k, gh_send.at[to])
        crossing(to).start()
        input_part(to, k, gh_own.at[to])

    spread = Spread(me, copies, head_tot)
    total = SmallSum(me, copies, work, plane, pair, line)
    local.wait()
    for copy in late:
        copy.wait()
    s_up.first()
    s_up.second()
    queries(1)
    l_down.meet()
    queries(3)
    l_down.close()
    s_gate.finish_resumed(own_g.at[0], own_g.at[1])
    l_gate.start()
    queries(2)
    l_gate.meet()
    l_down.spread()
    queries(0)

    @pl.loop(0, 4)
    def _(i):
        at = pl.ds(pl.multiple_of(i * block, block), block)
        g_u, g_gain = head_back(g_k[at, :] * SCALE, proj[at, k_at], cosines[at, :], sines[at, :], gain_k)
        g_proj[at, k_at] = g_u.astype(BF16)
        g_proj[at, v_at] = g_v[at, :].astype(BF16)
        work[17:18, :] += g_gain

    parts_to(far_first(3))
    s_up.relay()

    @pl.loop(0, 4)
    def _(i):
        h_load(i).wait()
        product = dot_tn(h_all[i % 2], g_proj[...])
        p_head[i] = product.astype(BF16)
        with_weights = product * w_head[i].astype(F32)
        sums = dot_nt(jnp.ones((8, with_weights.shape[1]), F32), with_weights, precision=HIGHEST)[0:1, :]
        sums = sums / gain_row[0:1, pl.ds(pl.multiple_of(i * rows, rows), rows)]
        for j in range(2):
            work[pl.ds(2 * i + j, 1), :] = sums[:, j * 128 : (j + 1) * 128]

        @pl.when(i < 2)
        def _():
            h_load(i + 2).start()

    l_gate.close()
    s_head.first()
    s_head.second()
    parts_to(far_first(1))
    parts_to(far_first(0))
    join(far_first(3))
    total.first()
    end_send(3)
    l_gate.spread()
    s_head.relay()
    inner_send(3)
    scattered(s_up, l_up, own_u)
    s_out.first()
    s_out.second()
    join(far_first(0))
    s_head.finish(head_tot.at[c, 0], head_tot.at[c, 1])
    spread.start()
    parts_to(far_first(2))
    inner_send(0)
    l_up.meet()
    s_out.relay()
    scattered(s_out, l_out, own_o)
    spread.step(1)
    l_up.close()
    finish(0)
    finish(1)
    l_out.meet()
    l_up.spread()
    l_out.close()
    join(far_first(2))
    l_out.spread()
    end_send(2)
    inner_send(2)
    join(far_first(1))
    spread.step(2)
    finish(2)
    total.second()
    total.third()
    end_send(1)
    finish(3)

    @pl.when(z > 0)
    def _():
        rightward(z).wait_recv()

    @pl.when(z < 3)
    def _():
        copies.at(left_base + z, gh_own.at[z], gh_in.at[4], (f, c - 2)).wait_recv()

    @pl.when(z == 0)
    def _():
        gh_in[0] = jnp.zeros(gh_in.shape[1:], BF16)

    @pl.when(z == 3)
    def _():
        gh_in[4] = jnp.zeros(gh_in.shape[1:], BF16)

    @pl.loop(0, rows // 64)
    def _(i):
        at = pl.ds(pl.multiple_of(i * 64, 64), 64)
        g = gh_own[z, at, :].astype(F32) + gh_in[z, at, :].astype(F32) + gh_in[4, at, :].astype(F32)
        xin = x[at, :].astype(F32)
        r = lax.rsqrt(jnp.mean(xin * xin, axis=-1, keepdims=True) + EPSILON)
        n = xin * r
        g = g * gain_row[0:1, :]
        grad_in[at, :] = g_x2[at, :] + r * (g - n * jnp.mean(g * n, axis=-1, keepdims=True))

    writes.append(local.alone(grad_in, grad_out))


    spread.step(3)
    total.finish(small_tot)
    for hop in range(4):
        spread.crossed(hop)
    writes.append(local.alone(head_tot, head_out))
    for i in range(4):
        crossing(i).wait_send()

        @pl.when(i > z)
        def _(i=i):
            rightward(i).wait_send()

        @pl.when(i < z)
        def _(i=i):
            leftward(i).wait_send()

    spread.drain()
    total.drain()
    s_gate.drain_resumed()
    for scatter in (s_up, s_out, s_head):
        scatter.drain()
    for entry in lines:
        entry.drain()
    for copy in swaps:
        copy.wait()
    for copy in writes:
        copy.wait()


def backward(g_o, gate_pass, parts, saved, x, g_x2, gains_all, small):
    rows, width = x.shape
    tokens = 8 * rows
    sizes = [(2 * parts[0].shape[1], width)] + [p.shape[1:] for p in parts[1:]]
    head = (width // 4, HEAD_COLUMNS)

    def held(a):
        return pltpu.VMEM(a.shape, a.dtype)

    pieces = pltpu.VMEM((4, rows, width), BF16)
    scatters = [pltpu.VMEM((10, r // 2, n), BF16) for r, n in sizes[1:] + [head]]
    own = [pltpu.VMEM((2, r // 2, n), BF16) for r, n in sizes]
    line = [pltpu.VMEM((5, r // 2, n), BF16) for r, n in sizes]
    return transfer(
        kernel_backward, "backward", 2,
        (g_o, gate_pass) + tuple(parts) + tuple(saved) + (x, g_x2, gains_all, small),
        [HBM] * 16 + [VM] * 2,
        [shape((2,) + s, BF16) for s in sizes]
        + [
            shape((8, 2, head[0] // 2, head[1]), BF16),
            shape((rows, width), F32),
            shape(small.shape, F32),
        ],
        [HBM] * 6 + [VM],
        [pltpu.VMEM((tokens, GROUP * HEAD_SIZE), BF16)]
        + [held(a) for a in saved[:6]]
        + [pltpu.VMEM((2, tokens, rows), BF16), held(saved[7])]
        + [
            pltpu.VMEM((tokens, HEAD_COLUMNS), BF16),
            pltpu.VMEM((tokens, HEAD_SIZE), F32),
            pltpu.VMEM((tokens, HEAD_SIZE), F32),
            pltpu.VMEM((4,) + head, BF16),
            pltpu.VMEM((8, 2, head[0] // 2, head[1]), BF16),
            held(x), held(g_x2), pltpu.VMEM((rows, width), F32),
            pieces, pieces, pieces, pltpu.VMEM((5, rows, width), BF16),
            pltpu.VMEM((8, width), F32),
            pltpu.VMEM(small.shape, F32),
            pltpu.VMEM((4,) + small.shape, F32),
            pltpu.VMEM((2,) + small.shape, F32),
            pltpu.VMEM((4,) + small.shape, F32),
        ]
        + scatters + own + line,
        24 + 32 + 8 + 12 + 7 + 13, 7 + 4 + 1 + 1 + 16 + 8 + 2 + 4,
    )


def chip_step(
    hidden_in, teacher, valid, positions, norm_attn, w_query, key_projection, value_projection,
    gain_query, gain_key, w_out, norm_mlp, w_gate, w_up, w_down,
):
    rows = hidden_in.shape[1]
    width = hidden_in.shape[2]
    half_width = HEAD_SIZE // 2
    freq = 1000000.0 ** (-2.0 * np.arange(half_width) / HEAD_SIZE)
    freq = np.broadcast_to(np.concatenate([freq, freq]), (8, HEAD_SIZE)).astype(np.float32)
    (
        x_pair, t_pair, misc_all, gains_all, count, w_head, wo, wo_more, wg, wu, wd,
        h_all, proj, qkv, att, lse, cosines, sines, att_all,
    ) = forward(
        w_query, key_projection, value_projection, w_out, w_gate, w_up, w_down,
        hidden_in[0], teacher[0], positions, valid, norm_attn, norm_mlp, gain_query, gain_key, freq,
    )
    loss_scale = rows * lax.axis_size("ctx") * lax.axis_size("fsdp") / 4.0
    output, g_o, p_gate, p_up, p_out, s_down, gate_pass, g_x2, small = middle(
        att_all, wo, wo_more, wg, wu, wd, x_pair, t_pair, misc_all, gains_all, count, loss_scale
    )
    down, gate, up, out, heads, grad_input, small = backward(
        g_o, gate_pass, (s_down, p_gate, p_up, p_out),
        (qkv, att, lse, proj, cosines, sines, h_all, w_head),
        hidden_in[0], g_x2, gains_all, small,
    )

    g_gate, g_up, g_q, g_k, g_v, g_down, g_out, g_norm_a, g_norm_m, g_gain_q, g_gain_k, loss, output, grad_input = assemble(
        gate, up, heads.reshape(8, -1, HEAD_COLUMNS), down, out, small, count, output, grad_input
    )
    return (
        output[None],
        loss.reshape(()),
        grad_input[None],
        g_norm_a.reshape(-1),
        g_q,
        g_k,
        g_v,
        g_gain_q.reshape(-1),
        g_gain_k.reshape(-1),
        g_out.reshape(-1, width),
        g_norm_m.reshape(-1),
        g_gate,
        g_up,
        g_down.reshape(-1, width),
    )


def solution(mesh):
    chips = mesh.shape["fsdp"] == 4 and mesh.shape["ctx"] == KEY_VALUE_HEADS
    return jax.shard_map(
        chip_step if chips else per_device,
        mesh=mesh,
        in_specs=(
            P("fsdp", "ctx", None),
            P("fsdp", "ctx", None),
            P("fsdp", "ctx"),
            P("fsdp", "ctx"),
            P("fsdp"),
            P("fsdp", None),
            P("fsdp", None),
            P("fsdp", None),
            P("fsdp"),
            P("fsdp"),
            P("fsdp", None),
            P("fsdp"),
            P("fsdp", None),
            P("fsdp", None),
            P("fsdp", None),
        ),
        out_specs=(
            P("fsdp", "ctx", None),
            P(),
            P("fsdp", "ctx", None),
            P("fsdp"),
            P("fsdp", None),
            P("fsdp", None),
            P("fsdp", None),
            P("fsdp"),
            P("fsdp"),
            P("fsdp", None),
            P("fsdp"),
            P("fsdp", None),
            P("fsdp", None),
            P("fsdp", None),
        ),
        check_vma=False,
    )
```
